32 devices in a mesh: band: 4 (over x, core), dom: 8 (over z, y).
Axes of the slice: x: 2, y: 2, z: 4, core: 2. Of those that a mesh axis runs over, the one named last changes fastest.
Arguments:
- orbitals: float32 [32, 32, 48, 512], P('dom', None, None, 'band'), may hold values from -6 to 6
- potential: float32 [32, 32, 48], P('dom'), may hold values from -1 to 2
- projectors: float32 [64, 4, 4608], P('dom'), may hold values from -0.09375 to 0.09375
- coupling: float32 [64, 4, 4], P('dom'), may hold values from -4 to 4
- atom_plane: int32 [64], P('dom'), may hold values from 0 to 31, as said below
- projector_count: int32 [64], P('dom'), may hold values from 1 to 4
Outputs:
- filtered: float32 [32, 32, 48, 512], P('dom', None, None, 'band')
- gram: float32 [512, 512], replicated
The draws below stay inside these ranges and needn't reach their ends.
Inputs may be any that keep to these rules, and one draw needn't show every extreme that they name: `atom_plane`: atom a's first plane lies among the 4 planes of dom index a // 8, that is from (a // 8) * 4 to (a // 8) * 4 + 3; the last atom of each dom index starts on that index's last plane.
All inputs are finite; a program needn't handle non-finite values.
Results may differ from the reference program's by a relative error of at most 0.0003.
Values sent between devices are 32-bit elements; how exact they have to be, the bound alone decides.
No kernel may reach another device: no remote copies, remote signals or barrier semaphores. Data moves between devices by JAX's collectives and lax.ppermute only.
A program may use at most 192 MiB of HBM per device.

```python
import jax
import jax.numpy as jnp
from jax import lax

NORB = 512
CX = 4
NY = 32
NZ = 48
SPAN = 3
MAXPROJ = 4
ATOM_DEV = 8
ATOMS = 64
NX = 32


def draw_atom_plane(key, part):
    key = jax.random.fold_in(key, 11)
    atom_ids = jnp.arange(ATOMS, dtype=jnp.int32)
    owners = atom_ids // ATOM_DEV
    offsets = jax.random.randint(key, (ATOMS,), 0, CX, dtype=jnp.int32)
    is_last = atom_ids % ATOM_DEV == ATOM_DEV - 1
    offsets = jnp.where(is_last, CX - 1, offsets)
    offsets = offsets.at[0].set(0)
    return owners * CX + offsets


def draw_projector_count(key, part):
    key = jax.random.fold_in(key, 23)
    counts = jax.random.randint(key, (ATOMS,), 1, MAXPROJ + 1, dtype=jnp.int32)
    return counts.at[0].set(MAXPROJ).at[1].set(1)


def block_levels(key, extent, cuts, smallest, top_value):
    factor_of, own = 1.0, jax.random.fold_in(key, 6)
    for axis_at, parts in cuts:
        heights = jnp.exp(jax.random.uniform(jax.random.fold_in(own, axis_at), (parts,), jnp.float32, smallest / len(cuts), top_value / len(cuts)))
        factor_of = factor_of * jnp.repeat(heights, extent[axis_at] // parts).reshape([-1 if axis == axis_at else 1 for axis in range(len(extent))])
    return factor_of


def centred(stream_key, extent, scale, bound, pieces=(), kind=jnp.bfloat16):
    result = scale * jax.random.normal(stream_key, extent, jnp.float32)
    if pieces:
        result = result * block_levels(stream_key, extent, pieces, -0.22, 0.18)
    return jnp.clip(result, -bound, bound).astype(kind)


def setup_inputs(seed: int = 0) -> dict:
    streams_of = jax.random.split(jax.random.key(seed), 7)
    return {
        "orbitals": centred(streams_of[0], (NX, NY, NZ, NORB), 1.0, 6.0, ((0, 8), (3, 4)), jnp.float32),
        "potential": jnp.clip(-1.0 + 3.0 * jax.random.uniform(streams_of[1], (NX, NY, NZ), jnp.float32) ** block_levels(streams_of[1], (NX, NY, NZ), ((0, 8),), -0.2, 0.2), -1.0, 2.0),
        "projectors": centred(streams_of[2], (ATOMS, MAXPROJ, SPAN * NY * NZ), (SPAN * NY * NZ) ** -0.5, 0.09375, ((0, 8),), jnp.float32),
        "coupling": centred(streams_of[3], (ATOMS, MAXPROJ, MAXPROJ), 1.0, 4.0, ((0, 8),), jnp.float32),
        "atom_plane": draw_atom_plane(jax.random.fold_in(streams_of[6], 71), 0),
        "projector_count": draw_projector_count(jax.random.fold_in(streams_of[6], 71), 0),
    }


center_weight = -205.0 / 72.0
side_weights = (8.0 / 5.0, -1.0 / 5.0, 8.0 / 315.0, -1.0 / 560.0)
HIGH = lax.Precision.HIGHEST

def laplacian(orbital_field):
    total = 3.0 * center_weight * orbital_field
    for offset in range(1, 5):
        weight = side_weights[offset - 1]
        for axis_number in range(3):
            total = total + weight * (jnp.roll(orbital_field, offset, axis_number) + jnp.roll(orbital_field, -offset, axis_number))
    return total

def nonlocal_term(orbital_field, projectors, coupling, atom_plane, projector_count):
    padded = jnp.concatenate([orbital_field, orbital_field[:SPAN - 1]], axis=0)
    slots = jnp.arange(MAXPROJ, dtype=jnp.int32)

    def one_atom(accumulated, inputs):
        beta, couple, first_plane, count = inputs
        live_mask = (slots < count).astype(jnp.float32)
        window_cells = lax.dynamic_slice_in_dim(padded, first_plane.astype(jnp.int32), SPAN, 0).reshape(SPAN * NY * NZ, NORB)
        correlations = jnp.dot(beta.astype(jnp.float32), window_cells.astype(jnp.float32), precision=HIGH, preferred_element_type=jnp.float32) * live_mask[:, None]
        sym_coupling = 0.5 * (couple + couple.T)
        weighted = jnp.dot(sym_coupling.astype(jnp.float32), correlations.astype(jnp.float32), precision=HIGH, preferred_element_type=jnp.float32) * live_mask[:, None]
        added = jnp.dot(beta.T.astype(jnp.float32), weighted.astype(jnp.float32), precision=HIGH, preferred_element_type=jnp.float32).reshape(SPAN, NY, NZ, NORB)
        current = lax.dynamic_slice_in_dim(accumulated, first_plane.astype(jnp.int32), SPAN, 0)
        accumulated = lax.dynamic_update_slice_in_dim(accumulated, current + added, first_plane.astype(jnp.int32), 0)
        return (accumulated, None)
    accumulated, _ = lax.scan(one_atom, jnp.zeros_like(padded), (projectors, coupling, atom_plane, projector_count))
    head = accumulated[:SPAN - 1] + accumulated[NX:]
    return jnp.concatenate([head, accumulated[SPAN - 1:NX]], axis=0)

def hamiltonian(orbital_field, potential, projectors, coupling, atom_plane, projector_count):
    return -0.5 * laplacian(orbital_field) + potential[:, :, :, None] * orbital_field + nonlocal_term(orbital_field, projectors, coupling, atom_plane, projector_count)

def reference(orbitals, potential, projectors, coupling, atom_plane, projector_count):
    extra = (potential, projectors, coupling, atom_plane, projector_count)
    first = (hamiltonian(orbitals, *extra) - 7.0 * orbitals) / 6.0
    second = 2.0 * (hamiltonian(first, *extra) - 7.0 * first) / 6.0 - orbitals
    flat = second.reshape(NX * NY * NZ, NORB)
    gram = jnp.dot(flat.T.astype(jnp.float32), flat.astype(jnp.float32), precision=HIGH, preferred_element_type=jnp.float32) * (1.0 / (NX * NY * NZ))
    lower = jnp.linalg.cholesky(gram)
    inverse = jax.scipy.linalg.solve_triangular(lower, jnp.eye(NORB, dtype=jnp.float32), lower=True)
    filtered = jnp.dot(flat.astype(jnp.float32), inverse.T.astype(jnp.float32), precision=HIGH, preferred_element_type=jnp.float32)
    return (filtered.reshape(NX, NY, NZ, NORB), gram)
```

```python
import functools

import jax
import jax.numpy as jnp
from jax import lax
from jax.experimental import pallas as pl
from jax.experimental.pallas import tpu as pltpu
from jax.sharding import PartitionSpec as P

SPAN = 3
MAXPROJ = 4
PAD = 8
LANES = 128

center_weight = -205.0 / 72.0
side_weights = (8.0 / 5.0, -1.0 / 5.0, 8.0 / 315.0, -1.0 / 560.0)
HIGH = lax.Precision.HIGH
VMEM_LIMIT = 60 * 1024 * 1024


def halves(value):
    high = value.astype(jnp.bfloat16)
    return high, (value - high.astype(jnp.float32)).astype(jnp.bfloat16)


def dot3(left, right):
    dot = functools.partial(jnp.dot, preferred_element_type=jnp.float32)
    return dot(left[0], right[0]) + (dot(left[0], right[1]) + dot(left[1], right[0]))


def swapped(blocks, lane):
    count = len(blocks)
    width = LANES // count
    blocks = list(blocks)
    bit = 1
    while bit < count:
        clear = (lane // (bit * width)) % 2 == 0
        for low in range(count):
            if low & bit:
                continue
            first, second = blocks[low], blocks[low | bit]
            blocks[low] = jnp.where(clear, first, pltpu.roll(second, bit * width, 1))
            blocks[low | bit] = jnp.where(clear, pltpu.roll(first, LANES - bit * width, 1), second)
        bit *= 2
    return blocks


def swap_kernel(count, rows, in_ref, out_ref):
    lane = lax.broadcasted_iota(jnp.int32, (8, LANES), 1)

    def step(tile, carry):
        at = pl.ds(pl.multiple_of(tile * 8, 8), 8)
        in_blocks = [in_ref[index, at, :] for index in range(count)]
        for index, block in enumerate(swapped(in_blocks, lane)):
            out_ref[index, at, :] = block
        return carry

    lax.fori_loop(0, rows // 8, step, 0)


def swap_blocks(value, planes_first_in, planes_first_out):
    planes, count = value.shape[:2] if planes_first_in else value.shape[1::-1]
    rows = value.shape[2]

    def spec(planes_first):
        if planes_first:
            return pl.BlockSpec((None, count, rows, LANES), lambda p: (p, 0, 0, 0))
        return pl.BlockSpec((count, None, rows, LANES), lambda p: (0, p, 0, 0))

    lead = (planes, count) if planes_first_out else (count, planes)
    return pl.pallas_call(
        functools.partial(swap_kernel, count, rows),
        grid=(planes,),
        in_specs=[spec(planes_first_in)],
        out_specs=spec(planes_first_out),
        out_shape=jax.ShapeDtypeStruct((*lead, rows, LANES), jnp.float32),
        compiler_params=pltpu.CompilerParams(vmem_limit_bytes=VMEM_LIMIT),
    )(value)


def nonlocal_into(field, near, projector, coupling_ref, mask_ref, planes, width):
    inner = outer = None
    for plane in range(planes):
        parts = halves(field(plane))
        term = dot3(projector(plane), parts)
        inner = term if inner is None else inner + term
        if plane < SPAN - 1:
            term = dot3(projector(planes + plane), parts)
            outer = term if outer is None else outer + term
    correlations = (inner + pltpu.roll(outer, LANES - width, 1)) * mask_ref[...]
    weighted = dot3(halves(coupling_ref[...]), halves(correlations))
    moved = pltpu.roll(weighted, width, 1)
    here, next_block = halves(weighted.T), halves(moved.T)
    for plane in range(planes):
        total = dot3(here, projector(plane))
        if plane < SPAN - 1:
            total = total + dot3(next_block, projector(planes + plane))
        near[plane] = total.T


def filter_kernel(planes, side_y, side_z, width, field_ref, potential_ref, high_ref, low_ref, coupling_ref, mask_ref, out_ref, padded, first, near, *staged):
    cells = side_y * side_z
    tile = 16

    def projector(plane):
        at = pl.ds(plane * cells, cells)
        if not staged:
            return high_ref[:, at], low_ref[:, at]
        high_buffer, low_buffer, sems = staged
        copies = [
            pltpu.make_async_copy(high_ref.at[:, at], high_buffer, sems.at[0]),
            pltpu.make_async_copy(low_ref.at[:, at], low_buffer, sems.at[1]),
        ]
        for copy in copies:
            copy.start()
        for copy in copies:
            copy.wait()
        return high_buffer[...], low_buffer[...]

    def fill(y, carry):
        for plane in range(planes):
            row = field_ref[plane, pl.ds(pl.multiple_of(y * side_z, 8), side_z), :]
            padded[plane, y, pl.ds(PAD, side_z), :] = row
            padded[plane, y, pl.ds(PAD - 4, 4), :] = row[side_z - 4 :]
            padded[plane, y, pl.ds(PAD + side_z, 4), :] = row[:4]
        return carry

    lax.fori_loop(0, side_y, fill, 0)

    def apply(source, finish):
        def row(y, carry):
            for start in range(0, side_z, tile):
                def load(plane, y_at, shift):
                    return source[plane, y_at, pl.ds(PAD + start + shift, tile), :]

                inside = [load(plane, y, 0) for plane in range(planes)]
                before = [pltpu.roll(value, width, 1) for value in inside]
                after = [pltpu.roll(value, LANES - width, 1) for value in inside]
                line = before + inside + after
                at = pl.ds(pl.multiple_of(y * side_z + start, 8), tile)
                for plane in range(planes):
                    own = inside[plane]
                    total = (potential_ref[plane, at, :] - 1.5 * center_weight - 7.0) * own + near[plane, at, :]
                    for offset in range(1, 5):
                        around = line[planes + plane + offset] + line[planes + plane - offset]
                        around = around + (load(plane, y, offset) + load(plane, y, -offset))
                        up = lax.rem(y + offset, side_y)
                        down = lax.rem(y + side_y - offset, side_y)
                        around = around + (load(plane, up, 0) + load(plane, down, 0))
                        total = total - (0.5 * side_weights[offset - 1]) * around
                    finish(plane, y, start, at, total)
            return carry

        lax.fori_loop(0, side_y, row, 0)

    common = (projector, coupling_ref, mask_ref, planes, width)
    nonlocal_into(lambda plane: field_ref[plane], near, *common)

    def finish_first(plane, y, start, at, total):
        value = total * (1.0 / 6.0)
        first[plane, y, pl.ds(PAD + start, tile), :] = value
        out_ref[plane, at, :] = value
        if start == 0:
            first[plane, y, pl.ds(PAD + side_z, 4), :] = value[:4]
        if start == side_z - tile:
            first[plane, y, pl.ds(PAD - 4, 4), :] = value[tile - 4 :]

    apply(padded, finish_first)
    nonlocal_into(lambda plane: out_ref[plane], near, *common)

    def finish_second(plane, y, start, at, total):
        out_ref[plane, at, :] = total * (2.0 / 6.0) - field_ref[plane, at, :]

    apply(first, finish_second)


def filter_orbitals(field, potential, high, low, coupling, mask, side_y, side_z, width):
    planes, cells, _ = field.shape
    whole = pl.BlockSpec(memory_space=pltpu.VMEM)
    stay, staged = whole, []
    if high.size > 8 * 1024 * 1024:
        stay = pl.BlockSpec(memory_space=pl.ANY)
        staged = [pltpu.VMEM((high.shape[0], cells), jnp.bfloat16)] * 2 + [pltpu.SemaphoreType.DMA((2,))]
    return pl.pallas_call(
        functools.partial(filter_kernel, planes, side_y, side_z, width),
        in_specs=[whole, whole, stay, stay, whole, whole],
        out_specs=whole,
        out_shape=jax.ShapeDtypeStruct(field.shape, jnp.float32),
        scratch_shapes=[
            pltpu.VMEM((planes, side_y, side_z + 2 * PAD, LANES), jnp.float32),
            pltpu.VMEM((planes, side_y, side_z + 2 * PAD, LANES), jnp.float32),
            pltpu.VMEM((planes, cells, LANES), jnp.float32),
            *staged,
        ],
        compiler_params=pltpu.CompilerParams(vmem_limit_bytes=VMEM_LIMIT),
    )(field, potential, high, low, coupling, mask)


def gathered_projectors(projectors, coupling, atom_plane, projector_count, planes, cells, width):
    bands, blocks = lax.axis_size("band"), lax.axis_size("dom")
    share = projectors.shape[0] // bands
    slots = jnp.arange(MAXPROJ, dtype=jnp.int32)
    live = (slots[None, :] < projector_count[:, None]).astype(jnp.float32)
    coupled = 0.5 * (coupling + jnp.transpose(coupling, (0, 2, 1))) * live[:, :, None] * live[:, None, :]
    offset = (atom_plane - lax.axis_index("dom") * planes).astype(jnp.float32)
    extra = jnp.concatenate(
        [
            coupled,
            jnp.broadcast_to(offset[:, None, None], (*coupled.shape[:2], 1)),
            jnp.zeros((*coupled.shape[:2], LANES - MAXPROJ - 1), jnp.float32),
        ],
        axis=2,
    )
    packed = jnp.concatenate([projectors, extra], axis=2)
    mine = lax.dynamic_slice_in_dim(packed, lax.axis_index("band") * share, share, 0)
    mine = mine.reshape(share * MAXPROJ, -1)
    everyone = lax.all_gather(lax.all_gather(mine, "dom"), "band")
    count = bands * blocks * share * MAXPROJ
    everyone = everyone.reshape(count, -1)
    beta, extra = everyone[:, : SPAN * cells], everyone[:, SPAN * cells :]
    offset = extra[:, MAXPROJ]
    placed = []
    for plane in range(planes + SPAN - 1):
        value = 0.0
        for part in range(SPAN):
            value = value + jnp.where(
                (offset == plane - part)[:, None], beta[:, part * cells : (part + 1) * cells], 0.0
            )
        placed.append(value)
    high, low = halves(jnp.concatenate(placed, axis=1))
    row = jnp.arange(count, dtype=jnp.int32)
    same_atom = row[:, None] // MAXPROJ == row[None, :] // MAXPROJ
    matrix = jnp.where(same_atom, jnp.tile(extra[:, :MAXPROJ], (1, count // MAXPROJ)), 0.0)
    block_of = (row // (share * MAXPROJ)) % blocks
    lanes = jnp.arange(LANES, dtype=jnp.int32) // width
    mask = (block_of[:, None] == lanes[None, :]).astype(jnp.float32)
    return high, low, matrix, mask


def shards(orbitals, potential, projectors, coupling, atom_plane, projector_count):
    planes, side_y, side_z, local_orbs = orbitals.shape
    blocks, bands = lax.axis_size("dom"), lax.axis_size("band")
    cells = side_y * side_z
    rows = cells // blocks
    width = local_orbs // blocks
    norb = local_orbs * bands

    high, low, matrix, mask = gathered_projectors(
        projectors, coupling, atom_plane, projector_count, planes, cells, width
    )
    levels = lax.all_gather(potential.reshape(planes, cells), "dom")
    levels = jnp.transpose(levels, (1, 2, 0))
    levels = jnp.broadcast_to(levels[..., None], (planes, cells, blocks, width)).reshape(planes, cells, LANES)

    packed = swap_blocks(orbitals.reshape(planes, blocks, rows, local_orbs), True, False)
    arrived = lax.all_to_all(packed, "dom", 0, 0, tiled=True)
    field = swap_blocks(arrived, False, True).reshape(planes, cells, LANES)

    second = filter_orbitals(field, levels, high, low, matrix, mask, side_y, side_z, width)

    packed = swap_blocks(second.reshape(planes, blocks, rows, LANES), True, False)
    arrived = lax.all_to_all(packed, "dom", 0, 0, tiled=True)
    own = swap_blocks(arrived, False, True).reshape(planes * cells, local_orbs)

    panels = lax.all_gather(own, "band")
    part = jnp.einsum("co,bcq->obq", own, panels, precision=HIGH, preferred_element_type=jnp.float32)
    own_gram = lax.psum(part.reshape(local_orbs, norb), "dom")
    gram = lax.all_gather(own_gram, "band", axis=0, tiled=True) * (1.0 / (planes * cells * blocks))
    lower = jnp.linalg.cholesky(gram)
    inverse = jax.scipy.linalg.solve_triangular(lower, jnp.eye(norb, dtype=jnp.float32), lower=True)
    own_rows = lax.dynamic_slice_in_dim(inverse, lax.axis_index("band") * local_orbs, local_orbs, 0)
    result = jnp.einsum(
        "bcq,obq->co",
        panels,
        own_rows.reshape(local_orbs, bands, local_orbs),
        precision=HIGH,
        preferred_element_type=jnp.float32,
    )
    return (result.reshape(planes, side_y, side_z, local_orbs), gram)


def solution(mesh):
    placed = (
        P("dom", None, None, "band"),
        P("dom", None, None),
        P("dom", None, None),
        P("dom", None, None),
        P("dom"),
        P("dom"),
    )
    return jax.shard_map(
        shards,
        mesh=mesh,
        in_specs=placed,
        out_specs=(P("dom", None, None, "band"), P()),
        check_vma=False,
    )
```

```python
import functools

import jax
import jax.numpy as jnp
from jax import lax
from jax.experimental import pallas as pl
from jax.experimental.pallas import tpu as pltpu
from jax.sharding import PartitionSpec as P

SPAN = 3
MAXPROJ = 4
PAD = 8
LANES = 128
GROUP = 8

center_weight = -205.0 / 72.0
side_weights = (8.0 / 5.0, -1.0 / 5.0, 8.0 / 315.0, -1.0 / 560.0)
HIGHEST = lax.Precision.HIGHEST
WHOLE = pl.BlockSpec(memory_space=pltpu.VMEM)
PARAMS = pltpu.CompilerParams(vmem_limit_bytes=60 * 1024 * 1024)


def cost(flops, bytes_accessed):
    return pl.CostEstimate(flops=int(flops), bytes_accessed=int(bytes_accessed), transcendentals=0)


def halves(value):
    high = value.astype(jnp.bfloat16)
    return high, (value - high.astype(jnp.float32)).astype(jnp.bfloat16)


def side_by_side(value):
    return jnp.concatenate(halves(value), axis=1)


def dot_halves(left, right):
    dot = functools.partial(jnp.dot, preferred_element_type=jnp.float32)
    return dot(left[0], right) + dot(left[1], right)


def folded(value):
    return value[:, :LANES] + value[:, LANES:]


def swapped(blocks, lane):
    count = len(blocks)
    width = LANES // count
    blocks = list(blocks)
    bit = 1
    while bit < count:
        clear = (lane // (bit * width)) % 2 == 0
        for low in range(count):
            if low & bit:
                continue
            first, second = blocks[low], blocks[low | bit]
            blocks[low] = jnp.where(clear, first, pltpu.roll(second, bit * width, 1))
            blocks[low | bit] = jnp.where(clear, pltpu.roll(first, LANES - bit * width, 1), second)
        bit *= 2
    return blocks


def swap_into(read, write, count, rows):
    tile = 8 * max(1, 32 // count)
    lane = lax.broadcasted_iota(jnp.int32, (tile, LANES), 1)

    def step(index, carry):
        start = pl.multiple_of(index * tile, 8)
        for block, value in enumerate(swapped([read(block, start, tile) for block in range(count)], lane)):
            write(block, start, tile, value)
        return carry

    lax.fori_loop(0, rows // tile, step, 0)


def swap_kernel(count, rows, in_ref, out_ref):
    def read(block, start, tile):
        return in_ref[block, pl.ds(start, tile), :]

    def write(block, start, tile, value):
        out_ref[block, pl.ds(start, tile), :] = value

    swap_into(read, write, count, rows)


def swap_in(value):
    planes, count, rows, _ = value.shape
    return pl.pallas_call(
        functools.partial(swap_kernel, count, rows),
        grid=(planes,),
        in_specs=[pl.BlockSpec((None, count, rows, LANES), lambda p: (p, 0, 0, 0))],
        out_specs=pl.BlockSpec((count, None, rows, LANES), lambda p: (0, p, 0, 0)),
        out_shape=jax.ShapeDtypeStruct((count, planes, rows, LANES), jnp.float32),
        compiler_params=PARAMS,
        cost_estimate=cost(0, 8 * value.size),
    )(value)


def swap_out(value):
    count, rows, _ = value.shape
    return pl.pallas_call(
        functools.partial(swap_kernel, count, rows),
        in_specs=[WHOLE],
        out_specs=WHOLE,
        out_shape=jax.ShapeDtypeStruct(value.shape, jnp.float32),
        compiler_params=PARAMS,
        cost_estimate=cost(0, 8 * value.size),
    )(value)


def nonlocal_into(field, near, projector, transposed, coupling_ref, mask_ref, planes, cells, width):
    inner = outer = None
    for plane in range(planes):
        parts = side_by_side(field(plane))
        term = dot_halves(projector(plane), parts)
        inner = term if inner is None else inner + term
        if plane < SPAN - 1:
            term = dot_halves(projector(planes + plane), parts)
            outer = term if outer is None else outer + term
    correlations = (folded(inner) + pltpu.roll(folded(outer), LANES - width, 1)) * mask_ref[...]
    weighted = folded(dot_halves(halves(coupling_ref[...]), side_by_side(correlations)))
    here, shifted = side_by_side(weighted), side_by_side(pltpu.roll(weighted, width, 1))
    tile = 256

    def add(plane, right, fresh):
        high, low, base = transposed(plane)

        def step(index, carry):
            start = pl.multiple_of(index * tile, tile)
            at, to = pl.ds(base + start, tile), pl.ds(start, tile)
            value = folded(dot_halves((high[at, :], low[at, :]), right))
            where = plane if fresh else plane - planes
            near[where, to, :] = value if fresh else near[where, to, :] + value
            return carry

        lax.fori_loop(0, cells // tile, step, 0)

    for plane in range(planes):
        add(plane, here, True)
        if plane < SPAN - 1:
            add(planes + plane, shifted, False)


def filter_kernel(
    planes, side_y, side_z, width, arrived_ref, potential_ref, high_ref, low_ref, high_t_ref, low_t_ref, coupling_ref, mask_ref, *rest
):
    outs, (field, padded, first, flat, near, *staged) = rest[:planes], rest[planes:]
    cells = side_y * side_z
    count, _, rows, _ = arrived_ref.shape
    tile = 16

    def copied(pairs):
        copies = [pltpu.make_async_copy(source, target, staged[4].at[at]) for at, (source, target) in enumerate(pairs)]
        for copy in copies:
            copy.start()
        for copy in copies:
            copy.wait()

    def projector(plane):
        at = pl.ds(plane * cells, cells)
        if not staged:
            return high_ref[:, at], low_ref[:, at]
        copied([(high_ref.at[:, at], staged[0]), (low_ref.at[:, at], staged[1])])
        return staged[0][...], staged[1][...]

    def transposed(plane):
        if not staged:
            return high_t_ref, low_t_ref, plane * cells
        at = pl.ds(plane * cells, cells)
        copied([(high_t_ref.at[at, :], staged[2]), (low_t_ref.at[at, :], staged[3])])
        return staged[2], staged[3], 0

    for plane in range(planes):
        swap_into(
            lambda block, start, size: arrived_ref[block, plane, pl.ds(start, size), :],
            lambda block, start, size, value: field.__setitem__(
                (plane, pl.ds(pl.multiple_of(block * rows + start, 8), size), slice(None)), value
            ),
            count,
            rows,
        )

    def fill(y, carry):
        for plane in range(planes):
            row = field[plane, pl.ds(pl.multiple_of(y * side_z, 8), side_z), :]
            padded[plane, y, pl.ds(PAD, side_z), :] = row
            padded[plane, y, pl.ds(PAD - 4, 4), :] = row[side_z - 4 :]
            padded[plane, y, pl.ds(PAD + side_z, 4), :] = row[:4]
        return carry

    lax.fori_loop(0, side_y, fill, 0)

    def apply(source, finish):
        def row(y, carry):
            for start in range(0, side_z, tile):
                def load(plane, y_at, shift):
                    return source[plane, y_at, pl.ds(PAD + start + shift, tile), :]

                inside = [load(plane, y, 0) for plane in range(planes)]
                before = [pltpu.roll(value, width, 1) for value in inside]
                after = [pltpu.roll(value, LANES - width, 1) for value in inside]
                line = before + inside + after
                at = pl.ds(pl.multiple_of(y * side_z + start, 8), tile)
                for plane in range(planes):
                    own = inside[plane]
                    total = (potential_ref[plane, at, :] - 1.5 * center_weight - 7.0) * own + near[plane, at, :]
                    for offset in range(1, 5):
                        around = line[planes + plane + offset] + line[planes + plane - offset]
                        around = around + (load(plane, y, offset) + load(plane, y, -offset))
                        up = lax.rem(y + offset, side_y)
                        down = lax.rem(y + side_y - offset, side_y)
                        around = around + (load(plane, up, 0) + load(plane, down, 0))
                        total = total - (0.5 * side_weights[offset - 1]) * around
                    finish(plane, y, start, at, total)
            return carry

        lax.fori_loop(0, side_y, row, 0)

    common = (projector, transposed, coupling_ref, mask_ref, planes, cells, width)
    nonlocal_into(lambda plane: field[plane], near, *common)

    def finish_first(plane, y, start, at, total):
        value = total * (1.0 / 6.0)
        first[plane, y, pl.ds(PAD + start, tile), :] = value
        flat[plane, at, :] = value
        if start == 0:
            first[plane, y, pl.ds(PAD + side_z, 4), :] = value[:4]
        if start == side_z - tile:
            first[plane, y, pl.ds(PAD - 4, 4), :] = value[tile - 4 :]

    apply(padded, finish_first)
    nonlocal_into(lambda plane: flat[plane], near, *common)

    def finish_second(plane, y, start, at, total):
        flat[plane, at, :] = total * (2.0 / 6.0) - field[plane, at, :]

    apply(first, finish_second)
    for plane in range(planes):
        swap_into(
            lambda block, start, size: flat[plane, pl.ds(pl.multiple_of(block * rows + start, 8), size), :],
            lambda block, start, size, value: outs[plane].__setitem__((block, pl.ds(start, size), slice(None)), value),
            count,
            rows,
        )


def filter_orbitals(arrived, potential, high, low, coupling, mask, side_y, side_z, width):
    count, planes, rows, _ = arrived.shape
    cells = side_y * side_z
    stay, staged = WHOLE, []
    if high.size > 8 * 1024 * 1024:
        stay = pl.BlockSpec(memory_space=pl.ANY)
        staged = [pltpu.VMEM((high.shape[0], cells), jnp.bfloat16)] * 2
        staged += [pltpu.VMEM((cells, high.shape[0]), jnp.bfloat16)] * 2
        staged += [pltpu.SemaphoreType.DMA((2,))]
    flat = pltpu.VMEM((planes, cells, LANES), jnp.float32)
    high_side = pltpu.VMEM((planes, side_y, side_z + 2 * PAD, LANES), jnp.float32)
    return pl.pallas_call(
        functools.partial(filter_kernel, planes, side_y, side_z, width),
        in_specs=[WHOLE, WHOLE, stay, stay, stay, stay, WHOLE, WHOLE],
        out_specs=[WHOLE] * planes,
        out_shape=[jax.ShapeDtypeStruct((count, rows, LANES), jnp.float32)] * planes,
        scratch_shapes=[flat, high_side, high_side, flat, flat, *staged],
        compiler_params=PARAMS,
        cost_estimate=cost(12 * high.size * LANES, 16 * high.size + 12 * arrived.size),
    )(arrived, potential, high, low, high.T, low.T, coupling, mask)


def gathered_parts(potential, projectors, coupling, atom_plane, projector_count, planes, cells, width):
    bands, blocks = lax.axis_size("band"), lax.axis_size("dom")
    band = lax.axis_index("band")
    share = projectors.shape[0] // bands
    lines = share * MAXPROJ
    slots = jnp.arange(MAXPROJ, dtype=jnp.int32)
    live = (slots[None, :] < projector_count[:, None]).astype(jnp.float32)
    coupled = 0.5 * (coupling + jnp.transpose(coupling, (0, 2, 1))) * live[:, :, None] * live[:, None, :]
    offset = (atom_plane - lax.axis_index("dom") * planes).astype(jnp.float32)
    offset = jnp.broadcast_to(offset[:, None, None], (*coupled.shape[:2], 1))
    extra = jnp.concatenate([coupled, offset], axis=2)
    piece = planes * cells // (bands * lines)
    levels = lax.dynamic_slice_in_dim(potential.reshape(bands * lines, piece), band * lines, lines, 0)
    mine = [
        lax.dynamic_slice_in_dim(projectors, band * share, share, 0).reshape(lines, -1),
        levels,
        lax.dynamic_slice_in_dim(extra, band * share, share, 0).reshape(lines, -1),
    ]
    mine.append(jnp.zeros((lines, -(piece + MAXPROJ + 1) % LANES), jnp.float32))
    everyone = lax.all_gather(jnp.concatenate(mine, axis=1), ("band", "dom"))
    count = bands * blocks * lines
    everyone = everyone.reshape(count, -1)
    beta = everyone[:, : SPAN * cells]
    levels = everyone[:, SPAN * cells : SPAN * cells + piece].reshape(bands, blocks, lines * piece)
    extra = everyone[:, SPAN * cells + piece :]
    levels = jnp.transpose(levels, (0, 2, 1)).reshape(planes, cells, blocks)
    levels = jnp.broadcast_to(levels[..., None], (*levels.shape, width)).reshape(planes, cells, LANES)
    offset = extra[:, MAXPROJ]
    placed = []
    for plane in range(planes + SPAN - 1):
        value = 0.0
        for part in range(SPAN):
            value = value + jnp.where(
                (offset == plane - part)[:, None], beta[:, part * cells : (part + 1) * cells], 0.0
            )
        placed.append(value)
    placed = jnp.concatenate(placed, axis=1)
    high = lax.reduce_precision(placed, 8, 7)
    low = (placed - high).astype(jnp.bfloat16)
    high = high.astype(jnp.bfloat16)
    row = jnp.arange(count, dtype=jnp.int32)
    same_atom = row[:, None] // MAXPROJ == row[None, :] // MAXPROJ
    matrix = jnp.where(same_atom, jnp.tile(extra[:, :MAXPROJ], (1, count // MAXPROJ)), 0.0)
    block_of = (row // lines) % blocks
    lanes = jnp.arange(LANES, dtype=jnp.int32) // width
    mask = (block_of[:, None] == lanes[None, :]).astype(jnp.float32)
    return levels, high, low, matrix, mask


def gram_kernel(own_ref, panels_ref, out_ref):
    @pl.when(pl.program_id(0) == 0)
    def _():
        out_ref[...] = jnp.zeros_like(out_ref)

    left = halves(own_ref[...].T)
    for band in range(panels_ref.shape[0]):
        at = pl.ds(band * LANES, LANES)
        out_ref[:, at] = out_ref[:, at] + folded(dot_halves(left, side_by_side(panels_ref[band])))


def gram_rows(own, panels):
    bands, cells, _ = panels.shape
    tile = cells // 4
    return pl.pallas_call(
        gram_kernel,
        grid=(cells // tile,),
        in_specs=[
            pl.BlockSpec((tile, LANES), lambda i: (i, 0)),
            pl.BlockSpec((bands, tile, LANES), lambda i: (0, i, 0)),
        ],
        out_specs=pl.BlockSpec((LANES, bands * LANES), lambda i: (0, 0)),
        out_shape=jax.ShapeDtypeStruct((LANES, bands * LANES), jnp.float32),
        compiler_params=PARAMS,
        cost_estimate=cost(8 * cells * LANES * LANES * bands, 4 * (own.size + panels.size)),
    )(own, panels)


def rotate_kernel(inverse_ref, *rest):
    panels, out_ref = rest[:-1], rest[-1]
    right = side_by_side(inverse_ref[...].T)
    for plane, panel in enumerate(panels):
        left = halves(jnp.concatenate([panel[band] for band in range(panel.shape[0])], axis=1))
        out_ref[plane] = folded(dot_halves(left, right))


def rotated(inverse_rows, panels):
    bands, cells, _ = panels[0].shape
    tile = cells // 4
    return pl.pallas_call(
        rotate_kernel,
        grid=(cells // tile,),
        in_specs=[pl.BlockSpec(inverse_rows.shape, lambda i: (0, 0))]
        + [pl.BlockSpec((bands, tile, LANES), lambda i: (0, i, 0))] * len(panels),
        out_specs=pl.BlockSpec((len(panels), tile, LANES), lambda i: (0, i, 0)),
        out_shape=jax.ShapeDtypeStruct((len(panels), cells, LANES), jnp.float32),
        compiler_params=PARAMS,
    )(inverse_rows, *panels)


def thirds(value):
    first = value.astype(jnp.bfloat16).astype(jnp.float32)
    rest = value - first
    second = rest.astype(jnp.bfloat16).astype(jnp.float32)
    return first, second, rest - second


def eliminate(work, result):
    sublane = lax.broadcasted_iota(jnp.int32, (GROUP, LANES), 0)
    for top in range(0, LANES, GROUP):
        left = [jnp.broadcast_to(work[pl.ds(top + i, 1), :LANES], (GROUP, LANES)) for i in range(GROUP)]
        right = [jnp.broadcast_to(work[pl.ds(top + i, 1), LANES:], (GROUP, LANES)) for i in range(GROUP)]
        entry = {
            (i, j): jnp.broadcast_to(left[i][:, top + j : top + j + 1], (GROUP, LANES))
            for i in range(GROUP)
            for j in range(i, GROUP)
        }
        for i in range(GROUP):
            scale = lax.rsqrt(entry[i, i])
            left[i] = left[i] * scale
            right[i] = right[i] * scale
            factor = {j: entry[i, j] * scale for j in range(i + 1, GROUP)}
            for m in range(i + 1, GROUP):
                for j in range(m, GROUP):
                    entry[m, j] = entry[m, j] - factor[m] * factor[j]
                left[m] = left[m] - factor[m] * left[i]
                right[m] = right[m] - factor[m] * right[i]
        upper, lower = left[0], right[0]
        for i in range(1, GROUP):
            upper = jnp.where(sublane == i, left[i], upper)
            lower = jnp.where(sublane == i, right[i], lower)
        result[pl.ds(top, GROUP), :] = lower
        below = top + GROUP
        if below < LANES:
            a, b, c = thirds(upper)
            x, y, z = thirds(lower)
            columns = jnp.concatenate([a, a, b, b, a, c], axis=0).T[below:].astype(jnp.bfloat16)
            rows = jnp.concatenate(
                [jnp.concatenate([a, b, a, b, c, a], axis=0), jnp.concatenate([x, y, x, y, z, x], axis=0)], axis=1
            ).astype(jnp.bfloat16)
            rest = pl.ds(below, LANES - below)
            work[rest, :] = work[rest, :] - jnp.dot(columns, rows, preferred_element_type=jnp.float32)


def cholesky_kernel(gram_ref, out_ref, matrix, work, corner, scaled):
    size = gram_ref.shape[0]
    dot = functools.partial(jnp.dot, precision=HIGHEST, preferred_element_type=jnp.float32)
    diagonal = lax.broadcasted_iota(jnp.int32, (LANES, LANES), 0) == lax.broadcasted_iota(jnp.int32, (LANES, LANES), 1)
    identity = diagonal.astype(jnp.float32)
    matrix[:, :size] = gram_ref[...]
    matrix[:, size:] = jnp.zeros((size, size), jnp.float32)
    for at in range(0, size, LANES):
        matrix[pl.ds(at, LANES), size + at : size + at + LANES] = identity

    def block(index, carry):
        start = pl.multiple_of(index * LANES, LANES)
        at = pl.ds(start, LANES)
        work[:, :LANES] = matrix[at, at]
        work[:, LANES:] = identity
        eliminate(work, corner)
        scaled[...] = dot(corner[...], matrix[at, :])
        out_ref[at, :] = scaled[:, size:]

        def below(other, carry):
            rows = pl.ds(pl.multiple_of(other * LANES, LANES), LANES)
            matrix[rows, :] = matrix[rows, :] - dot(scaled[:, rows].T, scaled[...])
            return carry

        lax.fori_loop(index + 1, size // LANES, below, 0)
        return carry

    lax.fori_loop(0, size // LANES, block, 0)


def cholesky_inverse(gram):
    size = gram.shape[0]
    whole = pl.BlockSpec(memory_space=pltpu.VMEM)
    return pl.pallas_call(
        cholesky_kernel,
        in_specs=[whole],
        out_specs=whole,
        out_shape=jax.ShapeDtypeStruct((size, size), jnp.float32),
        scratch_shapes=[
            pltpu.VMEM((size, 2 * size), jnp.float32),
            pltpu.VMEM((LANES, 2 * LANES), jnp.float32),
            pltpu.VMEM((LANES, LANES), jnp.float32),
            pltpu.VMEM((LANES, 2 * size), jnp.float32),
        ],
        compiler_params=PARAMS,
    )(gram)


def shards(orbitals, potential, projectors, coupling, atom_plane, projector_count):
    planes, side_y, side_z, local_orbs = orbitals.shape
    blocks, bands = lax.axis_size("dom"), lax.axis_size("band")
    cells = side_y * side_z
    rows = cells // blocks
    width = local_orbs // blocks
    norb = local_orbs * bands

    packed = swap_in(orbitals.reshape(planes, blocks, rows, local_orbs))
    arrived = lax.all_to_all(packed, "dom", 0, 0, tiled=True)
    parts = gathered_parts(potential, projectors, coupling, atom_plane, projector_count, planes, cells, width)
    seconds = filter_orbitals(arrived, *parts, side_y, side_z, width)

    panels, part = [], 0.0
    for packed in seconds:
        own = swap_out(lax.all_to_all(packed, "dom", 0, 0, tiled=True)).reshape(cells, local_orbs)
        panels.append(lax.all_gather(own, "band"))
        part = part + gram_rows(own, panels[-1])

    pieces = lax.all_to_all(part.reshape(blocks, width, norb), "dom", 0, 0, tiled=True)
    piece = jnp.sum(pieces, axis=0) * (1.0 / (planes * cells * blocks))
    gram = lax.all_gather(piece, ("band", "dom")).reshape(norb, norb)
    inverse = cholesky_inverse(gram)
    own_rows = lax.dynamic_slice_in_dim(inverse, lax.axis_index("band") * local_orbs, local_orbs, 0)
    result = rotated(own_rows, panels)
    return (result.reshape(planes, side_y, side_z, local_orbs), gram)


def solution(mesh):
    placed = (
        P("dom", None, None, "band"),
        P("dom", None, None),
        P("dom", None, None),
        P("dom", None, None),
        P("dom"),
        P("dom"),
    )
    return jax.shard_map(
        shards,
        mesh=mesh,
        in_specs=placed,
        out_specs=(P("dom", None, None, "band"), P()),
        check_vma=False,
    )
```

```python
import functools

import jax
import jax.numpy as jnp
from jax import lax
from jax.experimental import pallas as pl
from jax.experimental.pallas import tpu as pltpu
from jax.sharding import PartitionSpec as P

SPAN = 3
MAXPROJ = 4
HALO = 4
PAD = 8
LANES = 128
GROUP = 8
BEFORE, AFTER = 2, 1
NEAR = BEFORE + 1 + AFTER

center_weight = -205.0 / 72.0
side_weights = (8.0 / 5.0, -1.0 / 5.0, 8.0 / 315.0, -1.0 / 560.0)
HIGHEST = lax.Precision.HIGHEST
WHOLE = pl.BlockSpec(memory_space=pltpu.VMEM)
PARAMS = pltpu.CompilerParams(vmem_limit_bytes=60 * 1024 * 1024)


def cost(flops, bytes_accessed):
    return pl.CostEstimate(flops=int(flops), bytes_accessed=int(bytes_accessed), transcendentals=0)


def halves(value):
    high = value.astype(jnp.bfloat16)
    return high, (value - high.astype(jnp.float32)).astype(jnp.bfloat16)


def side_by_side(value):
    return jnp.concatenate(halves(value), axis=1)


def dot_halves(left, right):
    dot = functools.partial(jnp.dot, preferred_element_type=jnp.float32)
    return dot(left[0], right) + dot(left[1], right)


def folded(value):
    return value[:, :LANES] + value[:, LANES:]


def swapped(blocks, lane):
    count = len(blocks)
    width = LANES // count
    blocks = [pltpu.roll(value, at * width, 1) if at else value for at, value in enumerate(blocks)]
    bit = 1
    while bit < count:
        chosen = (lane // (bit * width)) % 2 == 1
        blocks = [jnp.where(chosen, blocks[(at + bit) % count], blocks[at]) for at in range(count)]
        bit *= 2
    blocks = [blocks[-at % count] for at in range(count)]
    return [pltpu.roll(value, LANES - at * width, 1) if at else value for at, value in enumerate(blocks)]


def swap_into(read, write, count, rows):
    tile = 8 * max(1, 32 // count)
    lane = lax.broadcasted_iota(jnp.int32, (tile, LANES), 1)

    def step(index, carry):
        start = pl.multiple_of(index * tile, 8)
        for block, value in enumerate(swapped([read(block, start, tile) for block in range(count)], lane)):
            write(block, start, tile, value)
        return carry

    lax.fori_loop(0, rows // tile, step, 0)


def swap_in_kernel(count, rows, in_ref, out_ref):
    def read(block, start, size):
        return in_ref[block, pl.ds(start, size), :]

    def write(block, start, size, value):
        out_ref[block, pl.ds(start, size), :] = value

    swap_into(read, write, count, rows)


def swap_in(value):
    planes, count, rows, _ = value.shape
    return pl.pallas_call(
        functools.partial(swap_in_kernel, count, rows),
        grid=(planes,),
        in_specs=[pl.BlockSpec((None, count, rows, LANES), lambda p: (p, 0, 0, 0))],
        out_specs=pl.BlockSpec((count, None, rows, LANES), lambda p: (0, p, 0, 0)),
        out_shape=jax.ShapeDtypeStruct((count, planes, rows, LANES), jnp.float32),
        compiler_params=PARAMS,
        cost_estimate=cost(0, 8 * value.size),
    )(value)


def swap_out_kernel(count, rows, arrived_ref, high_ref, low_ref, weights_ref, out_ref):
    planes = out_ref.shape[0]
    weights = side_by_side(weights_ref[...] * (1.0 / 18.0))
    for plane in range(planes):

        def read(block, start, size):
            return arrived_ref[block, plane, pl.ds(start, size), :]

        def write(block, start, size, value):
            at = pl.ds(pl.multiple_of(block * rows + start, 8), size)
            out_ref[plane, at, :] = value

        swap_into(read, write, count, rows)
        tile = rows * count // 6

        def add(index, carry):
            at = pl.ds(pl.multiple_of(index * tile, 8), tile)
            term = folded(dot_halves((high_ref[plane, at, :], low_ref[plane, at, :]), weights))
            out_ref[plane, at, :] = out_ref[plane, at, :] + term
            return carry

        lax.fori_loop(0, 6, add, 0)


def swap_out(arrived, high, low, weights, first_plane):
    count, planes, rows, _ = arrived.shape
    cells = count * rows
    basis = pl.BlockSpec((planes, cells, 2 * LANES), lambda i: (first_plane // planes, 0, 0))
    return pl.pallas_call(
        functools.partial(swap_out_kernel, count, rows),
        grid=(1,),
        in_specs=[
            pl.BlockSpec(arrived.shape, lambda i: (0, 0, 0, 0)),
            basis,
            basis,
            pl.BlockSpec(weights.shape, lambda i: (0, 0)),
        ],
        out_specs=pl.BlockSpec((planes, cells, LANES), lambda i: (0, 0, 0)),
        out_shape=jax.ShapeDtypeStruct((planes, cells, LANES), jnp.float32),
        compiler_params=PARAMS,
        cost_estimate=cost(0, 24 * arrived.size),
    )(arrived, high, low, weights)


def fill_row(target, plane, y, row, side_z):
    target[plane, y, pl.ds(PAD, side_z), :] = row
    target[plane, y, pl.ds(PAD - HALO, HALO), :] = row[side_z - HALO :]
    target[plane, y, pl.ds(PAD + side_z, HALO), :] = row[:HALO]


def local_part(source, potential_ref, planes, first, side_y, side_z, line_of, finish):
    tile = 16

    def row(y, carry):
        for start in range(0, side_z, tile):

            def load(plane, y_at, shift):
                return source[plane, y_at, pl.ds(PAD + start + shift, tile), :]

            line = line_of(lambda plane: load(plane, y, 0))
            at = pl.ds(pl.multiple_of(y * side_z + start, 8), tile)
            for plane in range(planes):
                here = first + plane
                total = (potential_ref[plane, at, :] - 1.5 * center_weight - 7.0) * line[HALO + plane]
                for offset in range(1, HALO + 1):
                    around = line[HALO + plane + offset] + line[HALO + plane - offset]
                    around = around + (load(here, y, offset) + load(here, y, -offset))
                    up = lax.rem(y + offset, side_y)
                    down = lax.rem(y + side_y - offset, side_y)
                    around = around + (load(here, up, 0) + load(here, down, 0))
                    total = total - (0.5 * side_weights[offset - 1]) * around
                finish(plane, y, start, at, total)
        return carry

    lax.fori_loop(0, side_y, row, 0)


def filter_kernel(planes, side_y, side_z, width, chunks, arrived_ref, potential_ref, *rest):
    outs, (field, padded, first, flat) = rest[: len(chunks)], rest[len(chunks) :]
    count, _, rows, _ = arrived_ref.shape
    tile = 16

    for plane in range(planes):

        def read_in(block, start, size):
            return arrived_ref[block, plane, pl.ds(start, size), :]

        def write_in(block, start, size, value):
            field[plane, pl.ds(pl.multiple_of(block * rows + start, 8), size), :] = value

        swap_into(read_in, write_in, count, rows)

    def fill(y, carry):
        for plane in range(planes):
            fill_row(padded, plane, y, field[plane, pl.ds(pl.multiple_of(y * side_z, 8), side_z), :], side_z)
        return carry

    lax.fori_loop(0, side_y, fill, 0)

    def line_of(load):
        inside = [load(plane) for plane in range(planes)]
        before = [pltpu.roll(value, width, 1) for value in inside]
        after = [pltpu.roll(value, LANES - width, 1) for value in inside]
        return before[planes - HALO :] + inside + after[:HALO]

    def finish_first(plane, y, start, at, total):
        first[plane, y, pl.ds(PAD + start, tile), :] = total
        if start == 0:
            first[plane, y, pl.ds(PAD + side_z, HALO), :] = total[:HALO]
        if start == side_z - tile:
            first[plane, y, pl.ds(PAD - HALO, HALO), :] = total[tile - HALO :]

    def finish_second(plane, y, start, at, total):
        flat[plane, at, :] = total * (1.0 / 18.0) - field[plane, at, :]

    local_part(padded, potential_ref, planes, 0, side_y, side_z, line_of, finish_first)
    local_part(first, potential_ref, planes, 0, side_y, side_z, line_of, finish_second)

    for (begin, size_of), out_ref in zip(chunks, outs):
        for plane in range(size_of):

            def read_out(block, start, size):
                return flat[begin + plane, pl.ds(pl.multiple_of(block * rows + start, 8), size), :]

            def write_out(block, start, size, value):
                out_ref[block, plane, pl.ds(start, size), :] = value

            swap_into(read_out, write_out, count, rows)


def filter_orbitals(arrived, potential, side_y, side_z, width, chunks):
    count, planes, rows, _ = arrived.shape
    flat = pltpu.VMEM((planes, side_y * side_z, LANES), jnp.float32)
    padded = pltpu.VMEM((planes, side_y, side_z + 2 * PAD, LANES), jnp.float32)
    return pl.pallas_call(
        functools.partial(filter_kernel, planes, side_y, side_z, width, chunks),
        in_specs=[WHOLE, WHOLE],
        out_specs=[WHOLE] * len(chunks),
        out_shape=[jax.ShapeDtypeStruct((count, size, rows, LANES), jnp.float32) for _, size in chunks],
        scratch_shapes=[flat, padded, padded, flat],
        compiler_params=PARAMS,
        cost_estimate=cost(100 * arrived.size, 12 * arrived.size),
    )(arrived, potential)


def basis_kernel(planes, side_y, side_z, raw_ref, offset_ref, potential_ref, orbitals_ref, high_ref, low_ref, parts_ref, turned, placed):
    cells = side_y * side_z
    bands = raw_ref.shape[0]
    for part in range(SPAN):
        at = pl.ds(part * cells, cells)
        stack = [raw_ref[band, block, :, at] for block in range(NEAR) for band in range(bands)]
        turned[part] = jnp.concatenate(stack, axis=0).T
    offset = offset_ref[0:1, :]

    def place(y, carry):
        at = pl.ds(pl.multiple_of(y * side_z, 8), side_z)
        values = [turned[part, at, :] for part in range(SPAN)]
        for plane in range(planes + 2 * HALO):
            row = jnp.zeros((side_z, LANES), jnp.float32)
            for part in range(SPAN):
                row = jnp.where(offset == float(plane - HALO - part), values[part], row)
            fill_row(placed, plane, y, row, side_z)
        return carry

    lax.fori_loop(0, side_y, place, 0)

    def line_of(load):
        return [load(plane) for plane in range(planes + 2 * HALO)]

    def finish(plane, y, start, at, total):
        own = placed[HALO + plane, y, pl.ds(PAD + start, 16), :]
        high, low = halves(jnp.concatenate([total, own], axis=1))
        high_ref[plane, at, :] = high
        low_ref[plane, at, :] = low

    local_part(placed, potential_ref, planes, HALO, side_y, side_z, line_of, finish)

    dot = functools.partial(jnp.dot, preferred_element_type=jnp.float32)
    with_orbitals = with_basis = 0.0
    for plane in range(planes):
        high, low = high_ref[plane], low_ref[plane]
        left = halves(orbitals_ref[plane].T)
        with_orbitals = with_orbitals + (dot(left[0], high) + (dot(left[0], low) + dot(left[1], high)))
        own_high, own_low = high[:, LANES:], low[:, LANES:]
        turned_high = own_high.astype(jnp.float32).T.astype(jnp.bfloat16)
        turned_low = own_low.astype(jnp.float32).T.astype(jnp.bfloat16)
        both = jnp.concatenate([own_high, own_low], axis=1)
        with_basis = with_basis + (dot(turned_high, both) + dot(turned_low, both))
    parts_ref[0] = with_orbitals[:, LANES:].T
    parts_ref[1] = with_orbitals[:, :LANES].T
    parts_ref[2] = folded(with_basis)


def build_basis(raw, offset, potential, orbitals, side_y, side_z):
    planes, cells, _ = orbitals.shape
    pair = jax.ShapeDtypeStruct((planes, cells, 2 * LANES), jnp.bfloat16)
    return pl.pallas_call(
        functools.partial(basis_kernel, planes, side_y, side_z),
        in_specs=[WHOLE] * 4,
        out_specs=[WHOLE] * 3,
        out_shape=[pair, pair, jax.ShapeDtypeStruct((3, LANES, LANES), jnp.float32)],
        scratch_shapes=[
            pltpu.VMEM((SPAN, cells, LANES), jnp.float32),
            pltpu.VMEM((planes + 2 * HALO, side_y, side_z + 2 * PAD, LANES), jnp.float32),
        ],
        compiler_params=PARAMS,
        cost_estimate=cost(200 * orbitals.size, 24 * orbitals.size),
    )(raw, offset, potential, orbitals)


def weights_kernel(me_ref, parts_ref, coupling_ref, out_ref):
    count = parts_ref.shape[0]
    size = LANES // NEAR
    me = me_ref[0]
    dot = functools.partial(jnp.dot, precision=HIGHEST, preferred_element_type=jnp.float32)

    def device(step):
        return lax.rem(me + step % count, count)

    def total(pick, block):
        shares = [pick(block - (near - BEFORE), pl.ds(near * size, size)) for near in range(NEAR)]
        return (shares[0] + shares[1]) + (shares[2] + shares[3])

    def couple(block, value):
        return dot(coupling_ref[device(block)], value)

    def kept(function):
        known = {}

        def look(step):
            if step % count not in known:
                known[step % count] = function(step)
            return known[step % count]

        return look

    weight = kept(lambda block: couple(block, total(lambda step, at: parts_ref[device(step), 0, at, :], block)))
    near_weights = kept(lambda step: jnp.concatenate([weight(step + near - BEFORE) for near in range(NEAR)], axis=0))
    overlap = kept(lambda step: dot(parts_ref[device(step), 2], near_weights(step)))
    out_ref[pl.ds(0, LANES), :] = near_weights(0)
    for near in range(NEAR):
        block = near - BEFORE

        def share(step, at):
            return parts_ref[device(step), 1, at, :] + overlap(step)[at.start : at.start + size]

        out_ref[pl.ds(LANES + near * size, size), :] = couple(block, total(share, block))


def near_weights(parts, coupling):
    return pl.pallas_call(
        weights_kernel,
        in_specs=[pl.BlockSpec(memory_space=pltpu.SMEM), WHOLE, WHOLE],
        out_specs=WHOLE,
        out_shape=jax.ShapeDtypeStruct((2 * LANES, LANES), jnp.float32),
        compiler_params=PARAMS,
        cost_estimate=cost(0, 8 * parts.size),
    )(lax.axis_index("dom").astype(jnp.int32).reshape(1), parts, coupling)


def shifted(value, axis, step):
    count = lax.axis_size(axis)
    return lax.ppermute(value, axis, [(source, (source + step) % count) for source in range(count)])


def crossed(value, bit):
    return lax.ppermute(value, "band", [(source, source ^ bit) for source in range(lax.axis_size("band"))])


def gram_kernel(own_ref, *rest):
    panels, out_ref = (own_ref, *rest[:-1]), rest[-1]

    @pl.when(pl.program_id(0) == 0)
    def _():
        out_ref[...] = jnp.zeros_like(out_ref)

    for plane in range(own_ref.shape[0]):
        left = halves(own_ref[plane].T)
        for index, panel in enumerate(panels):
            at = pl.ds(index * LANES, LANES)
            out_ref[:, at] = out_ref[:, at] + folded(dot_halves(left, side_by_side(panel[plane])))


def gram_rows(panels):
    planes, cells, _ = panels[0].shape
    tile = cells // 4
    return pl.pallas_call(
        gram_kernel,
        grid=(cells // tile,),
        in_specs=[pl.BlockSpec((planes, tile, LANES), lambda i: (0, i, 0))] * len(panels),
        out_specs=pl.BlockSpec((LANES, len(panels) * LANES), lambda i: (0, 0)),
        out_shape=jax.ShapeDtypeStruct((LANES, len(panels) * LANES), jnp.float32),
        compiler_params=PARAMS,
        cost_estimate=cost(8 * panels[0].size * LANES * len(panels), 4 * panels[0].size * len(panels)),
    )(*panels)


def rotate_kernel(chunks, bands, inverse_ref, *rest):
    panels, out_ref = rest[:-1], rest[-1]
    right = side_by_side(inverse_ref[...].T)
    for index, (begin, size) in enumerate(chunks):
        group = panels[index * bands : (index + 1) * bands]
        for plane in range(size):
            left = halves(jnp.concatenate([panel[plane] for panel in group], axis=1))
            out_ref[begin + plane] = folded(dot_halves(left, right))


def rotated(inverse_rows, panels, chunks):
    bands = len(panels[0])
    planes = sum(size for _, size in chunks)
    cells = panels[0][0].shape[1]
    tile = cells // 4
    specs = [pl.BlockSpec((size, tile, LANES), lambda i: (0, i, 0)) for _, size in chunks for _ in range(bands)]
    return pl.pallas_call(
        functools.partial(rotate_kernel, chunks, bands),
        grid=(cells // tile,),
        in_specs=[pl.BlockSpec(inverse_rows.shape, lambda i: (0, 0)), *specs],
        out_specs=pl.BlockSpec((planes, tile, LANES), lambda i: (0, i, 0)),
        out_shape=jax.ShapeDtypeStruct((planes, cells, LANES), jnp.float32),
        compiler_params=PARAMS,
    )(inverse_rows, *[panel for group in panels for panel in group])


def thirds(value):
    first = value.astype(jnp.bfloat16).astype(jnp.float32)
    rest = value - first
    second = rest.astype(jnp.bfloat16).astype(jnp.float32)
    return first, second, rest - second


def eliminate(work, result):
    sublane = lax.broadcasted_iota(jnp.int32, (GROUP, LANES), 0)
    for top in range(0, LANES, GROUP):
        left = [jnp.broadcast_to(work[pl.ds(top + i, 1), :LANES], (GROUP, LANES)) for i in range(GROUP)]
        right = [jnp.broadcast_to(work[pl.ds(top + i, 1), LANES:], (GROUP, LANES)) for i in range(GROUP)]
        entry = {
            (i, j): jnp.broadcast_to(left[i][:, top + j : top + j + 1], (GROUP, LANES))
            for i in range(GROUP)
            for j in range(i, GROUP)
        }
        for i in range(GROUP):
            scale = lax.rsqrt(entry[i, i])
            left[i] = left[i] * scale
            right[i] = right[i] * scale
            factor = {j: entry[i, j] * scale for j in range(i + 1, GROUP)}
            for m in range(i + 1, GROUP):
                for j in range(m, GROUP):
                    entry[m, j] = entry[m, j] - factor[m] * factor[j]
                left[m] = left[m] - factor[m] * left[i]
                right[m] = right[m] - factor[m] * right[i]
        upper, lower = left[0], right[0]
        for i in range(1, GROUP):
            upper = jnp.where(sublane == i, left[i], upper)
            lower = jnp.where(sublane == i, right[i], lower)
        result[pl.ds(top, GROUP), :] = lower
        below = top + GROUP
        if below < LANES:
            a, b, c = thirds(upper)
            x, y, z = thirds(lower)
            columns = jnp.concatenate([a, a, b, b, a, c], axis=0).T[below:].astype(jnp.bfloat16)
            rows = jnp.concatenate(
                [jnp.concatenate([a, b, a, b, c, a], axis=0), jnp.concatenate([x, y, x, y, z, x], axis=0)], axis=1
            ).astype(jnp.bfloat16)
            rest = pl.ds(below, LANES - below)
            work[rest, :] = work[rest, :] - jnp.dot(columns, rows, preferred_element_type=jnp.float32)


def cholesky_kernel(gram_ref, out_ref, matrix, work, corner, scaled):
    size = gram_ref.shape[0]
    dot = functools.partial(jnp.dot, precision=HIGHEST, preferred_element_type=jnp.float32)
    diagonal = lax.broadcasted_iota(jnp.int32, (LANES, LANES), 0) == lax.broadcasted_iota(jnp.int32, (LANES, LANES), 1)
    identity = diagonal.astype(jnp.float32)
    matrix[:, :size] = gram_ref[...]
    matrix[:, size:] = jnp.zeros((size, size), jnp.float32)
    for at in range(0, size, LANES):
        matrix[pl.ds(at, LANES), size + at : size + at + LANES] = identity

    def block(index, carry):
        start = pl.multiple_of(index * LANES, LANES)
        at = pl.ds(start, LANES)
        work[:, :LANES] = matrix[at, at]
        work[:, LANES:] = identity
        eliminate(work, corner)
        scaled[...] = dot(corner[...], matrix[at, :])
        out_ref[at, :] = scaled[:, size:]

        def below(other, carry):
            rows = pl.ds(pl.multiple_of(other * LANES, LANES), LANES)
            matrix[rows, :] = matrix[rows, :] - dot(scaled[:, rows].T, scaled[...])
            return carry

        lax.fori_loop(index + 1, size // LANES, below, 0)
        return carry

    lax.fori_loop(0, size // LANES, block, 0)


def cholesky_inverse(gram):
    size = gram.shape[0]
    whole = pl.BlockSpec(memory_space=pltpu.VMEM)
    return pl.pallas_call(
        cholesky_kernel,
        in_specs=[whole],
        out_specs=whole,
        out_shape=jax.ShapeDtypeStruct((size, size), jnp.float32),
        scratch_shapes=[
            pltpu.VMEM((size, 2 * size), jnp.float32),
            pltpu.VMEM((LANES, 2 * LANES), jnp.float32),
            pltpu.VMEM((LANES, LANES), jnp.float32),
            pltpu.VMEM((LANES, 2 * size), jnp.float32),
        ],
        compiler_params=PARAMS,
    )(gram)


def near_projectors(projectors, atom_plane, planes):
    bands, band, block = lax.axis_size("band"), lax.axis_index("band"), lax.axis_index("dom")
    share = projectors.shape[0] // bands
    lines = share * MAXPROJ
    first = (atom_plane - block * planes).astype(jnp.float32)
    first = jnp.broadcast_to(first[:, None, None], (projectors.shape[0], MAXPROJ, LANES))
    packed = jnp.concatenate([projectors, first], axis=2)
    mine = lax.dynamic_slice_in_dim(packed, band * share, share, 0).reshape(lines, -1)
    near = [mine if step == BEFORE else shifted(mine, "dom", BEFORE - step) for step in range(NEAR)]
    raw = lax.all_gather(jnp.stack(near), "band")
    first = raw[:, :, :, -1] + (planes * (jnp.arange(NEAR, dtype=jnp.float32) - BEFORE))[None, :, None]
    first = jnp.transpose(first, (1, 0, 2)).reshape(1, LANES)
    return raw, jnp.broadcast_to(first, (GROUP, LANES))


def shards(orbitals, potential, projectors, coupling, atom_plane, projector_count):
    planes, side_y, side_z, local_orbs = orbitals.shape
    blocks, bands = lax.axis_size("dom"), lax.axis_size("band")
    band = lax.axis_index("band")
    cells = side_y * side_z
    rows = cells // blocks
    width = local_orbs // blocks
    norb = local_orbs * bands
    chunks = ((0, 2), (2, 1), (3, 1))

    raw, first = near_projectors(projectors, atom_plane, planes)
    levels = lax.all_gather(potential.reshape(planes, cells), "dom")
    levels = jnp.transpose(levels, (1, 2, 0))
    levels = jnp.broadcast_to(levels[..., None], (planes, cells, blocks, width)).reshape(planes, cells, LANES)

    packed = swap_in(orbitals.reshape(planes, blocks, rows, local_orbs))
    arrived = lax.all_to_all(packed, "dom", 0, 0, tiled=True)

    own_levels = jnp.broadcast_to(potential.reshape(planes, cells, 1), (planes, cells, LANES))
    high, low, parts = build_basis(raw, first, own_levels, orbitals.reshape(planes, cells, LANES), side_y, side_z)
    atoms = projectors.shape[0]
    slots = jnp.arange(MAXPROJ, dtype=jnp.int32)
    live = (slots[None, :] < projector_count[:, None]).astype(jnp.float32)
    coupled = 0.5 * (coupling + jnp.transpose(coupling, (0, 2, 1))) * live[:, :, None] * live[:, None, :]
    vectors = atoms * MAXPROJ
    row = jnp.arange(vectors, dtype=jnp.int32) // MAXPROJ
    matrix = jnp.tile(coupled.reshape(vectors, MAXPROJ), (1, atoms))
    matrix = jnp.where(row[:, None] == row[None, :], matrix, 0.0)
    matrix = jnp.pad(matrix, ((0, 0), (0, LANES - vectors)))
    everyone = lax.all_gather(jnp.concatenate([parts.reshape(3 * LANES, LANES), matrix], axis=0), "dom")
    weights = near_weights(
        everyone[:, : 3 * LANES].reshape(blocks, 3, LANES, LANES), everyone[:, 3 * LANES :, :vectors]
    )

    seconds = filter_orbitals(arrived, levels, side_y, side_z, width, chunks)

    panels, part = [], 0.0
    for (begin, size), packed in zip(chunks, seconds):
        own = swap_out(lax.all_to_all(packed, "dom", 0, 0, tiled=True), high, low, weights, begin)
        across = crossed(own, 2)
        panels.append([own, crossed(own, 1), across, crossed(across, 1)])
        part = part + gram_rows(panels[-1])

    order = jnp.arange(bands, dtype=jnp.int32) ^ band
    part = jnp.take(part.reshape(local_orbs, bands, local_orbs), order, axis=1)
    pieces = lax.all_to_all(part.reshape(blocks, width, norb), "dom", 0, 0, tiled=True)
    piece = jnp.sum(pieces, axis=0) * (1.0 / (planes * cells * blocks))
    own_gram = lax.all_to_all(jnp.broadcast_to(piece, (blocks, width, norb)), "dom", 0, 0, tiled=True)
    gram = lax.all_gather(own_gram.reshape(local_orbs, norb), "band", axis=0, tiled=True)
    inverse = cholesky_inverse(gram)
    own_rows = lax.dynamic_slice_in_dim(inverse, band * local_orbs, local_orbs, 0)
    own_rows = jnp.take(own_rows.reshape(local_orbs, bands, local_orbs), order, axis=1).reshape(local_orbs, norb)
    result = rotated(own_rows, panels, chunks)
    return (result.reshape(planes, side_y, side_z, local_orbs), gram)


def solution(mesh):
    placed = (
        P("dom", None, None, "band"),
        P("dom", None, None),
        P("dom", None, None),
        P("dom", None, None),
        P("dom"),
        P("dom"),
    )
    return jax.shard_map(
        shards,
        mesh=mesh,
        in_specs=placed,
        out_specs=(P("dom", None, None, "band"), P()),
        check_vma=False,
    )
```

```python
import functools

import jax
import jax.numpy as jnp
from jax import lax
from jax.experimental import pallas as pl
from jax.experimental.pallas import tpu as pltpu
from jax.sharding import PartitionSpec as P

SPAN = 3
MAXPROJ = 4
HALO = 4
PAD = 8
LANES = 128
GROUP = 8
BEFORE, AFTER = 2, 1
NEAR = BEFORE + 1 + AFTER

center_weight = -205.0 / 72.0
side_weights = (8.0 / 5.0, -1.0 / 5.0, 8.0 / 315.0, -1.0 / 560.0)
HIGHEST = lax.Precision.HIGHEST
WHOLE = pl.BlockSpec(memory_space=pltpu.VMEM)
PARAMS = pltpu.CompilerParams(vmem_limit_bytes=60 * 1024 * 1024)


def cost(flops, bytes_accessed):
    return pl.CostEstimate(flops=int(flops), bytes_accessed=int(bytes_accessed), transcendentals=0)


def halves(value):
    high = value.astype(jnp.bfloat16)
    return high, (value - high.astype(jnp.float32)).astype(jnp.bfloat16)


def side_by_side(value):
    return jnp.concatenate(halves(value), axis=1)


def dot_halves(left, right):
    dot = functools.partial(jnp.dot, preferred_element_type=jnp.float32)
    return dot(left[0], right) + dot(left[1], right)


def folded(value):
    return value[:, :LANES] + value[:, LANES:]


def swapped(blocks, lane):
    count = len(blocks)
    width = LANES // count
    blocks = [pltpu.roll(value, at * width, 1) if at else value for at, value in enumerate(blocks)]
    bit = 1
    while bit < count:
        chosen = (lane // (bit * width)) % 2 == 1
        blocks = [jnp.where(chosen, blocks[(at + bit) % count], blocks[at]) for at in range(count)]
        bit *= 2
    blocks = [blocks[-at % count] for at in range(count)]
    return [pltpu.roll(value, LANES - at * width, 1) if at else value for at, value in enumerate(blocks)]


def swap_into(read, write, count, rows):
    tile = 8 * max(1, 32 // count)
    lane = lax.broadcasted_iota(jnp.int32, (tile, LANES), 1)

    def step(index, carry):
        start = pl.multiple_of(index * tile, 8)
        for block, value in enumerate(swapped([read(block, start, tile) for block in range(count)], lane)):
            write(block, start, tile, value)
        return carry

    lax.fori_loop(0, rows // tile, step, 0, unroll=True)


def swap_in_kernel(count, rows, levels_ref, in_ref, out_ref):
    def read(block, start, size):
        return in_ref[block, pl.ds(start, size), :]

    def write(block, start, size, value):
        out_ref[block, pl.ds(start, size), :] = value

    swap_into(read, write, count, rows)
    for block in range(count):
        out_ref[block, pl.ds(rows, levels_ref.shape[0]), :] = levels_ref[...]


def swap_in(levels, value):
    planes, count, rows, _ = value.shape
    extra = levels.shape[1]
    return pl.pallas_call(
        functools.partial(swap_in_kernel, count, rows),
        grid=(planes,),
        in_specs=[
            pl.BlockSpec((None, extra, LANES), lambda p: (p, 0, 0)),
            pl.BlockSpec((None, count, rows, LANES), lambda p: (p, 0, 0, 0)),
        ],
        out_specs=pl.BlockSpec((count, None, rows + extra, LANES), lambda p: (0, p, 0, 0)),
        out_shape=jax.ShapeDtypeStruct((count, planes, rows + extra, LANES), jnp.float32),
        compiler_params=PARAMS,
        cost_estimate=cost(0, 8 * value.size),
    )(levels, value)


def swap_out_kernel(count, rows, arrived_ref, high_ref, low_ref, weights_ref, out_ref):
    planes = out_ref.shape[0]
    weights = side_by_side(weights_ref[...] * (1.0 / 18.0))
    for plane in range(planes):

        def read(block, start, size):
            return arrived_ref[block, plane, pl.ds(start, size), :]

        def write(block, start, size, value):
            at = pl.ds(pl.multiple_of(block * rows + start, 8), size)
            out_ref[plane, at, :] = value

        swap_into(read, write, count, rows)
        tile = rows * count // 6

        def add(index, carry):
            at = pl.ds(pl.multiple_of(index * tile, 8), tile)
            term = folded(dot_halves((high_ref[plane, at, :], low_ref[plane, at, :]), weights))
            out_ref[plane, at, :] = out_ref[plane, at, :] + term
            return carry

        lax.fori_loop(0, 6, add, 0)


def swap_out(arrived, high, low, weights, first_plane):
    count, planes, rows, _ = arrived.shape
    cells = count * rows
    basis = pl.BlockSpec((planes, cells, 2 * LANES), lambda i: (first_plane // planes, 0, 0))
    return pl.pallas_call(
        functools.partial(swap_out_kernel, count, rows),
        grid=(1,),
        in_specs=[
            pl.BlockSpec(arrived.shape, lambda i: (0, 0, 0, 0)),
            basis,
            basis,
            pl.BlockSpec(weights.shape, lambda i: (0, 0)),
        ],
        out_specs=pl.BlockSpec((planes, cells, LANES), lambda i: (0, 0, 0)),
        out_shape=jax.ShapeDtypeStruct((planes, cells, LANES), jnp.float32),
        compiler_params=PARAMS,
        cost_estimate=cost(0, 24 * arrived.size),
    )(arrived, high, low, weights)


def fill_row(target, plane, y, row, side_z):
    target[plane, y, pl.ds(PAD, side_z), :] = row
    target[plane, y, pl.ds(PAD - HALO, HALO), :] = row[side_z - HALO :]
    target[plane, y, pl.ds(PAD + side_z, HALO), :] = row[:HALO]


def local_part(source, potential_ref, planes, first, side_y, side_z, line_of, finish):
    tile = 16

    def row(y, carry):
        for start in range(0, side_z, tile):

            def load(plane, y_at, shift):
                return source[plane, y_at, pl.ds(PAD + start + shift, tile), :]

            line = line_of(lambda plane: load(plane, y, 0))
            at = pl.ds(pl.multiple_of(y * side_z + start, 8), tile)
            for plane in range(planes):
                here = first + plane
                total = (potential_ref[plane, at, :] - 1.5 * center_weight - 7.0) * line[HALO + plane]
                for offset in range(1, HALO + 1):
                    around = line[HALO + plane + offset] + line[HALO + plane - offset]
                    around = around + (load(here, y, offset) + load(here, y, -offset))
                    up = lax.rem(y + offset, side_y)
                    down = lax.rem(y + side_y - offset, side_y)
                    around = around + (load(here, up, 0) + load(here, down, 0))
                    total = total - (0.5 * side_weights[offset - 1]) * around
                finish(plane, y, start, at, total)
        return carry

    lax.fori_loop(0, side_y, row, 0)


def filter_kernel(planes, side_y, side_z, width, chunks, arrived_ref, *rest):
    outs, (field, padded, first, flat, potential) = rest[: len(chunks)], rest[len(chunks) :]
    count = arrived_ref.shape[0]
    cells = side_y * side_z
    rows = cells // count
    tile = 16

    line = lax.broadcasted_iota(jnp.int32, (2 * count, LANES), 0) % count
    lane = lax.broadcasted_iota(jnp.int32, (2 * count, LANES), 1) // width
    spread = (line == lane).astype(jnp.bfloat16)
    for plane in range(planes):
        lines = [arrived_ref[:, plane, rows + at, :] for at in range(cells // LANES)]
        high, low = halves(jnp.concatenate(lines, axis=1))
        both = jnp.concatenate([high.astype(jnp.float32), low.astype(jnp.float32)], axis=0)
        potential[plane] = jnp.dot(both.T.astype(jnp.bfloat16), spread, preferred_element_type=jnp.float32)

    for plane in range(planes):

        def read_in(block, start, size):
            return arrived_ref[block, plane, pl.ds(start, size), :]

        def write_in(block, start, size, value):
            field[plane, pl.ds(pl.multiple_of(block * rows + start, 8), size), :] = value

        swap_into(read_in, write_in, count, rows)

    def fill(y, carry):
        for plane in range(planes):
            fill_row(padded, plane, y, field[plane, pl.ds(pl.multiple_of(y * side_z, 8), side_z), :], side_z)
        return carry

    lax.fori_loop(0, side_y, fill, 0)

    def line_of(load):
        inside = [load(plane) for plane in range(planes)]
        before = [pltpu.roll(value, width, 1) for value in inside]
        after = [pltpu.roll(value, LANES - width, 1) for value in inside]
        return before[planes - HALO :] + inside + after[:HALO]

    def finish_first(plane, y, start, at, total):
        first[plane, y, pl.ds(PAD + start, tile), :] = total
        if start == 0:
            first[plane, y, pl.ds(PAD + side_z, HALO), :] = total[:HALO]
        if start == side_z - tile:
            first[plane, y, pl.ds(PAD - HALO, HALO), :] = total[tile - HALO :]

    def finish_second(plane, y, start, at, total):
        flat[plane, at, :] = total * (1.0 / 18.0) - field[plane, at, :]

    local_part(padded, potential, planes, 0, side_y, side_z, line_of, finish_first)
    local_part(first, potential, planes, 0, side_y, side_z, line_of, finish_second)

    for (begin, size_of), out_ref in zip(chunks, outs):
        for plane in range(size_of):

            def read_out(block, start, size):
                return flat[begin + plane, pl.ds(pl.multiple_of(block * rows + start, 8), size), :]

            def write_out(block, start, size, value):
                out_ref[block, plane, pl.ds(start, size), :] = value

            swap_into(read_out, write_out, count, rows)


def filter_orbitals(arrived, side_y, side_z, width, chunks):
    count, planes = arrived.shape[:2]
    rows = side_y * side_z // count
    flat = pltpu.VMEM((planes, side_y * side_z, LANES), jnp.float32)
    padded = pltpu.VMEM((planes, side_y, side_z + 2 * PAD, LANES), jnp.float32)
    return pl.pallas_call(
        functools.partial(filter_kernel, planes, side_y, side_z, width, chunks),
        in_specs=[WHOLE],
        out_specs=[WHOLE] * len(chunks),
        out_shape=[jax.ShapeDtypeStruct((count, size, rows, LANES), jnp.float32) for _, size in chunks],
        scratch_shapes=[flat, padded, padded, flat, flat],
        compiler_params=PARAMS,
        cost_estimate=cost(100 * arrived.size, 12 * arrived.size),
    )(arrived)


def basis_kernel(planes, side_y, side_z, bands, *refs):
    raw_refs = refs[:bands]
    offset_ref, potential_ref, orbitals_ref, high_ref, low_ref, parts_ref, turned, placed = refs[bands:]
    cells = side_y * side_z
    for part in range(SPAN):
        at = pl.ds(part * cells, cells)
        stack = [raw_ref[block, :, at] for raw_ref in raw_refs for block in range(NEAR)]
        turned[part] = jnp.concatenate(stack, axis=0).T
    offset = offset_ref[0:1, :]

    def place(y, carry):
        at = pl.ds(pl.multiple_of(y * side_z, 8), side_z)
        values = [turned[part, at, :] for part in range(SPAN)]
        for plane in range(planes + 2 * HALO):
            row = jnp.zeros((side_z, LANES), jnp.float32)
            for part in range(SPAN):
                row = jnp.where(offset == float(plane - HALO - part), values[part], row)
            fill_row(placed, plane, y, row, side_z)
        return carry

    lax.fori_loop(0, side_y, place, 0)

    def line_of(load):
        return [load(plane) for plane in range(planes + 2 * HALO)]

    def finish(plane, y, start, at, total):
        own = placed[HALO + plane, y, pl.ds(PAD + start, 16), :]
        high, low = halves(jnp.concatenate([total, own], axis=1))
        high_ref[plane, at, :] = high
        low_ref[plane, at, :] = low

    local_part(placed, potential_ref, planes, HALO, side_y, side_z, line_of, finish)

    dot = functools.partial(jnp.dot, preferred_element_type=jnp.float32)
    with_orbitals = with_basis = 0.0
    for plane in range(planes):
        high, low = high_ref[plane], low_ref[plane]
        left = halves(orbitals_ref[plane].T)
        with_orbitals = with_orbitals + (dot(left[0], high) + (dot(left[0], low) + dot(left[1], high)))
        own_high, own_low = high[:, LANES:], low[:, LANES:]
        turned_high = own_high.astype(jnp.float32).T.astype(jnp.bfloat16)
        turned_low = own_low.astype(jnp.float32).T.astype(jnp.bfloat16)
        both = jnp.concatenate([own_high, own_low], axis=1)
        with_basis = with_basis + (dot(turned_high, both) + dot(turned_low, both))
    parts_ref[0] = with_orbitals[:, LANES:].T
    parts_ref[1] = with_orbitals[:, :LANES].T
    parts_ref[2] = folded(with_basis)


def build_basis(raw, offset, potential, orbitals, side_y, side_z):
    planes, cells, _ = orbitals.shape
    pair = jax.ShapeDtypeStruct((planes, cells, 2 * LANES), jnp.bfloat16)
    return pl.pallas_call(
        functools.partial(basis_kernel, planes, side_y, side_z, len(raw)),
        in_specs=[WHOLE] * (len(raw) + 3),
        out_specs=[WHOLE] * 3,
        out_shape=[pair, pair, jax.ShapeDtypeStruct((3, LANES, LANES), jnp.float32)],
        scratch_shapes=[
            pltpu.VMEM((SPAN, cells, LANES), jnp.float32),
            pltpu.VMEM((planes + 2 * HALO, side_y, side_z + 2 * PAD, LANES), jnp.float32),
        ],
        compiler_params=PARAMS,
        cost_estimate=cost(200 * orbitals.size, 24 * orbitals.size),
    )(*raw, offset, potential, orbitals)


def weights_kernel(bands, me_ref, parts_ref, coupling_ref, out_ref):
    count = parts_ref.shape[0]
    size = LANES // NEAR
    lines = size // bands
    me = me_ref[0]
    dot = functools.partial(jnp.dot, precision=HIGHEST, preferred_element_type=jnp.float32)

    def device(step):
        return lax.rem(me + step % count, count)

    def total(pick, block):
        shares = [pick(block - (near - BEFORE), near) for near in range(NEAR)]
        return (shares[0] + shares[1]) + (shares[2] + shares[3])

    def of_block(value, near):
        starts = [(band * NEAR + near) * lines for band in range(bands)]
        return jnp.concatenate([value[start : start + lines] for start in starts], axis=0)

    def joined(values):
        return jnp.concatenate(
            [values[near][band * lines : (band + 1) * lines] for band in range(bands) for near in range(NEAR)], axis=0
        )

    def couple(block, value):
        return dot(coupling_ref[device(block)], value)

    def kept(function):
        known = {}

        def look(step):
            if step % count not in known:
                known[step % count] = function(step)
            return known[step % count]

        return look

    weight = kept(
        lambda block: couple(block, total(lambda step, near: of_block(parts_ref[device(step), 0], near), block))
    )
    weights = kept(lambda step: joined([weight(step + near - BEFORE) for near in range(NEAR)]))
    second = kept(lambda step: parts_ref[device(step), 1] + dot(parts_ref[device(step), 2], weights(step)))
    out_ref[pl.ds(0, LANES), :] = weights(0)
    out_ref[pl.ds(LANES, LANES), :] = joined(
        [
            couple(near - BEFORE, total(lambda step, at: of_block(second(step), at), near - BEFORE))
            for near in range(NEAR)
        ]
    )


def near_weights(parts, coupling):
    return pl.pallas_call(
        functools.partial(weights_kernel, lax.axis_size("band")),
        in_specs=[pl.BlockSpec(memory_space=pltpu.SMEM), WHOLE, WHOLE],
        out_specs=WHOLE,
        out_shape=jax.ShapeDtypeStruct((2 * LANES, LANES), jnp.float32),
        compiler_params=PARAMS,
        cost_estimate=cost(0, 8 * parts.size),
    )(lax.axis_index("dom").astype(jnp.int32).reshape(1), parts, coupling)


def shifted(value, axis, step):
    count = lax.axis_size(axis)
    return lax.ppermute(value, axis, [(source, (source + step) % count) for source in range(count)])


def crossed(value, bit):
    return lax.ppermute(value, "band", [(source, source ^ bit) for source in range(lax.axis_size("band"))])


def gram_kernel(own_ref, *rest):
    panels, out_ref = (own_ref, *rest[:-1]), rest[-1]

    @pl.when(pl.program_id(0) == 0)
    def _():
        out_ref[...] = jnp.zeros_like(out_ref)

    for plane in range(own_ref.shape[0]):
        left = halves(own_ref[plane].T)
        for index, panel in enumerate(panels):
            at = pl.ds(index * LANES, LANES)
            out_ref[:, at] = out_ref[:, at] + folded(dot_halves(left, side_by_side(panel[plane])))


def gram_rows(panels):
    planes, cells, _ = panels[0].shape
    tile = cells // 4
    return pl.pallas_call(
        gram_kernel,
        grid=(cells // tile,),
        in_specs=[pl.BlockSpec((planes, tile, LANES), lambda i: (0, i, 0))] * len(panels),
        out_specs=pl.BlockSpec((LANES, len(panels) * LANES), lambda i: (0, 0)),
        out_shape=jax.ShapeDtypeStruct((LANES, len(panels) * LANES), jnp.float32),
        compiler_params=PARAMS,
        cost_estimate=cost(8 * panels[0].size * LANES * len(panels), 4 * panels[0].size * len(panels)),
    )(*panels)


def rotate_kernel(chunks, bands, inverse_ref, *rest):
    panels, out_ref = rest[:-1], rest[-1]
    right = side_by_side(inverse_ref[...].T)
    for index, (begin, size) in enumerate(chunks):
        group = panels[index * bands : (index + 1) * bands]
        for plane in range(size):
            left = halves(jnp.concatenate([panel[plane] for panel in group], axis=1))
            out_ref[begin + plane] = folded(dot_halves(left, right))


def rotated(inverse_rows, panels, chunks):
    bands = len(panels[0])
    planes = sum(size for _, size in chunks)
    cells = panels[0][0].shape[1]
    tile = cells // 4
    specs = [pl.BlockSpec((size, tile, LANES), lambda i: (0, i, 0)) for _, size in chunks for _ in range(bands)]
    return pl.pallas_call(
        functools.partial(rotate_kernel, chunks, bands),
        grid=(cells // tile,),
        in_specs=[pl.BlockSpec(inverse_rows.shape, lambda i: (0, 0)), *specs],
        out_specs=pl.BlockSpec((planes, tile, LANES), lambda i: (0, i, 0)),
        out_shape=jax.ShapeDtypeStruct((planes, cells, LANES), jnp.float32),
        compiler_params=PARAMS,
    )(inverse_rows, *[panel for group in panels for panel in group])


def thirds(value):
    first = value.astype(jnp.bfloat16).astype(jnp.float32)
    rest = value - first
    second = rest.astype(jnp.bfloat16).astype(jnp.float32)
    return first, second, rest - second


def eliminate(work, result):
    sublane = lax.broadcasted_iota(jnp.int32, (GROUP, LANES), 0)
    for top in range(0, LANES, GROUP):
        left = [jnp.broadcast_to(work[pl.ds(top + i, 1), :LANES], (GROUP, LANES)) for i in range(GROUP)]
        right = [jnp.broadcast_to(work[pl.ds(top + i, 1), LANES:], (GROUP, LANES)) for i in range(GROUP)]
        entry = {
            (i, j): jnp.broadcast_to(left[i][:, top + j : top + j + 1], (GROUP, LANES))
            for i in range(GROUP)
            for j in range(i, GROUP)
        }
        for i in range(GROUP):
            scale = lax.rsqrt(entry[i, i])
            left[i] = left[i] * scale
            right[i] = right[i] * scale
            factor = {j: entry[i, j] * scale for j in range(i + 1, GROUP)}
            for m in range(i + 1, GROUP):
                for j in range(m, GROUP):
                    entry[m, j] = entry[m, j] - factor[m] * factor[j]
                left[m] = left[m] - factor[m] * left[i]
                right[m] = right[m] - factor[m] * right[i]
        upper, lower = left[0], right[0]
        for i in range(1, GROUP):
            upper = jnp.where(sublane == i, left[i], upper)
            lower = jnp.where(sublane == i, right[i], lower)
        result[pl.ds(top, GROUP), :] = lower
        below = top + GROUP
        if below < LANES:
            a, b, c = thirds(upper)
            x, y, z = thirds(lower)
            columns = jnp.concatenate([a, a, b, b, a, c], axis=0).T[below:].astype(jnp.bfloat16)
            rows = jnp.concatenate(
                [jnp.concatenate([a, b, a, b, c, a], axis=0), jnp.concatenate([x, y, x, y, z, x], axis=0)], axis=1
            ).astype(jnp.bfloat16)
            rest = pl.ds(below, LANES - below)
            work[rest, :] = work[rest, :] - jnp.dot(columns, rows, preferred_element_type=jnp.float32)


def cholesky_kernel(band_ref, *refs):
    rows_refs, (gram_ref, own_ref, inverse, matrix, work, corner, scaled) = refs[:-7], refs[-7:]
    size = gram_ref.shape[0]
    bands = len(rows_refs)
    band = band_ref[0]

    def block_of(member):
        return pl.ds(pl.multiple_of((band ^ member) * LANES, LANES), LANES)

    for member, rows_ref in enumerate(rows_refs):
        for other in range(bands):
            gram_ref[block_of(member), block_of(member ^ other)] = rows_ref[:, other * LANES : (other + 1) * LANES]
    dot = functools.partial(jnp.dot, precision=HIGHEST, preferred_element_type=jnp.float32)
    diagonal = lax.broadcasted_iota(jnp.int32, (LANES, LANES), 0) == lax.broadcasted_iota(jnp.int32, (LANES, LANES), 1)
    identity = diagonal.astype(jnp.float32)
    matrix[:, :size] = gram_ref[...]
    matrix[:, size:] = jnp.zeros((size, size), jnp.float32)
    for at in range(0, size, LANES):
        matrix[pl.ds(at, LANES), size + at : size + at + LANES] = identity

    def block(index, carry):
        start = pl.multiple_of(index * LANES, LANES)
        at = pl.ds(start, LANES)
        work[:, :LANES] = matrix[at, at]
        work[:, LANES:] = identity
        eliminate(work, corner)
        scaled[...] = dot(corner[...], matrix[at, :])
        inverse[at, :] = scaled[:, size:]

        def below(other, carry):
            rows = pl.ds(pl.multiple_of(other * LANES, LANES), LANES)
            matrix[rows, :] = matrix[rows, :] - dot(scaled[:, rows].T, scaled[...])
            return carry

        lax.fori_loop(index + 1, size // LANES, below, 0)
        return carry

    lax.fori_loop(0, size // LANES, block, 0)
    for member in range(bands):
        own_ref[:, member * LANES : (member + 1) * LANES] = inverse[block_of(0), block_of(member)]


def cholesky_inverse(band, rows):
    size = rows[0].shape[1]
    whole = pl.BlockSpec(memory_space=pltpu.VMEM)
    return pl.pallas_call(
        cholesky_kernel,
        in_specs=[pl.BlockSpec(memory_space=pltpu.SMEM)] + [whole] * len(rows),
        out_specs=[whole] * 2,
        out_shape=[
            jax.ShapeDtypeStruct((size, size), jnp.float32),
            jax.ShapeDtypeStruct((LANES, size), jnp.float32),
        ],
        scratch_shapes=[
            pltpu.VMEM((size, size), jnp.float32),
            pltpu.VMEM((size, 2 * size), jnp.float32),
            pltpu.VMEM((LANES, 2 * LANES), jnp.float32),
            pltpu.VMEM((LANES, LANES), jnp.float32),
            pltpu.VMEM((LANES, 2 * size), jnp.float32),
        ],
        compiler_params=PARAMS,
    )(band.astype(jnp.int32).reshape(1), *rows)


def packed_projectors(projectors, atom_plane, planes):
    share = projectors.shape[0] // lax.axis_size("band")
    first = (atom_plane - lax.axis_index("dom") * planes).astype(jnp.float32)
    first = jnp.broadcast_to(first[:, None, None], (projectors.shape[0], MAXPROJ, LANES))
    packed = jnp.concatenate([projectors, first], axis=2)
    mine = lax.dynamic_slice_in_dim(packed, lax.axis_index("band") * share, share, 0)
    return mine.reshape(share * MAXPROJ, -1)


def near_projectors(mine, planes):
    near = [mine if step == BEFORE else shifted(mine, "dom", BEFORE - step) for step in range(NEAR)]
    near = jnp.stack(near)
    across = crossed(near, 2)
    raw = [near, crossed(near, 1), across, crossed(across, 1)]
    moved = (planes * (jnp.arange(NEAR, dtype=jnp.float32) - BEFORE))[:, None]
    first = jnp.stack([member[:, :, -1] + moved for member in raw]).reshape(1, LANES)
    return raw, jnp.broadcast_to(first, (GROUP, LANES))


def shards(orbitals, potential, projectors, coupling, atom_plane, projector_count):
    planes, side_y, side_z, local_orbs = orbitals.shape
    blocks, bands = lax.axis_size("dom"), lax.axis_size("band")
    band = lax.axis_index("band")
    cells = side_y * side_z
    rows = cells // blocks
    width = local_orbs // blocks
    norb = local_orbs * bands
    chunks = ((0, 2), (2, 1), (3, 1))

    order = jnp.arange(bands, dtype=jnp.int32) ^ band

    mine = packed_projectors(projectors, atom_plane, planes)
    mine, levels = lax.optimization_barrier((mine, potential.reshape(planes, cells // LANES, LANES)))
    raw, first = near_projectors(mine, planes)
    levels = jnp.pad(levels, ((0, 0), (0, -levels.shape[1] % GROUP), (0, 0)))
    packed = swap_in(levels, orbitals.reshape(planes, blocks, rows, local_orbs))
    arrived = lax.all_to_all(packed, "dom", 0, 0, tiled=True)

    own_levels = jnp.broadcast_to(potential.reshape(planes, cells, 1), (planes, cells, LANES))
    high, low, parts = build_basis(raw, first, own_levels, orbitals.reshape(planes, cells, LANES), side_y, side_z)
    atoms = projectors.shape[0]
    slots = jnp.arange(MAXPROJ, dtype=jnp.int32)
    live = (slots[None, :] < projector_count[:, None]).astype(jnp.float32)
    coupled = 0.5 * (coupling + jnp.transpose(coupling, (0, 2, 1))) * live[:, :, None] * live[:, None, :]
    coupled = jnp.take(coupled.reshape(bands, -1, MAXPROJ, MAXPROJ), order, axis=0)
    vectors = atoms * MAXPROJ
    row = jnp.arange(vectors, dtype=jnp.int32) // MAXPROJ
    matrix = jnp.tile(coupled.reshape(vectors, MAXPROJ), (1, atoms))
    matrix = jnp.where(row[:, None] == row[None, :], matrix, 0.0)
    matrix = jnp.pad(matrix, ((0, 0), (0, LANES - vectors)))
    everyone = lax.all_gather(jnp.concatenate([parts.reshape(3 * LANES, LANES), matrix], axis=0), "dom")
    weights = near_weights(
        everyone[:, : 3 * LANES].reshape(blocks, 3, LANES, LANES), everyone[:, 3 * LANES :, :vectors]
    )

    seconds = filter_orbitals(arrived, side_y, side_z, width, chunks)

    panels, part = [], 0.0
    for (begin, size), packed in zip(chunks, seconds):
        own = swap_out(lax.all_to_all(packed, "dom", 0, 0, tiled=True), high, low, weights, begin)
        across = crossed(own, 2)
        panels.append([own, crossed(own, 1), across, crossed(across, 1)])
        part = part + gram_rows(panels[-1])

    pieces = lax.all_to_all(part.reshape(blocks, width, norb), "dom", 0, 0, tiled=True)
    piece = jnp.sum(pieces, axis=0) * (1.0 / (planes * cells * blocks))
    own_gram = lax.all_to_all(jnp.broadcast_to(piece, (blocks, width, norb)), "dom", 0, 0, tiled=True)
    own_gram = own_gram.reshape(local_orbs, norb)
    across = crossed(own_gram, 2)
    gram, own_rows = cholesky_inverse(band, [own_gram, crossed(own_gram, 1), across, crossed(across, 1)])
    result = rotated(own_rows, panels, chunks)
    return (result.reshape(planes, side_y, side_z, local_orbs), gram)


def solution(mesh):
    placed = (
        P("dom", None, None, "band"),
        P("dom", None, None),
        P("dom", None, None),
        P("dom", None, None),
        P("dom"),
        P("dom"),
    )
    return jax.shard_map(
        shards,
        mesh=mesh,
        in_specs=placed,
        out_specs=(P("dom", None, None, "band"), P()),
        check_vma=False,
    )
```

```python
import functools

import jax
import jax.numpy as jnp
from jax import lax
from jax.experimental import pallas as pl
from jax.experimental.pallas import tpu as pltpu
from jax.sharding import PartitionSpec as P

SPAN = 3
MAXPROJ = 4
HALO = 4
PAD = 8
LANES = 128
GROUP = 8
BEFORE, AFTER = 2, 1
NEAR = BEFORE + 1 + AFTER

center_weight = -205.0 / 72.0
side_weights = (8.0 / 5.0, -1.0 / 5.0, 8.0 / 315.0, -1.0 / 560.0)
HIGHEST = lax.Precision.HIGHEST
WHOLE = pl.BlockSpec(memory_space=pltpu.VMEM)


def params(mebibytes):
    return pltpu.CompilerParams(vmem_limit_bytes=mebibytes * 1024 * 1024)


def cost(flops, bytes_accessed):
    return pl.CostEstimate(flops=int(flops), bytes_accessed=int(bytes_accessed), transcendentals=0)


def halves(value):
    high = value.astype(jnp.bfloat16)
    return high, (value - high.astype(jnp.float32)).astype(jnp.bfloat16)


def side_by_side(value):
    return jnp.concatenate(halves(value), axis=1)


def dot_halves(left, right):
    dot = functools.partial(jnp.dot, preferred_element_type=jnp.float32)
    return dot(left[0], right) + dot(left[1], right)


def folded(value):
    return value[:, :LANES] + value[:, LANES:]


def swapped(blocks, lane):
    count = len(blocks)
    width = LANES // count
    blocks = [pltpu.roll(value, at * width, 1) if at else value for at, value in enumerate(blocks)]
    bit = 1
    while bit < count:
        chosen = (lane // (bit * width)) % 2 == 1
        blocks = [jnp.where(chosen, blocks[(at + bit) % count], blocks[at]) for at in range(count)]
        bit *= 2
    blocks = [blocks[-at % count] for at in range(count)]
    return [pltpu.roll(value, LANES - at * width, 1) if at else value for at, value in enumerate(blocks)]


def swap_into(read, write, count, rows):
    tile = 8 * max(1, 32 // count)
    lane = lax.broadcasted_iota(jnp.int32, (tile, LANES), 1)

    def step(index, carry):
        start = pl.multiple_of(index * tile, 8)
        for block, value in enumerate(swapped([read(block, start, tile) for block in range(count)], lane)):
            write(block, start, tile, value)
        return carry

    lax.fori_loop(0, rows // tile, step, 0, unroll=True)


def swap_in_kernel(count, rows, levels_ref, in_ref, out_ref):
    def read(block, start, size):
        return in_ref[block, pl.ds(start, size), :]

    def write(block, start, size, value):
        out_ref[block, pl.ds(start, size), :] = value

    swap_into(read, write, count, rows)
    for block in range(count):
        out_ref[block, pl.ds(rows, levels_ref.shape[0]), :] = levels_ref[...]


def swap_in(levels, value):
    planes, count, rows, _ = value.shape
    extra = levels.shape[1]
    return pl.pallas_call(
        functools.partial(swap_in_kernel, count, rows),
        grid=(planes,),
        in_specs=[
            pl.BlockSpec((None, extra, LANES), lambda p: (p, 0, 0)),
            pl.BlockSpec((None, count, rows, LANES), lambda p: (p, 0, 0, 0)),
        ],
        out_specs=pl.BlockSpec((count, None, rows + extra, LANES), lambda p: (0, p, 0, 0)),
        out_shape=jax.ShapeDtypeStruct((count, planes, rows + extra, LANES), jnp.float32),
        compiler_params=params(12),
        cost_estimate=cost(0, 8 * value.size),
    )(levels, value)


def swap_out_kernel(count, rows, arrived_ref, high_ref, low_ref, weights_ref, out_ref):
    planes = out_ref.shape[0]
    weights = side_by_side(weights_ref[...] * (1.0 / 18.0))
    for plane in range(planes):

        def read(block, start, size):
            return arrived_ref[block, plane, pl.ds(start, size), :]

        def write(block, start, size, value):
            at = pl.ds(pl.multiple_of(block * rows + start, 8), size)
            out_ref[plane, at, :] = value

        swap_into(read, write, count, rows)
        tile = rows * count // 6

        def add(index, carry):
            at = pl.ds(pl.multiple_of(index * tile, 8), tile)
            term = folded(dot_halves((high_ref[plane, at, :], low_ref[plane, at, :]), weights))
            out_ref[plane, at, :] = out_ref[plane, at, :] + term
            return carry

        lax.fori_loop(0, 6, add, 0)


def swap_out(arrived, high, low, weights, first_plane):
    count, planes, rows, _ = arrived.shape
    cells = count * rows
    basis = pl.BlockSpec((planes, cells, 2 * LANES), lambda i: (first_plane // planes, 0, 0))
    return pl.pallas_call(
        functools.partial(swap_out_kernel, count, rows),
        grid=(1,),
        in_specs=[
            pl.BlockSpec(arrived.shape, lambda i: (0, 0, 0, 0)),
            basis,
            basis,
            pl.BlockSpec(weights.shape, lambda i: (0, 0)),
        ],
        out_specs=pl.BlockSpec((planes, cells, LANES), lambda i: (0, 0, 0)),
        out_shape=jax.ShapeDtypeStruct((planes, cells, LANES), jnp.float32),
        compiler_params=params(24),
        cost_estimate=cost(0, 24 * arrived.size),
    )(arrived, high, low, weights)


def fill_row(target, plane, y, row, side_z):
    target[plane, y, pl.ds(PAD, side_z), :] = row
    target[plane, y, pl.ds(PAD - HALO, HALO), :] = row[side_z - HALO :]
    target[plane, y, pl.ds(PAD + side_z, HALO), :] = row[:HALO]


def local_part(source, potential_ref, planes, first, side_y, side_z, line_of, finish):
    tile = 16

    def row(y, carry):
        for start in range(0, side_z, tile):

            def load(plane, y_at, shift):
                return source[plane, y_at, pl.ds(PAD + start + shift, tile), :]

            line = line_of(lambda plane: load(plane, y, 0))
            at = pl.ds(pl.multiple_of(y * side_z + start, 8), tile)
            for plane in range(planes):
                here = first + plane
                total = (potential_ref[plane, at, :] - 1.5 * center_weight - 7.0) * line[HALO + plane]
                for offset in range(1, HALO + 1):
                    around = line[HALO + plane + offset] + line[HALO + plane - offset]
                    around = around + (load(here, y, offset) + load(here, y, -offset))
                    up = lax.rem(y + offset, side_y)
                    down = lax.rem(y + side_y - offset, side_y)
                    around = around + (load(here, up, 0) + load(here, down, 0))
                    total = total - (0.5 * side_weights[offset - 1]) * around
                finish(plane, y, start, at, total)
        return carry

    lax.fori_loop(0, side_y, row, 0)


def filter_kernel(planes, side_y, side_z, width, chunks, arrived_ref, *rest):
    outs, (field, padded, first, flat, potential) = rest[: len(chunks)], rest[len(chunks) :]
    count = arrived_ref.shape[0]
    cells = side_y * side_z
    rows = cells // count
    tile = 16

    line = lax.broadcasted_iota(jnp.int32, (2 * count, LANES), 0) % count
    lane = lax.broadcasted_iota(jnp.int32, (2 * count, LANES), 1) // width
    spread = (line == lane).astype(jnp.bfloat16)
    for plane in range(planes):
        lines = [arrived_ref[:, plane, rows + at, :] for at in range(cells // LANES)]
        high, low = halves(jnp.concatenate(lines, axis=1))
        both = jnp.concatenate([high.astype(jnp.float32), low.astype(jnp.float32)], axis=0)
        potential[plane] = jnp.dot(both.T.astype(jnp.bfloat16), spread, preferred_element_type=jnp.float32)

    for plane in range(planes):

        def read_in(block, start, size):
            return arrived_ref[block, plane, pl.ds(start, size), :]

        def write_in(block, start, size, value):
            field[plane, pl.ds(pl.multiple_of(block * rows + start, 8), size), :] = value

        swap_into(read_in, write_in, count, rows)

    def fill(y, carry):
        for plane in range(planes):
            fill_row(padded, plane, y, field[plane, pl.ds(pl.multiple_of(y * side_z, 8), side_z), :], side_z)
        return carry

    lax.fori_loop(0, side_y, fill, 0)

    def line_of(load):
        inside = [load(plane) for plane in range(planes)]
        before = [pltpu.roll(value, width, 1) for value in inside]
        after = [pltpu.roll(value, LANES - width, 1) for value in inside]
        return before[planes - HALO :] + inside + after[:HALO]

    def finish_first(plane, y, start, at, total):
        first[plane, y, pl.ds(PAD + start, tile), :] = total
        if start == 0:
            first[plane, y, pl.ds(PAD + side_z, HALO), :] = total[:HALO]
        if start == side_z - tile:
            first[plane, y, pl.ds(PAD - HALO, HALO), :] = total[tile - HALO :]

    def finish_second(plane, y, start, at, total):
        flat[plane, at, :] = total * (1.0 / 18.0) - field[plane, at, :]

    local_part(padded, potential, planes, 0, side_y, side_z, line_of, finish_first)
    local_part(first, potential, planes, 0, side_y, side_z, line_of, finish_second)

    for (begin, size_of), out_ref in zip(chunks, outs):
        for plane in range(size_of):

            def read_out(block, start, size):
                return flat[begin + plane, pl.ds(pl.multiple_of(block * rows + start, 8), size), :]

            def write_out(block, start, size, value):
                out_ref[block, plane, pl.ds(start, size), :] = value

            swap_into(read_out, write_out, count, rows)


def filter_orbitals(arrived, side_y, side_z, width, chunks):
    count, planes = arrived.shape[:2]
    rows = side_y * side_z // count
    flat = pltpu.VMEM((planes, side_y * side_z, LANES), jnp.float32)
    padded = pltpu.VMEM((planes, side_y, side_z + 2 * PAD, LANES), jnp.float32)
    return pl.pallas_call(
        functools.partial(filter_kernel, planes, side_y, side_z, width, chunks),
        in_specs=[WHOLE],
        out_specs=[WHOLE] * len(chunks),
        out_shape=[jax.ShapeDtypeStruct((count, size, rows, LANES), jnp.float32) for _, size in chunks],
        scratch_shapes=[flat, padded, padded, flat, flat],
        compiler_params=params(56),
        cost_estimate=cost(100 * arrived.size, 12 * arrived.size),
    )(arrived)


def basis_kernel(planes, side_y, side_z, bands, *refs):
    raw_refs = refs[:bands]
    offset_ref, potential_ref, orbitals_ref, high_ref, low_ref, parts_ref, turned, placed = refs[bands:]
    cells = side_y * side_z
    for part in range(SPAN):
        at = pl.ds(part * cells, cells)
        stack = [raw_ref[block, :, at] for raw_ref in raw_refs for block in range(NEAR)]
        turned[part] = jnp.concatenate(stack, axis=0).T
    offset = offset_ref[0:1, :]

    def place(y, carry):
        at = pl.ds(pl.multiple_of(y * side_z, 8), side_z)
        values = [turned[part, at, :] for part in range(SPAN)]
        for plane in range(planes + 2 * HALO):
            row = jnp.zeros((side_z, LANES), jnp.float32)
            for part in range(SPAN):
                row = jnp.where(offset == float(plane - HALO - part), values[part], row)
            fill_row(placed, plane, y, row, side_z)
        return carry

    lax.fori_loop(0, side_y, place, 0)

    def line_of(load):
        return [load(plane) for plane in range(planes + 2 * HALO)]

    def finish(plane, y, start, at, total):
        own = placed[HALO + plane, y, pl.ds(PAD + start, 16), :]
        high, low = halves(jnp.concatenate([total, own], axis=1))
        high_ref[plane, at, :] = high
        low_ref[plane, at, :] = low

    local_part(placed, potential_ref, planes, HALO, side_y, side_z, line_of, finish)

    dot = functools.partial(jnp.dot, preferred_element_type=jnp.float32)
    with_orbitals = with_basis = 0.0
    for plane in range(planes):
        high, low = high_ref[plane], low_ref[plane]
        left = halves(orbitals_ref[plane].T)
        with_orbitals = with_orbitals + (dot(left[0], high) + (dot(left[0], low) + dot(left[1], high)))
        own_high, own_low = high[:, LANES:], low[:, LANES:]
        turned_high = own_high.astype(jnp.float32).T.astype(jnp.bfloat16)
        turned_low = own_low.astype(jnp.float32).T.astype(jnp.bfloat16)
        both = jnp.concatenate([own_high, own_low], axis=1)
        with_basis = with_basis + (dot(turned_high, both) + dot(turned_low, both))
    parts_ref[0] = with_orbitals[:, LANES:].T
    parts_ref[1] = with_orbitals[:, :LANES].T
    parts_ref[2] = folded(with_basis)


def build_basis(raw, offset, potential, orbitals, side_y, side_z):
    planes, cells, _ = orbitals.shape
    pair = jax.ShapeDtypeStruct((planes, cells, 2 * LANES), jnp.bfloat16)
    return pl.pallas_call(
        functools.partial(basis_kernel, planes, side_y, side_z, len(raw)),
        in_specs=[WHOLE] * (len(raw) + 3),
        out_specs=[WHOLE] * 3,
        out_shape=[pair, pair, jax.ShapeDtypeStruct((3, LANES, LANES), jnp.float32)],
        scratch_shapes=[
            pltpu.VMEM((SPAN, cells, LANES), jnp.float32),
            pltpu.VMEM((planes + 2 * HALO, side_y, side_z + 2 * PAD, LANES), jnp.float32),
        ],
        compiler_params=params(56),
        cost_estimate=cost(200 * orbitals.size, 24 * orbitals.size),
    )(*raw, offset, potential, orbitals)


def weights_kernel(bands, me_ref, parts_ref, coupling_ref, out_ref):
    count = parts_ref.shape[0]
    size = LANES // NEAR
    lines = size // bands
    me = me_ref[0]
    dot = functools.partial(jnp.dot, precision=HIGHEST, preferred_element_type=jnp.float32)

    def device(step):
        return lax.rem(me + step % count, count)

    def total(pick, block):
        shares = [pick(block - (near - BEFORE), near) for near in range(NEAR)]
        return (shares[0] + shares[1]) + (shares[2] + shares[3])

    def of_block(value, near):
        starts = [(band * NEAR + near) * lines for band in range(bands)]
        return jnp.concatenate([value[start : start + lines] for start in starts], axis=0)

    def joined(values):
        return jnp.concatenate(
            [values[near][band * lines : (band + 1) * lines] for band in range(bands) for near in range(NEAR)], axis=0
        )

    def couple(block, value):
        return dot(coupling_ref[device(block)], value)

    def kept(function):
        known = {}

        def look(step):
            if step % count not in known:
                known[step % count] = function(step)
            return known[step % count]

        return look

    weight = kept(
        lambda block: couple(block, total(lambda step, near: of_block(parts_ref[device(step), 0], near), block))
    )
    weights = kept(lambda step: joined([weight(step + near - BEFORE) for near in range(NEAR)]))
    second = kept(lambda step: parts_ref[device(step), 1] + dot(parts_ref[device(step), 2], weights(step)))
    out_ref[pl.ds(0, LANES), :] = weights(0)
    out_ref[pl.ds(LANES, LANES), :] = joined(
        [
            couple(near - BEFORE, total(lambda step, at: of_block(second(step), at), near - BEFORE))
            for near in range(NEAR)
        ]
    )


def near_weights(parts, coupling):
    return pl.pallas_call(
        functools.partial(weights_kernel, lax.axis_size("band")),
        in_specs=[pl.BlockSpec(memory_space=pltpu.SMEM), WHOLE, WHOLE],
        out_specs=WHOLE,
        out_shape=jax.ShapeDtypeStruct((2 * LANES, LANES), jnp.float32),
        compiler_params=params(24),
        cost_estimate=cost(0, 8 * parts.size),
    )(lax.axis_index("dom").astype(jnp.int32).reshape(1), parts, coupling)


def shifted(value, axis, step):
    count = lax.axis_size(axis)
    return lax.ppermute(value, axis, [(source, (source + step) % count) for source in range(count)])


def crossed(value, bit):
    return lax.ppermute(value, "band", [(source, source ^ bit) for source in range(lax.axis_size("band"))])


def gram_kernel(own_ref, *rest):
    panels, out_ref = (own_ref, *rest[:-1]), rest[-1]

    @pl.when(pl.program_id(0) == 0)
    def _():
        out_ref[...] = jnp.zeros_like(out_ref)

    for plane in range(own_ref.shape[0]):
        left = halves(own_ref[plane].T)
        both = jnp.concatenate([side_by_side(panel[plane]) for panel in panels], axis=1)
        value = dot_halves(left, both)
        for index in range(len(panels)):
            at = pl.ds(index * LANES, LANES)
            out_ref[:, at] = out_ref[:, at] + folded(value[:, 2 * index * LANES : 2 * (index + 1) * LANES])


def gram_rows(panels):
    planes, cells, _ = panels[0].shape
    tile = cells // 2
    return pl.pallas_call(
        gram_kernel,
        grid=(cells // tile,),
        in_specs=[pl.BlockSpec((planes, tile, LANES), lambda i: (0, i, 0))] * len(panels),
        out_specs=pl.BlockSpec((LANES, len(panels) * LANES), lambda i: (0, 0)),
        out_shape=jax.ShapeDtypeStruct((LANES, len(panels) * LANES), jnp.float32),
        compiler_params=params(16),
        cost_estimate=cost(8 * panels[0].size * LANES * len(panels), 4 * panels[0].size * len(panels)),
    )(*panels)


def rotate_kernel(chunks, bands, inverse_ref, *rest):
    panels, out_ref = rest[:-1], rest[-1]
    right = side_by_side(inverse_ref[...].T)
    for index, (begin, size) in enumerate(chunks):
        group = panels[index * bands : (index + 1) * bands]
        for plane in range(size):
            left = halves(jnp.concatenate([panel[plane] for panel in group], axis=1))
            out_ref[begin + plane] = folded(dot_halves(left, right))


def rotated(inverse_rows, panels, chunks):
    bands = len(panels[0])
    planes = sum(size for _, size in chunks)
    cells = panels[0][0].shape[1]
    tile = cells // 4
    specs = [pl.BlockSpec((size, tile, LANES), lambda i: (0, i, 0)) for _, size in chunks for _ in range(bands)]
    return pl.pallas_call(
        functools.partial(rotate_kernel, chunks, bands),
        grid=(cells // tile,),
        in_specs=[pl.BlockSpec(inverse_rows.shape, lambda i: (0, 0)), *specs],
        out_specs=pl.BlockSpec((planes, tile, LANES), lambda i: (0, i, 0)),
        out_shape=jax.ShapeDtypeStruct((planes, cells, LANES), jnp.float32),
        compiler_params=params(24),
    )(inverse_rows, *[panel for group in panels for panel in group])


def thirds(value):
    first = value.astype(jnp.bfloat16).astype(jnp.float32)
    rest = value - first
    second = rest.astype(jnp.bfloat16).astype(jnp.float32)
    return first, second, rest - second


def eliminate(work, result):
    sublane = lax.broadcasted_iota(jnp.int32, (GROUP, LANES), 0)

    def splat(row, column):
        return jnp.broadcast_to(row[:, column : column + 1], (GROUP, LANES))

    def load(top):
        left = [jnp.broadcast_to(work[pl.ds(top + i, 1), :LANES], (GROUP, LANES)) for i in range(GROUP)]
        right = [jnp.broadcast_to(work[pl.ds(top + i, 1), LANES:], (GROUP, LANES)) for i in range(GROUP)]
        return left, right

    def factored(top, left, right):
        entry = {(i, j): splat(left[i], top + j) for i in range(GROUP) for j in range(i, GROUP)}
        for i in range(GROUP):
            scale = lax.rsqrt(entry[i, i])
            left[i] = left[i] * scale
            right[i] = right[i] * scale
            factor = {j: entry[i, j] * scale for j in range(i + 1, GROUP)}
            for m in range(i + 1, GROUP):
                for j in range(m, GROUP):
                    entry[m, j] = entry[m, j] - factor[m] * factor[j]
                left[m] = left[m] - factor[m] * left[i]
                right[m] = right[m] - factor[m] * right[i]

    def gathered(rows):
        value = rows[0]
        for i in range(1, GROUP):
            value = jnp.where(sublane == i, rows[i], value)
        return value

    for top in range(0, LANES, 2 * GROUP):
        left, right = load(top)
        factored(top, left, right)
        middle = top + GROUP
        next_left, next_right = load(middle)
        for m in range(GROUP):
            for i in range(GROUP):
                factor = splat(left[i], middle + m)
                next_left[m] = next_left[m] - factor * left[i]
                next_right[m] = next_right[m] - factor * right[i]
        factored(middle, next_left, next_right)
        upper = jnp.concatenate([gathered(left), gathered(next_left)], axis=0)
        lower = jnp.concatenate([gathered(right), gathered(next_right)], axis=0)
        result[pl.ds(top, 2 * GROUP), :] = lower
        below = middle + GROUP
        if below < LANES:
            a, b, c = thirds(upper)
            x, y, z = thirds(lower)
            columns = jnp.concatenate([a, a, b, b, a, c], axis=0).T[below:].astype(jnp.bfloat16)
            rows = jnp.concatenate(
                [jnp.concatenate([a, b, a, b, c, a], axis=0), jnp.concatenate([x, y, x, y, z, x], axis=0)], axis=1
            ).astype(jnp.bfloat16)
            rest = pl.ds(below, LANES - below)
            work[rest, :] = work[rest, :] - jnp.dot(columns, rows, preferred_element_type=jnp.float32)


def cholesky_kernel(band_ref, *refs):
    rows_refs, (gram_ref, own_ref, inverse, matrix, work, corner, scaled) = refs[:-7], refs[-7:]
    size = gram_ref.shape[0]
    bands = len(rows_refs)
    band = band_ref[0]

    def block_of(member):
        return pl.ds(pl.multiple_of((band ^ member) * LANES, LANES), LANES)

    for member, rows_ref in enumerate(rows_refs):
        for other in range(bands):
            gram_ref[block_of(member), block_of(member ^ other)] = rows_ref[:, other * LANES : (other + 1) * LANES]
    dot = functools.partial(jnp.dot, precision=HIGHEST, preferred_element_type=jnp.float32)
    diagonal = lax.broadcasted_iota(jnp.int32, (LANES, LANES), 0) == lax.broadcasted_iota(jnp.int32, (LANES, LANES), 1)
    identity = diagonal.astype(jnp.float32)
    matrix[:, :size] = gram_ref[...]
    matrix[:, size:] = jnp.zeros((size, size), jnp.float32)
    for at in range(0, size, LANES):
        matrix[pl.ds(at, LANES), size + at : size + at + LANES] = identity

    def block(index, carry):
        start = pl.multiple_of(index * LANES, LANES)
        at = pl.ds(start, LANES)
        work[:, :LANES] = matrix[at, at]
        work[:, LANES:] = identity
        eliminate(work, corner)
        scaled[...] = dot(corner[...], matrix[at, :])
        inverse[at, :] = scaled[:, size:]

        def below(other, carry):
            rows = pl.ds(pl.multiple_of(other * LANES, LANES), LANES)
            matrix[rows, :] = matrix[rows, :] - dot(scaled[:, rows].T, scaled[...])
            return carry

        lax.fori_loop(index + 1, size // LANES, below, 0)
        return carry

    lax.fori_loop(0, size // LANES, block, 0)
    for member in range(bands):
        own_ref[:, member * LANES : (member + 1) * LANES] = inverse[block_of(0), block_of(member)]


def cholesky_inverse(band, rows):
    size = rows[0].shape[1]
    return pl.pallas_call(
        cholesky_kernel,
        in_specs=[pl.BlockSpec(memory_space=pltpu.SMEM)] + [WHOLE] * len(rows),
        out_specs=[WHOLE] * 2,
        out_shape=[
            jax.ShapeDtypeStruct((size, size), jnp.float32),
            jax.ShapeDtypeStruct((LANES, size), jnp.float32),
        ],
        scratch_shapes=[
            pltpu.VMEM((size, size), jnp.float32),
            pltpu.VMEM((size, 2 * size), jnp.float32),
            pltpu.VMEM((LANES, 2 * LANES), jnp.float32),
            pltpu.VMEM((LANES, LANES), jnp.float32),
            pltpu.VMEM((LANES, 2 * size), jnp.float32),
        ],
        compiler_params=params(14),
    )(band.astype(jnp.int32).reshape(1), *rows)


def packed_projectors(projectors, atom_plane, planes):
    share = projectors.shape[0] // lax.axis_size("band")
    first = (atom_plane - lax.axis_index("dom") * planes).astype(jnp.float32)
    first = jnp.broadcast_to(first[:, None, None], (projectors.shape[0], MAXPROJ, LANES))
    packed = jnp.concatenate([projectors, first], axis=2)
    mine = lax.dynamic_slice_in_dim(packed, lax.axis_index("band") * share, share, 0)
    return mine.reshape(share * MAXPROJ, -1)


def near_shares(mine):
    return jnp.stack([mine if step == BEFORE else shifted(mine, "dom", BEFORE - step) for step in range(NEAR)])


def near_projectors(near, planes):
    across = crossed(near, 2)
    raw = [near, crossed(near, 1), across, crossed(across, 1)]
    moved = (planes * (jnp.arange(NEAR, dtype=jnp.float32) - BEFORE))[:, None]
    first = jnp.stack([member[:, :, -1] + moved for member in raw]).reshape(1, LANES)
    return raw, jnp.broadcast_to(first, (GROUP, LANES))


def shards(orbitals, potential, projectors, coupling, atom_plane, projector_count):
    planes, side_y, side_z, local_orbs = orbitals.shape
    blocks, bands = lax.axis_size("dom"), lax.axis_size("band")
    band = lax.axis_index("band")
    cells = side_y * side_z
    rows = cells // blocks
    width = local_orbs // blocks
    norb = local_orbs * bands
    chunks = ((0, 2), (2, 1), (3, 1))

    order = jnp.arange(bands, dtype=jnp.int32) ^ band

    mine = packed_projectors(projectors, atom_plane, planes)
    mine, levels = lax.optimization_barrier((mine, potential.reshape(planes, cells // LANES, LANES)))
    near = near_shares(mine)
    levels = jnp.pad(levels, ((0, 0), (0, -levels.shape[1] % GROUP), (0, 0)))
    packed = swap_in(levels, orbitals.reshape(planes, blocks, rows, local_orbs))
    packed, near = lax.optimization_barrier((packed, near))
    raw, first = near_projectors(near, planes)
    arrived = lax.all_to_all(packed, "dom", 0, 0, tiled=True)

    own_levels = jnp.broadcast_to(potential.reshape(planes, cells, 1), (planes, cells, LANES))
    high, low, parts = build_basis(raw, first, own_levels, orbitals.reshape(planes, cells, LANES), side_y, side_z)
    atoms = projectors.shape[0]
    slots = jnp.arange(MAXPROJ, dtype=jnp.int32)
    live = (slots[None, :] < projector_count[:, None]).astype(jnp.float32)
    coupled = 0.5 * (coupling + jnp.transpose(coupling, (0, 2, 1))) * live[:, :, None] * live[:, None, :]
    coupled = jnp.take(coupled.reshape(bands, -1, MAXPROJ, MAXPROJ), order, axis=0)
    vectors = atoms * MAXPROJ
    row = jnp.arange(vectors, dtype=jnp.int32) // MAXPROJ
    matrix = jnp.tile(coupled.reshape(vectors, MAXPROJ), (1, atoms))
    matrix = jnp.where(row[:, None] == row[None, :], matrix, 0.0)
    matrix = jnp.pad(matrix, ((0, 0), (0, LANES - vectors)))
    everyone = lax.all_gather(jnp.concatenate([parts.reshape(3 * LANES, LANES), matrix], axis=0), "dom")
    weights = near_weights(
        everyone[:, : 3 * LANES].reshape(blocks, 3, LANES, LANES), everyone[:, 3 * LANES :, :vectors]
    )

    seconds = filter_orbitals(arrived, side_y, side_z, width, chunks)

    panels, part = [], 0.0
    for (begin, size), packed in zip(chunks, seconds):
        own = swap_out(lax.all_to_all(packed, "dom", 0, 0, tiled=True), high, low, weights, begin)
        across = crossed(own, 2)
        if panels:
            across, part = lax.optimization_barrier((across, part))
        panels.append([own, crossed(own, 1), across, crossed(across, 1)])
        part = part + gram_rows(panels[-1])

    pieces = lax.all_to_all(part.reshape(blocks, width, norb), "dom", 0, 0, tiled=True)
    piece = jnp.sum(pieces, axis=0) * (1.0 / (planes * cells * blocks))
    own_gram = lax.all_to_all(jnp.broadcast_to(piece, (blocks, width, norb)), "dom", 0, 0, tiled=True)
    own_gram = own_gram.reshape(local_orbs, norb)
    across = crossed(own_gram, 2)
    gram, own_rows = cholesky_inverse(band, [own_gram, crossed(own_gram, 1), across, crossed(across, 1)])
    result = rotated(own_rows, panels, chunks)
    return (result.reshape(planes, side_y, side_z, local_orbs), gram)


def solution(mesh):
    placed = (
        P("dom", None, None, "band"),
        P("dom", None, None),
        P("dom", None, None),
        P("dom", None, None),
        P("dom"),
        P("dom"),
    )
    return jax.shard_map(
        shards,
        mesh=mesh,
        in_specs=placed,
        out_specs=(P("dom", None, None, "band"), P()),
        check_vma=False,
    )
```

```python
import functools

import jax
import jax.numpy as jnp
from jax import lax
from jax.experimental import pallas as pl
from jax.experimental.pallas import tpu as pltpu
from jax.sharding import PartitionSpec as P

SPAN = 3
MAXPROJ = 4
HALO = 4
PAD = 8
LANES = 128
GROUP = 8
BEFORE, AFTER = 2, 1
NEAR = BEFORE + 1 + AFTER

center_weight = -205.0 / 72.0
side_weights = (8.0 / 5.0, -1.0 / 5.0, 8.0 / 315.0, -1.0 / 560.0)
HIGHEST = lax.Precision.HIGHEST
WHOLE = pl.BlockSpec(memory_space=pltpu.VMEM)


def params(mebibytes):
    return pltpu.CompilerParams(vmem_limit_bytes=mebibytes * 1024 * 1024)


def cost(flops, bytes_accessed):
    return pl.CostEstimate(flops=int(flops), bytes_accessed=int(bytes_accessed), transcendentals=0)


def halves(value):
    high = value.astype(jnp.bfloat16)
    return high, (value - high.astype(jnp.float32)).astype(jnp.bfloat16)


def side_by_side(value):
    return jnp.concatenate(halves(value), axis=1)


def dot_halves(left, right):
    dot = functools.partial(jnp.dot, preferred_element_type=jnp.float32)
    return dot(left[0], right) + dot(left[1], right)


def folded(value):
    return value[:, :LANES] + value[:, LANES:]


def swapped(blocks, lane):
    count = len(blocks)
    width = LANES // count
    blocks = [pltpu.roll(value, at * width, 1) if at else value for at, value in enumerate(blocks)]
    bit = 1
    while bit < count:
        chosen = (lane // (bit * width)) % 2 == 1
        blocks = [jnp.where(chosen, blocks[(at + bit) % count], blocks[at]) for at in range(count)]
        bit *= 2
    blocks = [blocks[-at % count] for at in range(count)]
    return [pltpu.roll(value, LANES - at * width, 1) if at else value for at, value in enumerate(blocks)]


def swap_into(read, write, count, rows):
    tile = 8 * max(1, 32 // count)
    lane = lax.broadcasted_iota(jnp.int32, (tile, LANES), 1)

    def step(index, carry):
        start = pl.multiple_of(index * tile, 8)
        for block, value in enumerate(swapped([read(block, start, tile) for block in range(count)], lane)):
            write(block, start, tile, value)
        return carry

    lax.fori_loop(0, rows // tile, step, 0, unroll=True)


def swap_in_kernel(count, rows, levels_ref, in_ref, out_ref):
    def read(block, start, size):
        return in_ref[block, pl.ds(start, size), :]

    def write(block, start, size, value):
        out_ref[block, pl.ds(start, size), :] = value

    swap_into(read, write, count, rows)
    for block in range(count):
        out_ref[block, pl.ds(rows, levels_ref.shape[0]), :] = levels_ref[...]


def swap_in(levels, value):
    planes, count, rows, _ = value.shape
    extra = levels.shape[1]
    return pl.pallas_call(
        functools.partial(swap_in_kernel, count, rows),
        grid=(planes,),
        in_specs=[
            pl.BlockSpec((None, extra, LANES), lambda p: (p, 0, 0)),
            pl.BlockSpec((None, count, rows, LANES), lambda p: (p, 0, 0, 0)),
        ],
        out_specs=pl.BlockSpec((count, None, rows + extra, LANES), lambda p: (0, p, 0, 0)),
        out_shape=jax.ShapeDtypeStruct((count, planes, rows + extra, LANES), jnp.float32),
        compiler_params=params(12),
        cost_estimate=cost(0, 8 * value.size),
    )(levels, value)


def swap_out_kernel(count, rows, arrived_ref, high_ref, low_ref, weights_ref, out_ref):
    planes = out_ref.shape[0]
    weights = side_by_side(weights_ref[...] * (1.0 / 18.0))
    for plane in range(planes):

        def read(block, start, size):
            return arrived_ref[block, plane, pl.ds(start, size), :]

        def write(block, start, size, value):
            at = pl.ds(pl.multiple_of(block * rows + start, 8), size)
            out_ref[plane, at, :] = value

        swap_into(read, write, count, rows)
        tile = rows * count // 6

        def add(index, carry):
            at = pl.ds(pl.multiple_of(index * tile, 8), tile)
            term = folded(dot_halves((high_ref[plane, at, :], low_ref[plane, at, :]), weights))
            out_ref[plane, at, :] = out_ref[plane, at, :] + term
            return carry

        lax.fori_loop(0, 6, add, 0)


def swap_out(arrived, high, low, weights, first_plane):
    count, planes, rows, _ = arrived.shape
    cells = count * rows
    basis = pl.BlockSpec((planes, cells, 2 * LANES), lambda i: (first_plane // planes, 0, 0))
    return pl.pallas_call(
        functools.partial(swap_out_kernel, count, rows),
        grid=(1,),
        in_specs=[
            pl.BlockSpec(arrived.shape, lambda i: (0, 0, 0, 0)),
            basis,
            basis,
            pl.BlockSpec(weights.shape, lambda i: (0, 0)),
        ],
        out_specs=pl.BlockSpec((planes, cells, LANES), lambda i: (0, 0, 0)),
        out_shape=jax.ShapeDtypeStruct((planes, cells, LANES), jnp.float32),
        compiler_params=params(18),
        cost_estimate=cost(0, 24 * arrived.size),
    )(arrived, high, low, weights)


def fill_row(target, plane, y, row, side_z):
    target[plane, y, pl.ds(PAD, side_z), :] = row
    target[plane, y, pl.ds(PAD - HALO, HALO), :] = row[side_z - HALO :]
    target[plane, y, pl.ds(PAD + side_z, HALO), :] = row[:HALO]


def local_part(source, potential_ref, planes, first, side_y, side_z, line_of, finish):
    tile = 16

    def row(y, carry):
        for start in range(0, side_z, tile):

            def load(plane, y_at, shift):
                return source[plane, y_at, pl.ds(PAD + start + shift, tile), :]

            line = line_of(lambda plane: load(plane, y, 0))
            at = pl.ds(pl.multiple_of(y * side_z + start, 8), tile)
            for plane in range(planes):
                here = first + plane
                total = (potential_ref[plane, at, :] - 1.5 * center_weight - 7.0) * line[HALO + plane]
                for offset in range(1, HALO + 1):
                    around = line[HALO + plane + offset] + line[HALO + plane - offset]
                    around = around + (load(here, y, offset) + load(here, y, -offset))
                    up = lax.rem(y + offset, side_y)
                    down = lax.rem(y + side_y - offset, side_y)
                    around = around + (load(here, up, 0) + load(here, down, 0))
                    total = total - (0.5 * side_weights[offset - 1]) * around
                finish(plane, y, start, at, total)
        return carry

    lax.fori_loop(0, side_y, row, 0)


def filter_kernel(planes, side_y, side_z, width, chunks, arrived_ref, *rest):
    outs, (field, padded, first, flat, potential) = rest[: len(chunks)], rest[len(chunks) :]
    count = arrived_ref.shape[0]
    cells = side_y * side_z
    rows = cells // count
    tile = 16

    line = lax.broadcasted_iota(jnp.int32, (2 * count, LANES), 0) % count
    lane = lax.broadcasted_iota(jnp.int32, (2 * count, LANES), 1) // width
    spread = (line == lane).astype(jnp.bfloat16)
    for plane in range(planes):
        lines = [arrived_ref[:, plane, rows + at, :] for at in range(cells // LANES)]
        high, low = halves(jnp.concatenate(lines, axis=1))
        both = jnp.concatenate([high.astype(jnp.float32), low.astype(jnp.float32)], axis=0)
        potential[plane] = jnp.dot(both.T.astype(jnp.bfloat16), spread, preferred_element_type=jnp.float32)

    for plane in range(planes):

        def read_in(block, start, size):
            return arrived_ref[block, plane, pl.ds(start, size), :]

        def write_in(block, start, size, value):
            field[plane, pl.ds(pl.multiple_of(block * rows + start, 8), size), :] = value

        swap_into(read_in, write_in, count, rows)

    def fill(y, carry):
        for plane in range(planes):
            fill_row(padded, plane, y, field[plane, pl.ds(pl.multiple_of(y * side_z, 8), side_z), :], side_z)
        return carry

    lax.fori_loop(0, side_y, fill, 0)

    def line_of(load):
        inside = [load(plane) for plane in range(planes)]
        before = [pltpu.roll(value, width, 1) for value in inside]
        after = [pltpu.roll(value, LANES - width, 1) for value in inside]
        return before[planes - HALO :] + inside + after[:HALO]

    def finish_first(plane, y, start, at, total):
        first[plane, y, pl.ds(PAD + start, tile), :] = total
        if start == 0:
            first[plane, y, pl.ds(PAD + side_z, HALO), :] = total[:HALO]
        if start == side_z - tile:
            first[plane, y, pl.ds(PAD - HALO, HALO), :] = total[tile - HALO :]

    def finish_second(plane, y, start, at, total):
        flat[plane, at, :] = total * (1.0 / 18.0) - field[plane, at, :]

    local_part(padded, potential, planes, 0, side_y, side_z, line_of, finish_first)
    local_part(first, potential, planes, 0, side_y, side_z, line_of, finish_second)

    for (begin, size_of), out_ref in zip(chunks, outs):
        for plane in range(size_of):

            def read_out(block, start, size):
                return flat[begin + plane, pl.ds(pl.multiple_of(block * rows + start, 8), size), :]

            def write_out(block, start, size, value):
                out_ref[block, plane, pl.ds(start, size), :] = value

            swap_into(read_out, write_out, count, rows)


def filter_orbitals(arrived, side_y, side_z, width, chunks):
    count, planes = arrived.shape[:2]
    rows = side_y * side_z // count
    flat = pltpu.VMEM((planes, side_y * side_z, LANES), jnp.float32)
    padded = pltpu.VMEM((planes, side_y, side_z + 2 * PAD, LANES), jnp.float32)
    return pl.pallas_call(
        functools.partial(filter_kernel, planes, side_y, side_z, width, chunks),
        in_specs=[WHOLE],
        out_specs=[WHOLE] * len(chunks),
        out_shape=[jax.ShapeDtypeStruct((count, size, rows, LANES), jnp.float32) for _, size in chunks],
        scratch_shapes=[flat, padded, padded, flat, flat],
        compiler_params=params(30),
        cost_estimate=cost(100 * arrived.size, 12 * arrived.size),
    )(arrived)


def basis_kernel(planes, side_y, side_z, bands, *refs):
    raw_refs = refs[:bands]
    offset_ref, potential_ref, orbitals_ref, high_ref, low_ref, parts_ref, turned, placed = refs[bands:]
    cells = side_y * side_z
    for part in range(SPAN):
        at = pl.ds(part * cells, cells)
        stack = [raw_ref[block, :, at] for raw_ref in raw_refs for block in range(NEAR)]
        turned[part] = jnp.concatenate(stack, axis=0).T
    offset = offset_ref[0:1, :]

    def place(y, carry):
        at = pl.ds(pl.multiple_of(y * side_z, 8), side_z)
        values = [turned[part, at, :] for part in range(SPAN)]
        for plane in range(planes + 2 * HALO):
            row = jnp.zeros((side_z, LANES), jnp.float32)
            for part in range(SPAN):
                row = jnp.where(offset == float(plane - HALO - part), values[part], row)
            fill_row(placed, plane, y, row, side_z)
        return carry

    lax.fori_loop(0, side_y, place, 0)

    def line_of(load):
        return [load(plane) for plane in range(planes + 2 * HALO)]

    def finish(plane, y, start, at, total):
        own = placed[HALO + plane, y, pl.ds(PAD + start, 16), :]
        high, low = halves(jnp.concatenate([total, own], axis=1))
        high_ref[plane, at, :] = high
        low_ref[plane, at, :] = low

    local_part(placed, potential_ref, planes, HALO, side_y, side_z, line_of, finish)

    dot = functools.partial(jnp.dot, preferred_element_type=jnp.float32)
    with_orbitals = with_basis = 0.0
    for plane in range(planes):
        high, low = high_ref[plane], low_ref[plane]
        left = halves(orbitals_ref[plane].T)
        with_orbitals = with_orbitals + (dot(left[0], high) + (dot(left[0], low) + dot(left[1], high)))
        own_high, own_low = high[:, LANES:], low[:, LANES:]
        turned_high = own_high.astype(jnp.float32).T.astype(jnp.bfloat16)
        turned_low = own_low.astype(jnp.float32).T.astype(jnp.bfloat16)
        both = jnp.concatenate([own_high, own_low], axis=1)
        with_basis = with_basis + (dot(turned_high, both) + dot(turned_low, both))
    parts_ref[0] = with_orbitals[:, LANES:].T
    parts_ref[1] = with_orbitals[:, :LANES].T
    parts_ref[2] = folded(with_basis)


def build_basis(raw, offset, potential, orbitals, side_y, side_z):
    planes, cells, _ = orbitals.shape
    pair = jax.ShapeDtypeStruct((planes, cells, 2 * LANES), jnp.bfloat16)
    return pl.pallas_call(
        functools.partial(basis_kernel, planes, side_y, side_z, len(raw)),
        in_specs=[WHOLE] * (len(raw) + 3),
        out_specs=[WHOLE] * 3,
        out_shape=[pair, pair, jax.ShapeDtypeStruct((3, LANES, LANES), jnp.float32)],
        scratch_shapes=[
            pltpu.VMEM((SPAN, cells, LANES), jnp.float32),
            pltpu.VMEM((planes + 2 * HALO, side_y, side_z + 2 * PAD, LANES), jnp.float32),
        ],
        compiler_params=params(40),
        cost_estimate=cost(200 * orbitals.size, 24 * orbitals.size),
    )(*raw, offset, potential, orbitals)


def weights_kernel(bands, me_ref, parts_ref, coupling_ref, out_ref):
    count = parts_ref.shape[0]
    size = LANES // NEAR
    lines = size // bands
    me = me_ref[0]
    dot = functools.partial(jnp.dot, precision=HIGHEST, preferred_element_type=jnp.float32)

    def device(step):
        return lax.rem(me + step % count, count)

    def total(pick, block):
        shares = [pick(block - (near - BEFORE), near) for near in range(NEAR)]
        return (shares[0] + shares[1]) + (shares[2] + shares[3])

    def of_block(value, near):
        starts = [(band * NEAR + near) * lines for band in range(bands)]
        return jnp.concatenate([value[start : start + lines] for start in starts], axis=0)

    def joined(values):
        return jnp.concatenate(
            [values[near][band * lines : (band + 1) * lines] for band in range(bands) for near in range(NEAR)], axis=0
        )

    def couple(block, value):
        return dot(coupling_ref[device(block)], value)

    def kept(function):
        known = {}

        def look(step):
            if step % count not in known:
                known[step % count] = function(step)
            return known[step % count]

        return look

    weight = kept(
        lambda block: couple(block, total(lambda step, near: of_block(parts_ref[device(step), 0], near), block))
    )
    weights = kept(lambda step: joined([weight(step + near - BEFORE) for near in range(NEAR)]))
    second = kept(lambda step: parts_ref[device(step), 1] + dot(parts_ref[device(step), 2], weights(step)))
    out_ref[pl.ds(0, LANES), :] = weights(0)
    out_ref[pl.ds(LANES, LANES), :] = joined(
        [
            couple(near - BEFORE, total(lambda step, at: of_block(second(step), at), near - BEFORE))
            for near in range(NEAR)
        ]
    )


def near_weights(parts, coupling):
    return pl.pallas_call(
        functools.partial(weights_kernel, lax.axis_size("band")),
        in_specs=[pl.BlockSpec(memory_space=pltpu.SMEM), WHOLE, WHOLE],
        out_specs=WHOLE,
        out_shape=jax.ShapeDtypeStruct((2 * LANES, LANES), jnp.float32),
        compiler_params=params(18),
        cost_estimate=cost(0, 8 * parts.size),
    )(lax.axis_index("dom").astype(jnp.int32).reshape(1), parts, coupling)


def shifted(value, axis, step):
    count = lax.axis_size(axis)
    return lax.ppermute(value, axis, [(source, (source + step) % count) for source in range(count)])


def crossed(value, bit):
    return lax.ppermute(value, "band", [(source, source ^ bit) for source in range(lax.axis_size("band"))])


def gram_kernel(own_ref, *rest):
    panels, out_ref = (own_ref, *rest[:-1]), rest[-1]

    @pl.when(pl.program_id(0) == 0)
    def _():
        out_ref[...] = jnp.zeros_like(out_ref)

    for plane in range(own_ref.shape[0]):
        left = halves(own_ref[plane].T)
        both = jnp.concatenate([side_by_side(panel[plane]) for panel in panels], axis=1)
        value = dot_halves(left, both)
        for index in range(len(panels)):
            at = pl.ds(index * LANES, LANES)
            out_ref[:, at] = out_ref[:, at] + folded(value[:, 2 * index * LANES : 2 * (index + 1) * LANES])


def gram_rows(panels):
    planes, cells, _ = panels[0].shape
    tile = cells // 2
    return pl.pallas_call(
        gram_kernel,
        grid=(cells // tile,),
        in_specs=[pl.BlockSpec((planes, tile, LANES), lambda i: (0, i, 0))] * len(panels),
        out_specs=pl.BlockSpec((LANES, len(panels) * LANES), lambda i: (0, 0)),
        out_shape=jax.ShapeDtypeStruct((LANES, len(panels) * LANES), jnp.float32),
        compiler_params=params(16),
        cost_estimate=cost(8 * panels[0].size * LANES * len(panels), 4 * panels[0].size * len(panels)),
    )(*panels)


def rotate_kernel(chunks, bands, inverse_ref, *rest):
    panels, out_ref = rest[:-1], rest[-1]
    right = side_by_side(inverse_ref[...].T)
    for index, (begin, size) in enumerate(chunks):
        group = panels[index * bands : (index + 1) * bands]
        for plane in range(size):
            left = halves(jnp.concatenate([panel[plane] for panel in group], axis=1))
            out_ref[begin + plane] = folded(dot_halves(left, right))


def rotated(inverse_rows, panels, chunks):
    bands = len(panels[0])
    planes = sum(size for _, size in chunks)
    cells = panels[0][0].shape[1]
    tile = cells // 4
    specs = [pl.BlockSpec((size, tile, LANES), lambda i: (0, i, 0)) for _, size in chunks for _ in range(bands)]
    return pl.pallas_call(
        functools.partial(rotate_kernel, chunks, bands),
        grid=(cells // tile,),
        in_specs=[pl.BlockSpec(inverse_rows.shape, lambda i: (0, 0)), *specs],
        out_specs=pl.BlockSpec((planes, tile, LANES), lambda i: (0, i, 0)),
        out_shape=jax.ShapeDtypeStruct((planes, cells, LANES), jnp.float32),
        compiler_params=params(18),
    )(inverse_rows, *[panel for group in panels for panel in group])


def thirds(value):
    first = value.astype(jnp.bfloat16).astype(jnp.float32)
    rest = value - first
    second = rest.astype(jnp.bfloat16).astype(jnp.float32)
    return first, second, rest - second


def eliminate(work, result):
    sublane = lax.broadcasted_iota(jnp.int32, (GROUP, LANES), 0)

    def splat(row, column):
        return jnp.broadcast_to(row[:, column : column + 1], (GROUP, LANES))

    def load(top):
        left = [jnp.broadcast_to(work[pl.ds(top + i, 1), :LANES], (GROUP, LANES)) for i in range(GROUP)]
        right = [jnp.broadcast_to(work[pl.ds(top + i, 1), LANES:], (GROUP, LANES)) for i in range(GROUP)]
        return left, right

    def factored(top, left, right):
        entry = {(i, j): splat(left[i], top + j) for i in range(GROUP) for j in range(i, GROUP)}
        for i in range(GROUP):
            scale = lax.rsqrt(entry[i, i])
            left[i] = left[i] * scale
            right[i] = right[i] * scale
            factor = {j: entry[i, j] * scale for j in range(i + 1, GROUP)}
            for m in range(i + 1, GROUP):
                for j in range(m, GROUP):
                    entry[m, j] = entry[m, j] - factor[m] * factor[j]
                left[m] = left[m] - factor[m] * left[i]
                right[m] = right[m] - factor[m] * right[i]

    def gathered(rows):
        value = rows[0]
        for i in range(1, GROUP):
            value = jnp.where(sublane == i, rows[i], value)
        return value

    for top in range(0, LANES, 2 * GROUP):
        left, right = load(top)
        factored(top, left, right)
        middle = top + GROUP
        next_left, next_right = load(middle)
        for m in range(GROUP):
            for i in range(GROUP):
                factor = splat(left[i], middle + m)
                next_left[m] = next_left[m] - factor * left[i]
                next_right[m] = next_right[m] - factor * right[i]
        factored(middle, next_left, next_right)
        upper = jnp.concatenate([gathered(left), gathered(next_left)], axis=0)
        lower = jnp.concatenate([gathered(right), gathered(next_right)], axis=0)
        result[pl.ds(top, 2 * GROUP), :] = lower
        below = middle + GROUP
        if below < LANES:
            a, b, c = thirds(upper)
            x, y, z = thirds(lower)
            columns = jnp.concatenate([a, a, b, b, a, c], axis=0).T[below:].astype(jnp.bfloat16)
            rows = jnp.concatenate(
                [jnp.concatenate([a, b, a, b, c, a], axis=0), jnp.concatenate([x, y, x, y, z, x], axis=0)], axis=1
            ).astype(jnp.bfloat16)
            rest = pl.ds(below, LANES - below)
            work[rest, :] = work[rest, :] - jnp.dot(columns, rows, preferred_element_type=jnp.float32)


def cholesky_kernel(band_ref, *refs):
    rows_refs, (gram_ref, own_ref, inverse, matrix, work, corner, scaled) = refs[:-7], refs[-7:]
    size = gram_ref.shape[0]
    bands = len(rows_refs)
    band = band_ref[0]

    def block_of(member):
        return pl.ds(pl.multiple_of((band ^ member) * LANES, LANES), LANES)

    for member, rows_ref in enumerate(rows_refs):
        for other in range(bands):
            gram_ref[block_of(member), block_of(member ^ other)] = rows_ref[:, other * LANES : (other + 1) * LANES]
    dot = functools.partial(jnp.dot, precision=HIGHEST, preferred_element_type=jnp.float32)
    diagonal = lax.broadcasted_iota(jnp.int32, (LANES, LANES), 0) == lax.broadcasted_iota(jnp.int32, (LANES, LANES), 1)
    identity = diagonal.astype(jnp.float32)
    matrix[:, :size] = gram_ref[...]
    matrix[:, size:] = jnp.zeros((size, size), jnp.float32)
    for at in range(0, size, LANES):
        matrix[pl.ds(at, LANES), size + at : size + at + LANES] = identity

    def block(index, carry):
        start = pl.multiple_of(index * LANES, LANES)
        at = pl.ds(start, LANES)
        work[:, :LANES] = matrix[at, at]
        work[:, LANES:] = identity
        eliminate(work, corner)
        scaled[...] = dot(corner[...], matrix[at, :])
        inverse[at, :] = scaled[:, size:]

        def below(other, carry):
            rows = pl.ds(pl.multiple_of(other * LANES, LANES), LANES)
            matrix[rows, :] = matrix[rows, :] - dot(scaled[:, rows].T, scaled[...])
            return carry

        lax.fori_loop(index + 1, size // LANES, below, 0)
        return carry

    lax.fori_loop(0, size // LANES, block, 0)
    for member in range(bands):
        own_ref[:, member * LANES : (member + 1) * LANES] = inverse[block_of(0), block_of(member)]


def cholesky_inverse(band, rows):
    size = rows[0].shape[1]
    return pl.pallas_call(
        cholesky_kernel,
        in_specs=[pl.BlockSpec(memory_space=pltpu.SMEM)] + [WHOLE] * len(rows),
        out_specs=[WHOLE] * 2,
        out_shape=[
            jax.ShapeDtypeStruct((size, size), jnp.float32),
            jax.ShapeDtypeStruct((LANES, size), jnp.float32),
        ],
        scratch_shapes=[
            pltpu.VMEM((size, size), jnp.float32),
            pltpu.VMEM((size, 2 * size), jnp.float32),
            pltpu.VMEM((LANES, 2 * LANES), jnp.float32),
            pltpu.VMEM((LANES, LANES), jnp.float32),
            pltpu.VMEM((LANES, 2 * size), jnp.float32),
        ],
        compiler_params=params(14),
    )(band.astype(jnp.int32).reshape(1), *rows)


def packed_projectors(projectors, atom_plane, planes):
    share = projectors.shape[0] // lax.axis_size("band")
    first = (atom_plane - lax.axis_index("dom") * planes).astype(jnp.float32)
    first = jnp.broadcast_to(first[:, None, None], (projectors.shape[0], MAXPROJ, LANES))
    packed = jnp.concatenate([projectors, first], axis=2)
    mine = lax.dynamic_slice_in_dim(packed, lax.axis_index("band") * share, share, 0)
    return mine.reshape(share * MAXPROJ, -1)


def near_shares(mine):
    return jnp.stack([mine if step == BEFORE else shifted(mine, "dom", BEFORE - step) for step in range(NEAR)])


def near_projectors(near, planes):
    across = crossed(near, 2)
    raw = [near, crossed(near, 1), across, crossed(across, 1)]
    moved = (planes * (jnp.arange(NEAR, dtype=jnp.float32) - BEFORE))[:, None]
    first = jnp.stack([member[:, :, -1] + moved for member in raw]).reshape(1, LANES)
    return raw, jnp.broadcast_to(first, (GROUP, LANES))


def shards(orbitals, potential, projectors, coupling, atom_plane, projector_count):
    planes, side_y, side_z, local_orbs = orbitals.shape
    blocks, bands = lax.axis_size("dom"), lax.axis_size("band")
    band = lax.axis_index("band")
    cells = side_y * side_z
    rows = cells // blocks
    width = local_orbs // blocks
    norb = local_orbs * bands
    chunks = ((0, 2), (2, 1), (3, 1))

    order = jnp.arange(bands, dtype=jnp.int32) ^ band

    mine = packed_projectors(projectors, atom_plane, planes)
    mine, levels = lax.optimization_barrier((mine, potential.reshape(planes, cells // LANES, LANES)))
    near = near_shares(mine)
    levels = jnp.pad(levels, ((0, 0), (0, -levels.shape[1] % GROUP), (0, 0)))
    packed = swap_in(levels, orbitals.reshape(planes, blocks, rows, local_orbs))
    packed, near = lax.optimization_barrier((packed, near))
    raw, first = near_projectors(near, planes)
    arrived = lax.all_to_all(packed, "dom", 0, 0, tiled=True)

    own_levels = jnp.broadcast_to(potential.reshape(planes, cells, 1), (planes, cells, LANES))
    high, low, parts = build_basis(raw, first, own_levels, orbitals.reshape(planes, cells, LANES), side_y, side_z)
    atoms = projectors.shape[0]
    slots = jnp.arange(MAXPROJ, dtype=jnp.int32)
    live = (slots[None, :] < projector_count[:, None]).astype(jnp.float32)
    coupled = 0.5 * (coupling + jnp.transpose(coupling, (0, 2, 1))) * live[:, :, None] * live[:, None, :]
    coupled = jnp.take(coupled.reshape(bands, -1, MAXPROJ, MAXPROJ), order, axis=0)
    vectors = atoms * MAXPROJ
    row = jnp.arange(vectors, dtype=jnp.int32) // MAXPROJ
    matrix = jnp.tile(coupled.reshape(vectors, MAXPROJ), (1, atoms))
    matrix = jnp.where(row[:, None] == row[None, :], matrix, 0.0)
    matrix = jnp.pad(matrix, ((0, 0), (0, LANES - vectors)))
    everyone = lax.all_gather(jnp.concatenate([parts.reshape(3 * LANES, LANES), matrix], axis=0), "dom")
    weights = near_weights(
        everyone[:, : 3 * LANES].reshape(blocks, 3, LANES, LANES), everyone[:, 3 * LANES :, :vectors]
    )

    seconds = filter_orbitals(arrived, side_y, side_z, width, chunks)

    sent = []
    for (begin, size), packed in zip(chunks, seconds):
        own = swap_out(lax.all_to_all(packed, "dom", 0, 0, tiled=True), high, low, weights, begin)
        sent.append((own, crossed(own, 1), crossed(own, 2)))
    panels, part = [], sent[-1][0]
    for own, beside, across in sent:
        across, part = lax.optimization_barrier((across, part))
        panels.append([own, beside, across, crossed(across, 1)])
        part = gram_rows(panels[-1]) + (part if len(panels) > 1 else 0.0)

    pieces = lax.all_to_all(part.reshape(blocks, width, norb), "dom", 0, 0, tiled=True)
    piece = jnp.sum(pieces, axis=0) * (1.0 / (planes * cells * blocks))
    own_gram = lax.all_to_all(jnp.broadcast_to(piece, (blocks, width, norb)), "dom", 0, 0, tiled=True)
    own_gram = own_gram.reshape(local_orbs, norb)
    across = crossed(own_gram, 2)
    gram, own_rows = cholesky_inverse(band, [own_gram, crossed(own_gram, 1), across, crossed(across, 1)])
    result = rotated(own_rows, panels, chunks)
    return (result.reshape(planes, side_y, side_z, local_orbs), gram)


def solution(mesh):
    placed = (
        P("dom", None, None, "band"),
        P("dom", None, None),
        P("dom", None, None),
        P("dom", None, None),
        P("dom"),
        P("dom"),
    )
    return jax.shard_map(
        shards,
        mesh=mesh,
        in_specs=placed,
        out_specs=(P("dom", None, None, "band"), P()),
        check_vma=False,
    )
```

```python
import functools

import jax
import jax.numpy as jnp
from jax import lax
from jax.experimental import pallas as pl
from jax.experimental.pallas import tpu as pltpu
from jax.sharding import PartitionSpec as P

SPAN = 3
MAXPROJ = 4
HALO = 4
PAD = 8
LANES = 128
GROUP = 8
BEFORE, AFTER = 2, 1
NEAR = BEFORE + 1 + AFTER

center_weight = -205.0 / 72.0
side_weights = (8.0 / 5.0, -1.0 / 5.0, 8.0 / 315.0, -1.0 / 560.0)
HIGHEST = lax.Precision.HIGHEST
WHOLE = pl.BlockSpec(memory_space=pltpu.VMEM)


def params(mebibytes):
    return pltpu.CompilerParams(vmem_limit_bytes=mebibytes * 1024 * 1024)


def cost(flops, bytes_accessed):
    return pl.CostEstimate(flops=int(flops), bytes_accessed=int(bytes_accessed), transcendentals=0)


def halves(value):
    high = value.astype(jnp.bfloat16)
    return high, (value - high.astype(jnp.float32)).astype(jnp.bfloat16)


def side_by_side(value):
    return jnp.concatenate(halves(value), axis=1)


def dot_halves(left, right):
    dot = functools.partial(jnp.dot, preferred_element_type=jnp.float32)
    return dot(left[0], right) + dot(left[1], right)


def folded(value):
    return value[:, :LANES] + value[:, LANES:]


def swapped(blocks, lane, before=None, after=None):
    count = len(blocks)
    width = LANES // count

    def turned(value, at, extra):
        if extra is None:
            return pltpu.roll(value, at % count * width, 1) if at else value
        return pltpu.roll(value, lax.rem((at % count + extra) * width, LANES), 1)

    blocks = [turned(value, at, None if before is None else count - before) for at, value in enumerate(blocks)]
    bit = 1
    while bit < count:
        chosen = (lane // (bit * width)) % 2 == 1
        blocks = [jnp.where(chosen, blocks[(at + bit) % count], blocks[at]) for at in range(count)]
        bit *= 2
    return [turned(blocks[-at % count], -at, after) for at in range(count)]


def swap_into(read, write, count, rows, before=None, after=None):
    tile = 8 * max(1, 32 // count)
    lane = lax.broadcasted_iota(jnp.int32, (tile, LANES), 1)

    def step(index, carry):
        start = pl.multiple_of(index * tile, 8)
        blocks = [read(block, start, tile) for block in range(count)]
        for block, value in enumerate(swapped(blocks, lane, before, after)):
            write(block, start, tile, value)
        return carry

    lax.fori_loop(0, rows // tile, step, 0, unroll=True)


def swap_in_kernel(count, rows, levels_ref, in_ref, out_ref):
    def read(block, start, size):
        return in_ref[block, pl.ds(start, size), :]

    def write(block, start, size, value):
        out_ref[block, pl.ds(start, size), :] = value

    swap_into(read, write, count, rows)
    for block in range(count):
        out_ref[block, pl.ds(rows, levels_ref.shape[0]), :] = levels_ref[...]


def swap_in(levels, value):
    planes, count, rows, _ = value.shape
    extra = levels.shape[1]
    return pl.pallas_call(
        functools.partial(swap_in_kernel, count, rows),
        grid=(planes,),
        in_specs=[
            pl.BlockSpec((None, extra, LANES), lambda p: (p, 0, 0)),
            pl.BlockSpec((None, count, rows, LANES), lambda p: (p, 0, 0, 0)),
        ],
        out_specs=pl.BlockSpec((count, None, rows + extra, LANES), lambda p: (0, p, 0, 0)),
        out_shape=jax.ShapeDtypeStruct((count, planes, rows + extra, LANES), jnp.float32),
        compiler_params=params(12),
        cost_estimate=cost(0, 8 * value.size),
    )(levels, value)


def swap_out_kernel(me_ref, high_ref, low_ref, weights_ref, *refs):
    arrived_refs, out_ref = refs[:-1], refs[-1]
    count = len(arrived_refs)
    planes, rows, _ = arrived_refs[0].shape
    weights = side_by_side(weights_ref[...] * (1.0 / 18.0))
    for plane in range(planes):

        def read(block, start, size):
            return arrived_refs[-block % count][plane, pl.ds(start, size), :]

        def write(block, start, size, value):
            at = pl.ds(pl.multiple_of(block * rows + start, 8), size)
            out_ref[plane, at, :] = value

        swap_into(read, write, count, rows, after=me_ref[0])
        tile = rows * count // 6

        def add(index, carry):
            at = pl.ds(pl.multiple_of(index * tile, 8), tile)
            term = folded(dot_halves((high_ref[plane, at, :], low_ref[plane, at, :]), weights))
            out_ref[plane, at, :] = out_ref[plane, at, :] + term
            return carry

        lax.fori_loop(0, 6, add, 0)


def swap_out(me, arrived, high, low, weights, first_plane):
    count = len(arrived)
    planes, rows, _ = arrived[0].shape
    cells = count * rows
    basis = pl.BlockSpec((planes, cells, 2 * LANES), lambda i: (first_plane // planes, 0, 0))
    return pl.pallas_call(
        swap_out_kernel,
        grid=(1,),
        in_specs=[
            pl.BlockSpec(memory_space=pltpu.SMEM),
            basis,
            basis,
            pl.BlockSpec(weights.shape, lambda i: (0, 0)),
        ]
        + [pl.BlockSpec(arrived[0].shape, lambda i: (0, 0, 0))] * count,
        out_specs=pl.BlockSpec((planes, cells, LANES), lambda i: (0, 0, 0)),
        out_shape=jax.ShapeDtypeStruct((planes, cells, LANES), jnp.float32),
        compiler_params=params(24),
        cost_estimate=cost(0, 24 * cells * planes * LANES),
    )(me, high, low, weights, *arrived)


def fill_row(target, plane, y, row, side_z):
    target[plane, y, pl.ds(PAD, side_z), :] = row
    target[plane, y, pl.ds(PAD - HALO, HALO), :] = row[side_z - HALO :]
    target[plane, y, pl.ds(PAD + side_z, HALO), :] = row[:HALO]


def local_part(source, potential_ref, planes, first, side_y, side_z, line_of, finish):
    tile = 16

    def row(y, carry):
        for start in range(0, side_z, tile):

            def load(plane, y_at, shift):
                return source[plane, y_at, pl.ds(PAD + start + shift, tile), :]

            line = line_of(lambda plane: load(plane, y, 0))
            at = pl.ds(pl.multiple_of(y * side_z + start, 8), tile)
            for plane in range(planes):
                here = first + plane
                total = (potential_ref[plane, at, :] - 1.5 * center_weight - 7.0) * line[HALO + plane]
                for offset in range(1, HALO + 1):
                    around = line[HALO + plane + offset] + line[HALO + plane - offset]
                    around = around + (load(here, y, offset) + load(here, y, -offset))
                    up = lax.rem(y + offset, side_y)
                    down = lax.rem(y + side_y - offset, side_y)
                    around = around + (load(here, up, 0) + load(here, down, 0))
                    total = total - (0.5 * side_weights[offset - 1]) * around
                finish(plane, y, start, at, total)
        return carry

    lax.fori_loop(0, side_y, row, 0)


def filter_kernel(planes, side_y, side_z, width, chunks, me_ref, arrived_ref, *rest):
    outs, (field, padded, first, flat, potential) = rest[:-5], rest[-5:]
    count = arrived_ref.shape[0]
    cells = side_y * side_z
    rows = cells // count
    tile = 16

    line = lax.broadcasted_iota(jnp.int32, (2 * count, LANES), 0) % count
    lane = lax.broadcasted_iota(jnp.int32, (2 * count, LANES), 1) // width
    spread = (line == lane).astype(jnp.bfloat16)
    for plane in range(planes):
        lines = [arrived_ref[:, plane, rows + at, :] for at in range(cells // LANES)]
        high, low = halves(jnp.concatenate(lines, axis=1))
        both = jnp.concatenate([high.astype(jnp.float32), low.astype(jnp.float32)], axis=0)
        potential[plane] = jnp.dot(both.T.astype(jnp.bfloat16), spread, preferred_element_type=jnp.float32)

    for plane in range(planes):

        def read_in(block, start, size):
            return arrived_ref[block, plane, pl.ds(start, size), :]

        def write_in(block, start, size, value):
            field[plane, pl.ds(pl.multiple_of(block * rows + start, 8), size), :] = value

        swap_into(read_in, write_in, count, rows)

    def fill(y, carry):
        for plane in range(planes):
            fill_row(padded, plane, y, field[plane, pl.ds(pl.multiple_of(y * side_z, 8), side_z), :], side_z)
        return carry

    lax.fori_loop(0, side_y, fill, 0)

    def line_of(load):
        inside = [load(plane) for plane in range(planes)]
        before = [pltpu.roll(value, width, 1) for value in inside]
        after = [pltpu.roll(value, LANES - width, 1) for value in inside]
        return before[planes - HALO :] + inside + after[:HALO]

    def finish_first(plane, y, start, at, total):
        first[plane, y, pl.ds(PAD + start, tile), :] = total
        if start == 0:
            first[plane, y, pl.ds(PAD + side_z, HALO), :] = total[:HALO]
        if start == side_z - tile:
            first[plane, y, pl.ds(PAD - HALO, HALO), :] = total[tile - HALO :]

    def finish_second(plane, y, start, at, total):
        flat[plane, at, :] = total * (1.0 / 18.0) - field[plane, at, :]

    local_part(padded, potential, planes, 0, side_y, side_z, line_of, finish_first)
    local_part(first, potential, planes, 0, side_y, side_z, line_of, finish_second)

    for index, (begin, size_of) in enumerate(chunks):
        group = outs[index * count : (index + 1) * count]
        for plane in range(size_of):

            def read_out(block, start, size):
                return flat[begin + plane, pl.ds(pl.multiple_of(block * rows + start, 8), size), :]

            def write_out(block, start, size, value):
                group[block][plane, pl.ds(start, size), :] = value

            swap_into(read_out, write_out, count, rows, before=me_ref[0])


def filter_orbitals(me, arrived, side_y, side_z, width, chunks):
    count, planes = arrived.shape[:2]
    rows = side_y * side_z // count
    flat = pltpu.VMEM((planes, side_y * side_z, LANES), jnp.float32)
    padded = pltpu.VMEM((planes, side_y, side_z + 2 * PAD, LANES), jnp.float32)
    shapes = [jax.ShapeDtypeStruct((size, rows, LANES), jnp.float32) for _, size in chunks for _ in range(count)]
    outs = pl.pallas_call(
        functools.partial(filter_kernel, planes, side_y, side_z, width, chunks),
        in_specs=[pl.BlockSpec(memory_space=pltpu.SMEM), WHOLE],
        out_specs=[WHOLE] * len(shapes),
        out_shape=shapes,
        scratch_shapes=[flat, padded, padded, flat, flat],
        compiler_params=params(56),
        cost_estimate=cost(100 * arrived.size, 12 * arrived.size),
    )(me, arrived)
    return [outs[index * count : (index + 1) * count] for index in range(len(chunks))]


def basis_kernel(planes, side_y, side_z, bands, *refs):
    raw_refs = refs[:bands]
    offset_ref, potential_ref, orbitals_ref, high_ref, low_ref, parts_ref, turned, placed = refs[bands:]
    cells = side_y * side_z
    for part in range(SPAN):
        at = pl.ds(part * cells, cells)
        stack = [raw_ref[block, :, at] for raw_ref in raw_refs for block in range(NEAR)]
        turned[part] = jnp.concatenate(stack, axis=0).T
    offset = offset_ref[0:1, :]

    def place(y, carry):
        at = pl.ds(pl.multiple_of(y * side_z, 8), side_z)
        values = [turned[part, at, :] for part in range(SPAN)]
        for plane in range(planes + 2 * HALO):
            row = jnp.zeros((side_z, LANES), jnp.float32)
            for part in range(SPAN):
                row = jnp.where(offset == float(plane - HALO - part), values[part], row)
            fill_row(placed, plane, y, row, side_z)
        return carry

    lax.fori_loop(0, side_y, place, 0)

    def line_of(load):
        return [load(plane) for plane in range(planes + 2 * HALO)]

    def finish(plane, y, start, at, total):
        own = placed[HALO + plane, y, pl.ds(PAD + start, 16), :]
        high, low = halves(jnp.concatenate([total, own], axis=1))
        high_ref[plane, at, :] = high
        low_ref[plane, at, :] = low

    local_part(placed, potential_ref, planes, HALO, side_y, side_z, line_of, finish)

    dot = functools.partial(jnp.dot, preferred_element_type=jnp.float32)
    with_orbitals = with_basis = 0.0
    for plane in range(planes):
        high, low = high_ref[plane], low_ref[plane]
        left = halves(orbitals_ref[plane].T)
        with_orbitals = with_orbitals + (dot(left[0], high) + (dot(left[0], low) + dot(left[1], high)))
        own_high, own_low = high[:, LANES:], low[:, LANES:]
        turned_high = own_high.astype(jnp.float32).T.astype(jnp.bfloat16)
        turned_low = own_low.astype(jnp.float32).T.astype(jnp.bfloat16)
        both = jnp.concatenate([own_high, own_low], axis=1)
        with_basis = with_basis + (dot(turned_high, both) + dot(turned_low, both))
    parts_ref[0] = with_orbitals[:, LANES:].T
    parts_ref[1] = with_orbitals[:, :LANES].T
    parts_ref[2] = folded(with_basis)


def build_basis(raw, offset, potential, orbitals, side_y, side_z):
    planes, cells, _ = orbitals.shape
    pair = jax.ShapeDtypeStruct((planes, cells, 2 * LANES), jnp.bfloat16)
    return pl.pallas_call(
        functools.partial(basis_kernel, planes, side_y, side_z, len(raw)),
        in_specs=[WHOLE] * (len(raw) + 3),
        out_specs=[WHOLE] * 3,
        out_shape=[pair, pair, jax.ShapeDtypeStruct((3, LANES, LANES), jnp.float32)],
        scratch_shapes=[
            pltpu.VMEM((SPAN, cells, LANES), jnp.float32),
            pltpu.VMEM((planes + 2 * HALO, side_y, side_z + 2 * PAD, LANES), jnp.float32),
        ],
        compiler_params=params(56),
        cost_estimate=cost(200 * orbitals.size, 24 * orbitals.size),
    )(*raw, offset, potential, orbitals)


def weights_kernel(bands, me_ref, parts_ref, coupling_ref, out_ref):
    count = parts_ref.shape[0]
    size = LANES // NEAR
    lines = size // bands
    me = me_ref[0]
    dot = functools.partial(jnp.dot, precision=HIGHEST, preferred_element_type=jnp.float32)

    def device(step):
        return lax.rem(me + step % count, count)

    def total(pick, block):
        shares = [pick(block - (near - BEFORE), near) for near in range(NEAR)]
        return (shares[0] + shares[1]) + (shares[2] + shares[3])

    def of_block(value, near):
        starts = [(band * NEAR + near) * lines for band in range(bands)]
        return jnp.concatenate([value[start : start + lines] for start in starts], axis=0)

    def joined(values):
        return jnp.concatenate(
            [values[near][band * lines : (band + 1) * lines] for band in range(bands) for near in range(NEAR)], axis=0
        )

    def couple(block, value):
        return dot(coupling_ref[device(block)], value)

    def kept(function):
        known = {}

        def look(step):
            if step % count not in known:
                known[step % count] = function(step)
            return known[step % count]

        return look

    weight = kept(
        lambda block: couple(block, total(lambda step, near: of_block(parts_ref[device(step), 0], near), block))
    )
    weights = kept(lambda step: joined([weight(step + near - BEFORE) for near in range(NEAR)]))
    second = kept(lambda step: parts_ref[device(step), 1] + dot(parts_ref[device(step), 2], weights(step)))
    out_ref[pl.ds(0, LANES), :] = weights(0)
    out_ref[pl.ds(LANES, LANES), :] = joined(
        [
            couple(near - BEFORE, total(lambda step, at: of_block(second(step), at), near - BEFORE))
            for near in range(NEAR)
        ]
    )


def near_weights(me, parts, coupling):
    return pl.pallas_call(
        functools.partial(weights_kernel, lax.axis_size("band")),
        in_specs=[pl.BlockSpec(memory_space=pltpu.SMEM), WHOLE, WHOLE],
        out_specs=WHOLE,
        out_shape=jax.ShapeDtypeStruct((2 * LANES, LANES), jnp.float32),
        compiler_params=params(24),
        cost_estimate=cost(0, 8 * parts.size),
    )(me, parts, coupling)


def shifted(value, axis, step):
    count = lax.axis_size(axis)
    return lax.ppermute(value, axis, [(source, (source + step) % count) for source in range(count)])


def exchanged(values):
    return [shifted(value, "dom", step) if step else value for step, value in enumerate(values)]


def crossed(value, bit):
    return lax.ppermute(value, "band", [(source, source ^ bit) for source in range(lax.axis_size("band"))])


def gram_kernel(own_ref, *rest):
    panels, out_ref = (own_ref, *rest[:-1]), rest[-1]

    @pl.when(pl.program_id(0) == 0)
    def _():
        out_ref[...] = jnp.zeros_like(out_ref)

    for plane in range(own_ref.shape[0]):
        left = halves(own_ref[plane].T)
        both = jnp.concatenate([side_by_side(panel[plane]) for panel in panels], axis=1)
        value = dot_halves(left, both)
        for index in range(len(panels)):
            at = pl.ds(index * LANES, LANES)
            out_ref[:, at] = out_ref[:, at] + folded(value[:, 2 * index * LANES : 2 * (index + 1) * LANES])


def gram_rows(panels):
    planes, cells, _ = panels[0].shape
    tile = cells // 2
    return pl.pallas_call(
        gram_kernel,
        grid=(cells // tile,),
        in_specs=[pl.BlockSpec((planes, tile, LANES), lambda i: (0, i, 0))] * len(panels),
        out_specs=pl.BlockSpec((LANES, len(panels) * LANES), lambda i: (0, 0)),
        out_shape=jax.ShapeDtypeStruct((LANES, len(panels) * LANES), jnp.float32),
        compiler_params=params(16),
        cost_estimate=cost(8 * panels[0].size * LANES * len(panels), 4 * panels[0].size * len(panels)),
    )(*panels)


def rotate_kernel(chunks, bands, inverse_ref, *rest):
    panels, out_ref = rest[:-1], rest[-1]
    right = side_by_side(inverse_ref[...].T)
    for index, (begin, size) in enumerate(chunks):
        group = panels[index * bands : (index + 1) * bands]
        for plane in range(size):
            left = halves(jnp.concatenate([panel[plane] for panel in group], axis=1))
            out_ref[begin + plane] = folded(dot_halves(left, right))


def rotated(inverse_rows, panels, chunks):
    bands = len(panels[0])
    planes = sum(size for _, size in chunks)
    cells = panels[0][0].shape[1]
    tile = cells // 4
    specs = [pl.BlockSpec((size, tile, LANES), lambda i: (0, i, 0)) for _, size in chunks for _ in range(bands)]
    return pl.pallas_call(
        functools.partial(rotate_kernel, chunks, bands),
        grid=(cells // tile,),
        in_specs=[pl.BlockSpec(inverse_rows.shape, lambda i: (0, 0)), *specs],
        out_specs=pl.BlockSpec((planes, tile, LANES), lambda i: (0, i, 0)),
        out_shape=jax.ShapeDtypeStruct((planes, cells, LANES), jnp.float32),
        compiler_params=params(24),
    )(inverse_rows, *[panel for group in panels for panel in group])


def thirds(value):
    first = value.astype(jnp.bfloat16).astype(jnp.float32)
    rest = value - first
    second = rest.astype(jnp.bfloat16).astype(jnp.float32)
    return first, second, rest - second


def eliminate(work, result):
    sublane = lax.broadcasted_iota(jnp.int32, (GROUP, LANES), 0)

    def splat(row, column):
        return jnp.broadcast_to(row[:, column : column + 1], (GROUP, LANES))

    def load(top):
        left = [jnp.broadcast_to(work[pl.ds(top + i, 1), :LANES], (GROUP, LANES)) for i in range(GROUP)]
        right = [jnp.broadcast_to(work[pl.ds(top + i, 1), LANES:], (GROUP, LANES)) for i in range(GROUP)]
        return left, right

    def factored(top, left, right):
        entry = {(i, j): splat(left[i], top + j) for i in range(GROUP) for j in range(i, GROUP)}
        for i in range(GROUP):
            scale = lax.rsqrt(entry[i, i])
            left[i] = left[i] * scale
            right[i] = right[i] * scale
            factor = {j: entry[i, j] * scale for j in range(i + 1, GROUP)}
            for m in range(i + 1, GROUP):
                for j in range(m, GROUP):
                    entry[m, j] = entry[m, j] - factor[m] * factor[j]
                left[m] = left[m] - factor[m] * left[i]
                right[m] = right[m] - factor[m] * right[i]

    def gathered(rows):
        value = rows[0]
        for i in range(1, GROUP):
            value = jnp.where(sublane == i, rows[i], value)
        return value

    for top in range(0, LANES, 2 * GROUP):
        left, right = load(top)
        factored(top, left, right)
        middle = top + GROUP
        next_left, next_right = load(middle)
        for m in range(GROUP):
            for i in range(GROUP):
                factor = splat(left[i], middle + m)
                next_left[m] = next_left[m] - factor * left[i]
                next_right[m] = next_right[m] - factor * right[i]
        factored(middle, next_left, next_right)
        upper = jnp.concatenate([gathered(left), gathered(next_left)], axis=0)
        lower = jnp.concatenate([gathered(right), gathered(next_right)], axis=0)
        result[pl.ds(top, 2 * GROUP), :] = lower
        below = middle + GROUP
        if below < LANES:
            a, b, c = thirds(upper)
            x, y, z = thirds(lower)
            columns = jnp.concatenate([a, a, b, b, a, c], axis=0).T[below:].astype(jnp.bfloat16)
            rows = jnp.concatenate(
                [jnp.concatenate([a, b, a, b, c, a], axis=0), jnp.concatenate([x, y, x, y, z, x], axis=0)], axis=1
            ).astype(jnp.bfloat16)
            rest = pl.ds(below, LANES - below)
            work[rest, :] = work[rest, :] - jnp.dot(columns, rows, preferred_element_type=jnp.float32)


def cholesky_kernel(band_ref, *refs):
    rows_refs, (gram_ref, own_ref, inverse, matrix, work, corner, scaled) = refs[:-7], refs[-7:]
    size = gram_ref.shape[0]
    bands = len(rows_refs)
    band = band_ref[0]

    def block_of(member):
        return pl.ds(pl.multiple_of((band ^ member) * LANES, LANES), LANES)

    for member, rows_ref in enumerate(rows_refs):
        for other in range(bands):
            gram_ref[block_of(member), block_of(member ^ other)] = rows_ref[:, other * LANES : (other + 1) * LANES]
    dot = functools.partial(jnp.dot, precision=HIGHEST, preferred_element_type=jnp.float32)
    diagonal = lax.broadcasted_iota(jnp.int32, (LANES, LANES), 0) == lax.broadcasted_iota(jnp.int32, (LANES, LANES), 1)
    identity = diagonal.astype(jnp.float32)
    matrix[:, :size] = gram_ref[...]
    matrix[:, size:] = jnp.zeros((size, size), jnp.float32)
    for at in range(0, size, LANES):
        matrix[pl.ds(at, LANES), size + at : size + at + LANES] = identity

    def block(index, carry):
        start = pl.multiple_of(index * LANES, LANES)
        at = pl.ds(start, LANES)
        work[:, :LANES] = matrix[at, at]
        work[:, LANES:] = identity
        eliminate(work, corner)
        scaled[...] = dot(corner[...], matrix[at, :])
        inverse[at, :] = scaled[:, size:]

        def below(other, carry):
            rows = pl.ds(pl.multiple_of(other * LANES, LANES), LANES)
            matrix[rows, :] = matrix[rows, :] - dot(scaled[:, rows].T, scaled[...])
            return carry

        lax.fori_loop(index + 1, size // LANES, below, 0)
        return carry

    lax.fori_loop(0, size // LANES, block, 0)
    for member in range(bands):
        own_ref[:, member * LANES : (member + 1) * LANES] = inverse[block_of(0), block_of(member)]


def cholesky_inverse(band, rows):
    size = rows[0].shape[1]
    return pl.pallas_call(
        cholesky_kernel,
        in_specs=[pl.BlockSpec(memory_space=pltpu.SMEM)] + [WHOLE] * len(rows),
        out_specs=[WHOLE] * 2,
        out_shape=[
            jax.ShapeDtypeStruct((size, size), jnp.float32),
            jax.ShapeDtypeStruct((LANES, size), jnp.float32),
        ],
        scratch_shapes=[
            pltpu.VMEM((size, size), jnp.float32),
            pltpu.VMEM((size, 2 * size), jnp.float32),
            pltpu.VMEM((LANES, 2 * LANES), jnp.float32),
            pltpu.VMEM((LANES, LANES), jnp.float32),
            pltpu.VMEM((LANES, 2 * size), jnp.float32),
        ],
        compiler_params=params(14),
    )(band.astype(jnp.int32).reshape(1), *rows)


def packed_projectors(projectors, atom_plane, planes):
    share = projectors.shape[0] // lax.axis_size("band")
    first = (atom_plane - lax.axis_index("dom") * planes).astype(jnp.float32)
    first = jnp.broadcast_to(first[:, None, None], (projectors.shape[0], MAXPROJ, LANES))
    packed = jnp.concatenate([projectors, first], axis=2)
    mine = lax.dynamic_slice_in_dim(packed, lax.axis_index("band") * share, share, 0)
    return mine.reshape(share * MAXPROJ, -1)


def near_shares(mine):
    return jnp.stack([mine if step == BEFORE else shifted(mine, "dom", BEFORE - step) for step in range(NEAR)])


def near_projectors(near, planes):
    across = crossed(near, 2)
    raw = [near, crossed(near, 1), across, crossed(across, 1)]
    moved = (planes * (jnp.arange(NEAR, dtype=jnp.float32) - BEFORE))[:, None]
    first = jnp.stack([member[:, :, -1] + moved for member in raw]).reshape(1, LANES)
    return raw, jnp.broadcast_to(first, (GROUP, LANES))


def shards(orbitals, potential, projectors, coupling, atom_plane, projector_count):
    planes, side_y, side_z, local_orbs = orbitals.shape
    blocks, bands = lax.axis_size("dom"), lax.axis_size("band")
    band = lax.axis_index("band")
    cells = side_y * side_z
    rows = cells // blocks
    width = local_orbs // blocks
    norb = local_orbs * bands
    chunks = tuple((plane, 1) for plane in range(planes))
    me = lax.axis_index("dom").astype(jnp.int32).reshape(1)

    order = jnp.arange(bands, dtype=jnp.int32) ^ band

    mine = packed_projectors(projectors, atom_plane, planes)
    mine, levels = lax.optimization_barrier((mine, potential.reshape(planes, cells // LANES, LANES)))
    near = near_shares(mine)
    levels = jnp.pad(levels, ((0, 0), (0, -levels.shape[1] % GROUP), (0, 0)))
    packed = swap_in(levels, orbitals.reshape(planes, blocks, rows, local_orbs))
    packed, near = lax.optimization_barrier((packed, near))
    raw, first = near_projectors(near, planes)
    arrived = lax.all_to_all(packed, "dom", 0, 0, tiled=True)

    own_levels = jnp.broadcast_to(potential.reshape(planes, cells, 1), (planes, cells, LANES))
    high, low, parts = build_basis(raw, first, own_levels, orbitals.reshape(planes, cells, LANES), side_y, side_z)
    atoms = projectors.shape[0]
    slots = jnp.arange(MAXPROJ, dtype=jnp.int32)
    live = (slots[None, :] < projector_count[:, None]).astype(jnp.float32)
    coupled = 0.5 * (coupling + jnp.transpose(coupling, (0, 2, 1))) * live[:, :, None] * live[:, None, :]
    coupled = jnp.take(coupled.reshape(bands, -1, MAXPROJ, MAXPROJ), order, axis=0)
    vectors = atoms * MAXPROJ
    row = jnp.arange(vectors, dtype=jnp.int32) // MAXPROJ
    matrix = jnp.tile(coupled.reshape(vectors, MAXPROJ), (1, atoms))
    matrix = jnp.where(row[:, None] == row[None, :], matrix, 0.0)
    matrix = jnp.pad(matrix, ((0, 0), (0, LANES - vectors)))
    payload = jnp.concatenate([parts.reshape(3 * LANES, LANES), matrix], axis=0)
    everyone = lax.all_gather(payload, "dom")
    weights = near_weights(
        me,
        everyone[:, : 3 * LANES].reshape(blocks, 3, LANES, LANES), everyone[:, 3 * LANES :, :vectors],
    )

    arrived, _ = lax.optimization_barrier((arrived, payload))
    seconds = filter_orbitals(me, arrived, side_y, side_z, width, chunks)

    sent, came = [], None
    for (begin, size), packed in zip(chunks, seconds):
        if came is not None:
            packed, _ = lax.optimization_barrier((packed, came))
        arrived = exchanged(packed)
        came = arrived[1]
        own = swap_out(me, arrived, high, low, weights, begin)
        sent.append((own, crossed(own, 1), crossed(own, 2)))
    panels, part = [], sent[-1][0]
    for own, beside, across in sent:
        across, part = lax.optimization_barrier((across, part))
        panels.append([own, beside, across, crossed(across, 1)])
        part = gram_rows(panels[-1]) + (part if len(panels) > 1 else 0.0)

    pieces = lax.all_to_all(part.reshape(blocks, width, norb), "dom", 0, 0, tiled=True)
    piece = jnp.sum(pieces, axis=0) * (1.0 / (planes * cells * blocks))
    own_gram = lax.all_to_all(jnp.broadcast_to(piece, (blocks, width, norb)), "dom", 0, 0, tiled=True)
    own_gram = own_gram.reshape(local_orbs, norb)
    across = crossed(own_gram, 2)
    gram, own_rows = cholesky_inverse(band, [own_gram, crossed(own_gram, 1), across, crossed(across, 1)])
    result = rotated(own_rows, panels, chunks)
    return (result.reshape(planes, side_y, side_z, local_orbs), gram)


def solution(mesh):
    placed = (
        P("dom", None, None, "band"),
        P("dom", None, None),
        P("dom", None, None),
        P("dom", None, None),
        P("dom"),
        P("dom"),
    )
    return jax.shard_map(
        shards,
        mesh=mesh,
        in_specs=placed,
        out_specs=(P("dom", None, None, "band"), P()),
        check_vma=False,
    )
```

```python
import functools

import jax
import jax.numpy as jnp
from jax import lax
from jax.experimental import pallas as pl
from jax.experimental.pallas import tpu as pltpu
from jax.sharding import PartitionSpec as P

SPAN = 3
MAXPROJ = 4
HALO = 4
PAD = 8
LANES = 128
GROUP = 8
BEFORE, AFTER = 2, 1
NEAR = BEFORE + 1 + AFTER

center_weight = -205.0 / 72.0
side_weights = (8.0 / 5.0, -1.0 / 5.0, 8.0 / 315.0, -1.0 / 560.0)
HIGHEST = lax.Precision.HIGHEST
WHOLE = pl.BlockSpec(memory_space=pltpu.VMEM)


def params(mebibytes):
    return pltpu.CompilerParams(vmem_limit_bytes=mebibytes * 1024 * 1024)


def cost(flops, bytes_accessed):
    return pl.CostEstimate(flops=int(flops), bytes_accessed=int(bytes_accessed), transcendentals=0)


def halves(value):
    high = value.astype(jnp.bfloat16)
    return high, (value - high.astype(jnp.float32)).astype(jnp.bfloat16)


def side_by_side(value):
    return jnp.concatenate(halves(value), axis=1)


def dot_halves(left, right):
    dot = functools.partial(jnp.dot, preferred_element_type=jnp.float32)
    return dot(left[0], right) + dot(left[1], right)


def folded(value):
    return value[:, :LANES] + value[:, LANES:]


def swapped(blocks, lane, before=None, after=None):
    count = len(blocks)
    width = LANES // count

    def turned(value, at, extra):
        if extra is None:
            return pltpu.roll(value, at % count * width, 1) if at else value
        return pltpu.roll(value, lax.rem((at % count + extra) * width, LANES), 1)

    blocks = [turned(value, at, None if before is None else count - before) for at, value in enumerate(blocks)]
    bit = 1
    while bit < count:
        chosen = (lane // (bit * width)) % 2 == 1
        blocks = [jnp.where(chosen, blocks[(at + bit) % count], blocks[at]) for at in range(count)]
        bit *= 2
    return [turned(blocks[-at % count], -at, after) for at in range(count)]


def swap_into(read, write, count, rows, before=None, after=None):
    tile = 8 * max(1, 32 // count)
    lane = lax.broadcasted_iota(jnp.int32, (tile, LANES), 1)

    def step(index, carry):
        start = pl.multiple_of(index * tile, 8)
        blocks = [read(block, start, tile) for block in range(count)]
        for block, value in enumerate(swapped(blocks, lane, before, after)):
            write(block, start, tile, value)
        return carry

    lax.fori_loop(0, rows // tile, step, 0, unroll=True)


def swap_in_kernel(count, rows, levels_ref, in_ref, out_ref):
    def read(block, start, size):
        return in_ref[block, pl.ds(start, size), :]

    def write(block, start, size, value):
        out_ref[block, pl.ds(start, size), :] = value

    swap_into(read, write, count, rows)
    for block in range(count):
        out_ref[block, pl.ds(rows, levels_ref.shape[0]), :] = levels_ref[...]


def swap_in(levels, value):
    planes, count, rows, _ = value.shape
    extra = levels.shape[1]
    return pl.pallas_call(
        functools.partial(swap_in_kernel, count, rows),
        grid=(planes,),
        in_specs=[
            pl.BlockSpec((None, extra, LANES), lambda p: (p, 0, 0)),
            pl.BlockSpec((None, count, rows, LANES), lambda p: (p, 0, 0, 0)),
        ],
        out_specs=pl.BlockSpec((count, None, rows + extra, LANES), lambda p: (0, p, 0, 0)),
        out_shape=jax.ShapeDtypeStruct((count, planes, rows + extra, LANES), jnp.float32),
        compiler_params=params(12),
        cost_estimate=cost(0, 8 * value.size),
    )(levels, value)


def swap_out_kernel(me_ref, high_ref, low_ref, weights_ref, *refs):
    arrived_refs, out_ref = refs[:-1], refs[-1]
    count = len(arrived_refs)
    planes, rows, _ = arrived_refs[0].shape
    weights = side_by_side(weights_ref[...] * (1.0 / 18.0))
    for plane in range(planes):

        def read(block, start, size):
            return arrived_refs[-block % count][plane, pl.ds(start, size), :]

        def write(block, start, size, value):
            at = pl.ds(pl.multiple_of(block * rows + start, 8), size)
            out_ref[plane, at, :] = value

        swap_into(read, write, count, rows, after=me_ref[0])
        tile = rows * count // 6

        def add(index, carry):
            at = pl.ds(pl.multiple_of(index * tile, 8), tile)
            term = folded(dot_halves((high_ref[plane, at, :], low_ref[plane, at, :]), weights))
            out_ref[plane, at, :] = out_ref[plane, at, :] + term
            return carry

        lax.fori_loop(0, 6, add, 0)


def swap_out(me, arrived, high, low, weights, first_plane):
    count = len(arrived)
    planes, rows, _ = arrived[0].shape
    cells = count * rows
    basis = pl.BlockSpec((planes, cells, 2 * LANES), lambda i: (first_plane // planes, 0, 0))
    return pl.pallas_call(
        swap_out_kernel,
        grid=(1,),
        in_specs=[
            pl.BlockSpec(memory_space=pltpu.SMEM),
            basis,
            basis,
            pl.BlockSpec(weights.shape, lambda i: (0, 0)),
        ]
        + [pl.BlockSpec(arrived[0].shape, lambda i: (0, 0, 0))] * count,
        out_specs=pl.BlockSpec((planes, cells, LANES), lambda i: (0, 0, 0)),
        out_shape=jax.ShapeDtypeStruct((planes, cells, LANES), jnp.float32),
        compiler_params=params(24),
        cost_estimate=cost(0, 24 * cells * planes * LANES),
    )(me, high, low, weights, *arrived)


def fill_row(target, plane, y, row, side_z):
    target[plane, y, pl.ds(PAD, side_z), :] = row
    target[plane, y, pl.ds(PAD - HALO, HALO), :] = row[side_z - HALO :]
    target[plane, y, pl.ds(PAD + side_z, HALO), :] = row[:HALO]


def local_part(source, potential_ref, planes, first, side_y, side_z, line_of, finish):
    tile = 16

    def row(y, carry):
        for start in range(0, side_z, tile):

            def load(plane, y_at, shift):
                return source[plane, y_at, pl.ds(PAD + start + shift, tile), :]

            line = line_of(lambda plane: load(plane, y, 0))
            at = pl.ds(pl.multiple_of(y * side_z + start, 8), tile)
            for plane in range(planes):
                here = first + plane
                total = (potential_ref[plane, at, :] - 1.5 * center_weight - 7.0) * line[HALO + plane]
                for offset in range(1, HALO + 1):
                    around = line[HALO + plane + offset] + line[HALO + plane - offset]
                    around = around + (load(here, y, offset) + load(here, y, -offset))
                    up = lax.rem(y + offset, side_y)
                    down = lax.rem(y + side_y - offset, side_y)
                    around = around + (load(here, up, 0) + load(here, down, 0))
                    total = total - (0.5 * side_weights[offset - 1]) * around
                finish(plane, y, start, at, total)
        return carry

    lax.fori_loop(0, side_y, row, 0)


def filter_kernel(planes, side_y, side_z, width, chunks, me_ref, arrived_ref, *rest):
    outs, (field, padded, first, flat, potential) = rest[:-5], rest[-5:]
    count = arrived_ref.shape[0]
    cells = side_y * side_z
    rows = cells // count
    tile = 16

    line = lax.broadcasted_iota(jnp.int32, (2 * count, LANES), 0) % count
    lane = lax.broadcasted_iota(jnp.int32, (2 * count, LANES), 1) // width
    spread = (line == lane).astype(jnp.bfloat16)
    for plane in range(planes):
        lines = [arrived_ref[:, plane, rows + at, :] for at in range(cells // LANES)]
        high, low = halves(jnp.concatenate(lines, axis=1))
        both = jnp.concatenate([high.astype(jnp.float32), low.astype(jnp.float32)], axis=0)
        potential[plane] = jnp.dot(both.T.astype(jnp.bfloat16), spread, preferred_element_type=jnp.float32)

    for plane in range(planes):

        def read_in(block, start, size):
            return arrived_ref[block, plane, pl.ds(start, size), :]

        def write_in(block, start, size, value):
            field[plane, pl.ds(pl.multiple_of(block * rows + start, 8), size), :] = value

        swap_into(read_in, write_in, count, rows)

    def fill(y, carry):
        for plane in range(planes):
            fill_row(padded, plane, y, field[plane, pl.ds(pl.multiple_of(y * side_z, 8), side_z), :], side_z)
        return carry

    lax.fori_loop(0, side_y, fill, 0)

    def line_of(load):
        inside = [load(plane) for plane in range(planes)]
        before = [pltpu.roll(value, width, 1) for value in inside]
        after = [pltpu.roll(value, LANES - width, 1) for value in inside]
        return before[planes - HALO :] + inside + after[:HALO]

    def finish_first(plane, y, start, at, total):
        first[plane, y, pl.ds(PAD + start, tile), :] = total
        if start == 0:
            first[plane, y, pl.ds(PAD + side_z, HALO), :] = total[:HALO]
        if start == side_z - tile:
            first[plane, y, pl.ds(PAD - HALO, HALO), :] = total[tile - HALO :]

    def finish_second(plane, y, start, at, total):
        flat[plane, at, :] = total * (1.0 / 18.0) - field[plane, at, :]

    local_part(padded, potential, planes, 0, side_y, side_z, line_of, finish_first)
    local_part(first, potential, planes, 0, side_y, side_z, line_of, finish_second)

    for index, (begin, size_of) in enumerate(chunks):
        group = outs[index * count : (index + 1) * count]
        for plane in range(size_of):

            def read_out(block, start, size):
                return flat[begin + plane, pl.ds(pl.multiple_of(block * rows + start, 8), size), :]

            def write_out(block, start, size, value):
                group[block][plane, pl.ds(start, size), :] = value

            swap_into(read_out, write_out, count, rows, before=me_ref[0])


def filter_orbitals(me, arrived, side_y, side_z, width, chunks):
    count, planes = arrived.shape[:2]
    rows = side_y * side_z // count
    flat = pltpu.VMEM((planes, side_y * side_z, LANES), jnp.float32)
    padded = pltpu.VMEM((planes, side_y, side_z + 2 * PAD, LANES), jnp.float32)
    shapes = [jax.ShapeDtypeStruct((size, rows, LANES), jnp.float32) for _, size in chunks for _ in range(count)]
    outs = pl.pallas_call(
        functools.partial(filter_kernel, planes, side_y, side_z, width, chunks),
        in_specs=[pl.BlockSpec(memory_space=pltpu.SMEM), WHOLE],
        out_specs=[WHOLE] * len(shapes),
        out_shape=shapes,
        scratch_shapes=[flat, padded, padded, flat, flat],
        compiler_params=params(56),
        cost_estimate=cost(100 * arrived.size, 12 * arrived.size),
    )(me, arrived)
    return [outs[index * count : (index + 1) * count] for index in range(len(chunks))]


def basis_kernel(planes, side_y, side_z, bands, *refs):
    raw_refs = refs[:bands]
    offset_ref, potential_ref, orbitals_ref, high_ref, low_ref, parts_ref, turned, placed = refs[bands:]
    cells = side_y * side_z
    for part in range(SPAN):
        at = pl.ds(part * cells, cells)
        stack = [raw_ref[block, :, at] for raw_ref in raw_refs for block in range(NEAR)]
        turned[part] = jnp.concatenate(stack, axis=0).T
    offset = offset_ref[0:1, :]

    def place(y, carry):
        at = pl.ds(pl.multiple_of(y * side_z, 8), side_z)
        values = [turned[part, at, :] for part in range(SPAN)]
        for plane in range(planes + 2 * HALO):
            row = jnp.zeros((side_z, LANES), jnp.float32)
            for part in range(SPAN):
                row = jnp.where(offset == float(plane - HALO - part), values[part], row)
            fill_row(placed, plane, y, row, side_z)
        return carry

    lax.fori_loop(0, side_y, place, 0)

    def line_of(load):
        return [load(plane) for plane in range(planes + 2 * HALO)]

    def finish(plane, y, start, at, total):
        own = placed[HALO + plane, y, pl.ds(PAD + start, 16), :]
        high, low = halves(jnp.concatenate([total, own], axis=1))
        high_ref[plane, at, :] = high
        low_ref[plane, at, :] = low

    local_part(placed, potential_ref, planes, HALO, side_y, side_z, line_of, finish)

    dot = functools.partial(jnp.dot, preferred_element_type=jnp.float32)
    with_orbitals = with_basis = 0.0
    for plane in range(planes):
        high, low = high_ref[plane], low_ref[plane]
        left = halves(orbitals_ref[plane].T)
        with_orbitals = with_orbitals + (dot(left[0], high) + (dot(left[0], low) + dot(left[1], high)))
        own_high, own_low = high[:, LANES:], low[:, LANES:]
        turned_high = own_high.astype(jnp.float32).T.astype(jnp.bfloat16)
        turned_low = own_low.astype(jnp.float32).T.astype(jnp.bfloat16)
        both = jnp.concatenate([own_high, own_low], axis=1)
        with_basis = with_basis + (dot(turned_high, both) + dot(turned_low, both))
    parts_ref[0] = with_orbitals[:, LANES:].T
    parts_ref[1] = with_orbitals[:, :LANES].T
    parts_ref[2] = folded(with_basis)


def build_basis(raw, offset, potential, orbitals, side_y, side_z):
    planes, cells, _ = orbitals.shape
    pair = jax.ShapeDtypeStruct((planes, cells, 2 * LANES), jnp.bfloat16)
    return pl.pallas_call(
        functools.partial(basis_kernel, planes, side_y, side_z, len(raw)),
        in_specs=[WHOLE] * (len(raw) + 3),
        out_specs=[WHOLE] * 3,
        out_shape=[pair, pair, jax.ShapeDtypeStruct((3, LANES, LANES), jnp.float32)],
        scratch_shapes=[
            pltpu.VMEM((SPAN, cells, LANES), jnp.float32),
            pltpu.VMEM((planes + 2 * HALO, side_y, side_z + 2 * PAD, LANES), jnp.float32),
        ],
        compiler_params=params(56),
        cost_estimate=cost(200 * orbitals.size, 24 * orbitals.size),
    )(*raw, offset, potential, orbitals)


def weights_kernel(bands, me_ref, parts_ref, coupling_ref, out_ref):
    count = parts_ref.shape[0]
    size = LANES // NEAR
    lines = size // bands
    me = me_ref[0]
    dot = functools.partial(jnp.dot, precision=HIGHEST, preferred_element_type=jnp.float32)

    def device(step):
        return lax.rem(me + step % count, count)

    def total(pick, block):
        shares = [pick(block - (near - BEFORE), near) for near in range(NEAR)]
        return (shares[0] + shares[1]) + (shares[2] + shares[3])

    def of_block(value, near):
        starts = [(band * NEAR + near) * lines for band in range(bands)]
        return jnp.concatenate([value[start : start + lines] for start in starts], axis=0)

    def joined(values):
        return jnp.concatenate(
            [values[near][band * lines : (band + 1) * lines] for band in range(bands) for near in range(NEAR)], axis=0
        )

    def couple(block, value):
        return dot(coupling_ref[device(block)], value)

    def kept(function):
        known = {}

        def look(step):
            if step % count not in known:
                known[step % count] = function(step)
            return known[step % count]

        return look

    weight = kept(
        lambda block: couple(block, total(lambda step, near: of_block(parts_ref[device(step), 0], near), block))
    )
    weights = kept(lambda step: joined([weight(step + near - BEFORE) for near in range(NEAR)]))
    second = kept(lambda step: parts_ref[device(step), 1] + dot(parts_ref[device(step), 2], weights(step)))
    out_ref[pl.ds(0, LANES), :] = weights(0)
    out_ref[pl.ds(LANES, LANES), :] = joined(
        [
            couple(near - BEFORE, total(lambda step, at: of_block(second(step), at), near - BEFORE))
            for near in range(NEAR)
        ]
    )


def near_weights(me, parts, coupling):
    return pl.pallas_call(
        functools.partial(weights_kernel, lax.axis_size("band")),
        in_specs=[pl.BlockSpec(memory_space=pltpu.SMEM), WHOLE, WHOLE],
        out_specs=WHOLE,
        out_shape=jax.ShapeDtypeStruct((2 * LANES, LANES), jnp.float32),
        compiler_params=params(24),
        cost_estimate=cost(0, 8 * parts.size),
    )(me, parts, coupling)


def shifted(value, axis, step):
    count = lax.axis_size(axis)
    return lax.ppermute(value, axis, [(source, (source + step) % count) for source in range(count)])


def exchanged(values):
    return [shifted(value, "dom", step) if step else value for step, value in enumerate(values)]


def crossed(value, bit):
    return lax.ppermute(value, "band", [(source, source ^ bit) for source in range(lax.axis_size("band"))])


def gram_kernel(own_ref, *rest):
    panels, out_ref = (own_ref, *rest[:-1]), rest[-1]

    @pl.when(pl.program_id(0) == 0)
    def _():
        out_ref[...] = jnp.zeros_like(out_ref)

    for plane in range(own_ref.shape[0]):
        left = halves(own_ref[plane].T)
        both = jnp.concatenate([side_by_side(panel[plane]) for panel in panels], axis=1)
        value = dot_halves(left, both)
        for index in range(len(panels)):
            at = pl.ds(index * LANES, LANES)
            out_ref[:, at] = out_ref[:, at] + folded(value[:, 2 * index * LANES : 2 * (index + 1) * LANES])


def gram_rows(panels):
    planes, cells, _ = panels[0].shape
    tile = cells // 2
    return pl.pallas_call(
        gram_kernel,
        grid=(cells // tile,),
        in_specs=[pl.BlockSpec((planes, tile, LANES), lambda i: (0, i, 0))] * len(panels),
        out_specs=pl.BlockSpec((LANES, len(panels) * LANES), lambda i: (0, 0)),
        out_shape=jax.ShapeDtypeStruct((LANES, len(panels) * LANES), jnp.float32),
        compiler_params=params(16),
        cost_estimate=cost(8 * panels[0].size * LANES * len(panels), 4 * panels[0].size * len(panels)),
    )(*panels)


def rotate_kernel(chunks, bands, inverse_ref, *rest):
    panels, out_ref = rest[:-1], rest[-1]
    right = side_by_side(inverse_ref[...].T)
    for index, (begin, size) in enumerate(chunks):
        group = panels[index * bands : (index + 1) * bands]
        for plane in range(size):
            left = halves(jnp.concatenate([panel[plane] for panel in group], axis=1))
            out_ref[begin + plane] = folded(dot_halves(left, right))


def rotated(inverse_rows, panels, chunks):
    bands = len(panels[0])
    planes = sum(size for _, size in chunks)
    cells = panels[0][0].shape[1]
    tile = cells // 4
    specs = [pl.BlockSpec((size, tile, LANES), lambda i: (0, i, 0)) for _, size in chunks for _ in range(bands)]
    return pl.pallas_call(
        functools.partial(rotate_kernel, chunks, bands),
        grid=(cells // tile,),
        in_specs=[pl.BlockSpec(inverse_rows.shape, lambda i: (0, 0)), *specs],
        out_specs=pl.BlockSpec((planes, tile, LANES), lambda i: (0, i, 0)),
        out_shape=jax.ShapeDtypeStruct((planes, cells, LANES), jnp.float32),
        compiler_params=params(56),
    )(inverse_rows, *[panel for group in panels for panel in group])


def thirds(value):
    first = value.astype(jnp.bfloat16).astype(jnp.float32)
    rest = value - first
    second = rest.astype(jnp.bfloat16).astype(jnp.float32)
    return first, second, rest - second


def eliminate(work, result):
    sublane = lax.broadcasted_iota(jnp.int32, (GROUP, LANES), 0)

    def splat(row, column):
        return jnp.broadcast_to(row[:, column : column + 1], (GROUP, LANES))

    def load(top):
        left = [jnp.broadcast_to(work[pl.ds(top + i, 1), :LANES], (GROUP, LANES)) for i in range(GROUP)]
        right = [jnp.broadcast_to(work[pl.ds(top + i, 1), LANES:], (GROUP, LANES)) for i in range(GROUP)]
        return left, right

    def factored(top, left, right):
        entry = {(i, j): splat(left[i], top + j) for i in range(GROUP) for j in range(i, GROUP)}
        for i in range(GROUP):
            scale = lax.rsqrt(entry[i, i])
            left[i] = left[i] * scale
            right[i] = right[i] * scale
            factor = {j: entry[i, j] * scale for j in range(i + 1, GROUP)}
            for m in range(i + 1, GROUP):
                for j in range(m, GROUP):
                    entry[m, j] = entry[m, j] - factor[m] * factor[j]
                left[m] = left[m] - factor[m] * left[i]
                right[m] = right[m] - factor[m] * right[i]

    def gathered(rows):
        value = rows[0]
        for i in range(1, GROUP):
            value = jnp.where(sublane == i, rows[i], value)
        return value

    for top in range(0, LANES, 2 * GROUP):
        left, right = load(top)
        factored(top, left, right)
        middle = top + GROUP
        next_left, next_right = load(middle)
        for m in range(GROUP):
            for i in range(GROUP):
                factor = splat(left[i], middle + m)
                next_left[m] = next_left[m] - factor * left[i]
                next_right[m] = next_right[m] - factor * right[i]
        factored(middle, next_left, next_right)
        upper = jnp.concatenate([gathered(left), gathered(next_left)], axis=0)
        lower = jnp.concatenate([gathered(right), gathered(next_right)], axis=0)
        result[pl.ds(top, 2 * GROUP), :] = lower
        below = middle + GROUP
        if below < LANES:
            a, b, c = thirds(upper)
            x, y, z = thirds(lower)
            columns = jnp.concatenate([a, a, b, b, a, c], axis=0).T[below:].astype(jnp.bfloat16)
            rows = jnp.concatenate(
                [jnp.concatenate([a, b, a, b, c, a], axis=0), jnp.concatenate([x, y, x, y, z, x], axis=0)], axis=1
            ).astype(jnp.bfloat16)
            rest = pl.ds(below, LANES - below)
            work[rest, :] = work[rest, :] - jnp.dot(columns, rows, preferred_element_type=jnp.float32)


def cholesky_kernel(band_ref, *refs):
    rows_refs, (gram_ref, own_ref, inverse, matrix, work, corner, scaled) = refs[:-7], refs[-7:]
    size = gram_ref.shape[0]
    bands = len(rows_refs)
    band = band_ref[0]

    def block_of(member):
        return pl.ds(pl.multiple_of((band ^ member) * LANES, LANES), LANES)

    for member, rows_ref in enumerate(rows_refs):
        for other in range(bands):
            gram_ref[block_of(member), block_of(member ^ other)] = rows_ref[:, other * LANES : (other + 1) * LANES]
    dot = functools.partial(jnp.dot, precision=HIGHEST, preferred_element_type=jnp.float32)
    diagonal = lax.broadcasted_iota(jnp.int32, (LANES, LANES), 0) == lax.broadcasted_iota(jnp.int32, (LANES, LANES), 1)
    identity = diagonal.astype(jnp.float32)
    matrix[:, :size] = gram_ref[...]
    matrix[:, size:] = jnp.zeros((size, size), jnp.float32)
    for at in range(0, size, LANES):
        matrix[pl.ds(at, LANES), size + at : size + at + LANES] = identity

    def block(index, carry):
        start = pl.multiple_of(index * LANES, LANES)
        at = pl.ds(start, LANES)
        work[:, :LANES] = matrix[at, at]
        work[:, LANES:] = identity
        eliminate(work, corner)
        scaled[...] = dot(corner[...], matrix[at, :])
        inverse[at, :] = scaled[:, size:]

        def below(other, carry):
            rows = pl.ds(pl.multiple_of(other * LANES, LANES), LANES)
            matrix[rows, :] = matrix[rows, :] - dot(scaled[:, rows].T, scaled[...])
            return carry

        lax.fori_loop(index + 1, size // LANES, below, 0)
        return carry

    lax.fori_loop(0, size // LANES, block, 0)
    for member in range(bands):
        own_ref[:, member * LANES : (member + 1) * LANES] = inverse[block_of(0), block_of(member)]


def cholesky_inverse(band, rows):
    size = rows[0].shape[1]
    return pl.pallas_call(
        cholesky_kernel,
        in_specs=[pl.BlockSpec(memory_space=pltpu.SMEM)] + [WHOLE] * len(rows),
        out_specs=[WHOLE] * 2,
        out_shape=[
            jax.ShapeDtypeStruct((size, size), jnp.float32),
            jax.ShapeDtypeStruct((LANES, size), jnp.float32),
        ],
        scratch_shapes=[
            pltpu.VMEM((size, size), jnp.float32),
            pltpu.VMEM((size, 2 * size), jnp.float32),
            pltpu.VMEM((LANES, 2 * LANES), jnp.float32),
            pltpu.VMEM((LANES, LANES), jnp.float32),
            pltpu.VMEM((LANES, 2 * size), jnp.float32),
        ],
        compiler_params=params(14),
    )(band.astype(jnp.int32).reshape(1), *rows)


def packed_projectors(projectors, atom_plane, planes):
    share = projectors.shape[0] // lax.axis_size("band")
    first = (atom_plane - lax.axis_index("dom") * planes).astype(jnp.float32)
    first = jnp.broadcast_to(first[:, None, None], (projectors.shape[0], MAXPROJ, LANES))
    packed = jnp.concatenate([projectors, first], axis=2)
    mine = lax.dynamic_slice_in_dim(packed, lax.axis_index("band") * share, share, 0)
    return mine.reshape(share * MAXPROJ, -1)


def near_shares(mine):
    return jnp.stack([mine if step == BEFORE else shifted(mine, "dom", BEFORE - step) for step in range(NEAR)])


def near_projectors(near, planes):
    across = crossed(near, 2)
    raw = [near, crossed(near, 1), across, crossed(across, 1)]
    moved = (planes * (jnp.arange(NEAR, dtype=jnp.float32) - BEFORE))[:, None]
    first = jnp.stack([member[:, :, -1] + moved for member in raw]).reshape(1, LANES)
    return raw, jnp.broadcast_to(first, (GROUP, LANES))


def shards(orbitals, potential, projectors, coupling, atom_plane, projector_count):
    planes, side_y, side_z, local_orbs = orbitals.shape
    blocks, bands = lax.axis_size("dom"), lax.axis_size("band")
    band = lax.axis_index("band")
    cells = side_y * side_z
    rows = cells // blocks
    width = local_orbs // blocks
    norb = local_orbs * bands
    chunks = tuple((plane, 1) for plane in range(planes))
    me = lax.axis_index("dom").astype(jnp.int32).reshape(1)

    order = jnp.arange(bands, dtype=jnp.int32) ^ band

    mine = packed_projectors(projectors, atom_plane, planes)
    mine, levels = lax.optimization_barrier((mine, potential.reshape(planes, cells // LANES, LANES)))
    near = near_shares(mine)
    levels = jnp.pad(levels, ((0, 0), (0, -levels.shape[1] % GROUP), (0, 0)))
    packed = swap_in(levels, orbitals.reshape(planes, blocks, rows, local_orbs))
    packed, near = lax.optimization_barrier((packed, near))
    raw, first = near_projectors(near, planes)
    arrived = lax.all_to_all(packed, "dom", 0, 0, tiled=True)

    own_levels = jnp.broadcast_to(potential.reshape(planes, cells, 1), (planes, cells, LANES))
    high, low, parts = build_basis(raw, first, own_levels, orbitals.reshape(planes, cells, LANES), side_y, side_z)
    atoms = projectors.shape[0]
    slots = jnp.arange(MAXPROJ, dtype=jnp.int32)
    live = (slots[None, :] < projector_count[:, None]).astype(jnp.float32)
    coupled = 0.5 * (coupling + jnp.transpose(coupling, (0, 2, 1))) * live[:, :, None] * live[:, None, :]
    coupled = jnp.take(coupled.reshape(bands, -1, MAXPROJ, MAXPROJ), order, axis=0)
    vectors = atoms * MAXPROJ
    row = jnp.arange(vectors, dtype=jnp.int32) // MAXPROJ
    matrix = jnp.tile(coupled.reshape(vectors, MAXPROJ), (1, atoms))
    matrix = jnp.where(row[:, None] == row[None, :], matrix, 0.0)
    matrix = jnp.pad(matrix, ((0, 0), (0, LANES - vectors)))
    payload = jnp.concatenate([parts.reshape(3 * LANES, LANES), matrix], axis=0)
    everyone = lax.all_gather(payload, "dom")
    weights = near_weights(
        me,
        everyone[:, : 3 * LANES].reshape(blocks, 3, LANES, LANES), everyone[:, 3 * LANES :, :vectors],
    )

    seconds = filter_orbitals(me, arrived, side_y, side_z, width, chunks)

    came, owns, besides, acrosses = exchanged(seconds[0]), [], [], []
    for index, (begin, size) in enumerate(chunks):
        if index + 1 < len(chunks):
            tied = (seconds[index + 1], came[1:3], acrosses[-1:])
            packed, came[1:3], acrosses[-1:] = lax.optimization_barrier(tied)
            coming = exchanged(packed)
        own = swap_out(me, came, high, low, weights, begin)
        owns.append(own)
        besides.append(crossed(own, 1))
        acrosses.append(crossed(own, 2))
        came = coming
    panels, part = [], None
    for index, across in enumerate(acrosses):
        if index + 1 < len(acrosses):
            across, owns[index + 1] = lax.optimization_barrier((across, owns[index + 1]))
        else:
            across, part = lax.optimization_barrier((across, part))
        panels.append([owns[index], besides[index], across, crossed(across, 1)])
        rows_of = gram_rows(panels[-1])
        part = rows_of if part is None else part + rows_of

    pieces = lax.all_to_all(part.reshape(blocks, width, norb), "dom", 0, 0, tiled=True)
    piece = jnp.sum(pieces, axis=0) * (1.0 / (planes * cells * blocks))
    own_gram = lax.all_to_all(jnp.broadcast_to(piece, (blocks, width, norb)), "dom", 0, 0, tiled=True)
    own_gram = own_gram.reshape(local_orbs, norb)
    across = crossed(own_gram, 2)
    gram, own_rows = cholesky_inverse(band, [own_gram, crossed(own_gram, 1), across, crossed(across, 1)])
    result = rotated(own_rows, panels, chunks)
    return (result.reshape(planes, side_y, side_z, local_orbs), gram)


def solution(mesh):
    placed = (
        P("dom", None, None, "band"),
        P("dom", None, None),
        P("dom", None, None),
        P("dom", None, None),
        P("dom"),
        P("dom"),
    )
    return jax.shard_map(
        shards,
        mesh=mesh,
        in_specs=placed,
        out_specs=(P("dom", None, None, "band"), P()),
        check_vma=False,
    )
```

```python
import functools

import jax
import jax.numpy as jnp
from jax import lax
from jax.experimental import pallas as pl
from jax.experimental.pallas import tpu as pltpu
from jax.sharding import PartitionSpec as P

SPAN = 3
MAXPROJ = 4
HALO = 4
PAD = 8
LANES = 128
GROUP = 8
BEFORE, AFTER = 2, 1
NEAR = BEFORE + 1 + AFTER

center_weight = -205.0 / 72.0
side_weights = (8.0 / 5.0, -1.0 / 5.0, 8.0 / 315.0, -1.0 / 560.0)
HIGHEST = lax.Precision.HIGHEST
WHOLE = pl.BlockSpec(memory_space=pltpu.VMEM)


def params(mebibytes):
    return pltpu.CompilerParams(vmem_limit_bytes=mebibytes * 1024 * 1024)


def cost(flops, bytes_accessed):
    return pl.CostEstimate(flops=int(flops), bytes_accessed=int(bytes_accessed), transcendentals=0)


def halves(value):
    high = value.astype(jnp.bfloat16)
    return high, (value - high.astype(jnp.float32)).astype(jnp.bfloat16)


def side_by_side(value):
    return jnp.concatenate(halves(value), axis=1)


def dot_halves(left, right):
    dot = functools.partial(jnp.dot, preferred_element_type=jnp.float32)
    return dot(left[0], right) + dot(left[1], right)


def folded(value):
    return value[:, :LANES] + value[:, LANES:]


def swapped(blocks, lane, before=None, after=None):
    count = len(blocks)
    width = LANES // count

    def turned(value, at, extra):
        if extra is None:
            return pltpu.roll(value, at % count * width, 1) if at else value
        return pltpu.roll(value, lax.rem((at % count + extra) * width, LANES), 1)

    blocks = [turned(value, at, None if before is None else count - before) for at, value in enumerate(blocks)]
    bit = 1
    while bit < count:
        chosen = (lane // (bit * width)) % 2 == 1
        blocks = [jnp.where(chosen, blocks[(at + bit) % count], blocks[at]) for at in range(count)]
        bit *= 2
    return [turned(blocks[-at % count], -at, after) for at in range(count)]


def swap_into(read, write, count, rows, before=None, after=None):
    tile = 8 * max(1, 32 // count)
    lane = lax.broadcasted_iota(jnp.int32, (tile, LANES), 1)

    def step(index, carry):
        start = pl.multiple_of(index * tile, 8)
        blocks = [read(block, start, tile) for block in range(count)]
        for block, value in enumerate(swapped(blocks, lane, before, after)):
            write(block, start, tile, value)
        return carry

    lax.fori_loop(0, rows // tile, step, 0, unroll=True)


def swap_in_kernel(count, rows, levels_ref, in_ref, out_ref):
    def read(block, start, size):
        return in_ref[block, pl.ds(start, size), :]

    def write(block, start, size, value):
        out_ref[block, pl.ds(start, size), :] = value

    swap_into(read, write, count, rows)
    for block in range(count):
        out_ref[block, pl.ds(rows, levels_ref.shape[0]), :] = levels_ref[...]


def swap_in(levels, value):
    planes, count, rows, _ = value.shape
    extra = levels.shape[1]
    return pl.pallas_call(
        functools.partial(swap_in_kernel, count, rows),
        grid=(planes,),
        in_specs=[
            pl.BlockSpec((None, extra, LANES), lambda p: (p, 0, 0)),
            pl.BlockSpec((None, count, rows, LANES), lambda p: (p, 0, 0, 0)),
        ],
        out_specs=pl.BlockSpec((count, None, rows + extra, LANES), lambda p: (0, p, 0, 0)),
        out_shape=jax.ShapeDtypeStruct((count, planes, rows + extra, LANES), jnp.float32),
        compiler_params=params(12),
        cost_estimate=cost(0, 8 * value.size),
    )(levels, value)


def swap_out_kernel(me_ref, high_ref, low_ref, weights_ref, *refs):
    planes, rows, _ = refs[0].shape
    arrived_refs, out_refs = refs[:-planes], refs[-planes:]
    count = len(arrived_refs)
    weights = side_by_side(weights_ref[...] * (1.0 / 18.0))
    for plane in range(planes):

        def read(block, start, size):
            return arrived_refs[-block % count][plane, pl.ds(start, size), :]

        def write(block, start, size, value):
            at = pl.ds(pl.multiple_of(block * rows + start, 8), size)
            out_refs[plane][at, :] = value

        swap_into(read, write, count, rows, after=me_ref[0])
        tile = rows * count // 6

        def add(index, carry):
            at = pl.ds(pl.multiple_of(index * tile, 8), tile)
            term = folded(dot_halves((high_ref[plane, at, :], low_ref[plane, at, :]), weights))
            out_refs[plane][at, :] = out_refs[plane][at, :] + term
            return carry

        lax.fori_loop(0, 6, add, 0)


def swap_out(me, arrived, high, low, weights, first_plane):
    count = len(arrived)
    planes, rows, _ = arrived[0].shape
    cells = count * rows
    basis = pl.BlockSpec((planes, cells, 2 * LANES), lambda i: (first_plane // planes, 0, 0))
    return pl.pallas_call(
        swap_out_kernel,
        grid=(1,),
        in_specs=[
            pl.BlockSpec(memory_space=pltpu.SMEM),
            basis,
            basis,
            pl.BlockSpec(weights.shape, lambda i: (0, 0)),
        ]
        + [pl.BlockSpec(arrived[0].shape, lambda i: (0, 0, 0))] * count,
        out_specs=[pl.BlockSpec((None, cells, LANES), lambda i: (0, 0, 0))] * planes,
        out_shape=[jax.ShapeDtypeStruct((1, cells, LANES), jnp.float32)] * planes,
        compiler_params=params(24),
        cost_estimate=cost(0, 24 * cells * planes * LANES),
    )(me, high, low, weights, *arrived)


def fill_row(target, plane, y, row, side_z):
    target[plane, y, pl.ds(PAD, side_z), :] = row
    target[plane, y, pl.ds(PAD - HALO, HALO), :] = row[side_z - HALO :]
    target[plane, y, pl.ds(PAD + side_z, HALO), :] = row[:HALO]


def local_part(source, potential_ref, planes, first, side_y, side_z, line_of, finish):
    tile = 16

    def row(y, carry):
        for start in range(0, side_z, tile):

            def load(plane, y_at, shift):
                return source[plane, y_at, pl.ds(PAD + start + shift, tile), :]

            line = line_of(lambda plane: load(plane, y, 0))
            at = pl.ds(pl.multiple_of(y * side_z + start, 8), tile)
            for plane in range(planes):
                here = first + plane
                total = (potential_ref[plane, at, :] - 1.5 * center_weight - 7.0) * line[HALO + plane]
                for offset in range(1, HALO + 1):
                    around = line[HALO + plane + offset] + line[HALO + plane - offset]
                    around = around + (load(here, y, offset) + load(here, y, -offset))
                    up = lax.rem(y + offset, side_y)
                    down = lax.rem(y + side_y - offset, side_y)
                    around = around + (load(here, up, 0) + load(here, down, 0))
                    total = total - (0.5 * side_weights[offset - 1]) * around
                finish(plane, y, start, at, total)
        return carry

    lax.fori_loop(0, side_y, row, 0)


def filter_kernel(planes, side_y, side_z, width, chunks, me_ref, arrived_ref, *rest):
    outs, (field, padded, first, flat, potential) = rest[:-5], rest[-5:]
    count = arrived_ref.shape[0]
    cells = side_y * side_z
    rows = cells // count
    tile = 16

    line = lax.broadcasted_iota(jnp.int32, (2 * count, LANES), 0) % count
    lane = lax.broadcasted_iota(jnp.int32, (2 * count, LANES), 1) // width
    spread = (line == lane).astype(jnp.bfloat16)
    for plane in range(planes):
        lines = [arrived_ref[:, plane, rows + at, :] for at in range(cells // LANES)]
        high, low = halves(jnp.concatenate(lines, axis=1))
        both = jnp.concatenate([high.astype(jnp.float32), low.astype(jnp.float32)], axis=0)
        potential[plane] = jnp.dot(both.T.astype(jnp.bfloat16), spread, preferred_element_type=jnp.float32)

    for plane in range(planes):

        def read_in(block, start, size):
            return arrived_ref[block, plane, pl.ds(start, size), :]

        def write_in(block, start, size, value):
            field[plane, pl.ds(pl.multiple_of(block * rows + start, 8), size), :] = value

        swap_into(read_in, write_in, count, rows)

    def fill(y, carry):
        for plane in range(planes):
            fill_row(padded, plane, y, field[plane, pl.ds(pl.multiple_of(y * side_z, 8), side_z), :], side_z)
        return carry

    lax.fori_loop(0, side_y, fill, 0)

    def line_of(load):
        inside = [load(plane) for plane in range(planes)]
        before = [pltpu.roll(value, width, 1) for value in inside]
        after = [pltpu.roll(value, LANES - width, 1) for value in inside]
        return before[planes - HALO :] + inside + after[:HALO]

    def finish_first(plane, y, start, at, total):
        first[plane, y, pl.ds(PAD + start, tile), :] = total
        if start == 0:
            first[plane, y, pl.ds(PAD + side_z, HALO), :] = total[:HALO]
        if start == side_z - tile:
            first[plane, y, pl.ds(PAD - HALO, HALO), :] = total[tile - HALO :]

    def finish_second(plane, y, start, at, total):
        flat[plane, at, :] = total * (1.0 / 18.0) - field[plane, at, :]

    local_part(padded, potential, planes, 0, side_y, side_z, line_of, finish_first)
    local_part(first, potential, planes, 0, side_y, side_z, line_of, finish_second)

    for index, (begin, size_of) in enumerate(chunks):
        group = outs[index * count : (index + 1) * count]
        for plane in range(size_of):

            def read_out(block, start, size):
                return flat[begin + plane, pl.ds(pl.multiple_of(block * rows + start, 8), size), :]

            def write_out(block, start, size, value):
                group[block][plane, pl.ds(start, size), :] = value

            swap_into(read_out, write_out, count, rows, before=me_ref[0])


def filter_orbitals(me, arrived, side_y, side_z, width, chunks):
    count, planes = arrived.shape[:2]
    rows = side_y * side_z // count
    flat = pltpu.VMEM((planes, side_y * side_z, LANES), jnp.float32)
    padded = pltpu.VMEM((planes, side_y, side_z + 2 * PAD, LANES), jnp.float32)
    shapes = [jax.ShapeDtypeStruct((size, rows, LANES), jnp.float32) for _, size in chunks for _ in range(count)]
    outs = pl.pallas_call(
        functools.partial(filter_kernel, planes, side_y, side_z, width, chunks),
        in_specs=[pl.BlockSpec(memory_space=pltpu.SMEM), WHOLE],
        out_specs=[WHOLE] * len(shapes),
        out_shape=shapes,
        scratch_shapes=[flat, padded, padded, flat, flat],
        compiler_params=params(56),
        cost_estimate=cost(100 * arrived.size, 12 * arrived.size),
    )(me, arrived)
    return [outs[index * count : (index + 1) * count] for index in range(len(chunks))]


def basis_kernel(planes, side_y, side_z, bands, *refs):
    raw_refs = refs[:bands]
    offset_ref, potential_ref, orbitals_ref, high_ref, low_ref, parts_ref, turned, placed = refs[bands:]
    cells = side_y * side_z
    for part in range(SPAN):
        at = pl.ds(part * cells, cells)
        stack = [raw_ref[block, :, at] for raw_ref in raw_refs for block in range(NEAR)]
        turned[part] = jnp.concatenate(stack, axis=0).T
    offset = offset_ref[0:1, :]

    def place(y, carry):
        at = pl.ds(pl.multiple_of(y * side_z, 8), side_z)
        values = [turned[part, at, :] for part in range(SPAN)]
        for plane in range(planes + 2 * HALO):
            row = jnp.zeros((side_z, LANES), jnp.float32)
            for part in range(SPAN):
                row = jnp.where(offset == float(plane - HALO - part), values[part], row)
            fill_row(placed, plane, y, row, side_z)
        return carry

    lax.fori_loop(0, side_y, place, 0)

    def line_of(load):
        return [load(plane) for plane in range(planes + 2 * HALO)]

    def finish(plane, y, start, at, total):
        own = placed[HALO + plane, y, pl.ds(PAD + start, 16), :]
        high, low = halves(jnp.concatenate([total, own], axis=1))
        high_ref[plane, at, :] = high
        low_ref[plane, at, :] = low

    local_part(placed, potential_ref, planes, HALO, side_y, side_z, line_of, finish)

    dot = functools.partial(jnp.dot, preferred_element_type=jnp.float32)
    with_orbitals = with_basis = 0.0
    for plane in range(planes):
        high, low = high_ref[plane], low_ref[plane]
        left = halves(orbitals_ref[plane].T)
        with_orbitals = with_orbitals + (dot(left[0], high) + (dot(left[0], low) + dot(left[1], high)))
        own_high, own_low = high[:, LANES:], low[:, LANES:]
        turned_high = own_high.astype(jnp.float32).T.astype(jnp.bfloat16)
        turned_low = own_low.astype(jnp.float32).T.astype(jnp.bfloat16)
        both = jnp.concatenate([own_high, own_low], axis=1)
        with_basis = with_basis + (dot(turned_high, both) + dot(turned_low, both))
    parts_ref[0] = with_orbitals[:, LANES:].T
    parts_ref[1] = with_orbitals[:, :LANES].T
    parts_ref[2] = folded(with_basis)


def build_basis(raw, offset, potential, orbitals, side_y, side_z):
    planes, cells, _ = orbitals.shape
    pair = jax.ShapeDtypeStruct((planes, cells, 2 * LANES), jnp.bfloat16)
    return pl.pallas_call(
        functools.partial(basis_kernel, planes, side_y, side_z, len(raw)),
        in_specs=[WHOLE] * (len(raw) + 3),
        out_specs=[WHOLE] * 3,
        out_shape=[pair, pair, jax.ShapeDtypeStruct((3, LANES, LANES), jnp.float32)],
        scratch_shapes=[
            pltpu.VMEM((SPAN, cells, LANES), jnp.float32),
            pltpu.VMEM((planes + 2 * HALO, side_y, side_z + 2 * PAD, LANES), jnp.float32),
        ],
        compiler_params=params(56),
        cost_estimate=cost(200 * orbitals.size, 24 * orbitals.size),
    )(*raw, offset, potential, orbitals)


def weights_kernel(bands, me_ref, parts_ref, coupling_ref, out_ref):
    count = parts_ref.shape[0]
    size = LANES // NEAR
    lines = size // bands
    me = me_ref[0]
    dot = functools.partial(jnp.dot, precision=HIGHEST, preferred_element_type=jnp.float32)

    def device(step):
        return lax.rem(me + step % count, count)

    def total(pick, block):
        shares = [pick(block - (near - BEFORE), near) for near in range(NEAR)]
        return (shares[0] + shares[1]) + (shares[2] + shares[3])

    def of_block(value, near):
        starts = [(band * NEAR + near) * lines for band in range(bands)]
        return jnp.concatenate([value[start : start + lines] for start in starts], axis=0)

    def joined(values):
        return jnp.concatenate(
            [values[near][band * lines : (band + 1) * lines] for band in range(bands) for near in range(NEAR)], axis=0
        )

    def couple(block, value):
        return dot(coupling_ref[device(block)], value)

    def kept(function):
        known = {}

        def look(step):
            if step % count not in known:
                known[step % count] = function(step)
            return known[step % count]

        return look

    weight = kept(
        lambda block: couple(block, total(lambda step, near: of_block(parts_ref[device(step), 0], near), block))
    )
    weights = kept(lambda step: joined([weight(step + near - BEFORE) for near in range(NEAR)]))
    second = kept(lambda step: parts_ref[device(step), 1] + dot(parts_ref[device(step), 2], weights(step)))
    out_ref[pl.ds(0, LANES), :] = weights(0)
    out_ref[pl.ds(LANES, LANES), :] = joined(
        [
            couple(near - BEFORE, total(lambda step, at: of_block(second(step), at), near - BEFORE))
            for near in range(NEAR)
        ]
    )


def near_weights(me, parts, coupling):
    return pl.pallas_call(
        functools.partial(weights_kernel, lax.axis_size("band")),
        in_specs=[pl.BlockSpec(memory_space=pltpu.SMEM), WHOLE, WHOLE],
        out_specs=WHOLE,
        out_shape=jax.ShapeDtypeStruct((2 * LANES, LANES), jnp.float32),
        compiler_params=params(24),
        cost_estimate=cost(0, 8 * parts.size),
    )(me, parts, coupling)


def shifted(value, axis, step):
    count = lax.axis_size(axis)
    return lax.ppermute(value, axis, [(source, (source + step) % count) for source in range(count)])


def exchanged(values):
    return [shifted(value, "dom", step) if step else value for step, value in enumerate(values)]


def crossed(value, bit):
    return lax.ppermute(value, "band", [(source, source ^ bit) for source in range(lax.axis_size("band"))])


def gram_kernel(own_ref, *rest):
    panels, out_ref = (own_ref, *rest[:-1]), rest[-1]

    @pl.when(pl.program_id(0) == 0)
    def _():
        out_ref[...] = jnp.zeros_like(out_ref)

    for plane in range(own_ref.shape[0]):
        left = halves(own_ref[plane].T)
        both = jnp.concatenate([side_by_side(panel[plane]) for panel in panels], axis=1)
        value = dot_halves(left, both)
        for index in range(len(panels)):
            at = pl.ds(index * LANES, LANES)
            out_ref[:, at] = out_ref[:, at] + folded(value[:, 2 * index * LANES : 2 * (index + 1) * LANES])


def gram_rows(panels):
    planes, cells, _ = panels[0].shape
    tile = cells // 2
    return pl.pallas_call(
        gram_kernel,
        grid=(cells // tile,),
        in_specs=[pl.BlockSpec((planes, tile, LANES), lambda i: (0, i, 0))] * len(panels),
        out_specs=pl.BlockSpec((LANES, len(panels) * LANES), lambda i: (0, 0)),
        out_shape=jax.ShapeDtypeStruct((LANES, len(panels) * LANES), jnp.float32),
        compiler_params=params(16),
        cost_estimate=cost(8 * panels[0].size * LANES * len(panels), 4 * panels[0].size * len(panels)),
    )(*panels)


def rotate_kernel(chunks, bands, inverse_ref, *rest):
    panels, out_ref = rest[:-1], rest[-1]
    right = side_by_side(inverse_ref[...].T)
    for index, (begin, size) in enumerate(chunks):
        group = panels[index * bands : (index + 1) * bands]
        for plane in range(size):
            left = halves(jnp.concatenate([panel[plane] for panel in group], axis=1))
            out_ref[begin + plane] = folded(dot_halves(left, right))


def rotated(inverse_rows, panels, chunks):
    bands = len(panels[0])
    planes = sum(size for _, size in chunks)
    cells = panels[0][0].shape[1]
    tile = cells // 4
    specs = [pl.BlockSpec((size, tile, LANES), lambda i: (0, i, 0)) for _, size in chunks for _ in range(bands)]
    return pl.pallas_call(
        functools.partial(rotate_kernel, chunks, bands),
        grid=(cells // tile,),
        in_specs=[pl.BlockSpec(inverse_rows.shape, lambda i: (0, 0)), *specs],
        out_specs=pl.BlockSpec((planes, tile, LANES), lambda i: (0, i, 0)),
        out_shape=jax.ShapeDtypeStruct((planes, cells, LANES), jnp.float32),
        compiler_params=params(56),
    )(inverse_rows, *[panel for group in panels for panel in group])


def thirds(value):
    first = value.astype(jnp.bfloat16).astype(jnp.float32)
    rest = value - first
    second = rest.astype(jnp.bfloat16).astype(jnp.float32)
    return first, second, rest - second


def eliminate(work, result):
    sublane = lax.broadcasted_iota(jnp.int32, (GROUP, LANES), 0)

    def splat(row, column):
        return jnp.broadcast_to(row[:, column : column + 1], (GROUP, LANES))

    def load(top):
        left = [jnp.broadcast_to(work[pl.ds(top + i, 1), :LANES], (GROUP, LANES)) for i in range(GROUP)]
        right = [jnp.broadcast_to(work[pl.ds(top + i, 1), LANES:], (GROUP, LANES)) for i in range(GROUP)]
        return left, right

    def factored(top, left, right):
        entry = {(i, j): splat(left[i], top + j) for i in range(GROUP) for j in range(i, GROUP)}
        for i in range(GROUP):
            scale = lax.rsqrt(entry[i, i])
            left[i] = left[i] * scale
            right[i] = right[i] * scale
            factor = {j: entry[i, j] * scale for j in range(i + 1, GROUP)}
            for m in range(i + 1, GROUP):
                for j in range(m, GROUP):
                    entry[m, j] = entry[m, j] - factor[m] * factor[j]
                left[m] = left[m] - factor[m] * left[i]
                right[m] = right[m] - factor[m] * right[i]

    def gathered(rows):
        value = rows[0]
        for i in range(1, GROUP):
            value = jnp.where(sublane == i, rows[i], value)
        return value

    for top in range(0, LANES, 2 * GROUP):
        left, right = load(top)
        factored(top, left, right)
        middle = top + GROUP
        next_left, next_right = load(middle)
        for m in range(GROUP):
            for i in range(GROUP):
                factor = splat(left[i], middle + m)
                next_left[m] = next_left[m] - factor * left[i]
                next_right[m] = next_right[m] - factor * right[i]
        factored(middle, next_left, next_right)
        upper = jnp.concatenate([gathered(left), gathered(next_left)], axis=0)
        lower = jnp.concatenate([gathered(right), gathered(next_right)], axis=0)
        result[pl.ds(top, 2 * GROUP), :] = lower
        below = middle + GROUP
        if below < LANES:
            a, b, c = thirds(upper)
            x, y, z = thirds(lower)
            columns = jnp.concatenate([a, a, b, b, a, c], axis=0).T[below:].astype(jnp.bfloat16)
            rows = jnp.concatenate(
                [jnp.concatenate([a, b, a, b, c, a], axis=0), jnp.concatenate([x, y, x, y, z, x], axis=0)], axis=1
            ).astype(jnp.bfloat16)
            rest = pl.ds(below, LANES - below)
            work[rest, :] = work[rest, :] - jnp.dot(columns, rows, preferred_element_type=jnp.float32)


def cholesky_kernel(band_ref, *refs):
    rows_refs, (gram_ref, own_ref, inverse, matrix, work, corner, scaled) = refs[:-7], refs[-7:]
    size = gram_ref.shape[0]
    bands = len(rows_refs)
    band = band_ref[0]

    def block_of(member):
        return pl.ds(pl.multiple_of((band ^ member) * LANES, LANES), LANES)

    for member, rows_ref in enumerate(rows_refs):
        for other in range(bands):
            gram_ref[block_of(member), block_of(member ^ other)] = rows_ref[:, other * LANES : (other + 1) * LANES]
    dot = functools.partial(jnp.dot, precision=HIGHEST, preferred_element_type=jnp.float32)
    diagonal = lax.broadcasted_iota(jnp.int32, (LANES, LANES), 0) == lax.broadcasted_iota(jnp.int32, (LANES, LANES), 1)
    identity = diagonal.astype(jnp.float32)
    matrix[:, :size] = gram_ref[...]
    matrix[:, size:] = jnp.zeros((size, size), jnp.float32)
    for at in range(0, size, LANES):
        matrix[pl.ds(at, LANES), size + at : size + at + LANES] = identity

    def block(index, carry):
        start = pl.multiple_of(index * LANES, LANES)
        at = pl.ds(start, LANES)
        work[:, :LANES] = matrix[at, at]
        work[:, LANES:] = identity
        eliminate(work, corner)
        scaled[...] = dot(corner[...], matrix[at, :])
        inverse[at, :] = scaled[:, size:]

        def below(other, carry):
            rows = pl.ds(pl.multiple_of(other * LANES, LANES), LANES)
            matrix[rows, :] = matrix[rows, :] - dot(scaled[:, rows].T, scaled[...])
            return carry

        lax.fori_loop(index + 1, size // LANES, below, 0)
        return carry

    lax.fori_loop(0, size // LANES, block, 0)
    for member in range(bands):
        own_ref[:, member * LANES : (member + 1) * LANES] = inverse[block_of(0), block_of(member)]


def cholesky_inverse(band, rows):
    size = rows[0].shape[1]
    return pl.pallas_call(
        cholesky_kernel,
        in_specs=[pl.BlockSpec(memory_space=pltpu.SMEM)] + [WHOLE] * len(rows),
        out_specs=[WHOLE] * 2,
        out_shape=[
            jax.ShapeDtypeStruct((size, size), jnp.float32),
            jax.ShapeDtypeStruct((LANES, size), jnp.float32),
        ],
        scratch_shapes=[
            pltpu.VMEM((size, size), jnp.float32),
            pltpu.VMEM((size, 2 * size), jnp.float32),
            pltpu.VMEM((LANES, 2 * LANES), jnp.float32),
            pltpu.VMEM((LANES, LANES), jnp.float32),
            pltpu.VMEM((LANES, 2 * size), jnp.float32),
        ],
        compiler_params=params(14),
    )(band.astype(jnp.int32).reshape(1), *rows)


def packed_projectors(projectors, atom_plane, planes):
    share = projectors.shape[0] // lax.axis_size("band")
    first = (atom_plane - lax.axis_index("dom") * planes).astype(jnp.float32)
    first = jnp.broadcast_to(first[:, None, None], (projectors.shape[0], MAXPROJ, LANES))
    packed = jnp.concatenate([projectors, first], axis=2)
    mine = lax.dynamic_slice_in_dim(packed, lax.axis_index("band") * share, share, 0)
    return mine.reshape(share * MAXPROJ, -1)


def near_shares(mine):
    return jnp.stack([mine if step == BEFORE else shifted(mine, "dom", BEFORE - step) for step in range(NEAR)])


def near_projectors(near, planes):
    across = crossed(near, 2)
    raw = [near, crossed(near, 1), across, crossed(across, 1)]
    moved = (planes * (jnp.arange(NEAR, dtype=jnp.float32) - BEFORE))[:, None]
    first = jnp.stack([member[:, :, -1] + moved for member in raw]).reshape(1, LANES)
    return raw, jnp.broadcast_to(first, (GROUP, LANES))


def shards(orbitals, potential, projectors, coupling, atom_plane, projector_count):
    planes, side_y, side_z, local_orbs = orbitals.shape
    blocks, bands = lax.axis_size("dom"), lax.axis_size("band")
    band = lax.axis_index("band")
    cells = side_y * side_z
    rows = cells // blocks
    width = local_orbs // blocks
    norb = local_orbs * bands
    chunks = tuple((plane, 1) for plane in range(planes))
    half = planes // 2
    groups = ((0, half), (half, half))
    me = lax.axis_index("dom").astype(jnp.int32).reshape(1)

    order = jnp.arange(bands, dtype=jnp.int32) ^ band

    mine = packed_projectors(projectors, atom_plane, planes)
    mine, levels = lax.optimization_barrier((mine, potential.reshape(planes, cells // LANES, LANES)))
    near = near_shares(mine)
    levels = jnp.pad(levels, ((0, 0), (0, -levels.shape[1] % GROUP), (0, 0)))
    packed = swap_in(levels, orbitals.reshape(planes, blocks, rows, local_orbs))
    packed, near = lax.optimization_barrier((packed, near))
    raw, first = near_projectors(near, planes)
    arrived = lax.all_to_all(packed, "dom", 0, 0, tiled=True)

    own_levels = jnp.broadcast_to(potential.reshape(planes, cells, 1), (planes, cells, LANES))
    high, low, parts = build_basis(raw, first, own_levels, orbitals.reshape(planes, cells, LANES), side_y, side_z)
    atoms = projectors.shape[0]
    slots = jnp.arange(MAXPROJ, dtype=jnp.int32)
    live = (slots[None, :] < projector_count[:, None]).astype(jnp.float32)
    coupled = 0.5 * (coupling + jnp.transpose(coupling, (0, 2, 1))) * live[:, :, None] * live[:, None, :]
    coupled = jnp.take(coupled.reshape(bands, -1, MAXPROJ, MAXPROJ), order, axis=0)
    vectors = atoms * MAXPROJ
    row = jnp.arange(vectors, dtype=jnp.int32) // MAXPROJ
    matrix = jnp.tile(coupled.reshape(vectors, MAXPROJ), (1, atoms))
    matrix = jnp.where(row[:, None] == row[None, :], matrix, 0.0)
    matrix = jnp.pad(matrix, ((0, 0), (0, LANES - vectors)))
    payload = jnp.concatenate([parts.reshape(3 * LANES, LANES), matrix], axis=0)
    everyone = lax.all_gather(payload, "dom")
    weights = near_weights(
        me,
        everyone[:, : 3 * LANES].reshape(blocks, 3, LANES, LANES), everyone[:, 3 * LANES :, :vectors],
    )

    seconds = filter_orbitals(me, arrived, side_y, side_z, width, groups)

    tie = lax.optimization_barrier
    came = exchanged(seconds[0])
    packed, came[1:3] = tie((seconds[1], came[1:3]))
    coming = exchanged(packed)
    owns = list(swap_out(me, came, high, low, weights, 0))
    acrosses = [crossed(own, 2) for own in owns]
    besides = [crossed(own, 1) for own in owns]
    coming, acrosses[0] = tie((coming, acrosses[0]))
    late = list(swap_out(me, coming, high, low, weights, half))
    late, acrosses[1:] = tie((late, acrosses[1:]))
    acrosses += [crossed(own, 2) for own in late]
    besides += [crossed(own, 1) for own in late]
    owns += late
    panels, part = [], None
    for index, across in enumerate(acrosses):
        if index >= half:
            across, part = tie((across, part))
        panels.append([owns[index], besides[index], across, crossed(across, 1)])
        rows_of = gram_rows(panels[-1])
        part = rows_of if part is None else part + rows_of

    pieces = lax.all_to_all(part.reshape(blocks, width, norb), "dom", 0, 0, tiled=True)
    piece = jnp.sum(pieces, axis=0) * (1.0 / (planes * cells * blocks))
    own_gram = lax.all_to_all(jnp.broadcast_to(piece, (blocks, width, norb)), "dom", 0, 0, tiled=True)
    own_gram = own_gram.reshape(local_orbs, norb)
    across = crossed(own_gram, 2)
    gram, own_rows = cholesky_inverse(band, [own_gram, crossed(own_gram, 1), across, crossed(across, 1)])
    result = rotated(own_rows, panels, chunks)
    return (result.reshape(planes, side_y, side_z, local_orbs), gram)


def solution(mesh):
    placed = (
        P("dom", None, None, "band"),
        P("dom", None, None),
        P("dom", None, None),
        P("dom", None, None),
        P("dom"),
        P("dom"),
    )
    return jax.shard_map(
        shards,
        mesh=mesh,
        in_specs=placed,
        out_specs=(P("dom", None, None, "band"), P()),
        check_vma=False,
    )
```

```python
import functools

import jax
import jax.numpy as jnp
from jax import lax
from jax.experimental import pallas as pl
from jax.experimental.pallas import tpu as pltpu
from jax.sharding import PartitionSpec as P

SPAN = 3
MAXPROJ = 4
HALO = 4
PAD = 8
LANES = 128
GROUP = 8
BEFORE, AFTER = 2, 1
NEAR = BEFORE + 1 + AFTER

center_weight = -205.0 / 72.0
side_weights = (8.0 / 5.0, -1.0 / 5.0, 8.0 / 315.0, -1.0 / 560.0)
HIGHEST = lax.Precision.HIGHEST
WHOLE = pl.BlockSpec(memory_space=pltpu.VMEM)


def params(mebibytes):
    return pltpu.CompilerParams(vmem_limit_bytes=mebibytes * 1024 * 1024)


def cost(flops, bytes_accessed):
    return pl.CostEstimate(flops=int(flops), bytes_accessed=int(bytes_accessed), transcendentals=0)


def halves(value):
    high = value.astype(jnp.bfloat16)
    return high, (value - high.astype(jnp.float32)).astype(jnp.bfloat16)


def side_by_side(value):
    return jnp.concatenate(halves(value), axis=1)


def dot_halves(left, right):
    dot = functools.partial(jnp.dot, preferred_element_type=jnp.float32)
    return dot(left[0], right) + dot(left[1], right)


def folded(value):
    return value[:, :LANES] + value[:, LANES:]


def swapped(blocks, lane, before=None, after=None):
    count = len(blocks)
    width = LANES // count

    def turned(value, at, extra):
        if extra is None:
            return pltpu.roll(value, at % count * width, 1) if at else value
        return pltpu.roll(value, lax.rem((at % count + extra) * width, LANES), 1)

    blocks = [turned(value, at, None if before is None else count - before) for at, value in enumerate(blocks)]
    bit = 1
    while bit < count:
        chosen = (lane // (bit * width)) % 2 == 1
        blocks = [jnp.where(chosen, blocks[(at + bit) % count], blocks[at]) for at in range(count)]
        bit *= 2
    return [turned(blocks[-at % count], -at, after) for at in range(count)]


def swap_into(read, write, count, rows, before=None, after=None):
    tile = 8 * max(1, 32 // count)
    lane = lax.broadcasted_iota(jnp.int32, (tile, LANES), 1)

    def step(index, carry):
        start = pl.multiple_of(index * tile, 8)
        blocks = [read(block, start, tile) for block in range(count)]
        for block, value in enumerate(swapped(blocks, lane, before, after)):
            write(block, start, tile, value)
        return carry

    lax.fori_loop(0, rows // tile, step, 0, unroll=True)


def swap_in_kernel(count, rows, me_ref, levels_ref, in_ref, *out_refs):
    def read(block, start, size):
        return in_ref[block, pl.ds(start, size), :]

    def write(block, start, size, value):
        out_refs[block][pl.ds(start, size), :] = value

    swap_into(read, write, count, rows, before=me_ref[0])
    for out_ref in out_refs:
        out_ref[pl.ds(rows, levels_ref.shape[0]), :] = levels_ref[...]


def swap_in(me, levels, value):
    planes, count, rows, _ = value.shape
    extra = levels.shape[1]
    return pl.pallas_call(
        functools.partial(swap_in_kernel, count, rows),
        grid=(planes,),
        in_specs=[
            pl.BlockSpec(memory_space=pltpu.SMEM),
            pl.BlockSpec((None, extra, LANES), lambda p: (p, 0, 0)),
            pl.BlockSpec((None, count, rows, LANES), lambda p: (p, 0, 0, 0)),
        ],
        out_specs=[pl.BlockSpec((None, rows + extra, LANES), lambda p: (p, 0, 0))] * count,
        out_shape=[jax.ShapeDtypeStruct((planes, rows + extra, LANES), jnp.float32)] * count,
        compiler_params=params(14),
        cost_estimate=cost(0, 8 * value.size),
    )(me, levels, value)


def swap_out_kernel(planes, count, me_ref, high_ref, low_ref, weights_ref, *refs):
    arrived_refs, out_refs = refs[:-planes], refs[-planes:]
    rows = arrived_refs[0].shape[-2]
    by_steps = len(arrived_refs) > 1
    weights = side_by_side(weights_ref[...] * (1.0 / 18.0))
    for plane in range(planes):

        def read(block, start, size):
            if by_steps:
                return arrived_refs[-block % count][plane, pl.ds(start, size), :]
            return arrived_refs[0][block, plane, pl.ds(start, size), :]

        def write(block, start, size, value):
            at = pl.ds(pl.multiple_of(block * rows + start, 8), size)
            out_refs[plane][at, :] = value

        swap_into(read, write, count, rows, after=me_ref[0] if by_steps else None)
        tile = rows * count // 6

        def add(index, carry):
            at = pl.ds(pl.multiple_of(index * tile, 8), tile)
            term = folded(dot_halves((high_ref[plane, at, :], low_ref[plane, at, :]), weights))
            out_refs[plane][at, :] = out_refs[plane][at, :] + term
            return carry

        lax.fori_loop(0, 6, add, 0)


def swap_out(me, arrived, high, low, weights, first_plane):
    count = len(arrived) if len(arrived) > 1 else arrived[0].shape[0]
    planes, rows = arrived[0].shape[-3:-1]
    cells = count * rows
    basis = pl.BlockSpec((planes, cells, 2 * LANES), lambda i: (first_plane // planes, 0, 0))
    return pl.pallas_call(
        functools.partial(swap_out_kernel, planes, count),
        grid=(1,),
        in_specs=[
            pl.BlockSpec(memory_space=pltpu.SMEM),
            basis,
            basis,
            pl.BlockSpec(weights.shape, lambda i: (0, 0)),
        ]
        + [pl.BlockSpec(arrived[0].shape, lambda i: (0,) * arrived[0].ndim)] * len(arrived),
        out_specs=[pl.BlockSpec((None, cells, LANES), lambda i: (0, 0, 0))] * planes,
        out_shape=[jax.ShapeDtypeStruct((1, cells, LANES), jnp.float32)] * planes,
        compiler_params=params(24),
        cost_estimate=cost(0, 24 * cells * planes * LANES),
    )(me, high, low, weights, *arrived)


def fill_row(target, plane, y, row, side_z):
    target[plane, y, pl.ds(PAD, side_z), :] = row
    target[plane, y, pl.ds(PAD - HALO, HALO), :] = row[side_z - HALO :]
    target[plane, y, pl.ds(PAD + side_z, HALO), :] = row[:HALO]


def local_part(source, potential_ref, planes, first, side_y, side_z, line_of, finish):
    tile = 16

    def row(y, carry):
        for start in range(0, side_z, tile):

            def load(plane, y_at, shift):
                return source[plane, y_at, pl.ds(PAD + start + shift, tile), :]

            line = line_of(lambda plane: load(plane, y, 0))
            at = pl.ds(pl.multiple_of(y * side_z + start, 8), tile)
            for plane in range(planes):
                here = first + plane
                total = (potential_ref[plane, at, :] - 1.5 * center_weight - 7.0) * line[HALO + plane]
                for offset in range(1, HALO + 1):
                    around = line[HALO + plane + offset] + line[HALO + plane - offset]
                    around = around + (load(here, y, offset) + load(here, y, -offset))
                    up = lax.rem(y + offset, side_y)
                    down = lax.rem(y + side_y - offset, side_y)
                    around = around + (load(here, up, 0) + load(here, down, 0))
                    total = total - (0.5 * side_weights[offset - 1]) * around
                finish(plane, y, start, at, total)
        return carry

    lax.fori_loop(0, side_y, row, 0)


def filter_kernel(planes, side_y, side_z, count, half, me_ref, *refs):
    arrived_refs = [refs[-group % count] for group in range(count)]
    near_refs, late_ref = refs[count : 2 * count], refs[2 * count]
    field, padded, first, flat, potential = refs[2 * count + 1 :]
    me = me_ref[0]
    width = LANES // count
    cells = side_y * side_z
    rows = cells // count
    tile = 16

    line = lax.broadcasted_iota(jnp.int32, (2 * count, LANES), 0) % count
    lane = lax.broadcasted_iota(jnp.int32, (2 * count, LANES), 1) // width
    spread = (line == lane).astype(jnp.bfloat16)
    for plane in range(planes):
        lines = [ref[plane, pl.ds(rows, -(-cells // LANES // GROUP) * GROUP), :] for ref in arrived_refs]
        lines = [
            jnp.concatenate([value[at : at + 1] for value in lines], axis=0) for at in range(cells // LANES)
        ]
        high, low = halves(jnp.concatenate(lines, axis=1))
        both = jnp.concatenate([high.astype(jnp.float32), low.astype(jnp.float32)], axis=0)
        potential[plane] = jnp.dot(both.T.astype(jnp.bfloat16), spread, preferred_element_type=jnp.float32)

    for plane in range(planes):

        def read_in(block, start, size):
            return arrived_refs[block][plane, pl.ds(start, size), :]

        def write_in(block, start, size, value):
            field[plane, pl.ds(pl.multiple_of(block * rows + start, 8), size), :] = value

        swap_into(read_in, write_in, count, rows)

    def fill(y, carry):
        for plane in range(planes):
            fill_row(padded, plane, y, field[plane, pl.ds(pl.multiple_of(y * side_z, 8), side_z), :], side_z)
        return carry

    lax.fori_loop(0, side_y, fill, 0)

    def line_of(load):
        inside = [load(plane) for plane in range(planes)]
        before = [pltpu.roll(value, width, 1) for value in inside]
        after = [pltpu.roll(value, LANES - width, 1) for value in inside]
        return before[planes - HALO :] + inside + after[:HALO]

    def finish_first(plane, y, start, at, total):
        first[plane, y, pl.ds(PAD + start, tile), :] = total
        if start == 0:
            first[plane, y, pl.ds(PAD + side_z, HALO), :] = total[:HALO]
        if start == side_z - tile:
            first[plane, y, pl.ds(PAD - HALO, HALO), :] = total[tile - HALO :]

    def finish_second(plane, y, start, at, total):
        flat[plane, at, :] = total * (1.0 / 18.0) - field[plane, at, :]

    local_part(padded, potential, planes, 0, side_y, side_z, line_of, finish_first)
    local_part(first, potential, planes, 0, side_y, side_z, line_of, finish_second)

    for plane in range(planes):

        def read_out(block, start, size):
            return flat[plane, pl.ds(pl.multiple_of(block * rows + start, 8), size), :]

        def write_out(block, start, size, value):
            if plane < half:
                near_refs[block][plane, pl.ds(start, size), :] = value
            else:
                late_ref[lax.rem(me + block, count), plane - half, pl.ds(start, size), :] = value

        swap_into(read_out, write_out, count, rows)


def filter_orbitals(me, arrived, side_y, side_z, half):
    count, planes = len(arrived), arrived[0].shape[0]
    rows = side_y * side_z // count
    size = planes * side_y * side_z * LANES
    flat = pltpu.VMEM((planes, side_y * side_z, LANES), jnp.float32)
    padded = pltpu.VMEM((planes, side_y, side_z + 2 * PAD, LANES), jnp.float32)
    shapes = [jax.ShapeDtypeStruct((half, rows, LANES), jnp.float32)] * count
    shapes += [jax.ShapeDtypeStruct((count, planes - half, rows, LANES), jnp.float32)]
    outs = pl.pallas_call(
        functools.partial(filter_kernel, planes, side_y, side_z, count, half),
        in_specs=[pl.BlockSpec(memory_space=pltpu.SMEM)] + [WHOLE] * count,
        out_specs=[WHOLE] * len(shapes),
        out_shape=shapes,
        scratch_shapes=[flat, padded, padded, flat, flat],
        compiler_params=params(56),
        cost_estimate=cost(100 * size, 12 * size),
    )(me, *arrived)
    return list(outs[:count]), outs[count]


def basis_kernel(planes, side_y, side_z, bands, *refs):
    raw_refs = refs[:bands]
    offset_ref, potential_ref, orbitals_ref, high_ref, low_ref, parts_ref, turned, placed = refs[bands:]
    cells = side_y * side_z
    for part in range(SPAN):
        at = pl.ds(part * cells, cells)
        stack = [raw_ref[block, :, at] for raw_ref in raw_refs for block in range(NEAR)]
        turned[part] = jnp.concatenate(stack, axis=0).T
    offset = offset_ref[0:1, :]

    def place(y, carry):
        at = pl.ds(pl.multiple_of(y * side_z, 8), side_z)
        values = [turned[part, at, :] for part in range(SPAN)]
        for plane in range(planes + 2 * HALO):
            row = jnp.zeros((side_z, LANES), jnp.float32)
            for part in range(SPAN):
                row = jnp.where(offset == float(plane - HALO - part), values[part], row)
            fill_row(placed, plane, y, row, side_z)
        return carry

    lax.fori_loop(0, side_y, place, 0)

    def line_of(load):
        return [load(plane) for plane in range(planes + 2 * HALO)]

    def finish(plane, y, start, at, total):
        own = placed[HALO + plane, y, pl.ds(PAD + start, 16), :]
        high, low = halves(jnp.concatenate([total, own], axis=1))
        high_ref[plane, at, :] = high
        low_ref[plane, at, :] = low

    local_part(placed, potential_ref, planes, HALO, side_y, side_z, line_of, finish)

    dot = functools.partial(jnp.dot, preferred_element_type=jnp.float32)
    with_orbitals = with_basis = 0.0
    for plane in range(planes):
        high, low = high_ref[plane], low_ref[plane]
        left = halves(orbitals_ref[plane].T)
        with_orbitals = with_orbitals + (dot(left[0], high) + (dot(left[0], low) + dot(left[1], high)))
        own_high, own_low = high[:, LANES:], low[:, LANES:]
        turned_high = own_high.astype(jnp.float32).T.astype(jnp.bfloat16)
        turned_low = own_low.astype(jnp.float32).T.astype(jnp.bfloat16)
        both = jnp.concatenate([own_high, own_low], axis=1)
        with_basis = with_basis + (dot(turned_high, both) + dot(turned_low, both))
    parts_ref[0] = with_orbitals[:, LANES:].T
    parts_ref[1] = with_orbitals[:, :LANES].T
    parts_ref[2] = folded(with_basis)


def build_basis(raw, offset, potential, orbitals, side_y, side_z):
    planes, cells, _ = orbitals.shape
    pair = jax.ShapeDtypeStruct((planes, cells, 2 * LANES), jnp.bfloat16)
    return pl.pallas_call(
        functools.partial(basis_kernel, planes, side_y, side_z, len(raw)),
        in_specs=[WHOLE] * (len(raw) + 3),
        out_specs=[WHOLE] * 3,
        out_shape=[pair, pair, jax.ShapeDtypeStruct((3, LANES, LANES), jnp.float32)],
        scratch_shapes=[
            pltpu.VMEM((SPAN, cells, LANES), jnp.float32),
            pltpu.VMEM((planes + 2 * HALO, side_y, side_z + 2 * PAD, LANES), jnp.float32),
        ],
        compiler_params=params(56),
        cost_estimate=cost(200 * orbitals.size, 24 * orbitals.size),
    )(*raw, offset, potential, orbitals)


def weights_kernel(bands, me_ref, parts_ref, coupling_ref, out_ref):
    count = parts_ref.shape[0]
    size = LANES // NEAR
    lines = size // bands
    me = me_ref[0]
    dot = functools.partial(jnp.dot, precision=HIGHEST, preferred_element_type=jnp.float32)

    def device(step):
        return lax.rem(me + step % count, count)

    def total(pick, block):
        shares = [pick(block - (near - BEFORE), near) for near in range(NEAR)]
        return (shares[0] + shares[1]) + (shares[2] + shares[3])

    def of_block(value, near):
        starts = [(band * NEAR + near) * lines for band in range(bands)]
        return jnp.concatenate([value[start : start + lines] for start in starts], axis=0)

    def joined(values):
        return jnp.concatenate(
            [values[near][band * lines : (band + 1) * lines] for band in range(bands) for near in range(NEAR)], axis=0
        )

    def couple(block, value):
        return dot(coupling_ref[device(block)], value)

    def kept(function):
        known = {}

        def look(step):
            if step % count not in known:
                known[step % count] = function(step)
            return known[step % count]

        return look

    weight = kept(
        lambda block: couple(block, total(lambda step, near: of_block(parts_ref[device(step), 0], near), block))
    )
    weights = kept(lambda step: joined([weight(step + near - BEFORE) for near in range(NEAR)]))
    second = kept(lambda step: parts_ref[device(step), 1] + dot(parts_ref[device(step), 2], weights(step)))
    out_ref[pl.ds(0, LANES), :] = weights(0)
    out_ref[pl.ds(LANES, LANES), :] = joined(
        [
            couple(near - BEFORE, total(lambda step, at: of_block(second(step), at), near - BEFORE))
            for near in range(NEAR)
        ]
    )


def near_weights(me, parts, coupling):
    return pl.pallas_call(
        functools.partial(weights_kernel, lax.axis_size("band")),
        in_specs=[pl.BlockSpec(memory_space=pltpu.SMEM), WHOLE, WHOLE],
        out_specs=WHOLE,
        out_shape=jax.ShapeDtypeStruct((2 * LANES, LANES), jnp.float32),
        compiler_params=params(24),
        cost_estimate=cost(0, 8 * parts.size),
    )(me, parts, coupling)


def shifted(value, axis, step):
    count = lax.axis_size(axis)
    return lax.ppermute(value, axis, [(source, (source + step) % count) for source in range(count)])


def exchanged(values):
    return [shifted(value, "dom", step) if step else value for step, value in enumerate(values)]


def crossed(value, bit):
    return lax.ppermute(value, "band", [(source, source ^ bit) for source in range(lax.axis_size("band"))])


def gram_kernel(own_ref, *rest):
    panels, out_ref = (own_ref, *rest[:-1]), rest[-1]

    @pl.when(pl.program_id(0) == 0)
    def _():
        out_ref[...] = jnp.zeros_like(out_ref)

    for plane in range(own_ref.shape[0]):
        left = halves(own_ref[plane].T)
        both = jnp.concatenate([side_by_side(panel[plane]) for panel in panels], axis=1)
        value = dot_halves(left, both)
        for index in range(len(panels)):
            at = pl.ds(index * LANES, LANES)
            out_ref[:, at] = out_ref[:, at] + folded(value[:, 2 * index * LANES : 2 * (index + 1) * LANES])


def gram_rows(panels):
    planes, cells, _ = panels[0].shape
    tile = cells // 2
    return pl.pallas_call(
        gram_kernel,
        grid=(cells // tile,),
        in_specs=[pl.BlockSpec((planes, tile, LANES), lambda i: (0, i, 0))] * len(panels),
        out_specs=pl.BlockSpec((LANES, len(panels) * LANES), lambda i: (0, 0)),
        out_shape=jax.ShapeDtypeStruct((LANES, len(panels) * LANES), jnp.float32),
        compiler_params=params(16),
        cost_estimate=cost(8 * panels[0].size * LANES * len(panels), 4 * panels[0].size * len(panels)),
    )(*panels)


def rotate_kernel(chunks, bands, inverse_ref, *rest):
    panels, out_ref = rest[:-1], rest[-1]
    right = side_by_side(inverse_ref[...].T)
    for index, (begin, size) in enumerate(chunks):
        group = panels[index * bands : (index + 1) * bands]
        for plane in range(size):
            left = halves(jnp.concatenate([panel[plane] for panel in group], axis=1))
            out_ref[begin + plane] = folded(dot_halves(left, right))


def rotated(inverse_rows, panels, chunks):
    bands = len(panels[0])
    planes = sum(size for _, size in chunks)
    cells = panels[0][0].shape[1]
    tile = cells // 4
    specs = [pl.BlockSpec((size, tile, LANES), lambda i: (0, i, 0)) for _, size in chunks for _ in range(bands)]
    return pl.pallas_call(
        functools.partial(rotate_kernel, chunks, bands),
        grid=(cells // tile,),
        in_specs=[pl.BlockSpec(inverse_rows.shape, lambda i: (0, 0)), *specs],
        out_specs=pl.BlockSpec((planes, tile, LANES), lambda i: (0, i, 0)),
        out_shape=jax.ShapeDtypeStruct((planes, cells, LANES), jnp.float32),
        compiler_params=params(56),
    )(inverse_rows, *[panel for group in panels for panel in group])


def thirds(value):
    first = value.astype(jnp.bfloat16).astype(jnp.float32)
    rest = value - first
    second = rest.astype(jnp.bfloat16).astype(jnp.float32)
    return first, second, rest - second


def eliminate(work, result):
    sublane = lax.broadcasted_iota(jnp.int32, (GROUP, LANES), 0)

    def splat(row, column):
        return jnp.broadcast_to(row[:, column : column + 1], (GROUP, LANES))

    def load(top):
        left = [jnp.broadcast_to(work[pl.ds(top + i, 1), :LANES], (GROUP, LANES)) for i in range(GROUP)]
        right = [jnp.broadcast_to(work[pl.ds(top + i, 1), LANES:], (GROUP, LANES)) for i in range(GROUP)]
        return left, right

    def factored(top, left, right):
        entry = {(i, j): splat(left[i], top + j) for i in range(GROUP) for j in range(i, GROUP)}
        for i in range(GROUP):
            scale = lax.rsqrt(entry[i, i])
            left[i] = left[i] * scale
            right[i] = right[i] * scale
            factor = {j: entry[i, j] * scale for j in range(i + 1, GROUP)}
            for m in range(i + 1, GROUP):
                for j in range(m, GROUP):
                    entry[m, j] = entry[m, j] - factor[m] * factor[j]
                left[m] = left[m] - factor[m] * left[i]
                right[m] = right[m] - factor[m] * right[i]

    def gathered(rows):
        value = rows[0]
        for i in range(1, GROUP):
            value = jnp.where(sublane == i, rows[i], value)
        return value

    for top in range(0, LANES, 2 * GROUP):
        left, right = load(top)
        factored(top, left, right)
        middle = top + GROUP
        next_left, next_right = load(middle)
        for m in range(GROUP):
            for i in range(GROUP):
                factor = splat(left[i], middle + m)
                next_left[m] = next_left[m] - factor * left[i]
                next_right[m] = next_right[m] - factor * right[i]
        factored(middle, next_left, next_right)
        upper = jnp.concatenate([gathered(left), gathered(next_left)], axis=0)
        lower = jnp.concatenate([gathered(right), gathered(next_right)], axis=0)
        result[pl.ds(top, 2 * GROUP), :] = lower
        below = middle + GROUP
        if below < LANES:
            a, b, c = thirds(upper)
            x, y, z = thirds(lower)
            columns = jnp.concatenate([a, a, b, b, a, c], axis=0).T[below:].astype(jnp.bfloat16)
            rows = jnp.concatenate(
                [jnp.concatenate([a, b, a, b, c, a], axis=0), jnp.concatenate([x, y, x, y, z, x], axis=0)], axis=1
            ).astype(jnp.bfloat16)
            rest = pl.ds(below, LANES - below)
            work[rest, :] = work[rest, :] - jnp.dot(columns, rows, preferred_element_type=jnp.float32)


def cholesky_kernel(band_ref, *refs):
    rows_refs, (gram_ref, own_ref, inverse, matrix, work, corner, scaled) = refs[:-7], refs[-7:]
    size = gram_ref.shape[0]
    bands = len(rows_refs)
    band = band_ref[0]

    def block_of(member):
        return pl.ds(pl.multiple_of((band ^ member) * LANES, LANES), LANES)

    for member, rows_ref in enumerate(rows_refs):
        for other in range(bands):
            gram_ref[block_of(member), block_of(member ^ other)] = rows_ref[:, other * LANES : (other + 1) * LANES]
    dot = functools.partial(jnp.dot, precision=HIGHEST, preferred_element_type=jnp.float32)
    diagonal = lax.broadcasted_iota(jnp.int32, (LANES, LANES), 0) == lax.broadcasted_iota(jnp.int32, (LANES, LANES), 1)
    identity = diagonal.astype(jnp.float32)
    matrix[:, :size] = gram_ref[...]
    matrix[:, size:] = jnp.zeros((size, size), jnp.float32)
    for at in range(0, size, LANES):
        matrix[pl.ds(at, LANES), size + at : size + at + LANES] = identity

    def block(index, carry):
        start = pl.multiple_of(index * LANES, LANES)
        at = pl.ds(start, LANES)
        work[:, :LANES] = matrix[at, at]
        work[:, LANES:] = identity
        eliminate(work, corner)
        scaled[...] = dot(corner[...], matrix[at, :])
        inverse[at, :] = scaled[:, size:]

        def below(other, carry):
            rows = pl.ds(pl.multiple_of(other * LANES, LANES), LANES)
            matrix[rows, :] = matrix[rows, :] - dot(scaled[:, rows].T, scaled[...])
            return carry

        lax.fori_loop(index + 1, size // LANES, below, 0)
        return carry

    lax.fori_loop(0, size // LANES, block, 0)
    for member in range(bands):
        own_ref[:, member * LANES : (member + 1) * LANES] = inverse[block_of(0), block_of(member)]


def cholesky_inverse(band, rows):
    size = rows[0].shape[1]
    return pl.pallas_call(
        cholesky_kernel,
        in_specs=[pl.BlockSpec(memory_space=pltpu.SMEM)] + [WHOLE] * len(rows),
        out_specs=[WHOLE] * 2,
        out_shape=[
            jax.ShapeDtypeStruct((size, size), jnp.float32),
            jax.ShapeDtypeStruct((LANES, size), jnp.float32),
        ],
        scratch_shapes=[
            pltpu.VMEM((size, size), jnp.float32),
            pltpu.VMEM((size, 2 * size), jnp.float32),
            pltpu.VMEM((LANES, 2 * LANES), jnp.float32),
            pltpu.VMEM((LANES, LANES), jnp.float32),
            pltpu.VMEM((LANES, 2 * size), jnp.float32),
        ],
        compiler_params=params(14),
    )(band.astype(jnp.int32).reshape(1), *rows)


def packed_projectors(projectors, atom_plane, planes):
    share = projectors.shape[0] // lax.axis_size("band")
    first = (atom_plane - lax.axis_index("dom") * planes).astype(jnp.float32)
    first = jnp.broadcast_to(first[:, None, None], (projectors.shape[0], MAXPROJ, LANES))
    packed = jnp.concatenate([projectors, first], axis=2)
    mine = lax.dynamic_slice_in_dim(packed, lax.axis_index("band") * share, share, 0)
    return mine.reshape(share * MAXPROJ, -1)


def near_shares(mine):
    return jnp.stack([mine if step == BEFORE else shifted(mine, "dom", BEFORE - step) for step in range(NEAR)])


def first_planes(raw, planes):
    moved = (planes * (jnp.arange(NEAR, dtype=jnp.float32) - BEFORE))[:, None]
    first = jnp.stack([member[:, :, -1] + moved for member in raw]).reshape(1, LANES)
    return jnp.broadcast_to(first, (GROUP, LANES))


def shards(orbitals, potential, projectors, coupling, atom_plane, projector_count):
    planes, side_y, side_z, local_orbs = orbitals.shape
    blocks, bands = lax.axis_size("dom"), lax.axis_size("band")
    band = lax.axis_index("band")
    cells = side_y * side_z
    rows = cells // blocks
    width = local_orbs // blocks
    norb = local_orbs * bands
    chunks = tuple((plane, 1) for plane in range(planes))
    half = planes // 2
    tie = lax.optimization_barrier
    me = lax.axis_index("dom").astype(jnp.int32).reshape(1)

    order = jnp.arange(bands, dtype=jnp.int32) ^ band

    mine = packed_projectors(projectors, atom_plane, planes)
    mine, levels = lax.optimization_barrier((mine, potential.reshape(planes, cells // LANES, LANES)))
    near = near_shares(mine)
    levels = jnp.pad(levels, ((0, 0), (0, -levels.shape[1] % GROUP), (0, 0)))
    packed = list(swap_in(me, levels, orbitals.reshape(planes, blocks, rows, local_orbs)))
    packed, near = tie((packed, near))
    across = crossed(near, 2)
    arrived = exchanged(packed)
    raw = [near, crossed(near, 1), across, crossed(across, 1)]
    raw, arrived[1:-1] = tie((raw, arrived[1:-1]))
    first = first_planes(raw, planes)

    own_levels = jnp.broadcast_to(potential.reshape(planes, cells, 1), (planes, cells, LANES))
    high, low, parts = build_basis(raw, first, own_levels, orbitals.reshape(planes, cells, LANES), side_y, side_z)
    atoms = projectors.shape[0]
    slots = jnp.arange(MAXPROJ, dtype=jnp.int32)
    live = (slots[None, :] < projector_count[:, None]).astype(jnp.float32)
    coupled = 0.5 * (coupling + jnp.transpose(coupling, (0, 2, 1))) * live[:, :, None] * live[:, None, :]
    coupled = jnp.take(coupled.reshape(bands, -1, MAXPROJ, MAXPROJ), order, axis=0)
    vectors = atoms * MAXPROJ
    row = jnp.arange(vectors, dtype=jnp.int32) // MAXPROJ
    matrix = jnp.tile(coupled.reshape(vectors, MAXPROJ), (1, atoms))
    matrix = jnp.where(row[:, None] == row[None, :], matrix, 0.0)
    matrix = jnp.pad(matrix, ((0, 0), (0, LANES - vectors)))
    payload = jnp.concatenate([parts.reshape(3 * LANES, LANES), matrix], axis=0)
    everyone = lax.all_gather(payload, "dom")
    weights = near_weights(
        me,
        everyone[:, : 3 * LANES].reshape(blocks, 3, LANES, LANES), everyone[:, 3 * LANES :, :vectors],
    )

    early, late = filter_orbitals(me, arrived, side_y, side_z, half)

    came = exchanged(early)
    late, came = tie((late, came))
    coming = lax.all_to_all(late, "dom", 0, 0, tiled=True)
    owns = list(swap_out(me, came, high, low, weights, 0))
    acrosses = [crossed(own, 2) for own in owns]
    besides = [crossed(own, 1) for own in owns]
    coming, acrosses[0] = tie((coming, acrosses[0]))
    late = list(swap_out(me, [coming], high, low, weights, half))
    late, acrosses[1:] = tie((late, acrosses[1:]))
    acrosses += [crossed(own, 2) for own in late]
    besides += [crossed(own, 1) for own in late]
    owns += late
    panels, part = [], None
    for index, across in enumerate(acrosses):
        if index >= half:
            across, part = tie((across, part))
        panels.append([owns[index], besides[index], across, crossed(across, 1)])
        rows_of = gram_rows(panels[-1])
        part = rows_of if part is None else part + rows_of

    pieces = lax.all_to_all(part.reshape(blocks, width, norb), "dom", 0, 0, tiled=True)
    piece = jnp.sum(pieces, axis=0) * (1.0 / (planes * cells * blocks))
    own_gram = lax.all_to_all(jnp.broadcast_to(piece, (blocks, width, norb)), "dom", 0, 0, tiled=True)
    own_gram = own_gram.reshape(local_orbs, norb)
    across = crossed(own_gram, 2)
    gram, own_rows = cholesky_inverse(band, [own_gram, crossed(own_gram, 1), across, crossed(across, 1)])
    result = rotated(own_rows, panels, chunks)
    return (result.reshape(planes, side_y, side_z, local_orbs), gram)


def solution(mesh):
    placed = (
        P("dom", None, None, "band"),
        P("dom", None, None),
        P("dom", None, None),
        P("dom", None, None),
        P("dom"),
        P("dom"),
    )
    return jax.shard_map(
        shards,
        mesh=mesh,
        in_specs=placed,
        out_specs=(P("dom", None, None, "band"), P()),
        check_vma=False,
    )
```

```python
import functools

import jax
import jax.numpy as jnp
from jax import lax
from jax.experimental import pallas as pl
from jax.experimental.pallas import tpu as pltpu
from jax.sharding import PartitionSpec as P

SPAN = 3
MAXPROJ = 4
HALO = 4
PAD = 8
LANES = 128
GROUP = 8
BEFORE, AFTER = 2, 1
NEAR = BEFORE + 1 + AFTER

center_weight = -205.0 / 72.0
side_weights = (8.0 / 5.0, -1.0 / 5.0, 8.0 / 315.0, -1.0 / 560.0)
HIGHEST = lax.Precision.HIGHEST
WHOLE = pl.BlockSpec(memory_space=pltpu.VMEM)


def params(mebibytes):
    return pltpu.CompilerParams(vmem_limit_bytes=mebibytes * 1024 * 1024)


def cost(flops, bytes_accessed):
    return pl.CostEstimate(flops=int(flops), bytes_accessed=int(bytes_accessed), transcendentals=0)


def halves(value):
    high = value.astype(jnp.bfloat16)
    return high, (value - high.astype(jnp.float32)).astype(jnp.bfloat16)


def side_by_side(value):
    return jnp.concatenate(halves(value), axis=1)


def dot_halves(left, right):
    dot = functools.partial(jnp.dot, preferred_element_type=jnp.float32)
    return dot(left[0], right) + dot(left[1], right)


def folded(value):
    return value[:, :LANES] + value[:, LANES:]


def swapped(blocks, lane, before=None, after=None):
    count = len(blocks)
    width = LANES // count

    def turned(value, at, extra):
        if extra is None:
            return pltpu.roll(value, at % count * width, 1) if at else value
        return pltpu.roll(value, lax.rem((at % count + extra) * width, LANES), 1)

    blocks = [turned(value, at, None if before is None else count - before) for at, value in enumerate(blocks)]
    bit = 1
    while bit < count:
        chosen = (lane // (bit * width)) % 2 == 1
        blocks = [jnp.where(chosen, blocks[(at + bit) % count], blocks[at]) for at in range(count)]
        bit *= 2
    return [turned(blocks[-at % count], -at, after) for at in range(count)]


def swap_into(read, write, count, rows, before=None, after=None):
    tile = 8 * max(1, 32 // count)
    lane = lax.broadcasted_iota(jnp.int32, (tile, LANES), 1)

    def step(index, carry):
        start = pl.multiple_of(index * tile, 8)
        blocks = [read(block, start, tile) for block in range(count)]
        for block, value in enumerate(swapped(blocks, lane, before, after)):
            write(block, start, tile, value)
        return carry

    lax.fori_loop(0, rows // tile, step, 0, unroll=True)


def swap_in_kernel(count, rows, levels_ref, in_ref, out_ref):
    def read(block, start, size):
        return in_ref[block, pl.ds(start, size), :]

    def write(block, start, size, value):
        out_ref[block, pl.ds(start, size), :] = value

    swap_into(read, write, count, rows)
    for block in range(count):
        out_ref[block, pl.ds(rows, levels_ref.shape[0]), :] = levels_ref[...]


def swap_in(levels, value):
    planes, count, rows, _ = value.shape
    extra = levels.shape[1]
    return pl.pallas_call(
        functools.partial(swap_in_kernel, count, rows),
        grid=(planes,),
        in_specs=[
            pl.BlockSpec((None, extra, LANES), lambda p: (p, 0, 0)),
            pl.BlockSpec((None, count, rows, LANES), lambda p: (p, 0, 0, 0)),
        ],
        out_specs=pl.BlockSpec((count, None, rows + extra, LANES), lambda p: (0, p, 0, 0)),
        out_shape=jax.ShapeDtypeStruct((count, planes, rows + extra, LANES), jnp.float32),
        compiler_params=params(12),
        cost_estimate=cost(0, 8 * value.size),
    )(levels, value)


def swap_out_kernel(planes, count, me_ref, high_ref, low_ref, weights_ref, *refs):
    arrived_refs, out_refs = refs[:-planes], refs[-planes:]
    rows = arrived_refs[0].shape[-2]
    by_steps = len(arrived_refs) > 1
    weights = side_by_side(weights_ref[...] * (1.0 / 18.0))
    for plane in range(planes):

        def read(block, start, size):
            if by_steps:
                return arrived_refs[-block % count][plane, pl.ds(start, size), :]
            return arrived_refs[0][block, plane, pl.ds(start, size), :]

        def write(block, start, size, value):
            at = pl.ds(pl.multiple_of(block * rows + start, 8), size)
            out_refs[plane][at, :] = value

        swap_into(read, write, count, rows, after=me_ref[0] if by_steps else None)
        tile = rows * count // 6

        def add(index, carry):
            at = pl.ds(pl.multiple_of(index * tile, 8), tile)
            term = folded(dot_halves((high_ref[plane, at, :], low_ref[plane, at, :]), weights))
            out_refs[plane][at, :] = out_refs[plane][at, :] + term
            return carry

        lax.fori_loop(0, 6, add, 0)


def swap_out(me, arrived, high, low, weights, first_plane):
    count = len(arrived) if len(arrived) > 1 else arrived[0].shape[0]
    planes, rows = arrived[0].shape[-3:-1]
    cells = count * rows
    basis = pl.BlockSpec((planes, cells, 2 * LANES), lambda i: (first_plane // planes, 0, 0))
    return pl.pallas_call(
        functools.partial(swap_out_kernel, planes, count),
        grid=(1,),
        in_specs=[
            pl.BlockSpec(memory_space=pltpu.SMEM),
            basis,
            basis,
            pl.BlockSpec(weights.shape, lambda i: (0, 0)),
        ]
        + [pl.BlockSpec(arrived[0].shape, lambda i: (0,) * arrived[0].ndim)] * len(arrived),
        out_specs=[pl.BlockSpec((None, cells, LANES), lambda i: (0, 0, 0))] * planes,
        out_shape=[jax.ShapeDtypeStruct((1, cells, LANES), jnp.float32)] * planes,
        compiler_params=params(24),
        cost_estimate=cost(0, 24 * cells * planes * LANES),
    )(me, high, low, weights, *arrived)


def fill_row(target, plane, y, row, side_z):
    target[plane, y, pl.ds(PAD, side_z), :] = row
    target[plane, y, pl.ds(PAD - HALO, HALO), :] = row[side_z - HALO :]
    target[plane, y, pl.ds(PAD + side_z, HALO), :] = row[:HALO]


def local_part(source, potential_ref, planes, first, side_y, side_z, line_of, finish):
    tile = 16

    def row(y, carry):
        for start in range(0, side_z, tile):

            def load(plane, y_at, shift):
                return source[plane, y_at, pl.ds(PAD + start + shift, tile), :]

            line = line_of(lambda plane: load(plane, y, 0))
            at = pl.ds(pl.multiple_of(y * side_z + start, 8), tile)
            for plane in range(planes):
                here = first + plane
                total = (potential_ref[plane, at, :] - 1.5 * center_weight - 7.0) * line[HALO + plane]
                for offset in range(1, HALO + 1):
                    around = line[HALO + plane + offset] + line[HALO + plane - offset]
                    around = around + (load(here, y, offset) + load(here, y, -offset))
                    up = lax.rem(y + offset, side_y)
                    down = lax.rem(y + side_y - offset, side_y)
                    around = around + (load(here, up, 0) + load(here, down, 0))
                    total = total - (0.5 * side_weights[offset - 1]) * around
                finish(plane, y, start, at, total)
        return carry

    lax.fori_loop(0, side_y, row, 0)


def filter_kernel(planes, side_y, side_z, width, half, me_ref, arrived_ref, *rest):
    near_refs, late_ref, (field, padded, first, flat, potential) = rest[:-6], rest[-6], rest[-5:]
    count = arrived_ref.shape[0]
    cells = side_y * side_z
    rows = cells // count
    tile = 16

    line = lax.broadcasted_iota(jnp.int32, (2 * count, LANES), 0) % count
    lane = lax.broadcasted_iota(jnp.int32, (2 * count, LANES), 1) // width
    spread = (line == lane).astype(jnp.bfloat16)
    for plane in range(planes):
        lines = [arrived_ref[:, plane, rows + at, :] for at in range(cells // LANES)]
        high, low = halves(jnp.concatenate(lines, axis=1))
        both = jnp.concatenate([high.astype(jnp.float32), low.astype(jnp.float32)], axis=0)
        potential[plane] = jnp.dot(both.T.astype(jnp.bfloat16), spread, preferred_element_type=jnp.float32)

    for plane in range(planes):

        def read_in(block, start, size):
            return arrived_ref[block, plane, pl.ds(start, size), :]

        def write_in(block, start, size, value):
            field[plane, pl.ds(pl.multiple_of(block * rows + start, 8), size), :] = value

        swap_into(read_in, write_in, count, rows)

    def fill(y, carry):
        for plane in range(planes):
            fill_row(padded, plane, y, field[plane, pl.ds(pl.multiple_of(y * side_z, 8), side_z), :], side_z)
        return carry

    lax.fori_loop(0, side_y, fill, 0)

    def line_of(load):
        inside = [load(plane) for plane in range(planes)]
        before = [pltpu.roll(value, width, 1) for value in inside]
        after = [pltpu.roll(value, LANES - width, 1) for value in inside]
        return before[planes - HALO :] + inside + after[:HALO]

    def finish_first(plane, y, start, at, total):
        first[plane, y, pl.ds(PAD + start, tile), :] = total
        if start == 0:
            first[plane, y, pl.ds(PAD + side_z, HALO), :] = total[:HALO]
        if start == side_z - tile:
            first[plane, y, pl.ds(PAD - HALO, HALO), :] = total[tile - HALO :]

    def finish_second(plane, y, start, at, total):
        flat[plane, at, :] = total * (1.0 / 18.0) - field[plane, at, :]

    local_part(padded, potential, planes, 0, side_y, side_z, line_of, finish_first)
    local_part(first, potential, planes, 0, side_y, side_z, line_of, finish_second)

    for plane in range(planes):

        def read_out(block, start, size):
            return flat[plane, pl.ds(pl.multiple_of(block * rows + start, 8), size), :]

        def write_out(block, start, size, value):
            if plane < half:
                near_refs[block][plane, pl.ds(start, size), :] = value
            else:
                late_ref[block, plane - half, pl.ds(start, size), :] = value

        swap_into(read_out, write_out, count, rows, before=me_ref[0] if plane < half else None)


def filter_orbitals(me, arrived, side_y, side_z, width, half):
    count, planes = arrived.shape[:2]
    rows = side_y * side_z // count
    flat = pltpu.VMEM((planes, side_y * side_z, LANES), jnp.float32)
    padded = pltpu.VMEM((planes, side_y, side_z + 2 * PAD, LANES), jnp.float32)
    shapes = [jax.ShapeDtypeStruct((half, rows, LANES), jnp.float32)] * count
    shapes += [jax.ShapeDtypeStruct((count, planes - half, rows, LANES), jnp.float32)]
    outs = pl.pallas_call(
        functools.partial(filter_kernel, planes, side_y, side_z, width, half),
        in_specs=[pl.BlockSpec(memory_space=pltpu.SMEM), WHOLE],
        out_specs=[WHOLE] * len(shapes),
        out_shape=shapes,
        scratch_shapes=[flat, padded, padded, flat, flat],
        compiler_params=params(56),
        cost_estimate=cost(100 * arrived.size, 12 * arrived.size),
    )(me, arrived)
    return list(outs[:count]), outs[count]


def basis_kernel(planes, side_y, side_z, bands, *refs):
    raw_refs = refs[:bands]
    offset_ref, potential_ref, orbitals_ref, high_ref, low_ref, parts_ref, turned, placed = refs[bands:]
    cells = side_y * side_z
    for part in range(SPAN):
        at = pl.ds(part * cells, cells)
        stack = [raw_ref[block, :, at] for raw_ref in raw_refs for block in range(NEAR)]
        turned[part] = jnp.concatenate(stack, axis=0).T
    offset = offset_ref[0:1, :]

    def place(y, carry):
        at = pl.ds(pl.multiple_of(y * side_z, 8), side_z)
        values = [turned[part, at, :] for part in range(SPAN)]
        for plane in range(planes + 2 * HALO):
            row = jnp.zeros((side_z, LANES), jnp.float32)
            for part in range(SPAN):
                row = jnp.where(offset == float(plane - HALO - part), values[part], row)
            fill_row(placed, plane, y, row, side_z)
        return carry

    lax.fori_loop(0, side_y, place, 0)

    def line_of(load):
        return [load(plane) for plane in range(planes + 2 * HALO)]

    def finish(plane, y, start, at, total):
        own = placed[HALO + plane, y, pl.ds(PAD + start, 16), :]
        high, low = halves(jnp.concatenate([total, own], axis=1))
        high_ref[plane, at, :] = high
        low_ref[plane, at, :] = low

    local_part(placed, potential_ref, planes, HALO, side_y, side_z, line_of, finish)

    dot = functools.partial(jnp.dot, preferred_element_type=jnp.float32)
    with_orbitals = with_basis = 0.0
    for plane in range(planes):
        high, low = high_ref[plane], low_ref[plane]
        left = halves(orbitals_ref[plane].T)
        with_orbitals = with_orbitals + (dot(left[0], high) + (dot(left[0], low) + dot(left[1], high)))
        own_high, own_low = high[:, LANES:], low[:, LANES:]
        turned_high = own_high.astype(jnp.float32).T.astype(jnp.bfloat16)
        turned_low = own_low.astype(jnp.float32).T.astype(jnp.bfloat16)
        both = jnp.concatenate([own_high, own_low], axis=1)
        with_basis = with_basis + (dot(turned_high, both) + dot(turned_low, both))
    parts_ref[0] = with_orbitals[:, LANES:].T
    parts_ref[1] = with_orbitals[:, :LANES].T
    parts_ref[2] = folded(with_basis)


def build_basis(raw, offset, potential, orbitals, side_y, side_z):
    planes, cells, _ = orbitals.shape
    pair = jax.ShapeDtypeStruct((planes, cells, 2 * LANES), jnp.bfloat16)
    return pl.pallas_call(
        functools.partial(basis_kernel, planes, side_y, side_z, len(raw)),
        in_specs=[WHOLE] * (len(raw) + 3),
        out_specs=[WHOLE] * 3,
        out_shape=[pair, pair, jax.ShapeDtypeStruct((3, LANES, LANES), jnp.float32)],
        scratch_shapes=[
            pltpu.VMEM((SPAN, cells, LANES), jnp.float32),
            pltpu.VMEM((planes + 2 * HALO, side_y, side_z + 2 * PAD, LANES), jnp.float32),
        ],
        compiler_params=params(56),
        cost_estimate=cost(200 * orbitals.size, 24 * orbitals.size),
    )(*raw, offset, potential, orbitals)


def weights_kernel(bands, me_ref, parts_ref, coupling_ref, out_ref):
    count = parts_ref.shape[0]
    size = LANES // NEAR
    lines = size // bands
    me = me_ref[0]
    dot = functools.partial(jnp.dot, precision=HIGHEST, preferred_element_type=jnp.float32)

    def device(step):
        return lax.rem(me + step % count, count)

    def total(pick, block):
        shares = [pick(block - (near - BEFORE), near) for near in range(NEAR)]
        return (shares[0] + shares[1]) + (shares[2] + shares[3])

    def of_block(value, near):
        starts = [(band * NEAR + near) * lines for band in range(bands)]
        return jnp.concatenate([value[start : start + lines] for start in starts], axis=0)

    def joined(values):
        return jnp.concatenate(
            [values[near][band * lines : (band + 1) * lines] for band in range(bands) for near in range(NEAR)], axis=0
        )

    def couple(block, value):
        return dot(coupling_ref[device(block)], value)

    def kept(function):
        known = {}

        def look(step):
            if step % count not in known:
                known[step % count] = function(step)
            return known[step % count]

        return look

    weight = kept(
        lambda block: couple(block, total(lambda step, near: of_block(parts_ref[device(step), 0], near), block))
    )
    weights = kept(lambda step: joined([weight(step + near - BEFORE) for near in range(NEAR)]))
    second = kept(lambda step: parts_ref[device(step), 1] + dot(parts_ref[device(step), 2], weights(step)))
    out_ref[pl.ds(0, LANES), :] = weights(0)
    out_ref[pl.ds(LANES, LANES), :] = joined(
        [
            couple(near - BEFORE, total(lambda step, at: of_block(second(step), at), near - BEFORE))
            for near in range(NEAR)
        ]
    )


def near_weights(me, parts, coupling):
    return pl.pallas_call(
        functools.partial(weights_kernel, lax.axis_size("band")),
        in_specs=[pl.BlockSpec(memory_space=pltpu.SMEM), WHOLE, WHOLE],
        out_specs=WHOLE,
        out_shape=jax.ShapeDtypeStruct((2 * LANES, LANES), jnp.float32),
        compiler_params=params(24),
        cost_estimate=cost(0, 8 * parts.size),
    )(me, parts, coupling)


def shifted(value, axis, step):
    count = lax.axis_size(axis)
    return lax.ppermute(value, axis, [(source, (source + step) % count) for source in range(count)])


def exchanged(values):
    return [shifted(value, "dom", step) if step else value for step, value in enumerate(values)]


def crossed(value, bit):
    return lax.ppermute(value, "band", [(source, source ^ bit) for source in range(lax.axis_size("band"))])


def gram_kernel(own_ref, *rest):
    panels, out_ref = (own_ref, *rest[:-1]), rest[-1]

    @pl.when(pl.program_id(0) == 0)
    def _():
        out_ref[...] = jnp.zeros_like(out_ref)

    for plane in range(own_ref.shape[0]):
        left = halves(own_ref[plane].T)
        both = jnp.concatenate([side_by_side(panel[plane]) for panel in panels], axis=1)
        value = dot_halves(left, both)
        for index in range(len(panels)):
            at = pl.ds(index * LANES, LANES)
            out_ref[:, at] = out_ref[:, at] + folded(value[:, 2 * index * LANES : 2 * (index + 1) * LANES])


def gram_rows(panels):
    planes, cells, _ = panels[0].shape
    tile = cells // 2
    return pl.pallas_call(
        gram_kernel,
        grid=(cells // tile,),
        in_specs=[pl.BlockSpec((planes, tile, LANES), lambda i: (0, i, 0))] * len(panels),
        out_specs=pl.BlockSpec((LANES, len(panels) * LANES), lambda i: (0, 0)),
        out_shape=jax.ShapeDtypeStruct((LANES, len(panels) * LANES), jnp.float32),
        compiler_params=params(16),
        cost_estimate=cost(8 * panels[0].size * LANES * len(panels), 4 * panels[0].size * len(panels)),
    )(*panels)


def rotate_kernel(chunks, bands, inverse_ref, *rest):
    panels, out_ref = rest[:-1], rest[-1]
    right = side_by_side(inverse_ref[...].T)
    for index, (begin, size) in enumerate(chunks):
        group = panels[index * bands : (index + 1) * bands]
        for plane in range(size):
            left = halves(jnp.concatenate([panel[plane] for panel in group], axis=1))
            out_ref[begin + plane] = folded(dot_halves(left, right))


def rotated(inverse_rows, panels, chunks):
    bands = len(panels[0])
    planes = sum(size for _, size in chunks)
    cells = panels[0][0].shape[1]
    tile = cells // 4
    specs = [pl.BlockSpec((size, tile, LANES), lambda i: (0, i, 0)) for _, size in chunks for _ in range(bands)]
    return pl.pallas_call(
        functools.partial(rotate_kernel, chunks, bands),
        grid=(cells // tile,),
        in_specs=[pl.BlockSpec(inverse_rows.shape, lambda i: (0, 0)), *specs],
        out_specs=pl.BlockSpec((planes, tile, LANES), lambda i: (0, i, 0)),
        out_shape=jax.ShapeDtypeStruct((planes, cells, LANES), jnp.float32),
        compiler_params=params(56),
    )(inverse_rows, *[panel for group in panels for panel in group])


def thirds(value):
    first = value.astype(jnp.bfloat16).astype(jnp.float32)
    rest = value - first
    second = rest.astype(jnp.bfloat16).astype(jnp.float32)
    return first, second, rest - second


def eliminate(work, result):
    sublane = lax.broadcasted_iota(jnp.int32, (GROUP, LANES), 0)

    def splat(row, column):
        return jnp.broadcast_to(row[:, column : column + 1], (GROUP, LANES))

    def load(top):
        left = [jnp.broadcast_to(work[pl.ds(top + i, 1), :LANES], (GROUP, LANES)) for i in range(GROUP)]
        right = [jnp.broadcast_to(work[pl.ds(top + i, 1), LANES:], (GROUP, LANES)) for i in range(GROUP)]
        return left, right

    def factored(top, left, right):
        entry = {(i, j): splat(left[i], top + j) for i in range(GROUP) for j in range(i, GROUP)}
        for i in range(GROUP):
            scale = lax.rsqrt(entry[i, i])
            left[i] = left[i] * scale
            right[i] = right[i] * scale
            factor = {j: entry[i, j] * scale for j in range(i + 1, GROUP)}
            for m in range(i + 1, GROUP):
                for j in range(m, GROUP):
                    entry[m, j] = entry[m, j] - factor[m] * factor[j]
                left[m] = left[m] - factor[m] * left[i]
                right[m] = right[m] - factor[m] * right[i]

    def gathered(rows):
        value = rows[0]
        for i in range(1, GROUP):
            value = jnp.where(sublane == i, rows[i], value)
        return value

    for top in range(0, LANES, 2 * GROUP):
        left, right = load(top)
        factored(top, left, right)
        middle = top + GROUP
        next_left, next_right = load(middle)
        for m in range(GROUP):
            for i in range(GROUP):
                factor = splat(left[i], middle + m)
                next_left[m] = next_left[m] - factor * left[i]
                next_right[m] = next_right[m] - factor * right[i]
        factored(middle, next_left, next_right)
        upper = jnp.concatenate([gathered(left), gathered(next_left)], axis=0)
        lower = jnp.concatenate([gathered(right), gathered(next_right)], axis=0)
        result[pl.ds(top, 2 * GROUP), :] = lower
        below = middle + GROUP
        if below < LANES:
            a, b, c = thirds(upper)
            x, y, z = thirds(lower)
            columns = jnp.concatenate([a, a, b, b, a, c], axis=0).T[below:].astype(jnp.bfloat16)
            rows = jnp.concatenate(
                [jnp.concatenate([a, b, a, b, c, a], axis=0), jnp.concatenate([x, y, x, y, z, x], axis=0)], axis=1
            ).astype(jnp.bfloat16)
            rest = pl.ds(below, LANES - below)
            work[rest, :] = work[rest, :] - jnp.dot(columns, rows, preferred_element_type=jnp.float32)


def cholesky_kernel(band_ref, *refs):
    rows_refs, (gram_ref, own_ref, inverse, matrix, work, corner, scaled) = refs[:-7], refs[-7:]
    size = gram_ref.shape[0]
    bands = len(rows_refs)
    band = band_ref[0]

    def block_of(member):
        return pl.ds(pl.multiple_of((band ^ member) * LANES, LANES), LANES)

    for member, rows_ref in enumerate(rows_refs):
        for other in range(bands):
            gram_ref[block_of(member), block_of(member ^ other)] = rows_ref[:, other * LANES : (other + 1) * LANES]
    dot = functools.partial(jnp.dot, precision=HIGHEST, preferred_element_type=jnp.float32)
    diagonal = lax.broadcasted_iota(jnp.int32, (LANES, LANES), 0) == lax.broadcasted_iota(jnp.int32, (LANES, LANES), 1)
    identity = diagonal.astype(jnp.float32)
    matrix[:, :size] = gram_ref[...]
    matrix[:, size:] = jnp.zeros((size, size), jnp.float32)
    for at in range(0, size, LANES):
        matrix[pl.ds(at, LANES), size + at : size + at + LANES] = identity

    def block(index, carry):
        start = pl.multiple_of(index * LANES, LANES)
        at = pl.ds(start, LANES)
        work[:, :LANES] = matrix[at, at]
        work[:, LANES:] = identity
        eliminate(work, corner)
        scaled[...] = dot(corner[...], matrix[at, :])
        inverse[at, :] = scaled[:, size:]

        def below(other, carry):
            rows = pl.ds(pl.multiple_of(other * LANES, LANES), LANES)
            matrix[rows, :] = matrix[rows, :] - dot(scaled[:, rows].T, scaled[...])
            return carry

        lax.fori_loop(index + 1, size // LANES, below, 0)
        return carry

    lax.fori_loop(0, size // LANES, block, 0)
    for member in range(bands):
        own_ref[:, member * LANES : (member + 1) * LANES] = inverse[block_of(0), block_of(member)]


def cholesky_inverse(band, rows):
    size = rows[0].shape[1]
    return pl.pallas_call(
        cholesky_kernel,
        in_specs=[pl.BlockSpec(memory_space=pltpu.SMEM)] + [WHOLE] * len(rows),
        out_specs=[WHOLE] * 2,
        out_shape=[
            jax.ShapeDtypeStruct((size, size), jnp.float32),
            jax.ShapeDtypeStruct((LANES, size), jnp.float32),
        ],
        scratch_shapes=[
            pltpu.VMEM((size, size), jnp.float32),
            pltpu.VMEM((size, 2 * size), jnp.float32),
            pltpu.VMEM((LANES, 2 * LANES), jnp.float32),
            pltpu.VMEM((LANES, LANES), jnp.float32),
            pltpu.VMEM((LANES, 2 * size), jnp.float32),
        ],
        compiler_params=params(14),
    )(band.astype(jnp.int32).reshape(1), *rows)


def packed_projectors(projectors, atom_plane, planes):
    share = projectors.shape[0] // lax.axis_size("band")
    first = (atom_plane - lax.axis_index("dom") * planes).astype(jnp.float32)
    first = jnp.broadcast_to(first[:, None, None], (projectors.shape[0], MAXPROJ, LANES))
    packed = jnp.concatenate([projectors, first], axis=2)
    mine = lax.dynamic_slice_in_dim(packed, lax.axis_index("band") * share, share, 0)
    return mine.reshape(share * MAXPROJ, -1)


def near_shares(mine):
    return jnp.stack([mine if step == BEFORE else shifted(mine, "dom", BEFORE - step) for step in range(NEAR)])


def near_projectors(near, planes):
    across = crossed(near, 2)
    raw = [near, crossed(near, 1), across, crossed(across, 1)]
    moved = (planes * (jnp.arange(NEAR, dtype=jnp.float32) - BEFORE))[:, None]
    first = jnp.stack([member[:, :, -1] + moved for member in raw]).reshape(1, LANES)
    return raw, jnp.broadcast_to(first, (GROUP, LANES))


def shards(orbitals, potential, projectors, coupling, atom_plane, projector_count):
    planes, side_y, side_z, local_orbs = orbitals.shape
    blocks, bands = lax.axis_size("dom"), lax.axis_size("band")
    band = lax.axis_index("band")
    cells = side_y * side_z
    rows = cells // blocks
    width = local_orbs // blocks
    norb = local_orbs * bands
    chunks = tuple((plane, 1) for plane in range(planes))
    half = planes // 2
    tie = lax.optimization_barrier
    me = lax.axis_index("dom").astype(jnp.int32).reshape(1)

    order = jnp.arange(bands, dtype=jnp.int32) ^ band

    mine = packed_projectors(projectors, atom_plane, planes)
    mine, levels = lax.optimization_barrier((mine, potential.reshape(planes, cells // LANES, LANES)))
    near = near_shares(mine)
    levels = jnp.pad(levels, ((0, 0), (0, -levels.shape[1] % GROUP), (0, 0)))
    packed = swap_in(levels, orbitals.reshape(planes, blocks, rows, local_orbs))
    packed, near = lax.optimization_barrier((packed, near))
    raw, first = near_projectors(near, planes)
    arrived = lax.all_to_all(packed, "dom", 0, 0, tiled=True)

    own_levels = jnp.broadcast_to(potential.reshape(planes, cells, 1), (planes, cells, LANES))
    high, low, parts = build_basis(raw, first, own_levels, orbitals.reshape(planes, cells, LANES), side_y, side_z)
    atoms = projectors.shape[0]
    slots = jnp.arange(MAXPROJ, dtype=jnp.int32)
    live = (slots[None, :] < projector_count[:, None]).astype(jnp.float32)
    coupled = 0.5 * (coupling + jnp.transpose(coupling, (0, 2, 1))) * live[:, :, None] * live[:, None, :]
    coupled = jnp.take(coupled.reshape(bands, -1, MAXPROJ, MAXPROJ), order, axis=0)
    vectors = atoms * MAXPROJ
    row = jnp.arange(vectors, dtype=jnp.int32) // MAXPROJ
    matrix = jnp.tile(coupled.reshape(vectors, MAXPROJ), (1, atoms))
    matrix = jnp.where(row[:, None] == row[None, :], matrix, 0.0)
    matrix = jnp.pad(matrix, ((0, 0), (0, LANES - vectors)))
    payload = jnp.concatenate([parts.reshape(3 * LANES, LANES), matrix], axis=0)
    everyone = lax.all_gather(payload, "dom")
    weights = near_weights(
        me,
        everyone[:, : 3 * LANES].reshape(blocks, 3, LANES, LANES), everyone[:, 3 * LANES :, :vectors],
    )

    early, late = filter_orbitals(me, arrived, side_y, side_z, width, half)

    came = exchanged(early)
    late, came = tie((late, came))
    coming = lax.all_to_all(late, "dom", 0, 0, tiled=True)
    owns = list(swap_out(me, came, high, low, weights, 0))
    acrosses = [crossed(own, 2) for own in owns]
    besides = [crossed(own, 1) for own in owns]
    coming, acrosses[0] = tie((coming, acrosses[0]))
    late = list(swap_out(me, [coming], high, low, weights, half))
    late, acrosses[1:] = tie((late, acrosses[1:]))
    acrosses += [crossed(own, 2) for own in late]
    besides += [crossed(own, 1) for own in late]
    owns += late
    panels, part = [], None
    for index, across in enumerate(acrosses):
        if index >= half:
            across, part = tie((across, part))
        panels.append([owns[index], besides[index], across, crossed(across, 1)])
        rows_of = gram_rows(panels[-1])
        part = rows_of if part is None else part + rows_of

    pieces = lax.all_to_all(part.reshape(blocks, width, norb), "dom", 0, 0, tiled=True)
    piece = jnp.sum(pieces, axis=0) * (1.0 / (planes * cells * blocks))
    own_gram = lax.all_to_all(jnp.broadcast_to(piece, (blocks, width, norb)), "dom", 0, 0, tiled=True)
    own_gram = own_gram.reshape(local_orbs, norb)
    across = crossed(own_gram, 2)
    gram, own_rows = cholesky_inverse(band, [own_gram, crossed(own_gram, 1), across, crossed(across, 1)])
    result = rotated(own_rows, panels, chunks)
    return (result.reshape(planes, side_y, side_z, local_orbs), gram)


def solution(mesh):
    placed = (
        P("dom", None, None, "band"),
        P("dom", None, None),
        P("dom", None, None),
        P("dom", None, None),
        P("dom"),
        P("dom"),
    )
    return jax.shard_map(
        shards,
        mesh=mesh,
        in_specs=placed,
        out_specs=(P("dom", None, None, "band"), P()),
        check_vma=False,
    )
```

```python
import functools

import jax
import jax.numpy as jnp
from jax import lax
from jax.experimental import pallas as pl
from jax.experimental.pallas import tpu as pltpu
from jax.sharding import PartitionSpec as P

SPAN = 3
MAXPROJ = 4
HALO = 4
PAD = 8
LANES = 128
GROUP = 8
BEFORE, AFTER = 2, 1
NEAR = BEFORE + 1 + AFTER

center_weight = -205.0 / 72.0
side_weights = (8.0 / 5.0, -1.0 / 5.0, 8.0 / 315.0, -1.0 / 560.0)
HIGHEST = lax.Precision.HIGHEST
WHOLE = pl.BlockSpec(memory_space=pltpu.VMEM)


def params(mebibytes):
    return pltpu.CompilerParams(vmem_limit_bytes=mebibytes * 1024 * 1024)


def cost(flops, bytes_accessed):
    return pl.CostEstimate(flops=int(flops), bytes_accessed=int(bytes_accessed), transcendentals=0)


def halves(value):
    high = value.astype(jnp.bfloat16)
    return high, (value - high.astype(jnp.float32)).astype(jnp.bfloat16)


def side_by_side(value):
    return jnp.concatenate(halves(value), axis=1)


def dot_halves(left, right):
    dot = functools.partial(jnp.dot, preferred_element_type=jnp.float32)
    return dot(left[0], right) + dot(left[1], right)


def folded(value):
    return value[:, :LANES] + value[:, LANES:]


def swapped(blocks, lane, before=None, after=None):
    count = len(blocks)
    width = LANES // count

    def turned(value, at, extra):
        if extra is None:
            return pltpu.roll(value, at % count * width, 1) if at else value
        return pltpu.roll(value, lax.rem((at % count + extra) * width, LANES), 1)

    blocks = [turned(value, at, None if before is None else count - before) for at, value in enumerate(blocks)]
    bit = 1
    while bit < count:
        chosen = (lane // (bit * width)) % 2 == 1
        blocks = [jnp.where(chosen, blocks[(at + bit) % count], blocks[at]) for at in range(count)]
        bit *= 2
    return [turned(blocks[-at % count], -at, after) for at in range(count)]


def swap_into(read, write, count, rows, before=None, after=None):
    tile = 8 * max(1, 32 // count)
    lane = lax.broadcasted_iota(jnp.int32, (tile, LANES), 1)

    def step(index, carry):
        start = pl.multiple_of(index * tile, 8)
        blocks = [read(block, start, tile) for block in range(count)]
        for block, value in enumerate(swapped(blocks, lane, before, after)):
            write(block, start, tile, value)
        return carry

    lax.fori_loop(0, rows // tile, step, 0, unroll=True)


def swap_in_kernel(count, rows, levels_ref, in_ref, out_ref):
    def read(block, start, size):
        return in_ref[block, pl.ds(start, size), :]

    def write(block, start, size, value):
        out_ref[block, pl.ds(start, size), :] = value

    swap_into(read, write, count, rows)
    for block in range(count):
        out_ref[block, pl.ds(rows, levels_ref.shape[0]), :] = levels_ref[...]


def swap_in(levels, value):
    planes, count, rows, _ = value.shape
    extra = levels.shape[1]
    return pl.pallas_call(
        functools.partial(swap_in_kernel, count, rows),
        grid=(planes,),
        in_specs=[
            pl.BlockSpec((None, extra, LANES), lambda p: (p, 0, 0)),
            pl.BlockSpec((None, count, rows, LANES), lambda p: (p, 0, 0, 0)),
        ],
        out_specs=pl.BlockSpec((count, None, rows + extra, LANES), lambda p: (0, p, 0, 0)),
        out_shape=jax.ShapeDtypeStruct((count, planes, rows + extra, LANES), jnp.float32),
        compiler_params=params(12),
        cost_estimate=cost(0, 8 * value.size),
    )(levels, value)


def swap_out_kernel(planes, count, me_ref, added_ref, *refs):
    arrived_refs, out_refs = refs[:-planes], refs[-planes:]
    rows = arrived_refs[0].shape[-2]
    by_steps = len(arrived_refs) > 1
    for plane in range(planes):

        def read(block, start, size):
            if by_steps:
                return arrived_refs[-block % count][plane, pl.ds(start, size), :]
            return arrived_refs[0][block, plane, pl.ds(start, size), :]

        def write(block, start, size, value):
            at = pl.ds(pl.multiple_of(block * rows + start, 8), size)
            out_refs[plane][at, :] = value + added_ref[plane, at, :]

        swap_into(read, write, count, rows, after=me_ref[0] if by_steps else None)


def swap_out(me, arrived, added, first_plane):
    count = len(arrived) if len(arrived) > 1 else arrived[0].shape[0]
    planes, rows = arrived[0].shape[-3:-1]
    cells = count * rows
    return pl.pallas_call(
        functools.partial(swap_out_kernel, planes, count),
        grid=(1,),
        in_specs=[
            pl.BlockSpec(memory_space=pltpu.SMEM),
            pl.BlockSpec((planes, cells, LANES), lambda i: (first_plane // planes, 0, 0)),
        ]
        + [pl.BlockSpec(arrived[0].shape, lambda i: (0,) * arrived[0].ndim)] * len(arrived),
        out_specs=[pl.BlockSpec((None, cells, LANES), lambda i: (0, 0, 0))] * planes,
        out_shape=[jax.ShapeDtypeStruct((1, cells, LANES), jnp.float32)] * planes,
        compiler_params=params(24),
        cost_estimate=cost(0, 24 * cells * planes * LANES),
    )(me, added, *arrived)


def spread_kernel(high_ref, low_ref, weights_ref, out_ref):
    weights = side_by_side(weights_ref[...] * (1.0 / 18.0))
    tile = out_ref.shape[0] // 6

    def step(index, carry):
        at = pl.ds(pl.multiple_of(index * tile, 8), tile)
        out_ref[at, :] = folded(dot_halves((high_ref[at, :], low_ref[at, :]), weights))
        return carry

    lax.fori_loop(0, 6, step, 0)


def spread(high, low, weights):
    planes, cells, _ = high.shape
    basis = pl.BlockSpec((None, cells, 2 * LANES), lambda i: (i, 0, 0))
    return pl.pallas_call(
        spread_kernel,
        grid=(planes,),
        in_specs=[basis, basis, pl.BlockSpec(weights.shape, lambda i: (0, 0))],
        out_specs=pl.BlockSpec((None, cells, LANES), lambda i: (i, 0, 0)),
        out_shape=jax.ShapeDtypeStruct((planes, cells, LANES), jnp.float32),
        compiler_params=params(24),
        cost_estimate=cost(0, 8 * high.size),
    )(high, low, weights)


def fill_row(target, plane, y, row, side_z):
    target[plane, y, pl.ds(PAD, side_z), :] = row
    target[plane, y, pl.ds(PAD - HALO, HALO), :] = row[side_z - HALO :]
    target[plane, y, pl.ds(PAD + side_z, HALO), :] = row[:HALO]


def local_part(source, potential_ref, planes, first, side_y, side_z, line_of, finish):
    tile = 16

    def row(y, carry):
        for start in range(0, side_z, tile):

            def load(plane, y_at, shift):
                return source[plane, y_at, pl.ds(PAD + start + shift, tile), :]

            line = line_of(lambda plane: load(plane, y, 0))
            at = pl.ds(pl.multiple_of(y * side_z + start, 8), tile)
            for plane in range(planes):
                here = first + plane
                total = (potential_ref[plane, at, :] - 1.5 * center_weight - 7.0) * line[HALO + plane]
                for offset in range(1, HALO + 1):
                    around = line[HALO + plane + offset] + line[HALO + plane - offset]
                    around = around + (load(here, y, offset) + load(here, y, -offset))
                    up = lax.rem(y + offset, side_y)
                    down = lax.rem(y + side_y - offset, side_y)
                    around = around + (load(here, up, 0) + load(here, down, 0))
                    total = total - (0.5 * side_weights[offset - 1]) * around
                finish(plane, y, start, at, total)
        return carry

    lax.fori_loop(0, side_y, row, 0)


def filter_kernel(planes, side_y, side_z, width, half, me_ref, arrived_ref, *rest):
    near_refs, late_refs, (field, padded, first, flat, potential) = rest[: -5 - planes + half], rest[-5 - planes + half : -5], rest[-5:]
    count = arrived_ref.shape[0]
    cells = side_y * side_z
    rows = cells // count
    tile = 16

    line = lax.broadcasted_iota(jnp.int32, (2 * count, LANES), 0) % count
    lane = lax.broadcasted_iota(jnp.int32, (2 * count, LANES), 1) // width
    spread = (line == lane).astype(jnp.bfloat16)
    for plane in range(planes):
        lines = [arrived_ref[:, plane, rows + at, :] for at in range(cells // LANES)]
        high, low = halves(jnp.concatenate(lines, axis=1))
        both = jnp.concatenate([high.astype(jnp.float32), low.astype(jnp.float32)], axis=0)
        potential[plane] = jnp.dot(both.T.astype(jnp.bfloat16), spread, preferred_element_type=jnp.float32)

    for plane in range(planes):

        def read_in(block, start, size):
            return arrived_ref[block, plane, pl.ds(start, size), :]

        def write_in(block, start, size, value):
            field[plane, pl.ds(pl.multiple_of(block * rows + start, 8), size), :] = value

        swap_into(read_in, write_in, count, rows)

    def fill(y, carry):
        for plane in range(planes):
            fill_row(padded, plane, y, field[plane, pl.ds(pl.multiple_of(y * side_z, 8), side_z), :], side_z)
        return carry

    lax.fori_loop(0, side_y, fill, 0)

    def line_of(load):
        inside = [load(plane) for plane in range(planes)]
        before = [pltpu.roll(value, width, 1) for value in inside]
        after = [pltpu.roll(value, LANES - width, 1) for value in inside]
        return before[planes - HALO :] + inside + after[:HALO]

    def finish_first(plane, y, start, at, total):
        first[plane, y, pl.ds(PAD + start, tile), :] = total
        if start == 0:
            first[plane, y, pl.ds(PAD + side_z, HALO), :] = total[:HALO]
        if start == side_z - tile:
            first[plane, y, pl.ds(PAD - HALO, HALO), :] = total[tile - HALO :]

    def finish_second(plane, y, start, at, total):
        flat[plane, at, :] = total * (1.0 / 18.0) - field[plane, at, :]

    local_part(padded, potential, planes, 0, side_y, side_z, line_of, finish_first)
    local_part(first, potential, planes, 0, side_y, side_z, line_of, finish_second)

    for plane in range(planes):

        def read_out(block, start, size):
            return flat[plane, pl.ds(pl.multiple_of(block * rows + start, 8), size), :]

        def write_out(block, start, size, value):
            if plane < half:
                near_refs[block][plane, pl.ds(start, size), :] = value
            else:
                late_refs[plane - half][block, 0, pl.ds(start, size), :] = value

        swap_into(read_out, write_out, count, rows, before=me_ref[0] if plane < half else None)


def filter_orbitals(me, arrived, side_y, side_z, width, half):
    count, planes = arrived.shape[:2]
    rows = side_y * side_z // count
    flat = pltpu.VMEM((planes, side_y * side_z, LANES), jnp.float32)
    padded = pltpu.VMEM((planes, side_y, side_z + 2 * PAD, LANES), jnp.float32)
    shapes = [jax.ShapeDtypeStruct((half, rows, LANES), jnp.float32)] * count
    shapes += [jax.ShapeDtypeStruct((count, 1, rows, LANES), jnp.float32)] * (planes - half)
    outs = pl.pallas_call(
        functools.partial(filter_kernel, planes, side_y, side_z, width, half),
        in_specs=[pl.BlockSpec(memory_space=pltpu.SMEM), WHOLE],
        out_specs=[WHOLE] * len(shapes),
        out_shape=shapes,
        scratch_shapes=[flat, padded, padded, flat, flat],
        compiler_params=params(56),
        cost_estimate=cost(100 * arrived.size, 12 * arrived.size),
    )(me, arrived)
    return list(outs[:count]), list(outs[count:])


def basis_kernel(planes, side_y, side_z, bands, *refs):
    raw_refs = refs[:bands]
    offset_ref, potential_ref, orbitals_ref, high_ref, low_ref, parts_ref, turned, placed = refs[bands:]
    cells = side_y * side_z
    for part in range(SPAN):
        at = pl.ds(part * cells, cells)
        stack = [raw_ref[block, :, at] for raw_ref in raw_refs for block in range(NEAR)]
        turned[part] = jnp.concatenate(stack, axis=0).T
    offset = offset_ref[0:1, :]

    def place(y, carry):
        at = pl.ds(pl.multiple_of(y * side_z, 8), side_z)
        values = [turned[part, at, :] for part in range(SPAN)]
        for plane in range(planes + 2 * HALO):
            row = jnp.zeros((side_z, LANES), jnp.float32)
            for part in range(SPAN):
                row = jnp.where(offset == float(plane - HALO - part), values[part], row)
            fill_row(placed, plane, y, row, side_z)
        return carry

    lax.fori_loop(0, side_y, place, 0)

    def line_of(load):
        return [load(plane) for plane in range(planes + 2 * HALO)]

    def finish(plane, y, start, at, total):
        own = placed[HALO + plane, y, pl.ds(PAD + start, 16), :]
        high, low = halves(jnp.concatenate([total, own], axis=1))
        high_ref[plane, at, :] = high
        low_ref[plane, at, :] = low

    local_part(placed, potential_ref, planes, HALO, side_y, side_z, line_of, finish)

    dot = functools.partial(jnp.dot, preferred_element_type=jnp.float32)
    with_orbitals = with_basis = 0.0
    for plane in range(planes):
        high, low = high_ref[plane], low_ref[plane]
        left = halves(orbitals_ref[plane].T)
        with_orbitals = with_orbitals + (dot(left[0], high) + (dot(left[0], low) + dot(left[1], high)))
        own_high, own_low = high[:, LANES:], low[:, LANES:]
        turned_high = own_high.astype(jnp.float32).T.astype(jnp.bfloat16)
        turned_low = own_low.astype(jnp.float32).T.astype(jnp.bfloat16)
        both = jnp.concatenate([own_high, own_low], axis=1)
        with_basis = with_basis + (dot(turned_high, both) + dot(turned_low, both))
    parts_ref[0] = with_orbitals[:, LANES:].T
    parts_ref[1] = with_orbitals[:, :LANES].T
    parts_ref[2] = folded(with_basis)


def build_basis(raw, offset, potential, orbitals, side_y, side_z):
    planes, cells, _ = orbitals.shape
    pair = jax.ShapeDtypeStruct((planes, cells, 2 * LANES), jnp.bfloat16)
    return pl.pallas_call(
        functools.partial(basis_kernel, planes, side_y, side_z, len(raw)),
        in_specs=[WHOLE] * (len(raw) + 3),
        out_specs=[WHOLE] * 3,
        out_shape=[pair, pair, jax.ShapeDtypeStruct((3, LANES, LANES), jnp.float32)],
        scratch_shapes=[
            pltpu.VMEM((SPAN, cells, LANES), jnp.float32),
            pltpu.VMEM((planes + 2 * HALO, side_y, side_z + 2 * PAD, LANES), jnp.float32),
        ],
        compiler_params=params(56),
        cost_estimate=cost(200 * orbitals.size, 24 * orbitals.size),
    )(*raw, offset, potential, orbitals)


def weights_kernel(bands, me_ref, parts_ref, coupling_ref, out_ref):
    count = parts_ref.shape[0]
    size = LANES // NEAR
    lines = size // bands
    me = me_ref[0]
    dot = functools.partial(jnp.dot, precision=HIGHEST, preferred_element_type=jnp.float32)

    def device(step):
        return lax.rem(me + step % count, count)

    def total(pick, block):
        shares = [pick(block - (near - BEFORE), near) for near in range(NEAR)]
        return (shares[0] + shares[1]) + (shares[2] + shares[3])

    def of_block(value, near):
        starts = [(band * NEAR + near) * lines for band in range(bands)]
        return jnp.concatenate([value[start : start + lines] for start in starts], axis=0)

    def joined(values):
        return jnp.concatenate(
            [values[near][band * lines : (band + 1) * lines] for band in range(bands) for near in range(NEAR)], axis=0
        )

    def couple(block, value):
        return dot(coupling_ref[device(block)], value)

    def kept(function):
        known = {}

        def look(step):
            if step % count not in known:
                known[step % count] = function(step)
            return known[step % count]

        return look

    weight = kept(
        lambda block: couple(block, total(lambda step, near: of_block(parts_ref[device(step), 0], near), block))
    )
    weights = kept(lambda step: joined([weight(step + near - BEFORE) for near in range(NEAR)]))
    second = kept(lambda step: parts_ref[device(step), 1] + dot(parts_ref[device(step), 2], weights(step)))
    out_ref[pl.ds(0, LANES), :] = weights(0)
    out_ref[pl.ds(LANES, LANES), :] = joined(
        [
            couple(near - BEFORE, total(lambda step, at: of_block(second(step), at), near - BEFORE))
            for near in range(NEAR)
        ]
    )


def near_weights(me, parts, coupling):
    return pl.pallas_call(
        functools.partial(weights_kernel, lax.axis_size("band")),
        in_specs=[pl.BlockSpec(memory_space=pltpu.SMEM), WHOLE, WHOLE],
        out_specs=WHOLE,
        out_shape=jax.ShapeDtypeStruct((2 * LANES, LANES), jnp.float32),
        compiler_params=params(24),
        cost_estimate=cost(0, 8 * parts.size),
    )(me, parts, coupling)


def shifted(value, axis, step):
    count = lax.axis_size(axis)
    return lax.ppermute(value, axis, [(source, (source + step) % count) for source in range(count)])


def exchanged(values):
    return [shifted(value, "dom", step) if step else value for step, value in enumerate(values)]


def crossed(value, bit):
    return lax.ppermute(value, "band", [(source, source ^ bit) for source in range(lax.axis_size("band"))])


def gram_kernel(own_ref, *rest):
    panels, out_ref = (own_ref, *rest[:-1]), rest[-1]

    @pl.when(pl.program_id(0) == 0)
    def _():
        out_ref[...] = jnp.zeros_like(out_ref)

    for plane in range(own_ref.shape[0]):
        left = halves(own_ref[plane].T)
        both = jnp.concatenate([side_by_side(panel[plane]) for panel in panels], axis=1)
        value = dot_halves(left, both)
        for index in range(len(panels)):
            at = pl.ds(index * LANES, LANES)
            out_ref[:, at] = out_ref[:, at] + folded(value[:, 2 * index * LANES : 2 * (index + 1) * LANES])


def gram_rows(panels):
    planes, cells, _ = panels[0].shape
    tile = cells // 2
    return pl.pallas_call(
        gram_kernel,
        grid=(cells // tile,),
        in_specs=[pl.BlockSpec((planes, tile, LANES), lambda i: (0, i, 0))] * len(panels),
        out_specs=pl.BlockSpec((LANES, len(panels) * LANES), lambda i: (0, 0)),
        out_shape=jax.ShapeDtypeStruct((LANES, len(panels) * LANES), jnp.float32),
        compiler_params=params(16),
        cost_estimate=cost(8 * panels[0].size * LANES * len(panels), 4 * panels[0].size * len(panels)),
    )(*panels)


def rotate_kernel(chunks, bands, inverse_ref, *rest):
    panels, out_ref = rest[:-1], rest[-1]
    right = side_by_side(inverse_ref[...].T)
    for index, (begin, size) in enumerate(chunks):
        group = panels[index * bands : (index + 1) * bands]
        for plane in range(size):
            left = halves(jnp.concatenate([panel[plane] for panel in group], axis=1))
            out_ref[begin + plane] = folded(dot_halves(left, right))


def rotated(inverse_rows, panels, chunks):
    bands = len(panels[0])
    planes = sum(size for _, size in chunks)
    cells = panels[0][0].shape[1]
    tile = cells // 4
    specs = [pl.BlockSpec((size, tile, LANES), lambda i: (0, i, 0)) for _, size in chunks for _ in range(bands)]
    return pl.pallas_call(
        functools.partial(rotate_kernel, chunks, bands),
        grid=(cells // tile,),
        in_specs=[pl.BlockSpec(inverse_rows.shape, lambda i: (0, 0)), *specs],
        out_specs=pl.BlockSpec((planes, tile, LANES), lambda i: (0, i, 0)),
        out_shape=jax.ShapeDtypeStruct((planes, cells, LANES), jnp.float32),
        compiler_params=params(56),
    )(inverse_rows, *[panel for group in panels for panel in group])


def thirds(value):
    first = value.astype(jnp.bfloat16).astype(jnp.float32)
    rest = value - first
    second = rest.astype(jnp.bfloat16).astype(jnp.float32)
    return first, second, rest - second


def eliminate(work, result):
    sublane = lax.broadcasted_iota(jnp.int32, (GROUP, LANES), 0)

    def splat(row, column):
        return jnp.broadcast_to(row[:, column : column + 1], (GROUP, LANES))

    def load(top):
        left = [jnp.broadcast_to(work[pl.ds(top + i, 1), :LANES], (GROUP, LANES)) for i in range(GROUP)]
        right = [jnp.broadcast_to(work[pl.ds(top + i, 1), LANES:], (GROUP, LANES)) for i in range(GROUP)]
        return left, right

    def factored(top, left, right):
        entry = {(i, j): splat(left[i], top + j) for i in range(GROUP) for j in range(i, GROUP)}
        for i in range(GROUP):
            scale = lax.rsqrt(entry[i, i])
            left[i] = left[i] * scale
            right[i] = right[i] * scale
            factor = {j: entry[i, j] * scale for j in range(i + 1, GROUP)}
            for m in range(i + 1, GROUP):
                for j in range(m, GROUP):
                    entry[m, j] = entry[m, j] - factor[m] * factor[j]
                left[m] = left[m] - factor[m] * left[i]
                right[m] = right[m] - factor[m] * right[i]

    def gathered(rows):
        value = rows[0]
        for i in range(1, GROUP):
            value = jnp.where(sublane == i, rows[i], value)
        return value

    for top in range(0, LANES, 2 * GROUP):
        left, right = load(top)
        factored(top, left, right)
        middle = top + GROUP
        next_left, next_right = load(middle)
        for m in range(GROUP):
            for i in range(GROUP):
                factor = splat(left[i], middle + m)
                next_left[m] = next_left[m] - factor * left[i]
                next_right[m] = next_right[m] - factor * right[i]
        factored(middle, next_left, next_right)
        upper = jnp.concatenate([gathered(left), gathered(next_left)], axis=0)
        lower = jnp.concatenate([gathered(right), gathered(next_right)], axis=0)
        result[pl.ds(top, 2 * GROUP), :] = lower
        below = middle + GROUP
        if below < LANES:
            a, b, c = thirds(upper)
            x, y, z = thirds(lower)
            columns = jnp.concatenate([a, a, b, b, a, c], axis=0).T[below:].astype(jnp.bfloat16)
            rows = jnp.concatenate(
                [jnp.concatenate([a, b, a, b, c, a], axis=0), jnp.concatenate([x, y, x, y, z, x], axis=0)], axis=1
            ).astype(jnp.bfloat16)
            rest = pl.ds(below, LANES - below)
            work[rest, :] = work[rest, :] - jnp.dot(columns, rows, preferred_element_type=jnp.float32)


def cholesky_kernel(band_ref, *refs):
    rows_refs, (gram_ref, own_ref, inverse, matrix, work, corner, scaled) = refs[:-7], refs[-7:]
    size = gram_ref.shape[0]
    bands = len(rows_refs)
    band = band_ref[0]

    def block_of(member):
        return pl.ds(pl.multiple_of((band ^ member) * LANES, LANES), LANES)

    for member, rows_ref in enumerate(rows_refs):
        for other in range(bands):
            gram_ref[block_of(member), block_of(member ^ other)] = rows_ref[:, other * LANES : (other + 1) * LANES]
    dot = functools.partial(jnp.dot, precision=HIGHEST, preferred_element_type=jnp.float32)
    diagonal = lax.broadcasted_iota(jnp.int32, (LANES, LANES), 0) == lax.broadcasted_iota(jnp.int32, (LANES, LANES), 1)
    identity = diagonal.astype(jnp.float32)
    matrix[:, :size] = gram_ref[...]
    matrix[:, size:] = jnp.zeros((size, size), jnp.float32)
    for at in range(0, size, LANES):
        matrix[pl.ds(at, LANES), size + at : size + at + LANES] = identity

    def block(index, carry):
        start = pl.multiple_of(index * LANES, LANES)
        at = pl.ds(start, LANES)
        work[:, :LANES] = matrix[at, at]
        work[:, LANES:] = identity
        eliminate(work, corner)
        scaled[...] = dot(corner[...], matrix[at, :])
        inverse[at, :] = scaled[:, size:]

        def below(other, carry):
            rows = pl.ds(pl.multiple_of(other * LANES, LANES), LANES)
            matrix[rows, :] = matrix[rows, :] - dot(scaled[:, rows].T, scaled[...])
            return carry

        lax.fori_loop(index + 1, size // LANES, below, 0)
        return carry

    lax.fori_loop(0, size // LANES, block, 0)
    for member in range(bands):
        own_ref[:, member * LANES : (member + 1) * LANES] = inverse[block_of(0), block_of(member)]


def cholesky_inverse(band, rows):
    size = rows[0].shape[1]
    return pl.pallas_call(
        cholesky_kernel,
        in_specs=[pl.BlockSpec(memory_space=pltpu.SMEM)] + [WHOLE] * len(rows),
        out_specs=[WHOLE] * 2,
        out_shape=[
            jax.ShapeDtypeStruct((size, size), jnp.float32),
            jax.ShapeDtypeStruct((LANES, size), jnp.float32),
        ],
        scratch_shapes=[
            pltpu.VMEM((size, size), jnp.float32),
            pltpu.VMEM((size, 2 * size), jnp.float32),
            pltpu.VMEM((LANES, 2 * LANES), jnp.float32),
            pltpu.VMEM((LANES, LANES), jnp.float32),
            pltpu.VMEM((LANES, 2 * size), jnp.float32),
        ],
        compiler_params=params(14),
    )(band.astype(jnp.int32).reshape(1), *rows)


def packed_projectors(projectors, atom_plane, planes):
    share = projectors.shape[0] // lax.axis_size("band")
    first = (atom_plane - lax.axis_index("dom") * planes).astype(jnp.float32)
    first = jnp.broadcast_to(first[:, None, None], (projectors.shape[0], MAXPROJ, LANES))
    packed = jnp.concatenate([projectors, first], axis=2)
    mine = lax.dynamic_slice_in_dim(packed, lax.axis_index("band") * share, share, 0)
    return mine.reshape(share * MAXPROJ, -1)


def near_shares(mine):
    return jnp.stack([mine if step == BEFORE else shifted(mine, "dom", BEFORE - step) for step in range(NEAR)])


def near_projectors(near, planes):
    across = crossed(near, 2)
    raw = [near, crossed(near, 1), across, crossed(across, 1)]
    moved = (planes * (jnp.arange(NEAR, dtype=jnp.float32) - BEFORE))[:, None]
    first = jnp.stack([member[:, :, -1] + moved for member in raw]).reshape(1, LANES)
    return raw, jnp.broadcast_to(first, (GROUP, LANES))


def shards(orbitals, potential, projectors, coupling, atom_plane, projector_count):
    planes, side_y, side_z, local_orbs = orbitals.shape
    blocks, bands = lax.axis_size("dom"), lax.axis_size("band")
    band = lax.axis_index("band")
    cells = side_y * side_z
    rows = cells // blocks
    width = local_orbs // blocks
    norb = local_orbs * bands
    chunks = tuple((plane, 1) for plane in range(planes))
    half = planes // 2
    tie = lax.optimization_barrier
    me = lax.axis_index("dom").astype(jnp.int32).reshape(1)

    order = jnp.arange(bands, dtype=jnp.int32) ^ band

    mine = packed_projectors(projectors, atom_plane, planes)
    mine, levels = lax.optimization_barrier((mine, potential.reshape(planes, cells // LANES, LANES)))
    near = near_shares(mine)
    levels = jnp.pad(levels, ((0, 0), (0, -levels.shape[1] % GROUP), (0, 0)))
    packed = swap_in(levels, orbitals.reshape(planes, blocks, rows, local_orbs))
    packed, near = lax.optimization_barrier((packed, near))
    raw, first = near_projectors(near, planes)
    arrived = lax.all_to_all(packed, "dom", 0, 0, tiled=True)

    own_levels = jnp.broadcast_to(potential.reshape(planes, cells, 1), (planes, cells, LANES))
    high, low, parts = build_basis(raw, first, own_levels, orbitals.reshape(planes, cells, LANES), side_y, side_z)
    atoms = projectors.shape[0]
    slots = jnp.arange(MAXPROJ, dtype=jnp.int32)
    live = (slots[None, :] < projector_count[:, None]).astype(jnp.float32)
    coupled = 0.5 * (coupling + jnp.transpose(coupling, (0, 2, 1))) * live[:, :, None] * live[:, None, :]
    coupled = jnp.take(coupled.reshape(bands, -1, MAXPROJ, MAXPROJ), order, axis=0)
    vectors = atoms * MAXPROJ
    row = jnp.arange(vectors, dtype=jnp.int32) // MAXPROJ
    matrix = jnp.tile(coupled.reshape(vectors, MAXPROJ), (1, atoms))
    matrix = jnp.where(row[:, None] == row[None, :], matrix, 0.0)
    matrix = jnp.pad(matrix, ((0, 0), (0, LANES - vectors)))
    payload = jnp.concatenate([parts.reshape(3 * LANES, LANES), matrix], axis=0)
    everyone = lax.all_gather(payload, "dom")
    weights = near_weights(
        me,
        everyone[:, : 3 * LANES].reshape(blocks, 3, LANES, LANES), everyone[:, 3 * LANES :, :vectors],
    )

    early, late = filter_orbitals(me, arrived, side_y, side_z, width, half)

    came = exchanged(early)
    added = spread(high, low, weights)
    owns = list(swap_out(me, came, added, 0))
    acrosses = [crossed(own, 2) for own in owns]
    besides = [crossed(own, 1) for own in owns]
    for index, packed in enumerate(late):
        if index:
            packed, coming = tie((packed, coming))
            own = swap_out(me, [coming], added, half + index - 1)[0]
            own, acrosses[index] = tie((own, acrosses[index]))
            owns.append(own)
            acrosses.append(crossed(own, 2))
            besides.append(crossed(own, 1))
        else:
            packed, owns = tie((packed, owns))
        coming = lax.all_to_all(packed, "dom", 0, 0, tiled=True)
        coming, acrosses[index] = tie((coming, acrosses[index]))
    owns.append(swap_out(me, [coming], added, planes - 1)[0])
    acrosses.append(crossed(owns[-1], 2))
    besides.append(crossed(owns[-1], 1))
    panels, part = [], None
    for index, across in enumerate(acrosses):
        if index >= half:
            across, part = tie((across, part))
        panels.append([owns[index], besides[index], across, crossed(across, 1)])
        rows_of = gram_rows(panels[-1])
        part = rows_of if part is None else part + rows_of

    pieces = lax.all_to_all(part.reshape(blocks, width, norb), "dom", 0, 0, tiled=True)
    piece = jnp.sum(pieces, axis=0) * (1.0 / (planes * cells * blocks))
    own_gram = lax.all_to_all(jnp.broadcast_to(piece, (blocks, width, norb)), "dom", 0, 0, tiled=True)
    own_gram = own_gram.reshape(local_orbs, norb)
    across = crossed(own_gram, 2)
    gram, own_rows = cholesky_inverse(band, [own_gram, crossed(own_gram, 1), across, crossed(across, 1)])
    result = rotated(own_rows, panels, chunks)
    return (result.reshape(planes, side_y, side_z, local_orbs), gram)


def solution(mesh):
    placed = (
        P("dom", None, None, "band"),
        P("dom", None, None),
        P("dom", None, None),
        P("dom", None, None),
        P("dom"),
        P("dom"),
    )
    return jax.shard_map(
        shards,
        mesh=mesh,
        in_specs=placed,
        out_specs=(P("dom", None, None, "band"), P()),
        check_vma=False,
    )
```

```python
import functools

import jax
import jax.numpy as jnp
from jax import lax
from jax.experimental import pallas as pl
from jax.experimental.pallas import tpu as pltpu
from jax.sharding import PartitionSpec as P

SPAN = 3
MAXPROJ = 4
HALO = 4
PAD = 8
LANES = 128
GROUP = 8
BEFORE, AFTER = 2, 1
NEAR = BEFORE + 1 + AFTER

center_weight = -205.0 / 72.0
side_weights = (8.0 / 5.0, -1.0 / 5.0, 8.0 / 315.0, -1.0 / 560.0)
HIGHEST = lax.Precision.HIGHEST
WHOLE = pl.BlockSpec(memory_space=pltpu.VMEM)


def params(mebibytes):
    return pltpu.CompilerParams(vmem_limit_bytes=mebibytes * 1024 * 1024)


def cost(flops, bytes_accessed):
    return pl.CostEstimate(flops=int(flops), bytes_accessed=int(bytes_accessed), transcendentals=0)


def halves(value):
    high = value.astype(jnp.bfloat16)
    return high, (value - high.astype(jnp.float32)).astype(jnp.bfloat16)


def side_by_side(value):
    return jnp.concatenate(halves(value), axis=1)


def dot_halves(left, right):
    dot = functools.partial(jnp.dot, preferred_element_type=jnp.float32)
    return dot(left[0], right) + dot(left[1], right)


def folded(value):
    return value[:, :LANES] + value[:, LANES:]


def swapped(blocks, lane, before=None, after=None):
    count = len(blocks)
    width = LANES // count

    def turned(value, at, extra):
        if extra is None:
            return pltpu.roll(value, at % count * width, 1) if at else value
        return pltpu.roll(value, lax.rem((at % count + extra) * width, LANES), 1)

    blocks = [turned(value, at, None if before is None else count - before) for at, value in enumerate(blocks)]
    bit = 1
    while bit < count:
        chosen = (lane // (bit * width)) % 2 == 1
        blocks = [jnp.where(chosen, blocks[(at + bit) % count], blocks[at]) for at in range(count)]
        bit *= 2
    return [turned(blocks[-at % count], -at, after) for at in range(count)]


def swap_into(read, write, count, rows, before=None, after=None):
    tile = 8 * max(1, 32 // count)
    lane = lax.broadcasted_iota(jnp.int32, (tile, LANES), 1)

    def step(index, carry):
        start = pl.multiple_of(index * tile, 8)
        blocks = [read(block, start, tile) for block in range(count)]
        for block, value in enumerate(swapped(blocks, lane, before, after)):
            write(block, start, tile, value)
        return carry

    lax.fori_loop(0, rows // tile, step, 0, unroll=True)


def swap_in_kernel(count, rows, levels_ref, in_ref, out_ref):
    def read(block, start, size):
        return in_ref[block, pl.ds(start, size), :]

    def write(block, start, size, value):
        out_ref[block, pl.ds(start, size), :] = value

    swap_into(read, write, count, rows)
    for block in range(count):
        out_ref[block, pl.ds(rows, levels_ref.shape[0]), :] = levels_ref[...]


def swap_in(levels, value):
    planes, count, rows, _ = value.shape
    extra = levels.shape[1]
    return pl.pallas_call(
        functools.partial(swap_in_kernel, count, rows),
        grid=(planes,),
        in_specs=[
            pl.BlockSpec((None, extra, LANES), lambda p: (p, 0, 0)),
            pl.BlockSpec((None, count, rows, LANES), lambda p: (p, 0, 0, 0)),
        ],
        out_specs=pl.BlockSpec((count, None, rows + extra, LANES), lambda p: (0, p, 0, 0)),
        out_shape=jax.ShapeDtypeStruct((count, planes, rows + extra, LANES), jnp.float32),
        compiler_params=params(12),
        cost_estimate=cost(0, 8 * value.size),
    )(levels, value)


def swap_out_kernel(planes, count, me_ref, added_ref, *refs):
    arrived_refs, out_refs = refs[:-planes], refs[-planes:]
    rows = arrived_refs[0].shape[-2]
    by_steps = len(arrived_refs) > 1
    for plane in range(planes):

        def read(block, start, size):
            if by_steps:
                return arrived_refs[-block % count][plane, pl.ds(start, size), :]
            return arrived_refs[0][block, plane, pl.ds(start, size), :]

        def write(block, start, size, value):
            at = pl.ds(pl.multiple_of(block * rows + start, 8), size)
            out_refs[plane][at, :] = value + added_ref[plane, at, :]

        swap_into(read, write, count, rows, after=me_ref[0] if by_steps else None)


def swap_out(me, arrived, added, first_plane):
    count = len(arrived) if len(arrived) > 1 else arrived[0].shape[0]
    planes, rows = arrived[0].shape[-3:-1]
    cells = count * rows
    return pl.pallas_call(
        functools.partial(swap_out_kernel, planes, count),
        grid=(1,),
        in_specs=[
            pl.BlockSpec(memory_space=pltpu.SMEM),
            pl.BlockSpec((planes, cells, LANES), lambda i: (first_plane // planes, 0, 0)),
        ]
        + [pl.BlockSpec(arrived[0].shape, lambda i: (0,) * arrived[0].ndim)] * len(arrived),
        out_specs=[pl.BlockSpec((None, cells, LANES), lambda i: (0, 0, 0))] * planes,
        out_shape=[jax.ShapeDtypeStruct((1, cells, LANES), jnp.float32)] * planes,
        compiler_params=params(24),
        cost_estimate=cost(0, 24 * cells * planes * LANES),
    )(me, added, *arrived)


def spread_kernel(high_ref, low_ref, weights_ref, out_ref):
    weights = side_by_side(weights_ref[...] * (1.0 / 18.0))
    tile = out_ref.shape[0] // 6

    def step(index, carry):
        at = pl.ds(pl.multiple_of(index * tile, 8), tile)
        out_ref[at, :] = folded(dot_halves((high_ref[at, :], low_ref[at, :]), weights))
        return carry

    lax.fori_loop(0, 6, step, 0)


def spread(high, low, weights):
    planes, cells, _ = high.shape
    basis = pl.BlockSpec((None, cells, 2 * LANES), lambda i: (i, 0, 0))
    return pl.pallas_call(
        spread_kernel,
        grid=(planes,),
        in_specs=[basis, basis, pl.BlockSpec(weights.shape, lambda i: (0, 0))],
        out_specs=pl.BlockSpec((None, cells, LANES), lambda i: (i, 0, 0)),
        out_shape=jax.ShapeDtypeStruct((planes, cells, LANES), jnp.float32),
        compiler_params=params(24),
        cost_estimate=cost(0, 8 * high.size),
    )(high, low, weights)


def fill_row(target, plane, y, row, side_z):
    target[plane, y, pl.ds(PAD, side_z), :] = row
    target[plane, y, pl.ds(PAD - HALO, HALO), :] = row[side_z - HALO :]
    target[plane, y, pl.ds(PAD + side_z, HALO), :] = row[:HALO]


def local_part(source, potential_ref, planes, first, side_y, side_z, line_of, finish):
    tile = 16

    def row(y, carry):
        for start in range(0, side_z, tile):

            def load(plane, y_at, shift):
                return source[plane, y_at, pl.ds(PAD + start + shift, tile), :]

            line = line_of(lambda plane: load(plane, y, 0))
            at = pl.ds(pl.multiple_of(y * side_z + start, 8), tile)
            for plane in range(planes):
                here = first + plane
                total = (potential_ref[plane, at, :] - 1.5 * center_weight - 7.0) * line[HALO + plane]
                for offset in range(1, HALO + 1):
                    around = line[HALO + plane + offset] + line[HALO + plane - offset]
                    around = around + (load(here, y, offset) + load(here, y, -offset))
                    up = lax.rem(y + offset, side_y)
                    down = lax.rem(y + side_y - offset, side_y)
                    around = around + (load(here, up, 0) + load(here, down, 0))
                    total = total - (0.5 * side_weights[offset - 1]) * around
                finish(plane, y, start, at, total)
        return carry

    lax.fori_loop(0, side_y, row, 0)


def filter_kernel(planes, side_y, side_z, width, half, me_ref, arrived_ref, *rest):
    near_refs, late_refs, (field, padded, first, flat, potential) = rest[: -5 - planes + half], rest[-5 - planes + half : -5], rest[-5:]
    count = arrived_ref.shape[0]
    cells = side_y * side_z
    rows = cells // count
    tile = 16

    line = lax.broadcasted_iota(jnp.int32, (2 * count, LANES), 0) % count
    lane = lax.broadcasted_iota(jnp.int32, (2 * count, LANES), 1) // width
    spread = (line == lane).astype(jnp.bfloat16)
    for plane in range(planes):
        lines = [arrived_ref[:, plane, rows + at, :] for at in range(cells // LANES)]
        high, low = halves(jnp.concatenate(lines, axis=1))
        both = jnp.concatenate([high.astype(jnp.float32), low.astype(jnp.float32)], axis=0)
        potential[plane] = jnp.dot(both.T.astype(jnp.bfloat16), spread, preferred_element_type=jnp.float32)

    for plane in range(planes):

        def read_in(block, start, size):
            return arrived_ref[block, plane, pl.ds(start, size), :]

        def write_in(block, start, size, value):
            field[plane, pl.ds(pl.multiple_of(block * rows + start, 8), size), :] = value

        swap_into(read_in, write_in, count, rows)

    def fill(y, carry):
        for plane in range(planes):
            fill_row(padded, plane, y, field[plane, pl.ds(pl.multiple_of(y * side_z, 8), side_z), :], side_z)
        return carry

    lax.fori_loop(0, side_y, fill, 0)

    def line_of(load):
        inside = [load(plane) for plane in range(planes)]
        before = [pltpu.roll(value, width, 1) for value in inside]
        after = [pltpu.roll(value, LANES - width, 1) for value in inside]
        return before[planes - HALO :] + inside + after[:HALO]

    def finish_first(plane, y, start, at, total):
        first[plane, y, pl.ds(PAD + start, tile), :] = total
        if start == 0:
            first[plane, y, pl.ds(PAD + side_z, HALO), :] = total[:HALO]
        if start == side_z - tile:
            first[plane, y, pl.ds(PAD - HALO, HALO), :] = total[tile - HALO :]

    def finish_second(plane, y, start, at, total):
        flat[plane, at, :] = total * (1.0 / 18.0) - field[plane, at, :]

    local_part(padded, potential, planes, 0, side_y, side_z, line_of, finish_first)
    local_part(first, potential, planes, 0, side_y, side_z, line_of, finish_second)

    for plane in range(planes):

        def read_out(block, start, size):
            return flat[plane, pl.ds(pl.multiple_of(block * rows + start, 8), size), :]

        def write_out(block, start, size, value):
            if plane < half:
                near_refs[block][plane, pl.ds(start, size), :] = value
            else:
                late_refs[plane - half][block, 0, pl.ds(start, size), :] = value

        swap_into(read_out, write_out, count, rows, before=me_ref[0] if plane < half else None)


def filter_orbitals(me, arrived, side_y, side_z, width, half):
    count, planes = arrived.shape[:2]
    rows = side_y * side_z // count
    flat = pltpu.VMEM((planes, side_y * side_z, LANES), jnp.float32)
    padded = pltpu.VMEM((planes, side_y, side_z + 2 * PAD, LANES), jnp.float32)
    shapes = [jax.ShapeDtypeStruct((half, rows, LANES), jnp.float32)] * count
    shapes += [jax.ShapeDtypeStruct((count, 1, rows, LANES), jnp.float32)] * (planes - half)
    outs = pl.pallas_call(
        functools.partial(filter_kernel, planes, side_y, side_z, width, half),
        in_specs=[pl.BlockSpec(memory_space=pltpu.SMEM), WHOLE],
        out_specs=[WHOLE] * len(shapes),
        out_shape=shapes,
        scratch_shapes=[flat, padded, padded, flat, flat],
        compiler_params=params(56),
        cost_estimate=cost(100 * arrived.size, 12 * arrived.size),
    )(me, arrived)
    return list(outs[:count]), list(outs[count:])


def basis_kernel(planes, side_y, side_z, bands, *refs):
    raw_refs = refs[:bands]
    offset_ref, potential_ref, orbitals_ref, high_ref, low_ref, parts_ref, turned, placed = refs[bands:]
    cells = side_y * side_z
    for part in range(SPAN):
        at = pl.ds(part * cells, cells)
        stack = [raw_ref[block, :, at] for raw_ref in raw_refs for block in range(NEAR)]
        turned[part] = jnp.concatenate(stack, axis=0).T
    offset = offset_ref[0:1, :]

    def place(y, carry):
        at = pl.ds(pl.multiple_of(y * side_z, 8), side_z)
        values = [turned[part, at, :] for part in range(SPAN)]
        for plane in range(planes + 2 * HALO):
            row = jnp.zeros((side_z, LANES), jnp.float32)
            for part in range(SPAN):
                row = jnp.where(offset == float(plane - HALO - part), values[part], row)
            fill_row(placed, plane, y, row, side_z)
        return carry

    lax.fori_loop(0, side_y, place, 0)

    def line_of(load):
        return [load(plane) for plane in range(planes + 2 * HALO)]

    def finish(plane, y, start, at, total):
        own = placed[HALO + plane, y, pl.ds(PAD + start, 16), :]
        high, low = halves(jnp.concatenate([total, own], axis=1))
        high_ref[plane, at, :] = high
        low_ref[plane, at, :] = low

    local_part(placed, potential_ref, planes, HALO, side_y, side_z, line_of, finish)

    dot = functools.partial(jnp.dot, preferred_element_type=jnp.float32)
    with_orbitals = with_basis = 0.0
    for plane in range(planes):
        high, low = high_ref[plane], low_ref[plane]
        left = halves(orbitals_ref[plane].T)
        with_orbitals = with_orbitals + (dot(left[0], high) + (dot(left[0], low) + dot(left[1], high)))
        own_high, own_low = high[:, LANES:], low[:, LANES:]
        turned_high = own_high.astype(jnp.float32).T.astype(jnp.bfloat16)
        turned_low = own_low.astype(jnp.float32).T.astype(jnp.bfloat16)
        both = jnp.concatenate([own_high, own_low], axis=1)
        with_basis = with_basis + (dot(turned_high, both) + dot(turned_low, both))
    parts_ref[0] = with_orbitals[:, LANES:].T
    parts_ref[1] = with_orbitals[:, :LANES].T
    parts_ref[2] = folded(with_basis)


def build_basis(raw, offset, potential, orbitals, side_y, side_z):
    planes, cells, _ = orbitals.shape
    pair = jax.ShapeDtypeStruct((planes, cells, 2 * LANES), jnp.bfloat16)
    return pl.pallas_call(
        functools.partial(basis_kernel, planes, side_y, side_z, len(raw)),
        in_specs=[WHOLE] * (len(raw) + 3),
        out_specs=[WHOLE] * 3,
        out_shape=[pair, pair, jax.ShapeDtypeStruct((3, LANES, LANES), jnp.float32)],
        scratch_shapes=[
            pltpu.VMEM((SPAN, cells, LANES), jnp.float32),
            pltpu.VMEM((planes + 2 * HALO, side_y, side_z + 2 * PAD, LANES), jnp.float32),
        ],
        compiler_params=params(56),
        cost_estimate=cost(200 * orbitals.size, 24 * orbitals.size),
    )(*raw, offset, potential, orbitals)


def weights_kernel(bands, me_ref, parts_ref, coupling_ref, out_ref):
    count = parts_ref.shape[0]
    size = LANES // NEAR
    lines = size // bands
    me = me_ref[0]
    dot = functools.partial(jnp.dot, precision=HIGHEST, preferred_element_type=jnp.float32)

    def device(step):
        return lax.rem(me + step % count, count)

    def total(pick, block):
        shares = [pick(block - (near - BEFORE), near) for near in range(NEAR)]
        return (shares[0] + shares[1]) + (shares[2] + shares[3])

    def of_block(value, near):
        starts = [(band * NEAR + near) * lines for band in range(bands)]
        return jnp.concatenate([value[start : start + lines] for start in starts], axis=0)

    def joined(values):
        return jnp.concatenate(
            [values[near][band * lines : (band + 1) * lines] for band in range(bands) for near in range(NEAR)], axis=0
        )

    def couple(block, value):
        return dot(coupling_ref[device(block)], value)

    def kept(function):
        known = {}

        def look(step):
            if step % count not in known:
                known[step % count] = function(step)
            return known[step % count]

        return look

    weight = kept(
        lambda block: couple(block, total(lambda step, near: of_block(parts_ref[device(step), 0], near), block))
    )
    weights = kept(lambda step: joined([weight(step + near - BEFORE) for near in range(NEAR)]))
    second = kept(lambda step: parts_ref[device(step), 1] + dot(parts_ref[device(step), 2], weights(step)))
    out_ref[pl.ds(0, LANES), :] = weights(0)
    out_ref[pl.ds(LANES, LANES), :] = joined(
        [
            couple(near - BEFORE, total(lambda step, at: of_block(second(step), at), near - BEFORE))
            for near in range(NEAR)
        ]
    )


def near_weights(me, parts, coupling):
    return pl.pallas_call(
        functools.partial(weights_kernel, lax.axis_size("band")),
        in_specs=[pl.BlockSpec(memory_space=pltpu.SMEM), WHOLE, WHOLE],
        out_specs=WHOLE,
        out_shape=jax.ShapeDtypeStruct((2 * LANES, LANES), jnp.float32),
        compiler_params=params(24),
        cost_estimate=cost(0, 8 * parts.size),
    )(me, parts, coupling)


def shifted(value, axis, step):
    count = lax.axis_size(axis)
    return lax.ppermute(value, axis, [(source, (source + step) % count) for source in range(count)])


def exchanged(values):
    return [shifted(value, "dom", step) if step else value for step, value in enumerate(values)]


def crossed(value, bit):
    return lax.ppermute(value, "band", [(source, source ^ bit) for source in range(lax.axis_size("band"))])


def gram_kernel(own_ref, *rest):
    panels, out_ref = (own_ref, *rest[:-1]), rest[-1]

    @pl.when(pl.program_id(0) == 0)
    def _():
        out_ref[...] = jnp.zeros_like(out_ref)

    for plane in range(own_ref.shape[0]):
        left = halves(own_ref[plane].T)
        both = jnp.concatenate([side_by_side(panel[plane]) for panel in panels], axis=1)
        value = dot_halves(left, both)
        for index in range(len(panels)):
            at = pl.ds(index * LANES, LANES)
            out_ref[:, at] = out_ref[:, at] + folded(value[:, 2 * index * LANES : 2 * (index + 1) * LANES])


def gram_rows(panels):
    planes, cells, _ = panels[0].shape
    tile = cells // 2
    return pl.pallas_call(
        gram_kernel,
        grid=(cells // tile,),
        in_specs=[pl.BlockSpec((planes, tile, LANES), lambda i: (0, i, 0))] * len(panels),
        out_specs=pl.BlockSpec((LANES, len(panels) * LANES), lambda i: (0, 0)),
        out_shape=jax.ShapeDtypeStruct((LANES, len(panels) * LANES), jnp.float32),
        compiler_params=params(16),
        cost_estimate=cost(8 * panels[0].size * LANES * len(panels), 4 * panels[0].size * len(panels)),
    )(*panels)


def rotate_kernel(chunks, bands, inverse_ref, *rest):
    panels, out_ref = rest[:-1], rest[-1]
    right = side_by_side(inverse_ref[...].T)
    for index, (begin, size) in enumerate(chunks):
        group = panels[index * bands : (index + 1) * bands]
        for plane in range(size):
            left = halves(jnp.concatenate([panel[plane] for panel in group], axis=1))
            out_ref[begin + plane] = folded(dot_halves(left, right))


def rotated(inverse_rows, panels, chunks):
    bands = len(panels[0])
    planes = sum(size for _, size in chunks)
    cells = panels[0][0].shape[1]
    tile = cells // 4
    specs = [pl.BlockSpec((size, tile, LANES), lambda i: (0, i, 0)) for _, size in chunks for _ in range(bands)]
    return pl.pallas_call(
        functools.partial(rotate_kernel, chunks, bands),
        grid=(cells // tile,),
        in_specs=[pl.BlockSpec(inverse_rows.shape, lambda i: (0, 0)), *specs],
        out_specs=pl.BlockSpec((planes, tile, LANES), lambda i: (0, i, 0)),
        out_shape=jax.ShapeDtypeStruct((planes, cells, LANES), jnp.float32),
        compiler_params=params(56),
    )(inverse_rows, *[panel for group in panels for panel in group])


def thirds(value):
    first = value.astype(jnp.bfloat16).astype(jnp.float32)
    rest = value - first
    second = rest.astype(jnp.bfloat16).astype(jnp.float32)
    return first, second, rest - second


def eliminate(work, result):
    sublane = lax.broadcasted_iota(jnp.int32, (GROUP, LANES), 0)

    def splat(row, column):
        return jnp.broadcast_to(row[:, column : column + 1], (GROUP, LANES))

    def load(top):
        left = [jnp.broadcast_to(work[pl.ds(top + i, 1), :LANES], (GROUP, LANES)) for i in range(GROUP)]
        right = [jnp.broadcast_to(work[pl.ds(top + i, 1), LANES:], (GROUP, LANES)) for i in range(GROUP)]
        return left, right

    def factored(top, left, right):
        entry = {(i, j): splat(left[i], top + j) for i in range(GROUP) for j in range(i, GROUP)}
        for i in range(GROUP):
            scale = lax.rsqrt(entry[i, i])
            left[i] = left[i] * scale
            right[i] = right[i] * scale
            factor = {j: entry[i, j] * scale for j in range(i + 1, GROUP)}
            for m in range(i + 1, GROUP):
                for j in range(m, GROUP):
                    entry[m, j] = entry[m, j] - factor[m] * factor[j]
                left[m] = left[m] - factor[m] * left[i]
                right[m] = right[m] - factor[m] * right[i]

    def gathered(rows):
        value = rows[0]
        for i in range(1, GROUP):
            value = jnp.where(sublane == i, rows[i], value)
        return value

    for top in range(0, LANES, 2 * GROUP):
        left, right = load(top)
        factored(top, left, right)
        middle = top + GROUP
        next_left, next_right = load(middle)
        for m in range(GROUP):
            for i in range(GROUP):
                factor = splat(left[i], middle + m)
                next_left[m] = next_left[m] - factor * left[i]
                next_right[m] = next_right[m] - factor * right[i]
        factored(middle, next_left, next_right)
        upper = jnp.concatenate([gathered(left), gathered(next_left)], axis=0)
        lower = jnp.concatenate([gathered(right), gathered(next_right)], axis=0)
        result[pl.ds(top, 2 * GROUP), :] = lower
        below = middle + GROUP
        if below < LANES:
            a, b, c = thirds(upper)
            x, y, z = thirds(lower)
            columns = jnp.concatenate([a, a, b, b, a, c], axis=0).T[below:].astype(jnp.bfloat16)
            rows = jnp.concatenate(
                [jnp.concatenate([a, b, a, b, c, a], axis=0), jnp.concatenate([x, y, x, y, z, x], axis=0)], axis=1
            ).astype(jnp.bfloat16)
            rest = pl.ds(below, LANES - below)
            work[rest, :] = work[rest, :] - jnp.dot(columns, rows, preferred_element_type=jnp.float32)


def cholesky_kernel(band_ref, *refs):
    rows_refs, (gram_ref, own_ref, matrix, work, corner, scaled) = refs[:-6], refs[-6:]
    size = gram_ref.shape[0]
    bands = len(rows_refs)
    band = band_ref[0]

    def block_of(member):
        return pl.ds(pl.multiple_of((band ^ member) * LANES, LANES), LANES)

    for member, rows_ref in enumerate(rows_refs):
        for other in range(bands):
            gram_ref[block_of(member), block_of(member ^ other)] = rows_ref[:, other * LANES : (other + 1) * LANES]
    dot = functools.partial(jnp.dot, precision=HIGHEST, preferred_element_type=jnp.float32)
    diagonal = lax.broadcasted_iota(jnp.int32, (LANES, LANES), 0) == lax.broadcasted_iota(jnp.int32, (LANES, LANES), 1)
    identity = diagonal.astype(jnp.float32)
    matrix[:, :size] = gram_ref[...]
    matrix[:, size:] = jnp.zeros((size, size), jnp.float32)
    for at in range(0, size, LANES):
        matrix[pl.ds(at, LANES), size + at : size + at + LANES] = identity

    def block(index, carry):
        start = pl.multiple_of(index * LANES, LANES)
        at = pl.ds(start, LANES)
        live = pl.ds(pl.multiple_of(start + LANES, LANES), size)
        work[:, :LANES] = matrix[at, at]
        work[:, LANES:] = identity
        eliminate(work, corner)
        scaled[...] = dot(corner[...], matrix[at, live])
        matrix[at, live] = scaled[...]

        def below(other, carry):
            rows = pl.ds(pl.multiple_of(other * LANES, LANES), LANES)
            columns = pl.ds(pl.multiple_of((other - index - 1) * LANES, LANES), LANES)
            matrix[rows, live] = matrix[rows, live] - dot(scaled[:, columns].T, scaled[...])
            return carry

        lax.fori_loop(index + 1, size // LANES, below, 0)
        return carry

    lax.fori_loop(0, size // LANES, block, 0)
    for member in range(bands):
        columns = pl.ds(pl.multiple_of(size + (band ^ member) * LANES, LANES), LANES)
        own_ref[:, member * LANES : (member + 1) * LANES] = matrix[block_of(0), columns]


def cholesky_inverse(band, rows):
    size = rows[0].shape[1]
    return pl.pallas_call(
        cholesky_kernel,
        in_specs=[pl.BlockSpec(memory_space=pltpu.SMEM)] + [WHOLE] * len(rows),
        out_specs=[WHOLE] * 2,
        out_shape=[
            jax.ShapeDtypeStruct((size, size), jnp.float32),
            jax.ShapeDtypeStruct((LANES, size), jnp.float32),
        ],
        scratch_shapes=[
            pltpu.VMEM((size, 2 * size), jnp.float32),
            pltpu.VMEM((LANES, 2 * LANES), jnp.float32),
            pltpu.VMEM((LANES, LANES), jnp.float32),
            pltpu.VMEM((LANES, size), jnp.float32),
        ],
        compiler_params=params(14),
    )(band.astype(jnp.int32).reshape(1), *rows)


def packed_projectors(projectors, atom_plane, planes):
    share = projectors.shape[0] // lax.axis_size("band")
    first = (atom_plane - lax.axis_index("dom") * planes).astype(jnp.float32)
    first = jnp.broadcast_to(first[:, None, None], (projectors.shape[0], MAXPROJ, LANES))
    packed = jnp.concatenate([projectors, first], axis=2)
    mine = lax.dynamic_slice_in_dim(packed, lax.axis_index("band") * share, share, 0)
    return mine.reshape(share * MAXPROJ, -1)


def near_shares(mine):
    return jnp.stack([mine if step == BEFORE else shifted(mine, "dom", BEFORE - step) for step in range(NEAR)])


def near_projectors(near, planes):
    across = crossed(near, 2)
    raw = [near, crossed(near, 1), across, crossed(across, 1)]
    moved = (planes * (jnp.arange(NEAR, dtype=jnp.float32) - BEFORE))[:, None]
    first = jnp.stack([member[:, :, -1] + moved for member in raw]).reshape(1, LANES)
    return raw, jnp.broadcast_to(first, (GROUP, LANES))


def shards(orbitals, potential, projectors, coupling, atom_plane, projector_count):
    planes, side_y, side_z, local_orbs = orbitals.shape
    blocks, bands = lax.axis_size("dom"), lax.axis_size("band")
    band = lax.axis_index("band")
    cells = side_y * side_z
    rows = cells // blocks
    width = local_orbs // blocks
    norb = local_orbs * bands
    chunks = tuple((plane, 1) for plane in range(planes))
    half = planes // 2
    tie = lax.optimization_barrier
    me = lax.axis_index("dom").astype(jnp.int32).reshape(1)

    order = jnp.arange(bands, dtype=jnp.int32) ^ band

    mine = packed_projectors(projectors, atom_plane, planes)
    mine, levels = lax.optimization_barrier((mine, potential.reshape(planes, cells // LANES, LANES)))
    near = near_shares(mine)
    levels = jnp.pad(levels, ((0, 0), (0, -levels.shape[1] % GROUP), (0, 0)))
    packed = swap_in(levels, orbitals.reshape(planes, blocks, rows, local_orbs))
    packed, near = lax.optimization_barrier((packed, near))
    raw, first = near_projectors(near, planes)
    arrived = lax.all_to_all(packed, "dom", 0, 0, tiled=True)

    own_levels = jnp.broadcast_to(potential.reshape(planes, cells, 1), (planes, cells, LANES))
    high, low, parts = build_basis(raw, first, own_levels, orbitals.reshape(planes, cells, LANES), side_y, side_z)
    atoms = projectors.shape[0]
    slots = jnp.arange(MAXPROJ, dtype=jnp.int32)
    live = (slots[None, :] < projector_count[:, None]).astype(jnp.float32)
    coupled = 0.5 * (coupling + jnp.transpose(coupling, (0, 2, 1))) * live[:, :, None] * live[:, None, :]
    coupled = jnp.take(coupled.reshape(bands, -1, MAXPROJ, MAXPROJ), order, axis=0)
    vectors = atoms * MAXPROJ
    row = jnp.arange(vectors, dtype=jnp.int32) // MAXPROJ
    matrix = jnp.tile(coupled.reshape(vectors, MAXPROJ), (1, atoms))
    matrix = jnp.where(row[:, None] == row[None, :], matrix, 0.0)
    matrix = jnp.pad(matrix, ((0, 0), (0, LANES - vectors)))
    payload = jnp.concatenate([parts.reshape(3 * LANES, LANES), matrix], axis=0)
    everyone = lax.all_gather(payload, "dom")
    weights = near_weights(
        me,
        everyone[:, : 3 * LANES].reshape(blocks, 3, LANES, LANES), everyone[:, 3 * LANES :, :vectors],
    )

    early, late = filter_orbitals(me, arrived, side_y, side_z, width, half)

    came = exchanged(early)
    added = spread(high, low, weights)
    owns = list(swap_out(me, came, added, 0))
    acrosses = [crossed(own, 2) for own in owns]
    besides = [crossed(own, 1) for own in owns]
    for index, packed in enumerate(late):
        if index:
            packed, coming = tie((packed, coming))
        else:
            packed, acrosses[0] = tie((packed, acrosses[0]))
        arriving = lax.all_to_all(packed, "dom", 0, 0, tiled=True)
        if index:
            owns.append(swap_out(me, [coming], added, half + index - 1)[0])
            acrosses.append(crossed(owns[-1], 2))
            besides.append(crossed(owns[-1], 1))
        coming, acrosses[index + 1] = tie((arriving, acrosses[index + 1]))
    owns.append(swap_out(me, [coming], added, planes - 1)[0])
    acrosses.append(crossed(owns[-1], 2))
    besides.append(crossed(owns[-1], 1))
    panels, part = [], None
    for index, across in enumerate(acrosses):
        if index >= half:
            across, part = tie((across, part))
        panels.append([owns[index], besides[index], across, crossed(across, 1)])
        rows_of = gram_rows(panels[-1])
        part = rows_of if part is None else part + rows_of

    pieces = lax.all_to_all(part.reshape(blocks, width, norb), "dom", 0, 0, tiled=True)
    piece = jnp.sum(pieces, axis=0) * (1.0 / (planes * cells * blocks))
    own_gram = lax.all_to_all(jnp.broadcast_to(piece, (blocks, width, norb)), "dom", 0, 0, tiled=True)
    own_gram = own_gram.reshape(local_orbs, norb)
    across = crossed(own_gram, 2)
    gram, own_rows = cholesky_inverse(band, [own_gram, crossed(own_gram, 1), across, crossed(across, 1)])
    result = rotated(own_rows, panels, chunks)
    return (result.reshape(planes, side_y, side_z, local_orbs), gram)


def solution(mesh):
    placed = (
        P("dom", None, None, "band"),
        P("dom", None, None),
        P("dom", None, None),
        P("dom", None, None),
        P("dom"),
        P("dom"),
    )
    return jax.shard_map(
        shards,
        mesh=mesh,
        in_specs=placed,
        out_specs=(P("dom", None, None, "band"), P()),
        check_vma=False,
    )
```

```python
import functools

import jax
import jax.numpy as jnp
from jax import lax
from jax.experimental import pallas as pl
from jax.experimental.pallas import tpu as pltpu
from jax.sharding import PartitionSpec as P

SPAN = 3
MAXPROJ = 4
HALO = 4
PAD = 8
LANES = 128
GROUP = 8
BEFORE, AFTER = 2, 1
NEAR = BEFORE + 1 + AFTER

center_weight = -205.0 / 72.0
side_weights = (8.0 / 5.0, -1.0 / 5.0, 8.0 / 315.0, -1.0 / 560.0)
HIGHEST = lax.Precision.HIGHEST
WHOLE = pl.BlockSpec(memory_space=pltpu.VMEM)


def params(mebibytes):
    return pltpu.CompilerParams(vmem_limit_bytes=mebibytes * 1024 * 1024)


def cost(flops, bytes_accessed):
    return pl.CostEstimate(flops=int(flops), bytes_accessed=int(bytes_accessed), transcendentals=0)


def halves(value):
    high = value.astype(jnp.bfloat16)
    return high, (value - high.astype(jnp.float32)).astype(jnp.bfloat16)


def side_by_side(value):
    return jnp.concatenate(halves(value), axis=1)


def dot_halves(left, right):
    dot = functools.partial(jnp.dot, preferred_element_type=jnp.float32)
    return dot(left[0], right) + dot(left[1], right)


def folded(value):
    return value[:, :LANES] + value[:, LANES:]


def swapped(blocks, lane, before=None, after=None):
    count = len(blocks)
    width = LANES // count

    def turned(value, at, extra):
        if extra is None:
            return pltpu.roll(value, at % count * width, 1) if at else value
        return pltpu.roll(value, lax.rem((at % count + extra) * width, LANES), 1)

    blocks = [turned(value, at, None if before is None else count - before) for at, value in enumerate(blocks)]
    bit = 1
    while bit < count:
        chosen = (lane // (bit * width)) % 2 == 1
        blocks = [jnp.where(chosen, blocks[(at + bit) % count], blocks[at]) for at in range(count)]
        bit *= 2
    return [turned(blocks[-at % count], -at, after) for at in range(count)]


def swap_into(read, write, count, rows, before=None, after=None):
    tile = 8 * max(1, 32 // count)
    lane = lax.broadcasted_iota(jnp.int32, (tile, LANES), 1)

    def step(index, carry):
        start = pl.multiple_of(index * tile, 8)
        blocks = [read(block, start, tile) for block in range(count)]
        for block, value in enumerate(swapped(blocks, lane, before, after)):
            write(block, start, tile, value)
        return carry

    lax.fori_loop(0, rows // tile, step, 0, unroll=True)


def swap_in_kernel(count, rows, levels_ref, in_ref, out_ref):
    def read(block, start, size):
        return in_ref[block, pl.ds(start, size), :]

    def write(block, start, size, value):
        out_ref[block, pl.ds(start, size), :] = value

    swap_into(read, write, count, rows)
    for block in range(count):
        out_ref[block, pl.ds(rows, levels_ref.shape[0]), :] = levels_ref[...]


def swap_in(levels, value):
    planes, count, rows, _ = value.shape
    extra = levels.shape[1]
    return pl.pallas_call(
        functools.partial(swap_in_kernel, count, rows),
        grid=(planes,),
        in_specs=[
            pl.BlockSpec((None, extra, LANES), lambda p: (p, 0, 0)),
            pl.BlockSpec((None, count, rows, LANES), lambda p: (p, 0, 0, 0)),
        ],
        out_specs=pl.BlockSpec((count, None, rows + extra, LANES), lambda p: (0, p, 0, 0)),
        out_shape=jax.ShapeDtypeStruct((count, planes, rows + extra, LANES), jnp.float32),
        compiler_params=params(12),
        cost_estimate=cost(0, 8 * value.size),
    )(levels, value)


def swap_out_kernel(planes, count, me_ref, added_ref, *refs):
    arrived_refs, out_ref = refs[:-1], refs[-1]
    rows = arrived_refs[0].shape[-2]
    by_steps = len(arrived_refs) > 1
    for plane in range(planes):

        def read(block, start, size):
            if by_steps:
                return arrived_refs[-block % count][plane, pl.ds(start, size), :]
            return arrived_refs[0][block, plane, pl.ds(start, size), :]

        def write(block, start, size, value):
            at = pl.ds(pl.multiple_of(block * rows + start, 8), size)
            out_ref[plane, at, :] = value + added_ref[plane, at, :]

        swap_into(read, write, count, rows, after=me_ref[0] if by_steps else None)


def swap_out(me, arrived, added, first_plane):
    count = len(arrived) if len(arrived) > 1 else arrived[0].shape[0]
    planes, rows = arrived[0].shape[-3:-1]
    cells = count * rows
    return pl.pallas_call(
        functools.partial(swap_out_kernel, planes, count),
        grid=(1,),
        in_specs=[
            pl.BlockSpec(memory_space=pltpu.SMEM),
            pl.BlockSpec((planes, cells, LANES), lambda i: (first_plane // planes, 0, 0)),
        ]
        + [pl.BlockSpec(arrived[0].shape, lambda i: (0,) * arrived[0].ndim)] * len(arrived),
        out_specs=pl.BlockSpec((planes, cells, LANES), lambda i: (0, 0, 0)),
        out_shape=jax.ShapeDtypeStruct((planes, cells, LANES), jnp.float32),
        compiler_params=params(24),
        cost_estimate=cost(0, 24 * cells * planes * LANES),
    )(me, added, *arrived)


def spread_kernel(high_ref, low_ref, weights_ref, out_ref):
    weights = side_by_side(weights_ref[...] * (1.0 / 18.0))
    tile = out_ref.shape[0] // 6

    def step(index, carry):
        at = pl.ds(pl.multiple_of(index * tile, 8), tile)
        out_ref[at, :] = folded(dot_halves((high_ref[at, :], low_ref[at, :]), weights))
        return carry

    lax.fori_loop(0, 6, step, 0)


def spread(high, low, weights):
    planes, cells, _ = high.shape
    basis = pl.BlockSpec((None, cells, 2 * LANES), lambda i: (i, 0, 0))
    return pl.pallas_call(
        spread_kernel,
        grid=(planes,),
        in_specs=[basis, basis, pl.BlockSpec(weights.shape, lambda i: (0, 0))],
        out_specs=pl.BlockSpec((None, cells, LANES), lambda i: (i, 0, 0)),
        out_shape=jax.ShapeDtypeStruct((planes, cells, LANES), jnp.float32),
        compiler_params=params(24),
        cost_estimate=cost(0, 8 * high.size),
    )(high, low, weights)


def fill_row(target, plane, y, row, side_z):
    target[plane, y, pl.ds(PAD, side_z), :] = row
    target[plane, y, pl.ds(PAD - HALO, HALO), :] = row[side_z - HALO :]
    target[plane, y, pl.ds(PAD + side_z, HALO), :] = row[:HALO]


def local_part(source, potential_ref, planes, first, side_y, side_z, line_of, finish):
    tile = 16

    def row(y, carry):
        for start in range(0, side_z, tile):

            def load(plane, y_at, shift):
                return source[plane, y_at, pl.ds(PAD + start + shift, tile), :]

            line = line_of(lambda plane: load(plane, y, 0))
            at = pl.ds(pl.multiple_of(y * side_z + start, 8), tile)
            for plane in range(planes):
                here = first + plane
                total = (potential_ref[plane, at, :] - 1.5 * center_weight - 7.0) * line[HALO + plane]
                for offset in range(1, HALO + 1):
                    around = line[HALO + plane + offset] + line[HALO + plane - offset]
                    around = around + (load(here, y, offset) + load(here, y, -offset))
                    up = lax.rem(y + offset, side_y)
                    down = lax.rem(y + side_y - offset, side_y)
                    around = around + (load(here, up, 0) + load(here, down, 0))
                    total = total - (0.5 * side_weights[offset - 1]) * around
                finish(plane, y, start, at, total)
        return carry

    lax.fori_loop(0, side_y, row, 0)


def filter_kernel(planes, side_y, side_z, width, half, me_ref, arrived_ref, *rest):
    near_refs, late_ref, (field, padded, first, flat, potential) = rest[:-6], rest[-6], rest[-5:]
    count = arrived_ref.shape[0]
    cells = side_y * side_z
    rows = cells // count
    tile = 16

    line = lax.broadcasted_iota(jnp.int32, (2 * count, LANES), 0) % count
    lane = lax.broadcasted_iota(jnp.int32, (2 * count, LANES), 1) // width
    spread = (line == lane).astype(jnp.bfloat16)
    for plane in range(planes):
        lines = [arrived_ref[:, plane, rows + at, :] for at in range(cells // LANES)]
        high, low = halves(jnp.concatenate(lines, axis=1))
        both = jnp.concatenate([high.astype(jnp.float32), low.astype(jnp.float32)], axis=0)
        potential[plane] = jnp.dot(both.T.astype(jnp.bfloat16), spread, preferred_element_type=jnp.float32)

    for plane in range(planes):

        def read_in(block, start, size):
            return arrived_ref[block, plane, pl.ds(start, size), :]

        def write_in(block, start, size, value):
            field[plane, pl.ds(pl.multiple_of(block * rows + start, 8), size), :] = value

        swap_into(read_in, write_in, count, rows)

    def fill(y, carry):
        for plane in range(planes):
            fill_row(padded, plane, y, field[plane, pl.ds(pl.multiple_of(y * side_z, 8), side_z), :], side_z)
        return carry

    lax.fori_loop(0, side_y, fill, 0)

    def line_of(load):
        inside = [load(plane) for plane in range(planes)]
        before = [pltpu.roll(value, width, 1) for value in inside]
        after = [pltpu.roll(value, LANES - width, 1) for value in inside]
        return before[planes - HALO :] + inside + after[:HALO]

    def finish_first(plane, y, start, at, total):
        first[plane, y, pl.ds(PAD + start, tile), :] = total
        if start == 0:
            first[plane, y, pl.ds(PAD + side_z, HALO), :] = total[:HALO]
        if start == side_z - tile:
            first[plane, y, pl.ds(PAD - HALO, HALO), :] = total[tile - HALO :]

    def finish_second(plane, y, start, at, total):
        flat[plane, at, :] = total * (1.0 / 18.0) - field[plane, at, :]

    local_part(padded, potential, planes, 0, side_y, side_z, line_of, finish_first)
    local_part(first, potential, planes, 0, side_y, side_z, line_of, finish_second)

    for plane in range(planes):

        def read_out(block, start, size):
            return flat[plane, pl.ds(pl.multiple_of(block * rows + start, 8), size), :]

        def write_out(block, start, size, value):
            if plane < half:
                near_refs[block][plane, pl.ds(start, size), :] = value
            else:
                late_ref[block, plane - half, pl.ds(start, size), :] = value

        swap_into(read_out, write_out, count, rows, before=me_ref[0] if plane < half else None)


def filter_orbitals(me, arrived, side_y, side_z, width, half):
    count, planes = arrived.shape[:2]
    rows = side_y * side_z // count
    flat = pltpu.VMEM((planes, side_y * side_z, LANES), jnp.float32)
    padded = pltpu.VMEM((planes, side_y, side_z + 2 * PAD, LANES), jnp.float32)
    shapes = [jax.ShapeDtypeStruct((half, rows, LANES), jnp.float32)] * count
    shapes += [jax.ShapeDtypeStruct((count, planes - half, rows, LANES), jnp.float32)]
    outs = pl.pallas_call(
        functools.partial(filter_kernel, planes, side_y, side_z, width, half),
        in_specs=[pl.BlockSpec(memory_space=pltpu.SMEM), WHOLE],
        out_specs=[WHOLE] * len(shapes),
        out_shape=shapes,
        scratch_shapes=[flat, padded, padded, flat, flat],
        compiler_params=params(56),
        cost_estimate=cost(100 * arrived.size, 12 * arrived.size),
    )(me, arrived)
    return list(outs[:count]), outs[count]


def basis_kernel(planes, side_y, side_z, bands, *refs):
    raw_refs = refs[:bands]
    offset_ref, potential_ref, orbitals_ref, high_ref, low_ref, parts_ref, turned, placed = refs[bands:]
    cells = side_y * side_z
    for part in range(SPAN):
        at = pl.ds(part * cells, cells)
        stack = [raw_ref[block, :, at] for raw_ref in raw_refs for block in range(NEAR)]
        turned[part] = jnp.concatenate(stack, axis=0).T
    offset = offset_ref[0:1, :]

    def place(y, carry):
        at = pl.ds(pl.multiple_of(y * side_z, 8), side_z)
        values = [turned[part, at, :] for part in range(SPAN)]
        for plane in range(planes + 2 * HALO):
            row = jnp.zeros((side_z, LANES), jnp.float32)
            for part in range(SPAN):
                row = jnp.where(offset == float(plane - HALO - part), values[part], row)
            fill_row(placed, plane, y, row, side_z)
        return carry

    lax.fori_loop(0, side_y, place, 0)

    def line_of(load):
        return [load(plane) for plane in range(planes + 2 * HALO)]

    def finish(plane, y, start, at, total):
        own = placed[HALO + plane, y, pl.ds(PAD + start, 16), :]
        high, low = halves(jnp.concatenate([total, own], axis=1))
        high_ref[plane, at, :] = high
        low_ref[plane, at, :] = low

    local_part(placed, potential_ref, planes, HALO, side_y, side_z, line_of, finish)

    dot = functools.partial(jnp.dot, preferred_element_type=jnp.float32)
    with_orbitals = with_basis = 0.0
    for plane in range(planes):
        high, low = high_ref[plane], low_ref[plane]
        left = halves(orbitals_ref[plane].T)
        with_orbitals = with_orbitals + (dot(left[0], high) + (dot(left[0], low) + dot(left[1], high)))
        own_high, own_low = high[:, LANES:], low[:, LANES:]
        turned_high = own_high.astype(jnp.float32).T.astype(jnp.bfloat16)
        turned_low = own_low.astype(jnp.float32).T.astype(jnp.bfloat16)
        both = jnp.concatenate([own_high, own_low], axis=1)
        with_basis = with_basis + (dot(turned_high, both) + dot(turned_low, both))
    parts_ref[0] = with_orbitals[:, LANES:].T
    parts_ref[1] = with_orbitals[:, :LANES].T
    parts_ref[2] = folded(with_basis)


def build_basis(raw, offset, potential, orbitals, side_y, side_z):
    planes, cells, _ = orbitals.shape
    pair = jax.ShapeDtypeStruct((planes, cells, 2 * LANES), jnp.bfloat16)
    return pl.pallas_call(
        functools.partial(basis_kernel, planes, side_y, side_z, len(raw)),
        in_specs=[WHOLE] * (len(raw) + 3),
        out_specs=[WHOLE] * 3,
        out_shape=[pair, pair, jax.ShapeDtypeStruct((3, LANES, LANES), jnp.float32)],
        scratch_shapes=[
            pltpu.VMEM((SPAN, cells, LANES), jnp.float32),
            pltpu.VMEM((planes + 2 * HALO, side_y, side_z + 2 * PAD, LANES), jnp.float32),
        ],
        compiler_params=params(56),
        cost_estimate=cost(200 * orbitals.size, 24 * orbitals.size),
    )(*raw, offset, potential, orbitals)


def weights_kernel(bands, me_ref, parts_ref, coupling_ref, out_ref):
    count = parts_ref.shape[0]
    size = LANES // NEAR
    lines = size // bands
    me = me_ref[0]
    dot = functools.partial(jnp.dot, precision=HIGHEST, preferred_element_type=jnp.float32)

    def device(step):
        return lax.rem(me + step % count, count)

    def total(pick, block):
        shares = [pick(block - (near - BEFORE), near) for near in range(NEAR)]
        return (shares[0] + shares[1]) + (shares[2] + shares[3])

    def of_block(value, near):
        starts = [(band * NEAR + near) * lines for band in range(bands)]
        return jnp.concatenate([value[start : start + lines] for start in starts], axis=0)

    def joined(values):
        return jnp.concatenate(
            [values[near][band * lines : (band + 1) * lines] for band in range(bands) for near in range(NEAR)], axis=0
        )

    def couple(block, value):
        return dot(coupling_ref[device(block)], value)

    def kept(function):
        known = {}

        def look(step):
            if step % count not in known:
                known[step % count] = function(step)
            return known[step % count]

        return look

    weight = kept(
        lambda block: couple(block, total(lambda step, near: of_block(parts_ref[device(step), 0], near), block))
    )
    weights = kept(lambda step: joined([weight(step + near - BEFORE) for near in range(NEAR)]))
    second = kept(lambda step: parts_ref[device(step), 1] + dot(parts_ref[device(step), 2], weights(step)))
    out_ref[pl.ds(0, LANES), :] = weights(0)
    out_ref[pl.ds(LANES, LANES), :] = joined(
        [
            couple(near - BEFORE, total(lambda step, at: of_block(second(step), at), near - BEFORE))
            for near in range(NEAR)
        ]
    )


def near_weights(me, parts, coupling):
    return pl.pallas_call(
        functools.partial(weights_kernel, lax.axis_size("band")),
        in_specs=[pl.BlockSpec(memory_space=pltpu.SMEM), WHOLE, WHOLE],
        out_specs=WHOLE,
        out_shape=jax.ShapeDtypeStruct((2 * LANES, LANES), jnp.float32),
        compiler_params=params(24),
        cost_estimate=cost(0, 8 * parts.size),
    )(me, parts, coupling)


def shifted(value, axis, step):
    count = lax.axis_size(axis)
    return lax.ppermute(value, axis, [(source, (source + step) % count) for source in range(count)])


def exchanged(values):
    return [shifted(value, "dom", step) if step else value for step, value in enumerate(values)]


def crossed(value, bit):
    return lax.ppermute(value, "band", [(source, source ^ bit) for source in range(lax.axis_size("band"))])


def gram_kernel(own_ref, *rest):
    panels, out_ref = (own_ref, *rest[:-1]), rest[-1]

    @pl.when(pl.program_id(0) == 0)
    def _():
        out_ref[...] = jnp.zeros_like(out_ref)

    for plane in range(own_ref.shape[0]):
        left = halves(own_ref[plane].T)
        both = jnp.concatenate([side_by_side(panel[plane]) for panel in panels], axis=1)
        value = dot_halves(left, both)
        for index in range(len(panels)):
            at = pl.ds(index * LANES, LANES)
            out_ref[:, at] = out_ref[:, at] + folded(value[:, 2 * index * LANES : 2 * (index + 1) * LANES])


def gram_rows(panels):
    planes, cells, _ = panels[0].shape
    tile = cells // 2
    return pl.pallas_call(
        gram_kernel,
        grid=(cells // tile,),
        in_specs=[pl.BlockSpec((planes, tile, LANES), lambda i: (0, i, 0))] * len(panels),
        out_specs=pl.BlockSpec((LANES, len(panels) * LANES), lambda i: (0, 0)),
        out_shape=jax.ShapeDtypeStruct((LANES, len(panels) * LANES), jnp.float32),
        compiler_params=params(16),
        cost_estimate=cost(8 * panels[0].size * LANES * len(panels), 4 * panels[0].size * len(panels)),
    )(*panels)


def rotate_kernel(chunks, bands, inverse_ref, *rest):
    panels, out_ref = rest[:-1], rest[-1]
    right = side_by_side(inverse_ref[...].T)
    for index, (begin, size) in enumerate(chunks):
        group = panels[index * bands : (index + 1) * bands]
        for plane in range(size):
            left = halves(jnp.concatenate([panel[plane] for panel in group], axis=1))
            out_ref[begin + plane] = folded(dot_halves(left, right))


def rotated(inverse_rows, panels, chunks):
    bands = len(panels[0])
    planes = sum(size for _, size in chunks)
    cells = panels[0][0].shape[1]
    tile = cells // 4
    specs = [pl.BlockSpec((size, tile, LANES), lambda i: (0, i, 0)) for _, size in chunks for _ in range(bands)]
    return pl.pallas_call(
        functools.partial(rotate_kernel, chunks, bands),
        grid=(cells // tile,),
        in_specs=[pl.BlockSpec(inverse_rows.shape, lambda i: (0, 0)), *specs],
        out_specs=pl.BlockSpec((planes, tile, LANES), lambda i: (0, i, 0)),
        out_shape=jax.ShapeDtypeStruct((planes, cells, LANES), jnp.float32),
        compiler_params=params(56),
    )(inverse_rows, *[panel for group in panels for panel in group])


def thirds(value):
    first = value.astype(jnp.bfloat16).astype(jnp.float32)
    rest = value - first
    second = rest.astype(jnp.bfloat16).astype(jnp.float32)
    return first, second, rest - second


def eliminate(work, result):
    sublane = lax.broadcasted_iota(jnp.int32, (GROUP, LANES), 0)

    def splat(row, column):
        return jnp.broadcast_to(row[:, column : column + 1], (GROUP, LANES))

    def load(top):
        left = [jnp.broadcast_to(work[pl.ds(top + i, 1), :LANES], (GROUP, LANES)) for i in range(GROUP)]
        right = [jnp.broadcast_to(work[pl.ds(top + i, 1), LANES:], (GROUP, LANES)) for i in range(GROUP)]
        return left, right

    def factored(top, left, right):
        entry = {(i, j): splat(left[i], top + j) for i in range(GROUP) for j in range(i, GROUP)}
        for i in range(GROUP):
            scale = lax.rsqrt(entry[i, i])
            left[i] = left[i] * scale
            right[i] = right[i] * scale
            factor = {j: entry[i, j] * scale for j in range(i + 1, GROUP)}
            for m in range(i + 1, GROUP):
                for j in range(m, GROUP):
                    entry[m, j] = entry[m, j] - factor[m] * factor[j]
                left[m] = left[m] - factor[m] * left[i]
                right[m] = right[m] - factor[m] * right[i]

    def gathered(rows):
        value = rows[0]
        for i in range(1, GROUP):
            value = jnp.where(sublane == i, rows[i], value)
        return value

    for top in range(0, LANES, 2 * GROUP):
        left, right = load(top)
        factored(top, left, right)
        middle = top + GROUP
        next_left, next_right = load(middle)
        for m in range(GROUP):
            for i in range(GROUP):
                factor = splat(left[i], middle + m)
                next_left[m] = next_left[m] - factor * left[i]
                next_right[m] = next_right[m] - factor * right[i]
        factored(middle, next_left, next_right)
        upper = jnp.concatenate([gathered(left), gathered(next_left)], axis=0)
        lower = jnp.concatenate([gathered(right), gathered(next_right)], axis=0)
        result[pl.ds(top, 2 * GROUP), :] = lower
        below = middle + GROUP
        if below < LANES:
            a, b, c = thirds(upper)
            x, y, z = thirds(lower)
            columns = jnp.concatenate([a, a, b, b, a, c], axis=0).T[below:].astype(jnp.bfloat16)
            rows = jnp.concatenate(
                [jnp.concatenate([a, b, a, b, c, a], axis=0), jnp.concatenate([x, y, x, y, z, x], axis=0)], axis=1
            ).astype(jnp.bfloat16)
            rest = pl.ds(below, LANES - below)
            work[rest, :] = work[rest, :] - jnp.dot(columns, rows, preferred_element_type=jnp.float32)


def cholesky_kernel(band_ref, *refs):
    rows_refs, (gram_ref, own_ref, matrix, work, corner, scaled) = refs[:-6], refs[-6:]
    size = gram_ref.shape[0]
    bands = len(rows_refs)
    band = band_ref[0]

    def block_of(member):
        return pl.ds(pl.multiple_of((band ^ member) * LANES, LANES), LANES)

    for member, rows_ref in enumerate(rows_refs):
        for other in range(bands):
            gram_ref[block_of(member), block_of(member ^ other)] = rows_ref[:, other * LANES : (other + 1) * LANES]
    dot = functools.partial(jnp.dot, precision=HIGHEST, preferred_element_type=jnp.float32)
    diagonal = lax.broadcasted_iota(jnp.int32, (LANES, LANES), 0) == lax.broadcasted_iota(jnp.int32, (LANES, LANES), 1)
    identity = diagonal.astype(jnp.float32)
    matrix[:, :size] = gram_ref[...]
    matrix[:, size:] = jnp.zeros((size, size), jnp.float32)
    for at in range(0, size, LANES):
        matrix[pl.ds(at, LANES), size + at : size + at + LANES] = identity

    def block(index, carry):
        start = pl.multiple_of(index * LANES, LANES)
        at = pl.ds(start, LANES)
        live = pl.ds(pl.multiple_of(start + LANES, LANES), size)
        work[:, :LANES] = matrix[at, at]
        work[:, LANES:] = identity
        eliminate(work, corner)
        scaled[...] = dot(corner[...], matrix[at, live])
        matrix[at, live] = scaled[...]

        def below(other, carry):
            rows = pl.ds(pl.multiple_of(other * LANES, LANES), LANES)
            columns = pl.ds(pl.multiple_of((other - index - 1) * LANES, LANES), LANES)
            matrix[rows, live] = matrix[rows, live] - dot(scaled[:, columns].T, scaled[...])
            return carry

        lax.fori_loop(index + 1, size // LANES, below, 0)
        return carry

    lax.fori_loop(0, size // LANES, block, 0)
    for member in range(bands):
        columns = pl.ds(pl.multiple_of(size + (band ^ member) * LANES, LANES), LANES)
        own_ref[:, member * LANES : (member + 1) * LANES] = matrix[block_of(0), columns]


def cholesky_inverse(band, rows):
    size = rows[0].shape[1]
    return pl.pallas_call(
        cholesky_kernel,
        in_specs=[pl.BlockSpec(memory_space=pltpu.SMEM)] + [WHOLE] * len(rows),
        out_specs=[WHOLE] * 2,
        out_shape=[
            jax.ShapeDtypeStruct((size, size), jnp.float32),
            jax.ShapeDtypeStruct((LANES, size), jnp.float32),
        ],
        scratch_shapes=[
            pltpu.VMEM((size, 2 * size), jnp.float32),
            pltpu.VMEM((LANES, 2 * LANES), jnp.float32),
            pltpu.VMEM((LANES, LANES), jnp.float32),
            pltpu.VMEM((LANES, size), jnp.float32),
        ],
        compiler_params=params(14),
    )(band.astype(jnp.int32).reshape(1), *rows)


def packed_projectors(projectors, atom_plane, planes):
    share = projectors.shape[0] // lax.axis_size("band")
    first = (atom_plane - lax.axis_index("dom") * planes).astype(jnp.float32)
    first = jnp.broadcast_to(first[:, None, None], (projectors.shape[0], MAXPROJ, LANES))
    packed = jnp.concatenate([projectors, first], axis=2)
    mine = lax.dynamic_slice_in_dim(packed, lax.axis_index("band") * share, share, 0)
    return mine.reshape(share * MAXPROJ, -1)


def near_shares(mine):
    return jnp.stack([mine if step == BEFORE else shifted(mine, "dom", BEFORE - step) for step in range(NEAR)])


def near_projectors(near, planes):
    across = crossed(near, 2)
    raw = [near, crossed(near, 1), across, crossed(across, 1)]
    moved = (planes * (jnp.arange(NEAR, dtype=jnp.float32) - BEFORE))[:, None]
    first = jnp.stack([member[:, :, -1] + moved for member in raw]).reshape(1, LANES)
    return raw, jnp.broadcast_to(first, (GROUP, LANES))


def shards(orbitals, potential, projectors, coupling, atom_plane, projector_count):
    planes, side_y, side_z, local_orbs = orbitals.shape
    blocks, bands = lax.axis_size("dom"), lax.axis_size("band")
    band = lax.axis_index("band")
    cells = side_y * side_z
    rows = cells // blocks
    width = local_orbs // blocks
    norb = local_orbs * bands
    half = planes // 2
    chunks = ((0, half), (half, half))
    tie = lax.optimization_barrier
    me = lax.axis_index("dom").astype(jnp.int32).reshape(1)

    order = jnp.arange(bands, dtype=jnp.int32) ^ band

    mine = packed_projectors(projectors, atom_plane, planes)
    mine, levels = lax.optimization_barrier((mine, potential.reshape(planes, cells // LANES, LANES)))
    near = near_shares(mine)
    levels = jnp.pad(levels, ((0, 0), (0, -levels.shape[1] % GROUP), (0, 0)))
    packed = swap_in(levels, orbitals.reshape(planes, blocks, rows, local_orbs))
    packed, near = lax.optimization_barrier((packed, near))
    raw, first = near_projectors(near, planes)
    arrived = lax.all_to_all(packed, "dom", 0, 0, tiled=True)

    own_levels = jnp.broadcast_to(potential.reshape(planes, cells, 1), (planes, cells, LANES))
    high, low, parts = build_basis(raw, first, own_levels, orbitals.reshape(planes, cells, LANES), side_y, side_z)
    atoms = projectors.shape[0]
    slots = jnp.arange(MAXPROJ, dtype=jnp.int32)
    live = (slots[None, :] < projector_count[:, None]).astype(jnp.float32)
    coupled = 0.5 * (coupling + jnp.transpose(coupling, (0, 2, 1))) * live[:, :, None] * live[:, None, :]
    coupled = jnp.take(coupled.reshape(bands, -1, MAXPROJ, MAXPROJ), order, axis=0)
    vectors = atoms * MAXPROJ
    row = jnp.arange(vectors, dtype=jnp.int32) // MAXPROJ
    matrix = jnp.tile(coupled.reshape(vectors, MAXPROJ), (1, atoms))
    matrix = jnp.where(row[:, None] == row[None, :], matrix, 0.0)
    matrix = jnp.pad(matrix, ((0, 0), (0, LANES - vectors)))
    payload = jnp.concatenate([parts.reshape(3 * LANES, LANES), matrix], axis=0)
    everyone = lax.all_gather(payload, "dom")
    weights = near_weights(
        me,
        everyone[:, : 3 * LANES].reshape(blocks, 3, LANES, LANES), everyone[:, 3 * LANES :, :vectors],
    )

    early, late = filter_orbitals(me, arrived, side_y, side_z, width, half)

    came = exchanged(early)
    added = spread(high, low, weights)
    own = swap_out(me, came, added, 0)
    late, own = tie((late, own))
    coming = lax.all_to_all(late, "dom", 0, 0, tiled=True)
    across, beside = crossed(own, 2), crossed(own, 1)
    last = swap_out(me, [coming], added, half)
    across, last = tie((across, last))
    panels = [[own, beside, across, crossed(across, 1)]]
    part = gram_rows(panels[0])
    across, beside = crossed(last, 2), crossed(last, 1)
    across, part = tie((across, part))
    panels.append([last, beside, across, crossed(across, 1)])
    part = part + gram_rows(panels[1])

    pieces = lax.all_to_all(part.reshape(blocks, width, norb), "dom", 0, 0, tiled=True)
    piece = jnp.sum(pieces, axis=0) * (1.0 / (planes * cells * blocks))
    own_gram = lax.all_to_all(jnp.broadcast_to(piece, (blocks, width, norb)), "dom", 0, 0, tiled=True)
    own_gram = own_gram.reshape(local_orbs, norb)
    across = crossed(own_gram, 2)
    gram, own_rows = cholesky_inverse(band, [own_gram, crossed(own_gram, 1), across, crossed(across, 1)])
    result = rotated(own_rows, panels, chunks)
    return (result.reshape(planes, side_y, side_z, local_orbs), gram)


def solution(mesh):
    placed = (
        P("dom", None, None, "band"),
        P("dom", None, None),
        P("dom", None, None),
        P("dom", None, None),
        P("dom"),
        P("dom"),
    )
    return jax.shard_map(
        shards,
        mesh=mesh,
        in_specs=placed,
        out_specs=(P("dom", None, None, "band"), P()),
        check_vma=False,
    )
```

```python
import functools

import jax
import jax.numpy as jnp
from jax import lax
from jax.experimental import pallas as pl
from jax.experimental.pallas import tpu as pltpu
from jax.sharding import PartitionSpec as P

SPAN = 3
MAXPROJ = 4
HALO = 4
PAD = 8
LANES = 128
GROUP = 8
BEFORE, AFTER = 2, 1
NEAR = BEFORE + 1 + AFTER

center_weight = -205.0 / 72.0
side_weights = (8.0 / 5.0, -1.0 / 5.0, 8.0 / 315.0, -1.0 / 560.0)
HIGHEST = lax.Precision.HIGHEST
WHOLE = pl.BlockSpec(memory_space=pltpu.VMEM)


def params(mebibytes):
    return pltpu.CompilerParams(vmem_limit_bytes=mebibytes * 1024 * 1024)


def cost(flops, bytes_accessed):
    return pl.CostEstimate(flops=int(flops), bytes_accessed=int(bytes_accessed), transcendentals=0)


def halves(value):
    high = value.astype(jnp.bfloat16)
    return high, (value - high.astype(jnp.float32)).astype(jnp.bfloat16)


def side_by_side(value):
    return jnp.concatenate(halves(value), axis=1)


def dot_halves(left, right):
    dot = functools.partial(jnp.dot, preferred_element_type=jnp.float32)
    return dot(left[0], right) + dot(left[1], right)


def folded(value):
    return value[:, :LANES] + value[:, LANES:]


def swapped(blocks, lane, before=None, after=None):
    count = len(blocks)
    width = LANES // count

    def turned(value, at, extra):
        if extra is None:
            return pltpu.roll(value, at % count * width, 1) if at else value
        return pltpu.roll(value, lax.rem((at % count + extra) * width, LANES), 1)

    blocks = [turned(value, at, None if before is None else count - before) for at, value in enumerate(blocks)]
    bit = 1
    while bit < count:
        chosen = (lane // (bit * width)) % 2 == 1
        blocks = [jnp.where(chosen, blocks[(at + bit) % count], blocks[at]) for at in range(count)]
        bit *= 2
    return [turned(blocks[-at % count], -at, after) for at in range(count)]


def swap_into(read, write, count, rows, before=None, after=None):
    tile = 8 * max(1, 32 // count)
    lane = lax.broadcasted_iota(jnp.int32, (tile, LANES), 1)

    def step(index, carry):
        start = pl.multiple_of(index * tile, 8)
        blocks = [read(block, start, tile) for block in range(count)]
        for block, value in enumerate(swapped(blocks, lane, before, after)):
            write(block, start, tile, value)
        return carry

    lax.fori_loop(0, rows // tile, step, 0, unroll=True)


def swap_in_kernel(count, rows, levels_ref, in_ref, out_ref):
    def read(block, start, size):
        return in_ref[block, pl.ds(start, size), :]

    def write(block, start, size, value):
        out_ref[block, pl.ds(start, size), :] = value

    swap_into(read, write, count, rows)
    for block in range(count):
        out_ref[block, pl.ds(rows, levels_ref.shape[0]), :] = levels_ref[...]


def swap_in(levels, value):
    planes, count, rows, _ = value.shape
    extra = levels.shape[1]
    return pl.pallas_call(
        functools.partial(swap_in_kernel, count, rows),
        grid=(planes,),
        in_specs=[
            pl.BlockSpec((None, extra, LANES), lambda p: (p, 0, 0)),
            pl.BlockSpec((None, count, rows, LANES), lambda p: (p, 0, 0, 0)),
        ],
        out_specs=pl.BlockSpec((count, None, rows + extra, LANES), lambda p: (0, p, 0, 0)),
        out_shape=jax.ShapeDtypeStruct((count, planes, rows + extra, LANES), jnp.float32),
        compiler_params=params(12),
        cost_estimate=cost(0, 8 * value.size),
    )(levels, value)


def swap_out_kernel(planes, count, me_ref, added_ref, *refs):
    arrived_refs, out_ref = refs[:-1], refs[-1]
    rows = arrived_refs[0].shape[-2]
    by_steps = len(arrived_refs) > 1
    for plane in range(planes):

        def read(block, start, size):
            if by_steps:
                return arrived_refs[-block % count][plane, pl.ds(start, size), :]
            return arrived_refs[0][block, plane, pl.ds(start, size), :]

        def write(block, start, size, value):
            at = pl.ds(pl.multiple_of(block * rows + start, 8), size)
            out_ref[plane, at, :] = value + added_ref[plane, at, :]

        swap_into(read, write, count, rows, after=me_ref[0] if by_steps else None)


def swap_out(me, arrived, added, first_plane):
    count = len(arrived) if len(arrived) > 1 else arrived[0].shape[0]
    planes, rows = arrived[0].shape[-3:-1]
    cells = count * rows
    return pl.pallas_call(
        functools.partial(swap_out_kernel, planes, count),
        grid=(1,),
        in_specs=[
            pl.BlockSpec(memory_space=pltpu.SMEM),
            pl.BlockSpec((planes, cells, LANES), lambda i: (first_plane // planes, 0, 0)),
        ]
        + [pl.BlockSpec(arrived[0].shape, lambda i: (0,) * arrived[0].ndim)] * len(arrived),
        out_specs=pl.BlockSpec((planes, cells, LANES), lambda i: (0, 0, 0)),
        out_shape=jax.ShapeDtypeStruct((planes, cells, LANES), jnp.float32),
        compiler_params=params(24),
        cost_estimate=cost(0, 24 * cells * planes * LANES),
    )(me, added, *arrived)


def spread_kernel(high_ref, low_ref, weights_ref, out_ref):
    weights = side_by_side(weights_ref[...] * (1.0 / 18.0))
    tile = out_ref.shape[0] // 6

    def step(index, carry):
        at = pl.ds(pl.multiple_of(index * tile, 8), tile)
        out_ref[at, :] = folded(dot_halves((high_ref[at, :], low_ref[at, :]), weights))
        return carry

    lax.fori_loop(0, 6, step, 0)


def spread(high, low, weights):
    planes, cells, _ = high.shape
    basis = pl.BlockSpec((None, cells, 2 * LANES), lambda i: (i, 0, 0))
    return pl.pallas_call(
        spread_kernel,
        grid=(planes,),
        in_specs=[basis, basis, pl.BlockSpec(weights.shape, lambda i: (0, 0))],
        out_specs=pl.BlockSpec((None, cells, LANES), lambda i: (i, 0, 0)),
        out_shape=jax.ShapeDtypeStruct((planes, cells, LANES), jnp.float32),
        compiler_params=params(24),
        cost_estimate=cost(0, 8 * high.size),
    )(high, low, weights)


def fill_row(target, plane, y, row, side_z):
    target[plane, y, pl.ds(PAD, side_z), :] = row
    target[plane, y, pl.ds(PAD - HALO, HALO), :] = row[side_z - HALO :]
    target[plane, y, pl.ds(PAD + side_z, HALO), :] = row[:HALO]


def local_part(source, potential_ref, planes, first, side_y, side_z, line_of, finish):
    tile = 16

    def row(y, carry):
        for start in range(0, side_z, tile):

            def load(plane, y_at, shift):
                return source[plane, y_at, pl.ds(PAD + start + shift, tile), :]

            line = line_of(lambda plane: load(plane, y, 0))
            at = pl.ds(pl.multiple_of(y * side_z + start, 8), tile)
            for plane in range(planes):
                here = first + plane
                total = (potential_ref[plane, at, :] - 1.5 * center_weight - 7.0) * line[HALO + plane]
                for offset in range(1, HALO + 1):
                    around = line[HALO + plane + offset] + line[HALO + plane - offset]
                    around = around + (load(here, y, offset) + load(here, y, -offset))
                    up = lax.rem(y + offset, side_y)
                    down = lax.rem(y + side_y - offset, side_y)
                    around = around + (load(here, up, 0) + load(here, down, 0))
                    total = total - (0.5 * side_weights[offset - 1]) * around
                finish(plane, y, start, at, total)
        return carry

    lax.fori_loop(0, side_y, row, 0)


def filter_kernel(planes, side_y, side_z, width, half, me_ref, arrived_ref, *rest):
    near_refs, late_ref, (field, padded, first, flat, potential) = rest[:-6], rest[-6], rest[-5:]
    count = arrived_ref.shape[0]
    cells = side_y * side_z
    rows = cells // count
    tile = 16

    line = lax.broadcasted_iota(jnp.int32, (2 * count, LANES), 0) % count
    lane = lax.broadcasted_iota(jnp.int32, (2 * count, LANES), 1) // width
    spread = (line == lane).astype(jnp.bfloat16)
    for plane in range(planes):
        lines = [arrived_ref[:, plane, rows + at, :] for at in range(cells // LANES)]
        high, low = halves(jnp.concatenate(lines, axis=1))
        both = jnp.concatenate([high.astype(jnp.float32), low.astype(jnp.float32)], axis=0)
        potential[plane] = jnp.dot(both.T.astype(jnp.bfloat16), spread, preferred_element_type=jnp.float32)

    for plane in range(planes):

        def read_in(block, start, size):
            return arrived_ref[block, plane, pl.ds(start, size), :]

        def write_in(block, start, size, value):
            field[plane, pl.ds(pl.multiple_of(block * rows + start, 8), size), :] = value

        swap_into(read_in, write_in, count, rows)

    def fill(y, carry):
        for plane in range(planes):
            fill_row(padded, plane, y, field[plane, pl.ds(pl.multiple_of(y * side_z, 8), side_z), :], side_z)
        return carry

    lax.fori_loop(0, side_y, fill, 0)

    def line_of(load):
        inside = [load(plane) for plane in range(planes)]
        before = [pltpu.roll(value, width, 1) for value in inside]
        after = [pltpu.roll(value, LANES - width, 1) for value in inside]
        return before[planes - HALO :] + inside + after[:HALO]

    def finish_first(plane, y, start, at, total):
        first[plane, y, pl.ds(PAD + start, tile), :] = total
        if start == 0:
            first[plane, y, pl.ds(PAD + side_z, HALO), :] = total[:HALO]
        if start == side_z - tile:
            first[plane, y, pl.ds(PAD - HALO, HALO), :] = total[tile - HALO :]

    def finish_second(plane, y, start, at, total):
        flat[plane, at, :] = total * (1.0 / 18.0) - field[plane, at, :]

    local_part(padded, potential, planes, 0, side_y, side_z, line_of, finish_first)
    local_part(first, potential, planes, 0, side_y, side_z, line_of, finish_second)

    for plane in range(planes):

        def read_out(block, start, size):
            return flat[plane, pl.ds(pl.multiple_of(block * rows + start, 8), size), :]

        def write_out(block, start, size, value):
            if plane < half:
                near_refs[block][plane, pl.ds(start, size), :] = value
            else:
                late_ref[block, plane - half, pl.ds(start, size), :] = value

        swap_into(read_out, write_out, count, rows, before=me_ref[0] if plane < half else None)


def filter_orbitals(me, arrived, side_y, side_z, width, half):
    count, planes = arrived.shape[:2]
    rows = side_y * side_z // count
    flat = pltpu.VMEM((planes, side_y * side_z, LANES), jnp.float32)
    padded = pltpu.VMEM((planes, side_y, side_z + 2 * PAD, LANES), jnp.float32)
    shapes = [jax.ShapeDtypeStruct((half, rows, LANES), jnp.float32)] * count
    shapes += [jax.ShapeDtypeStruct((count, planes - half, rows, LANES), jnp.float32)]
    outs = pl.pallas_call(
        functools.partial(filter_kernel, planes, side_y, side_z, width, half),
        in_specs=[pl.BlockSpec(memory_space=pltpu.SMEM), WHOLE],
        out_specs=[WHOLE] * len(shapes),
        out_shape=shapes,
        scratch_shapes=[flat, padded, padded, flat, flat],
        compiler_params=params(56),
        cost_estimate=cost(100 * arrived.size, 12 * arrived.size),
    )(me, arrived)
    return list(outs[:count]), outs[count]


def basis_kernel(planes, side_y, side_z, bands, *refs):
    raw_refs = refs[:bands]
    offset_ref, potential_ref, orbitals_ref, high_ref, low_ref, parts_ref, turned, placed = refs[bands:]
    cells = side_y * side_z
    for part in range(SPAN):
        at = pl.ds(part * cells, cells)
        stack = [raw_ref[block, :, at] for raw_ref in raw_refs for block in range(NEAR)]
        turned[part] = jnp.concatenate(stack, axis=0).T
    offset = offset_ref[0:1, :]

    def place(y, carry):
        at = pl.ds(pl.multiple_of(y * side_z, 8), side_z)
        values = [turned[part, at, :] for part in range(SPAN)]
        for plane in range(planes + 2 * HALO):
            row = jnp.zeros((side_z, LANES), jnp.float32)
            for part in range(SPAN):
                row = jnp.where(offset == float(plane - HALO - part), values[part], row)
            fill_row(placed, plane, y, row, side_z)
        return carry

    lax.fori_loop(0, side_y, place, 0)

    def line_of(load):
        return [load(plane) for plane in range(planes + 2 * HALO)]

    def finish(plane, y, start, at, total):
        own = placed[HALO + plane, y, pl.ds(PAD + start, 16), :]
        high, low = halves(jnp.concatenate([total, own], axis=1))
        high_ref[plane, at, :] = high
        low_ref[plane, at, :] = low

    local_part(placed, potential_ref, planes, HALO, side_y, side_z, line_of, finish)

    dot = functools.partial(jnp.dot, preferred_element_type=jnp.float32)
    with_orbitals = with_basis = 0.0
    for plane in range(planes):
        high, low = high_ref[plane], low_ref[plane]
        left = halves(orbitals_ref[plane].T)
        with_orbitals = with_orbitals + (dot(left[0], high) + (dot(left[0], low) + dot(left[1], high)))
        own_high, own_low = high[:, LANES:], low[:, LANES:]
        turned_high = own_high.astype(jnp.float32).T.astype(jnp.bfloat16)
        turned_low = own_low.astype(jnp.float32).T.astype(jnp.bfloat16)
        both = jnp.concatenate([own_high, own_low], axis=1)
        with_basis = with_basis + (dot(turned_high, both) + dot(turned_low, both))
    parts_ref[0] = with_orbitals[:, LANES:].T
    parts_ref[1] = with_orbitals[:, :LANES].T
    parts_ref[2] = folded(with_basis)


def build_basis(raw, offset, potential, orbitals, side_y, side_z):
    planes, cells, _ = orbitals.shape
    pair = jax.ShapeDtypeStruct((planes, cells, 2 * LANES), jnp.bfloat16)
    return pl.pallas_call(
        functools.partial(basis_kernel, planes, side_y, side_z, len(raw)),
        in_specs=[WHOLE] * (len(raw) + 3),
        out_specs=[WHOLE] * 3,
        out_shape=[pair, pair, jax.ShapeDtypeStruct((3, LANES, LANES), jnp.float32)],
        scratch_shapes=[
            pltpu.VMEM((SPAN, cells, LANES), jnp.float32),
            pltpu.VMEM((planes + 2 * HALO, side_y, side_z + 2 * PAD, LANES), jnp.float32),
        ],
        compiler_params=params(56),
        cost_estimate=cost(200 * orbitals.size, 24 * orbitals.size),
    )(*raw, offset, potential, orbitals)


def weights_kernel(bands, me_ref, parts_ref, coupling_ref, out_ref):
    count = parts_ref.shape[0]
    size = LANES // NEAR
    lines = size // bands
    me = me_ref[0]
    dot = functools.partial(jnp.dot, precision=HIGHEST, preferred_element_type=jnp.float32)

    def device(step):
        return lax.rem(me + step % count, count)

    def total(pick, block):
        shares = [pick(block - (near - BEFORE), near) for near in range(NEAR)]
        return (shares[0] + shares[1]) + (shares[2] + shares[3])

    def of_block(value, near):
        starts = [(band * NEAR + near) * lines for band in range(bands)]
        return jnp.concatenate([value[start : start + lines] for start in starts], axis=0)

    def joined(values):
        return jnp.concatenate(
            [values[near][band * lines : (band + 1) * lines] for band in range(bands) for near in range(NEAR)], axis=0
        )

    def couple(block, value):
        return dot(coupling_ref[device(block)], value)

    def kept(function):
        known = {}

        def look(step):
            if step % count not in known:
                known[step % count] = function(step)
            return known[step % count]

        return look

    weight = kept(
        lambda block: couple(block, total(lambda step, near: of_block(parts_ref[device(step), 0], near), block))
    )
    weights = kept(lambda step: joined([weight(step + near - BEFORE) for near in range(NEAR)]))
    second = kept(lambda step: parts_ref[device(step), 1] + dot(parts_ref[device(step), 2], weights(step)))
    out_ref[pl.ds(0, LANES), :] = weights(0)
    out_ref[pl.ds(LANES, LANES), :] = joined(
        [
            couple(near - BEFORE, total(lambda step, at: of_block(second(step), at), near - BEFORE))
            for near in range(NEAR)
        ]
    )


def near_weights(me, parts, coupling):
    return pl.pallas_call(
        functools.partial(weights_kernel, lax.axis_size("band")),
        in_specs=[pl.BlockSpec(memory_space=pltpu.SMEM), WHOLE, WHOLE],
        out_specs=WHOLE,
        out_shape=jax.ShapeDtypeStruct((2 * LANES, LANES), jnp.float32),
        compiler_params=params(24),
        cost_estimate=cost(0, 8 * parts.size),
    )(me, parts, coupling)


def shifted(value, axis, step):
    count = lax.axis_size(axis)
    return lax.ppermute(value, axis, [(source, (source + step) % count) for source in range(count)])


def exchanged(values):
    return [shifted(value, "dom", step) if step else value for step, value in enumerate(values)]


def crossed(value, bit):
    return lax.ppermute(value, "band", [(source, source ^ bit) for source in range(lax.axis_size("band"))])


def gram_kernel(own_ref, *rest):
    panels, out_ref = (own_ref, *rest[:-1]), rest[-1]

    @pl.when(pl.program_id(0) == 0)
    def _():
        out_ref[...] = jnp.zeros_like(out_ref)

    for plane in range(own_ref.shape[0]):
        left = halves(own_ref[plane].T)
        both = jnp.concatenate([side_by_side(panel[plane]) for panel in panels], axis=1)
        value = dot_halves(left, both)
        for index in range(len(panels)):
            at = pl.ds(index * LANES, LANES)
            out_ref[:, at] = out_ref[:, at] + folded(value[:, 2 * index * LANES : 2 * (index + 1) * LANES])


def gram_rows(panels):
    planes, cells, _ = panels[0].shape
    tile = cells // 2
    return pl.pallas_call(
        gram_kernel,
        grid=(cells // tile,),
        in_specs=[pl.BlockSpec((planes, tile, LANES), lambda i: (0, i, 0))] * len(panels),
        out_specs=pl.BlockSpec((LANES, len(panels) * LANES), lambda i: (0, 0)),
        out_shape=jax.ShapeDtypeStruct((LANES, len(panels) * LANES), jnp.float32),
        compiler_params=params(16),
        cost_estimate=cost(8 * panels[0].size * LANES * len(panels), 4 * panels[0].size * len(panels)),
    )(*panels)


def rotate_kernel(chunks, bands, inverse_ref, *rest):
    panels, out_ref = rest[:-1], rest[-1]
    right = side_by_side(inverse_ref[...].T)
    for index, (begin, size) in enumerate(chunks):
        group = panels[index * bands : (index + 1) * bands]
        for plane in range(size):
            left = halves(jnp.concatenate([panel[plane] for panel in group], axis=1))
            out_ref[begin + plane] = folded(dot_halves(left, right))


def rotated(inverse_rows, panels, chunks):
    bands = len(panels[0])
    planes = sum(size for _, size in chunks)
    cells = panels[0][0].shape[1]
    tile = cells // 6
    specs = [pl.BlockSpec((size, tile, LANES), lambda i: (0, i, 0)) for _, size in chunks for _ in range(bands)]
    return pl.pallas_call(
        functools.partial(rotate_kernel, chunks, bands),
        grid=(cells // tile,),
        in_specs=[pl.BlockSpec(inverse_rows.shape, lambda i: (0, 0)), *specs],
        out_specs=pl.BlockSpec((planes, tile, LANES), lambda i: (0, i, 0)),
        out_shape=jax.ShapeDtypeStruct((planes, cells, LANES), jnp.float32),
        compiler_params=params(56),
    )(inverse_rows, *[panel for group in panels for panel in group])


def thirds(value):
    first = value.astype(jnp.bfloat16).astype(jnp.float32)
    rest = value - first
    second = rest.astype(jnp.bfloat16).astype(jnp.float32)
    return first, second, rest - second


def eliminate(work, result):
    sublane = lax.broadcasted_iota(jnp.int32, (GROUP, LANES), 0)

    def splat(row, column):
        return jnp.broadcast_to(row[:, column : column + 1], (GROUP, LANES))

    def load(top):
        left = [jnp.broadcast_to(work[pl.ds(top + i, 1), :LANES], (GROUP, LANES)) for i in range(GROUP)]
        right = [jnp.broadcast_to(work[pl.ds(top + i, 1), LANES:], (GROUP, LANES)) for i in range(GROUP)]
        return left, right

    def factored(top, left, right):
        entry = {(i, j): splat(left[i], top + j) for i in range(GROUP) for j in range(i, GROUP)}
        for i in range(GROUP):
            scale = lax.rsqrt(entry[i, i])
            left[i] = left[i] * scale
            right[i] = right[i] * scale
            factor = {j: entry[i, j] * scale for j in range(i + 1, GROUP)}
            for m in range(i + 1, GROUP):
                for j in range(m, GROUP):
                    entry[m, j] = entry[m, j] - factor[m] * factor[j]
                left[m] = left[m] - factor[m] * left[i]
                right[m] = right[m] - factor[m] * right[i]

    def gathered(rows):
        value = rows[0]
        for i in range(1, GROUP):
            value = jnp.where(sublane == i, rows[i], value)
        return value

    for top in range(0, LANES, 2 * GROUP):
        left, right = load(top)
        factored(top, left, right)
        middle = top + GROUP
        next_left, next_right = load(middle)
        for m in range(GROUP):
            for i in range(GROUP):
                factor = splat(left[i], middle + m)
                next_left[m] = next_left[m] - factor * left[i]
                next_right[m] = next_right[m] - factor * right[i]
        factored(middle, next_left, next_right)
        upper = jnp.concatenate([gathered(left), gathered(next_left)], axis=0)
        lower = jnp.concatenate([gathered(right), gathered(next_right)], axis=0)
        result[pl.ds(top, 2 * GROUP), :] = lower
        below = middle + GROUP
        if below < LANES:
            a, b, c = thirds(upper)
            x, y, z = thirds(lower)
            columns = jnp.concatenate([a, a, b, b, a, c], axis=0).T[below:].astype(jnp.bfloat16)
            rows = jnp.concatenate(
                [jnp.concatenate([a, b, a, b, c, a], axis=0), jnp.concatenate([x, y, x, y, z, x], axis=0)], axis=1
            ).astype(jnp.bfloat16)
            rest = pl.ds(below, LANES - below)
            work[rest, :] = work[rest, :] - jnp.dot(columns, rows, preferred_element_type=jnp.float32)


def cholesky_kernel(band_ref, *refs):
    rows_refs, (gram_ref, own_ref, matrix, work, corner, scaled) = refs[:-6], refs[-6:]
    size = gram_ref.shape[0]
    bands = len(rows_refs)
    band = band_ref[0]

    def block_of(member):
        return pl.ds(pl.multiple_of((band ^ member) * LANES, LANES), LANES)

    for member, rows_ref in enumerate(rows_refs):
        for other in range(bands):
            gram_ref[block_of(member), block_of(member ^ other)] = rows_ref[:, other * LANES : (other + 1) * LANES]
    dot = functools.partial(jnp.dot, precision=HIGHEST, preferred_element_type=jnp.float32)
    diagonal = lax.broadcasted_iota(jnp.int32, (LANES, LANES), 0) == lax.broadcasted_iota(jnp.int32, (LANES, LANES), 1)
    identity = diagonal.astype(jnp.float32)
    matrix[:, :size] = gram_ref[...]
    matrix[:, size:] = jnp.zeros((size, size), jnp.float32)
    for at in range(0, size, LANES):
        matrix[pl.ds(at, LANES), size + at : size + at + LANES] = identity

    def block(index, carry):
        start = pl.multiple_of(index * LANES, LANES)
        at = pl.ds(start, LANES)
        live = pl.ds(pl.multiple_of(start + LANES, LANES), size)
        work[:, :LANES] = matrix[at, at]
        work[:, LANES:] = identity
        eliminate(work, corner)
        scaled[...] = dot(corner[...], matrix[at, live])
        matrix[at, live] = scaled[...]

        def below(other, carry):
            rows = pl.ds(pl.multiple_of(other * LANES, LANES), LANES)
            columns = pl.ds(pl.multiple_of((other - index - 1) * LANES, LANES), LANES)
            matrix[rows, live] = matrix[rows, live] - dot(scaled[:, columns].T, scaled[...])
            return carry

        lax.fori_loop(index + 1, size // LANES, below, 0)
        return carry

    lax.fori_loop(0, size // LANES, block, 0)
    for member in range(bands):
        columns = pl.ds(pl.multiple_of(size + (band ^ member) * LANES, LANES), LANES)
        own_ref[:, member * LANES : (member + 1) * LANES] = matrix[block_of(0), columns]


def cholesky_inverse(band, rows):
    size = rows[0].shape[1]
    return pl.pallas_call(
        cholesky_kernel,
        in_specs=[pl.BlockSpec(memory_space=pltpu.SMEM)] + [WHOLE] * len(rows),
        out_specs=[WHOLE] * 2,
        out_shape=[
            jax.ShapeDtypeStruct((size, size), jnp.float32),
            jax.ShapeDtypeStruct((LANES, size), jnp.float32),
        ],
        scratch_shapes=[
            pltpu.VMEM((size, 2 * size), jnp.float32),
            pltpu.VMEM((LANES, 2 * LANES), jnp.float32),
            pltpu.VMEM((LANES, LANES), jnp.float32),
            pltpu.VMEM((LANES, size), jnp.float32),
        ],
        compiler_params=params(14),
    )(band.astype(jnp.int32).reshape(1), *rows)


def packed_projectors(projectors, atom_plane, planes):
    share = projectors.shape[0] // lax.axis_size("band")
    first = (atom_plane - lax.axis_index("dom") * planes).astype(jnp.float32)
    first = jnp.broadcast_to(first[:, None, None], (projectors.shape[0], MAXPROJ, LANES))
    packed = jnp.concatenate([projectors, first], axis=2)
    mine = lax.dynamic_slice_in_dim(packed, lax.axis_index("band") * share, share, 0)
    return mine.reshape(share * MAXPROJ, -1)


def near_shares(mine):
    return jnp.stack([mine if step == BEFORE else shifted(mine, "dom", BEFORE - step) for step in range(NEAR)])


def near_projectors(near, planes):
    across = crossed(near, 2)
    raw = [near, crossed(near, 1), across, crossed(across, 1)]
    moved = (planes * (jnp.arange(NEAR, dtype=jnp.float32) - BEFORE))[:, None]
    first = jnp.stack([member[:, :, -1] + moved for member in raw]).reshape(1, LANES)
    return raw, jnp.broadcast_to(first, (GROUP, LANES))


def shards(orbitals, potential, projectors, coupling, atom_plane, projector_count):
    planes, side_y, side_z, local_orbs = orbitals.shape
    blocks, bands = lax.axis_size("dom"), lax.axis_size("band")
    band = lax.axis_index("band")
    cells = side_y * side_z
    rows = cells // blocks
    width = local_orbs // blocks
    norb = local_orbs * bands
    half = planes // 2
    chunks = ((0, half), (half, half))
    tie = lax.optimization_barrier
    me = lax.axis_index("dom").astype(jnp.int32).reshape(1)

    order = jnp.arange(bands, dtype=jnp.int32) ^ band

    mine = packed_projectors(projectors, atom_plane, planes)
    mine, levels = lax.optimization_barrier((mine, potential.reshape(planes, cells // LANES, LANES)))
    near = near_shares(mine)
    levels = jnp.pad(levels, ((0, 0), (0, -levels.shape[1] % GROUP), (0, 0)))
    packed = swap_in(levels, orbitals.reshape(planes, blocks, rows, local_orbs))
    packed, near = lax.optimization_barrier((packed, near))
    raw, first = near_projectors(near, planes)
    arrived = lax.all_to_all(packed, "dom", 0, 0, tiled=True)

    own_levels = jnp.broadcast_to(potential.reshape(planes, cells, 1), (planes, cells, LANES))
    high, low, parts = build_basis(raw, first, own_levels, orbitals.reshape(planes, cells, LANES), side_y, side_z)
    atoms = projectors.shape[0]
    slots = jnp.arange(MAXPROJ, dtype=jnp.int32)
    live = (slots[None, :] < projector_count[:, None]).astype(jnp.float32)
    coupled = 0.5 * (coupling + jnp.transpose(coupling, (0, 2, 1))) * live[:, :, None] * live[:, None, :]
    coupled = jnp.take(coupled.reshape(bands, -1, MAXPROJ, MAXPROJ), order, axis=0)
    vectors = atoms * MAXPROJ
    row = jnp.arange(vectors, dtype=jnp.int32) // MAXPROJ
    matrix = jnp.tile(coupled.reshape(vectors, MAXPROJ), (1, atoms))
    matrix = jnp.where(row[:, None] == row[None, :], matrix, 0.0)
    matrix = jnp.pad(matrix, ((0, 0), (0, LANES - vectors)))
    payload = jnp.concatenate([parts.reshape(3 * LANES, LANES), matrix], axis=0)
    everyone = lax.all_gather(payload, "dom")
    weights = near_weights(
        me,
        everyone[:, : 3 * LANES].reshape(blocks, 3, LANES, LANES), everyone[:, 3 * LANES :, :vectors],
    )

    early, late = filter_orbitals(me, arrived, side_y, side_z, width, half)

    came = exchanged(early)
    added = spread(high, low, weights)
    late, came, added = tie((late, came, added))
    coming = lax.all_to_all(late, "dom", 0, 0, tiled=True)
    own = swap_out(me, came, added, 0)
    across, beside = crossed(own, 2), crossed(own, 1)
    last = swap_out(me, [coming], added, half)
    across, last = tie((across, last))
    panels = [[own, beside, across, crossed(across, 1)]]
    part = gram_rows(panels[0])
    across, beside = crossed(last, 2), crossed(last, 1)
    across, part = tie((across, part))
    panels.append([last, beside, across, crossed(across, 1)])
    part = part + gram_rows(panels[1])

    pieces = lax.all_to_all(part.reshape(blocks, width, norb), "dom", 0, 0, tiled=True)
    piece = jnp.sum(pieces, axis=0) * (1.0 / (planes * cells * blocks))
    own_gram = lax.all_to_all(jnp.broadcast_to(piece, (blocks, width, norb)), "dom", 0, 0, tiled=True)
    own_gram = own_gram.reshape(local_orbs, norb)
    across = crossed(own_gram, 2)
    gram, own_rows = cholesky_inverse(band, [own_gram, crossed(own_gram, 1), across, crossed(across, 1)])
    result = rotated(own_rows, panels, chunks)
    return (result.reshape(planes, side_y, side_z, local_orbs), gram)


def solution(mesh):
    placed = (
        P("dom", None, None, "band"),
        P("dom", None, None),
        P("dom", None, None),
        P("dom", None, None),
        P("dom"),
        P("dom"),
    )
    return jax.shard_map(
        shards,
        mesh=mesh,
        in_specs=placed,
        out_specs=(P("dom", None, None, "band"), P()),
        check_vma=False,
    )
```

```python
import functools

import jax
import jax.numpy as jnp
from jax import lax
from jax.experimental import pallas as pl
from jax.experimental.pallas import tpu as pltpu
from jax.sharding import PartitionSpec as P

SPAN = 3
MAXPROJ = 4
HALO = 4
PAD = 8
LANES = 128
GROUP = 8
BEFORE, AFTER = 2, 1
NEAR = BEFORE + 1 + AFTER

center_weight = -205.0 / 72.0
side_weights = (8.0 / 5.0, -1.0 / 5.0, 8.0 / 315.0, -1.0 / 560.0)
HIGHEST = lax.Precision.HIGHEST
WHOLE = pl.BlockSpec(memory_space=pltpu.VMEM)


def params(mebibytes):
    return pltpu.CompilerParams(vmem_limit_bytes=mebibytes * 1024 * 1024)


def cost(flops, bytes_accessed):
    return pl.CostEstimate(flops=int(flops), bytes_accessed=int(bytes_accessed), transcendentals=0)


def halves(value):
    high = value.astype(jnp.bfloat16)
    return high, (value - high.astype(jnp.float32)).astype(jnp.bfloat16)


def side_by_side(value):
    return jnp.concatenate(halves(value), axis=1)


def dot_halves(left, right):
    dot = functools.partial(jnp.dot, preferred_element_type=jnp.float32)
    return dot(left[0], right) + dot(left[1], right)


def folded(value):
    return value[:, :LANES] + value[:, LANES:]


def swapped(blocks, lane, before=None, after=None):
    count = len(blocks)
    width = LANES // count

    def turned(value, at, extra):
        if extra is None:
            return pltpu.roll(value, at % count * width, 1) if at else value
        return pltpu.roll(value, lax.rem((at % count + extra) * width, LANES), 1)

    blocks = [turned(value, at, None if before is None else count - before) for at, value in enumerate(blocks)]
    bit = 1
    while bit < count:
        chosen = (lane // (bit * width)) % 2 == 1
        blocks = [jnp.where(chosen, blocks[(at + bit) % count], blocks[at]) for at in range(count)]
        bit *= 2
    return [turned(blocks[-at % count], -at, after) for at in range(count)]


def swap_into(read, write, count, rows, before=None, after=None):
    tile = 8 * max(1, 32 // count)
    lane = lax.broadcasted_iota(jnp.int32, (tile, LANES), 1)

    def step(index, carry):
        start = pl.multiple_of(index * tile, 8)
        blocks = [read(block, start, tile) for block in range(count)]
        for block, value in enumerate(swapped(blocks, lane, before, after)):
            write(block, start, tile, value)
        return carry

    lax.fori_loop(0, rows // tile, step, 0, unroll=True)


def swap_in_kernel(count, rows, levels_ref, in_ref, out_ref):
    def read(block, start, size):
        return in_ref[block, pl.ds(start, size), :]

    def write(block, start, size, value):
        out_ref[block, pl.ds(start, size), :] = value

    swap_into(read, write, count, rows)
    for block in range(count):
        out_ref[block, pl.ds(rows, levels_ref.shape[0]), :] = levels_ref[...]


def swap_in(levels, value):
    planes, count, rows, _ = value.shape
    extra = levels.shape[1]
    return pl.pallas_call(
        functools.partial(swap_in_kernel, count, rows),
        grid=(planes,),
        in_specs=[
            pl.BlockSpec((None, extra, LANES), lambda p: (p, 0, 0)),
            pl.BlockSpec((None, count, rows, LANES), lambda p: (p, 0, 0, 0)),
        ],
        out_specs=pl.BlockSpec((count, None, rows + extra, LANES), lambda p: (0, p, 0, 0)),
        out_shape=jax.ShapeDtypeStruct((count, planes, rows + extra, LANES), jnp.float32),
        compiler_params=params(12),
        cost_estimate=cost(0, 8 * value.size),
    )(levels, value)


def swap_out_kernel(planes, count, me_ref, added_ref, *refs):
    arrived_refs, out_ref = refs[:-1], refs[-1]
    rows = arrived_refs[0].shape[-2]
    by_steps = len(arrived_refs) > 1
    for plane in range(planes):

        def read(block, start, size):
            if by_steps:
                return arrived_refs[-block % count][plane, pl.ds(start, size), :]
            return arrived_refs[0][block, plane, pl.ds(start, size), :]

        def write(block, start, size, value):
            at = pl.ds(pl.multiple_of(block * rows + start, 8), size)
            out_ref[plane, at, :] = value + added_ref[plane, at, :]

        swap_into(read, write, count, rows, after=me_ref[0] if by_steps else None)


def swap_out(me, arrived, added, first_plane):
    count = len(arrived) if len(arrived) > 1 else arrived[0].shape[0]
    planes, rows = arrived[0].shape[-3:-1]
    cells = count * rows
    return pl.pallas_call(
        functools.partial(swap_out_kernel, planes, count),
        grid=(1,),
        in_specs=[
            pl.BlockSpec(memory_space=pltpu.SMEM),
            pl.BlockSpec((planes, cells, LANES), lambda i: (first_plane // planes, 0, 0)),
        ]
        + [pl.BlockSpec(arrived[0].shape, lambda i: (0,) * arrived[0].ndim)] * len(arrived),
        out_specs=pl.BlockSpec((planes, cells, LANES), lambda i: (0, 0, 0)),
        out_shape=jax.ShapeDtypeStruct((planes, cells, LANES), jnp.float32),
        compiler_params=params(24),
        cost_estimate=cost(0, 24 * cells * planes * LANES),
    )(me, added, *arrived)


def spread_kernel(high_ref, low_ref, weights_ref, out_ref):
    weights = side_by_side(weights_ref[...] * (1.0 / 18.0))
    tile = out_ref.shape[0] // 6

    def step(index, carry):
        at = pl.ds(pl.multiple_of(index * tile, 8), tile)
        out_ref[at, :] = folded(dot_halves((high_ref[at, :], low_ref[at, :]), weights))
        return carry

    lax.fori_loop(0, 6, step, 0)


def spread(high, low, weights):
    planes, cells, _ = high.shape
    basis = pl.BlockSpec((None, cells, 2 * LANES), lambda i: (i, 0, 0))
    return pl.pallas_call(
        spread_kernel,
        grid=(planes,),
        in_specs=[basis, basis, pl.BlockSpec(weights.shape, lambda i: (0, 0))],
        out_specs=pl.BlockSpec((None, cells, LANES), lambda i: (i, 0, 0)),
        out_shape=jax.ShapeDtypeStruct((planes, cells, LANES), jnp.float32),
        compiler_params=params(24),
        cost_estimate=cost(0, 8 * high.size),
    )(high, low, weights)


def fill_row(target, plane, y, row, side_z):
    target[plane, y, pl.ds(PAD, side_z), :] = row
    target[plane, y, pl.ds(PAD - HALO, HALO), :] = row[side_z - HALO :]
    target[plane, y, pl.ds(PAD + side_z, HALO), :] = row[:HALO]


def local_part(source, potential_ref, planes, first, side_y, side_z, line_of, finish):
    tile = 16

    def row(y, carry):
        for start in range(0, side_z, tile):

            def load(plane, y_at, shift):
                return source[plane, y_at, pl.ds(PAD + start + shift, tile), :]

            line = line_of(lambda plane: load(plane, y, 0))
            at = pl.ds(pl.multiple_of(y * side_z + start, 8), tile)
            for plane in range(planes):
                here = first + plane
                total = (potential_ref[plane, at, :] - 1.5 * center_weight - 7.0) * line[HALO + plane]
                for offset in range(1, HALO + 1):
                    around = line[HALO + plane + offset] + line[HALO + plane - offset]
                    around = around + (load(here, y, offset) + load(here, y, -offset))
                    up = lax.rem(y + offset, side_y)
                    down = lax.rem(y + side_y - offset, side_y)
                    around = around + (load(here, up, 0) + load(here, down, 0))
                    total = total - (0.5 * side_weights[offset - 1]) * around
                finish(plane, y, start, at, total)
        return carry

    lax.fori_loop(0, side_y, row, 0)


def filter_kernel(planes, side_y, side_z, width, half, me_ref, arrived_ref, *rest):
    near_refs, late_ref, (field, padded, first, flat, potential) = rest[:-6], rest[-6], rest[-5:]
    count = arrived_ref.shape[0]
    cells = side_y * side_z
    rows = cells // count
    tile = 16

    line = lax.broadcasted_iota(jnp.int32, (2 * count, LANES), 0) % count
    lane = lax.broadcasted_iota(jnp.int32, (2 * count, LANES), 1) // width
    spread = (line == lane).astype(jnp.bfloat16)
    for plane in range(planes):
        lines = [arrived_ref[:, plane, rows + at, :] for at in range(cells // LANES)]
        high, low = halves(jnp.concatenate(lines, axis=1))
        both = jnp.concatenate([high.astype(jnp.float32), low.astype(jnp.float32)], axis=0)
        potential[plane] = jnp.dot(both.T.astype(jnp.bfloat16), spread, preferred_element_type=jnp.float32)

    for plane in range(planes):

        def read_in(block, start, size):
            return arrived_ref[block, plane, pl.ds(start, size), :]

        def write_in(block, start, size, value):
            field[plane, pl.ds(pl.multiple_of(block * rows + start, 8), size), :] = value

        swap_into(read_in, write_in, count, rows)

    def fill(y, carry):
        for plane in range(planes):
            fill_row(padded, plane, y, field[plane, pl.ds(pl.multiple_of(y * side_z, 8), side_z), :], side_z)
        return carry

    lax.fori_loop(0, side_y, fill, 0)

    def line_of(load):
        inside = [load(plane) for plane in range(planes)]
        before = [pltpu.roll(value, width, 1) for value in inside]
        after = [pltpu.roll(value, LANES - width, 1) for value in inside]
        return before[planes - HALO :] + inside + after[:HALO]

    def finish_first(plane, y, start, at, total):
        first[plane, y, pl.ds(PAD + start, tile), :] = total
        if start == 0:
            first[plane, y, pl.ds(PAD + side_z, HALO), :] = total[:HALO]
        if start == side_z - tile:
            first[plane, y, pl.ds(PAD - HALO, HALO), :] = total[tile - HALO :]

    def finish_second(plane, y, start, at, total):
        flat[plane, at, :] = total * (1.0 / 18.0) - field[plane, at, :]

    local_part(padded, potential, planes, 0, side_y, side_z, line_of, finish_first)
    local_part(first, potential, planes, 0, side_y, side_z, line_of, finish_second)

    for plane in range(planes):

        def read_out(block, start, size):
            return flat[plane, pl.ds(pl.multiple_of(block * rows + start, 8), size), :]

        def write_out(block, start, size, value):
            if plane < half:
                near_refs[block][plane, pl.ds(start, size), :] = value
            else:
                late_ref[block, plane - half, pl.ds(start, size), :] = value

        swap_into(read_out, write_out, count, rows, before=me_ref[0] if plane < half else None)


def filter_orbitals(me, arrived, side_y, side_z, width, half):
    count, planes = arrived.shape[:2]
    rows = side_y * side_z // count
    flat = pltpu.VMEM((planes, side_y * side_z, LANES), jnp.float32)
    padded = pltpu.VMEM((planes, side_y, side_z + 2 * PAD, LANES), jnp.float32)
    shapes = [jax.ShapeDtypeStruct((half, rows, LANES), jnp.float32)] * count
    shapes += [jax.ShapeDtypeStruct((count, planes - half, rows, LANES), jnp.float32)]
    outs = pl.pallas_call(
        functools.partial(filter_kernel, planes, side_y, side_z, width, half),
        in_specs=[pl.BlockSpec(memory_space=pltpu.SMEM), WHOLE],
        out_specs=[WHOLE] * len(shapes),
        out_shape=shapes,
        scratch_shapes=[flat, padded, padded, flat, flat],
        compiler_params=params(56),
        cost_estimate=cost(100 * arrived.size, 12 * arrived.size),
    )(me, arrived)
    return list(outs[:count]), outs[count]


def basis_kernel(planes, side_y, side_z, bands, *refs):
    raw_refs = refs[:bands]
    offset_ref, potential_ref, orbitals_ref, high_ref, low_ref, parts_ref, turned, placed = refs[bands:]
    cells = side_y * side_z
    for part in range(SPAN):
        at = pl.ds(part * cells, cells)
        stack = [raw_ref[block, :, at] for raw_ref in raw_refs for block in range(NEAR)]
        turned[part] = jnp.concatenate(stack, axis=0).T
    offset = offset_ref[0:1, :]

    def place(y, carry):
        at = pl.ds(pl.multiple_of(y * side_z, 8), side_z)
        values = [turned[part, at, :] for part in range(SPAN)]
        for plane in range(planes + 2 * HALO):
            row = jnp.zeros((side_z, LANES), jnp.float32)
            for part in range(SPAN):
                row = jnp.where(offset == float(plane - HALO - part), values[part], row)
            fill_row(placed, plane, y, row, side_z)
        return carry

    lax.fori_loop(0, side_y, place, 0)

    def line_of(load):
        return [load(plane) for plane in range(planes + 2 * HALO)]

    def finish(plane, y, start, at, total):
        own = placed[HALO + plane, y, pl.ds(PAD + start, 16), :]
        high, low = halves(jnp.concatenate([total, own], axis=1))
        high_ref[plane, at, :] = high
        low_ref[plane, at, :] = low

    local_part(placed, potential_ref, planes, HALO, side_y, side_z, line_of, finish)

    dot = functools.partial(jnp.dot, preferred_element_type=jnp.float32)
    with_orbitals = with_basis = 0.0
    for plane in range(planes):
        high, low = high_ref[plane], low_ref[plane]
        left = halves(orbitals_ref[plane].T)
        with_orbitals = with_orbitals + (dot(left[0], high) + (dot(left[0], low) + dot(left[1], high)))
        own_high, own_low = high[:, LANES:], low[:, LANES:]
        turned_high = own_high.astype(jnp.float32).T.astype(jnp.bfloat16)
        turned_low = own_low.astype(jnp.float32).T.astype(jnp.bfloat16)
        both = jnp.concatenate([own_high, own_low], axis=1)
        with_basis = with_basis + (dot(turned_high, both) + dot(turned_low, both))
    parts_ref[0] = with_orbitals[:, LANES:].T
    parts_ref[1] = with_orbitals[:, :LANES].T
    parts_ref[2] = folded(with_basis)


def build_basis(raw, offset, potential, orbitals, side_y, side_z):
    planes, cells, _ = orbitals.shape
    pair = jax.ShapeDtypeStruct((planes, cells, 2 * LANES), jnp.bfloat16)
    return pl.pallas_call(
        functools.partial(basis_kernel, planes, side_y, side_z, len(raw)),
        in_specs=[WHOLE] * (len(raw) + 3),
        out_specs=[WHOLE] * 3,
        out_shape=[pair, pair, jax.ShapeDtypeStruct((3, LANES, LANES), jnp.float32)],
        scratch_shapes=[
            pltpu.VMEM((SPAN, cells, LANES), jnp.float32),
            pltpu.VMEM((planes + 2 * HALO, side_y, side_z + 2 * PAD, LANES), jnp.float32),
        ],
        compiler_params=params(56),
        cost_estimate=cost(200 * orbitals.size, 24 * orbitals.size),
    )(*raw, offset, potential, orbitals)


def weights_kernel(bands, me_ref, parts_ref, coupling_ref, out_ref):
    count = parts_ref.shape[0]
    size = LANES // NEAR
    lines = size // bands
    me = me_ref[0]
    dot = functools.partial(jnp.dot, precision=HIGHEST, preferred_element_type=jnp.float32)

    def device(step):
        return lax.rem(me + step % count, count)

    def total(pick, block):
        shares = [pick(block - (near - BEFORE), near) for near in range(NEAR)]
        return (shares[0] + shares[1]) + (shares[2] + shares[3])

    def of_block(value, near):
        starts = [(band * NEAR + near) * lines for band in range(bands)]
        return jnp.concatenate([value[start : start + lines] for start in starts], axis=0)

    def joined(values):
        return jnp.concatenate(
            [values[near][band * lines : (band + 1) * lines] for band in range(bands) for near in range(NEAR)], axis=0
        )

    def couple(block, value):
        return dot(coupling_ref[device(block)], value)

    def kept(function):
        known = {}

        def look(step):
            if step % count not in known:
                known[step % count] = function(step)
            return known[step % count]

        return look

    weight = kept(
        lambda block: couple(block, total(lambda step, near: of_block(parts_ref[device(step), 0], near), block))
    )
    weights = kept(lambda step: joined([weight(step + near - BEFORE) for near in range(NEAR)]))
    second = kept(lambda step: parts_ref[device(step), 1] + dot(parts_ref[device(step), 2], weights(step)))
    out_ref[pl.ds(0, LANES), :] = weights(0)
    out_ref[pl.ds(LANES, LANES), :] = joined(
        [
            couple(near - BEFORE, total(lambda step, at: of_block(second(step), at), near - BEFORE))
            for near in range(NEAR)
        ]
    )


def near_weights(me, parts, coupling):
    return pl.pallas_call(
        functools.partial(weights_kernel, lax.axis_size("band")),
        in_specs=[pl.BlockSpec(memory_space=pltpu.SMEM), WHOLE, WHOLE],
        out_specs=WHOLE,
        out_shape=jax.ShapeDtypeStruct((2 * LANES, LANES), jnp.float32),
        compiler_params=params(24),
        cost_estimate=cost(0, 8 * parts.size),
    )(me, parts, coupling)


def shifted(value, axis, step):
    count = lax.axis_size(axis)
    return lax.ppermute(value, axis, [(source, (source + step) % count) for source in range(count)])


def exchanged(values):
    return [shifted(value, "dom", step) if step else value for step, value in enumerate(values)]


def crossed(value, bit):
    return lax.ppermute(value, "band", [(source, source ^ bit) for source in range(lax.axis_size("band"))])


def gram_kernel(own_ref, *rest):
    panels, out_ref = (own_ref, *rest[:-1]), rest[-1]

    @pl.when(pl.program_id(0) == 0)
    def _():
        out_ref[...] = jnp.zeros_like(out_ref)

    for plane in range(own_ref.shape[0]):
        left = halves(own_ref[plane].T)
        both = jnp.concatenate([side_by_side(panel[plane]) for panel in panels], axis=1)
        value = dot_halves(left, both)
        for index in range(len(panels)):
            at = pl.ds(index * LANES, LANES)
            out_ref[:, at] = out_ref[:, at] + folded(value[:, 2 * index * LANES : 2 * (index + 1) * LANES])


def gram_rows(panels):
    planes, cells, _ = panels[0].shape
    tile = cells // 2
    return pl.pallas_call(
        gram_kernel,
        grid=(cells // tile,),
        in_specs=[pl.BlockSpec((planes, tile, LANES), lambda i: (0, i, 0))] * len(panels),
        out_specs=pl.BlockSpec((LANES, len(panels) * LANES), lambda i: (0, 0)),
        out_shape=jax.ShapeDtypeStruct((LANES, len(panels) * LANES), jnp.float32),
        compiler_params=params(16),
        cost_estimate=cost(8 * panels[0].size * LANES * len(panels), 4 * panels[0].size * len(panels)),
    )(*panels)


def rotate_kernel(chunks, bands, inverse_ref, *rest):
    panels, out_ref = rest[:-1], rest[-1]
    right = side_by_side(inverse_ref[...].T)
    for index, (begin, size) in enumerate(chunks):
        group = panels[index * bands : (index + 1) * bands]
        for plane in range(size):
            left = halves(jnp.concatenate([panel[plane] for panel in group], axis=1))
            out_ref[begin + plane] = folded(dot_halves(left, right))


def rotated(inverse_rows, panels, chunks):
    bands = len(panels[0])
    planes = sum(size for _, size in chunks)
    cells = panels[0][0].shape[1]
    tile = cells // 4
    specs = [pl.BlockSpec((size, tile, LANES), lambda i: (0, i, 0)) for _, size in chunks for _ in range(bands)]
    return pl.pallas_call(
        functools.partial(rotate_kernel, chunks, bands),
        grid=(cells // tile,),
        in_specs=[pl.BlockSpec(inverse_rows.shape, lambda i: (0, 0)), *specs],
        out_specs=pl.BlockSpec((planes, tile, LANES), lambda i: (0, i, 0)),
        out_shape=jax.ShapeDtypeStruct((planes, cells, LANES), jnp.float32),
        compiler_params=params(56),
    )(inverse_rows, *[panel for group in panels for panel in group])


def thirds(value):
    first = value.astype(jnp.bfloat16).astype(jnp.float32)
    rest = value - first
    second = rest.astype(jnp.bfloat16).astype(jnp.float32)
    return first, second, rest - second


def eliminate(work, result):
    sublane = lax.broadcasted_iota(jnp.int32, (GROUP, LANES), 0)

    def splat(row, column):
        return jnp.broadcast_to(row[:, column : column + 1], (GROUP, LANES))

    def load(top):
        left = [jnp.broadcast_to(work[pl.ds(top + i, 1), :LANES], (GROUP, LANES)) for i in range(GROUP)]
        right = [jnp.broadcast_to(work[pl.ds(top + i, 1), LANES:], (GROUP, LANES)) for i in range(GROUP)]
        return left, right

    def factored(top, left, right):
        entry = {(i, j): splat(left[i], top + j) for i in range(GROUP) for j in range(i, GROUP)}
        for i in range(GROUP):
            scale = lax.rsqrt(entry[i, i])
            left[i] = left[i] * scale
            right[i] = right[i] * scale
            factor = {j: entry[i, j] * scale for j in range(i + 1, GROUP)}
            for m in range(i + 1, GROUP):
                for j in range(m, GROUP):
                    entry[m, j] = entry[m, j] - factor[m] * factor[j]
                left[m] = left[m] - factor[m] * left[i]
                right[m] = right[m] - factor[m] * right[i]

    def gathered(rows):
        value = rows[0]
        for i in range(1, GROUP):
            value = jnp.where(sublane == i, rows[i], value)
        return value

    for top in range(0, LANES, 2 * GROUP):
        left, right = load(top)
        factored(top, left, right)
        middle = top + GROUP
        next_left, next_right = load(middle)
        for m in range(GROUP):
            for i in range(GROUP):
                factor = splat(left[i], middle + m)
                next_left[m] = next_left[m] - factor * left[i]
                next_right[m] = next_right[m] - factor * right[i]
        factored(middle, next_left, next_right)
        upper = jnp.concatenate([gathered(left), gathered(next_left)], axis=0)
        lower = jnp.concatenate([gathered(right), gathered(next_right)], axis=0)
        result[pl.ds(top, 2 * GROUP), :] = lower
        below = middle + GROUP
        if below < LANES:
            a, b, c = thirds(upper)
            x, y, z = thirds(lower)
            columns = jnp.concatenate([a, a, b, b, a, c], axis=0).T[below:].astype(jnp.bfloat16)
            rows = jnp.concatenate(
                [jnp.concatenate([a, b, a, b, c, a], axis=0), jnp.concatenate([x, y, x, y, z, x], axis=0)], axis=1
            ).astype(jnp.bfloat16)
            rest = pl.ds(below, LANES - below)
            work[rest, :] = work[rest, :] - jnp.dot(columns, rows, preferred_element_type=jnp.float32)


def cholesky_kernel(band_ref, *refs):
    rows_refs, (gram_ref, own_ref, matrix, work, corner, scaled) = refs[:-6], refs[-6:]
    size = gram_ref.shape[0]
    bands = len(rows_refs)
    band = band_ref[0]

    def block_of(member):
        return pl.ds(pl.multiple_of((band ^ member) * LANES, LANES), LANES)

    for member, rows_ref in enumerate(rows_refs):
        for other in range(bands):
            gram_ref[block_of(member), block_of(member ^ other)] = rows_ref[:, other * LANES : (other + 1) * LANES]
    dot = functools.partial(jnp.dot, precision=HIGHEST, preferred_element_type=jnp.float32)
    diagonal = lax.broadcasted_iota(jnp.int32, (LANES, LANES), 0) == lax.broadcasted_iota(jnp.int32, (LANES, LANES), 1)
    identity = diagonal.astype(jnp.float32)
    matrix[:, :size] = gram_ref[...]
    matrix[:, size:] = jnp.zeros((size, size), jnp.float32)
    for at in range(0, size, LANES):
        matrix[pl.ds(at, LANES), size + at : size + at + LANES] = identity

    def block(index, carry):
        start = pl.multiple_of(index * LANES, LANES)
        at = pl.ds(start, LANES)
        live = pl.ds(pl.multiple_of(start + LANES, LANES), size)
        work[:, :LANES] = matrix[at, at]
        work[:, LANES:] = identity
        eliminate(work, corner)
        scaled[...] = dot(corner[...], matrix[at, live])
        matrix[at, live] = scaled[...]

        def below(other, carry):
            rows = pl.ds(pl.multiple_of(other * LANES, LANES), LANES)
            columns = pl.ds(pl.multiple_of((other - index - 1) * LANES, LANES), LANES)
            matrix[rows, live] = matrix[rows, live] - dot(scaled[:, columns].T, scaled[...])
            return carry

        lax.fori_loop(index + 1, size // LANES, below, 0)
        return carry

    lax.fori_loop(0, size // LANES, block, 0)
    for member in range(bands):
        columns = pl.ds(pl.multiple_of(size + (band ^ member) * LANES, LANES), LANES)
        own_ref[:, member * LANES : (member + 1) * LANES] = matrix[block_of(0), columns]


def cholesky_inverse(band, rows):
    size = rows[0].shape[1]
    return pl.pallas_call(
        cholesky_kernel,
        in_specs=[pl.BlockSpec(memory_space=pltpu.SMEM)] + [WHOLE] * len(rows),
        out_specs=[WHOLE] * 2,
        out_shape=[
            jax.ShapeDtypeStruct((size, size), jnp.float32),
            jax.ShapeDtypeStruct((LANES, size), jnp.float32),
        ],
        scratch_shapes=[
            pltpu.VMEM((size, 2 * size), jnp.float32),
            pltpu.VMEM((LANES, 2 * LANES), jnp.float32),
            pltpu.VMEM((LANES, LANES), jnp.float32),
            pltpu.VMEM((LANES, size), jnp.float32),
        ],
        compiler_params=params(14),
    )(band.astype(jnp.int32).reshape(1), *rows)


def packed_projectors(projectors, atom_plane, planes):
    share = projectors.shape[0] // lax.axis_size("band")
    first = (atom_plane - lax.axis_index("dom") * planes).astype(jnp.float32)
    first = jnp.broadcast_to(first[:, None, None], (projectors.shape[0], MAXPROJ, LANES))
    packed = jnp.concatenate([projectors, first], axis=2)
    mine = lax.dynamic_slice_in_dim(packed, lax.axis_index("band") * share, share, 0)
    return mine.reshape(share * MAXPROJ, -1)


def near_shares(mine):
    return jnp.stack([mine if step == BEFORE else shifted(mine, "dom", BEFORE - step) for step in range(NEAR)])


def near_projectors(near, planes):
    across = crossed(near, 2)
    raw = [near, crossed(near, 1), across, crossed(across, 1)]
    moved = (planes * (jnp.arange(NEAR, dtype=jnp.float32) - BEFORE))[:, None]
    first = jnp.stack([member[:, :, -1] + moved for member in raw]).reshape(1, LANES)
    return raw, jnp.broadcast_to(first, (GROUP, LANES))


def shards(orbitals, potential, projectors, coupling, atom_plane, projector_count):
    planes, side_y, side_z, local_orbs = orbitals.shape
    blocks, bands = lax.axis_size("dom"), lax.axis_size("band")
    band = lax.axis_index("band")
    cells = side_y * side_z
    rows = cells // blocks
    width = local_orbs // blocks
    norb = local_orbs * bands
    half = planes // 2
    chunks = ((0, half), (half, half))
    tie = lax.optimization_barrier
    me = lax.axis_index("dom").astype(jnp.int32).reshape(1)

    order = jnp.arange(bands, dtype=jnp.int32) ^ band

    mine = packed_projectors(projectors, atom_plane, planes)
    mine, levels = lax.optimization_barrier((mine, potential.reshape(planes, cells // LANES, LANES)))
    near = near_shares(mine)
    levels = jnp.pad(levels, ((0, 0), (0, -levels.shape[1] % GROUP), (0, 0)))
    packed = swap_in(levels, orbitals.reshape(planes, blocks, rows, local_orbs))
    packed, near = lax.optimization_barrier((packed, near))
    raw, first = near_projectors(near, planes)
    arrived = lax.all_to_all(packed, "dom", 0, 0, tiled=True)

    own_levels = jnp.broadcast_to(potential.reshape(planes, cells, 1), (planes, cells, LANES))
    high, low, parts = build_basis(raw, first, own_levels, orbitals.reshape(planes, cells, LANES), side_y, side_z)
    atoms = projectors.shape[0]
    slots = jnp.arange(MAXPROJ, dtype=jnp.int32)
    live = (slots[None, :] < projector_count[:, None]).astype(jnp.float32)
    coupled = 0.5 * (coupling + jnp.transpose(coupling, (0, 2, 1))) * live[:, :, None] * live[:, None, :]
    coupled = jnp.take(coupled.reshape(bands, -1, MAXPROJ, MAXPROJ), order, axis=0)
    vectors = atoms * MAXPROJ
    row = jnp.arange(vectors, dtype=jnp.int32) // MAXPROJ
    matrix = jnp.tile(coupled.reshape(vectors, MAXPROJ), (1, atoms))
    matrix = jnp.where(row[:, None] == row[None, :], matrix, 0.0)
    matrix = jnp.pad(matrix, ((0, 0), (0, LANES - vectors)))
    payload = jnp.concatenate([parts.reshape(3 * LANES, LANES), matrix], axis=0)
    arrived, payload = tie((arrived, payload))
    everyone = lax.all_gather(payload, "dom")
    weights = near_weights(
        me,
        everyone[:, : 3 * LANES].reshape(blocks, 3, LANES, LANES), everyone[:, 3 * LANES :, :vectors],
    )

    early, late = filter_orbitals(me, arrived, side_y, side_z, width, half)

    came = exchanged(early)
    added = spread(high, low, weights)
    own = swap_out(me, came, added, 0)
    late, own = tie((late, own))
    coming = lax.all_to_all(late, "dom", 0, 0, tiled=True)
    across, beside = crossed(own, 2), crossed(own, 1)
    last = swap_out(me, [coming], added, half)
    across, last = tie((across, last))
    panels = [[own, beside, across, crossed(across, 1)]]
    part = gram_rows(panels[0])
    across, beside = crossed(last, 2), crossed(last, 1)
    across, part = tie((across, part))
    panels.append([last, beside, across, crossed(across, 1)])
    part = part + gram_rows(panels[1])

    pieces = lax.all_to_all(part.reshape(blocks, width, norb), "dom", 0, 0, tiled=True)
    piece = jnp.sum(pieces, axis=0) * (1.0 / (planes * cells * blocks))
    own_gram = lax.all_to_all(jnp.broadcast_to(piece, (blocks, width, norb)), "dom", 0, 0, tiled=True)
    own_gram = own_gram.reshape(local_orbs, norb)
    across = crossed(own_gram, 2)
    gram, own_rows = cholesky_inverse(band, [own_gram, crossed(own_gram, 1), across, crossed(across, 1)])
    result = rotated(own_rows, panels, chunks)
    return (result.reshape(planes, side_y, side_z, local_orbs), gram)


def solution(mesh):
    placed = (
        P("dom", None, None, "band"),
        P("dom", None, None),
        P("dom", None, None),
        P("dom", None, None),
        P("dom"),
        P("dom"),
    )
    return jax.shard_map(
        shards,
        mesh=mesh,
        in_specs=placed,
        out_specs=(P("dom", None, None, "band"), P()),
        check_vma=False,
    )
```
